32 devices in a mesh: dp: 16 (over z, x, core), tm: 2 (over y).
Axes of the slice: x: 2, y: 2, z: 4, core: 2. Of those that a mesh axis runs over, the one named last changes fastest.
Arguments:
- tokens: bfloat16 [16, 512, 1024], P('dp', 'tm'), may hold values from -6 to 6
- memory: bfloat16 [16, 512, 1024], P('dp', 'tm'), may hold values from -6 to 6
- compressed: bfloat16 [16, 512, 1024], P('dp', 'tm'), may hold values from -6 to 6
- mask_start: int32 [16], P('dp'), may hold values from 0 to 511, as said below
- norm1_gain: float32 [1024], replicated, may hold values from 0.5 to 1.5
- norm1_bias: float32 [1024], replicated, may hold values from -3 to 3
- query_weight: bfloat16 [1024, 1024], P('tm'), may hold values from -0.1875 to 0.1875
- key_weight: bfloat16 [1024, 1024], P('tm'), may hold values from -0.1875 to 0.1875
- value_weight: bfloat16 [1024, 1024], P('tm'), may hold values from -0.1875 to 0.1875
- out_weight: bfloat16 [1024, 1024], P('tm'), may hold values from -0.75 to 0.75
- slopes: float32 [8], replicated, may hold values from 0.002 to 0.08
- norm2_gain: float32 [1024], replicated, may hold values from 0.5 to 1.5
- norm2_bias: float32 [1024], replicated, may hold values from -3 to 3
- in_weight: bfloat16 [1024, 4096], P('tm'), may hold values from -0.1875 to 0.1875
- in_bias: float32 [4096], replicated, may hold values from -3 to 3
- hidden_weight: bfloat16 [4096, 1024], P('tm'), may hold values from -0.09375 to 0.09375
- hidden_bias: float32 [1024], replicated, may hold values from -3 to 3
- compress_weight: bfloat16 [3072, 1024], P('tm'), may hold values from -0.109375 to 0.109375
- compress_bias: float32 [1024], replicated, may hold values from -3 to 3
- grad_out: bfloat16 [16, 512, 1024], P('dp', 'tm'), may hold values from -6 to 6
- grad_compressed: bfloat16 [16, 172, 1024], P('dp', 'tm'), may hold values from -6 to 6
Outputs:
- output: bfloat16 [16, 512, 1024], P('dp', 'tm')
- new_compressed: bfloat16 [16, 172, 1024], P('dp', 'tm')
- grad_tokens: bfloat16 [16, 512, 1024], P('dp', 'tm')
- grad_norm1_gain: float32 [1024], replicated
- grad_norm1_bias: float32 [1024], replicated
- grad_query_weight: float32 [1024, 1024], P('tm', 'dp')
- grad_key_weight: float32 [1024, 1024], P('tm', 'dp')
- grad_value_weight: float32 [1024, 1024], P('tm', 'dp')
- grad_out_weight: float32 [1024, 1024], P('tm', 'dp')
- grad_slopes: float32 [8], replicated
- grad_norm2_gain: float32 [1024], replicated
- grad_norm2_bias: float32 [1024], replicated
- grad_in_weight: float32 [1024, 4096], P('tm', 'dp')
- grad_in_bias: float32 [4096], replicated
- grad_hidden_weight: float32 [4096, 1024], P('tm', 'dp')
- grad_hidden_bias: float32 [1024], replicated
- grad_compress_weight: float32 [3072, 1024], P('tm', 'dp')
- grad_compress_bias: float32 [1024], replicated
The draws below stay inside these ranges and needn't reach their ends.
Inputs may be any that keep to these rules, and one draw needn't show every extreme that they name: Some stream has mask_start 0 and some 512 - 1.
All inputs are finite; a program needn't handle non-finite values.
Results may differ from the reference program's by a relative error of at most 0.015.
Values may be sent and summed in bfloat16 or wider, within the bound.
No kernel may reach another device: no remote copies, remote signals or barrier semaphores. Data moves between devices by JAX's collectives and lax.ppermute only.
A program may use at most 256 MiB of HBM per device.

```python
import math
import jax
import jax.numpy as jnp
from jax import lax

D = 1024
HEADS = 8
FF = 4096
HD = 1024
SEG = 512
STREAMS = 16
NEWSLOTS = 172


def draw_mask_start(key, part):
    key = jax.random.fold_in(key, 11)
    draw_key, pick_key = jax.random.split(key)
    starts = jax.random.randint(draw_key, (STREAMS,), 0, SEG)
    shuffled = jax.random.permutation(pick_key, STREAMS)
    starts = starts.at[shuffled[0]].set(0)
    starts = starts.at[shuffled[1]].set(SEG - 1)
    return starts.astype(jnp.int32)


def strengthened(array, rng, source, target, shards_of, factor):
    owner, partner = [(jnp.arange(array.shape[axis_at]) // (array.shape[axis_at] // shards_of)).reshape([-1 if axis == axis_at else 1 for axis in range(array.ndim)]) for axis_at in (source, target)]
    chosen = jax.random.permutation(rng, shards_of)[partner]
    strong = (owner == chosen) | (owner == (partner + shards_of // 2) % shards_of)
    return jnp.where(strong, factor * array, array)


def steps_of(own_key, dims, shards, smallest, top_value):
    factor_of = 1.0
    for dim, shards_of in shards:
        draws = jax.random.uniform(jax.random.fold_in(jax.random.fold_in(own_key, 6), dim), (shards_of,), jnp.float32, smallest / len(shards), top_value / len(shards))
        factor_of = factor_of * jnp.repeat(jnp.exp(draws), dims[dim] // shards_of).reshape((-1,) + (1,) * (len(dims) - 1 - dim))
    return factor_of


def noise(rng, dims, width, reach, cuts=(), kind=jnp.bfloat16):
    values = jax.random.normal(rng, dims, jnp.float32) * width
    if len(cuts) > 0:
        values = steps_of(rng, dims, cuts, -0.22, 0.18) * values
    return jnp.clip(values, min=-reach, max=reach).astype(kind)


def bell_draw_with(stream_key, dims, scale, limit, cuts, heavy, held_as=jnp.bfloat16):
    result = scale * jax.random.normal(stream_key, dims, jnp.float32)
    if cuts:
        result = result * steps_of(stream_key, dims, cuts, -0.22, 0.18)
    return jnp.clip(strengthened(result, jax.random.fold_in(stream_key, 3), *heavy), -limit, limit).astype(held_as)


def setup_inputs(seed: int = 0) -> dict:
    seeds = jax.random.split(jax.random.key(seed), 22)
    return {
        "tokens": noise(seeds[0], (STREAMS, SEG, D), 1.0, 6.0, ((0, 16), (1, 2))),
        "memory": noise(seeds[1], (STREAMS, SEG, D), 1.0, 6.0, ((0, 16), (1, 2))),
        "compressed": noise(seeds[2], (STREAMS, SEG, D), 1.0, 6.0, ((0, 16), (1, 2))),
        "mask_start": draw_mask_start(jax.random.fold_in(seeds[21], 71), 0),
        "norm1_gain": jnp.clip(1.0 + 0.1 * jax.random.normal(seeds[4], (D,), jnp.float32), 0.5, 1.5),
        "norm1_bias": noise(seeds[5], (D,), 0.3, 3.0, (), jnp.float32),
        "query_weight": noise(seeds[6], (D, HD), D ** -0.5, 0.1875, ((0, 2),)),
        "key_weight": noise(seeds[7], (D, HD), D ** -0.5, 0.1875, ((0, 2),)),
        "value_weight": noise(seeds[8], (D, HD), D ** -0.5, 0.1875, ((0, 2),)),
        "out_weight": noise(seeds[9], (HD, D), (HD // 16) ** -0.5, 0.75, ((0, 2),)),
        "slopes": jnp.clip(jnp.exp(jax.random.uniform(seeds[10], (HEADS,), jnp.float32, math.log(0.002), math.log(0.08))), 0.002, 0.08),
        "norm2_gain": jnp.clip(1.0 + 0.1 * jax.random.normal(seeds[11], (D,), jnp.float32), 0.5, 1.5),
        "norm2_bias": noise(seeds[12], (D,), 0.3, 3.0, (), jnp.float32),
        "in_weight": noise(seeds[13], (D, FF), D ** -0.5, 0.1875, ((0, 2),)),
        "in_bias": noise(seeds[14], (FF,), 0.3, 3.0, (), jnp.float32),
        "hidden_weight": noise(seeds[15], (FF, D), FF ** -0.5, 0.09375, ((0, 2),)),
        "hidden_bias": noise(seeds[16], (D,), 0.3, 3.0, (), jnp.float32),
        "compress_weight": noise(seeds[17], (3 * D, D), (3 * D) ** -0.5, 0.109375, ((0, 2),)),
        "compress_bias": noise(seeds[18], (D,), 0.3, 3.0, (), jnp.float32),
        "grad_out": bell_draw_with(seeds[19], (STREAMS, SEG, D), 1.0, 6.0, ((0, 16), (1, 2)), (0, 2, 16, 2.0)),
        "grad_compressed": bell_draw_with(seeds[20], (STREAMS, NEWSLOTS, D), 1.0, 6.0, ((0, 16), (1, 2)), (0, 2, 16, 2.0)),
    }


EPS = 1e-05
NEG = -1e+30
HIGH = lax.Precision.HIGHEST

@jax.custom_vjp
def low(v):
    return lax.optimization_barrier(v.astype(jnp.bfloat16)).astype(jnp.float32)

@jax.custom_vjp
def low_back(v):
    return v

def low_keep(v):
    return (low(v), None)

def low_pass(kept, grad):
    return (grad,)

def back_keep(v):
    return (v, None)

def back_low(kept, grad):
    return (low(grad),)
low.defvjp(low_keep, low_pass)
low_back.defvjp(back_keep, back_low)

def normalize(matrix, norm_gain, norm_shift):
    row_mean = lax.optimization_barrier(jnp.mean(matrix, -1, keepdims=True))
    centered = matrix - row_mean
    spread = lax.optimization_barrier(jnp.mean(centered * centered, -1, keepdims=True))
    return centered * lax.rsqrt(spread + EPS) * norm_gain + norm_shift

def activate(pre_act):
    return jax.nn.gelu(pre_act, approximate=True)

def layout(time_index, group_size, row_count, first_slot):
    segment = group_size * row_count
    slot_index = jnp.arange(segment, dtype=jnp.int32)
    key_place = jnp.concatenate((-segment - 3 * (segment - slot_index), slot_index - segment, slot_index))
    query_place = time_index * row_count + jnp.arange(row_count, dtype=jnp.int32)
    kind_allowed = jnp.concatenate((slot_index >= first_slot, slot_index >= 0, slot_index >= 0))
    allowed = kind_allowed[None, :] & (key_place[None, :] <= query_place[:, None])
    distance = (query_place[:, None] - key_place[None, :]).astype(jnp.float32)
    return (allowed, distance)

def stream_layer(params, token_rows, memory_rows, compressed_rows, first_slot):
    norm1_gain, norm1_bias, query_weight, key_weight, value_weight, out_weight, slopes, norm2_gain, norm2_bias, in_weight, in_bias, hidden_weight, hidden_bias, compress_weight, compress_bias = params
    segment = token_rows.shape[0]
    head_count = slopes.shape[0]
    head_width = query_weight.shape[1] // head_count
    stacked = jnp.concatenate((compressed_rows, memory_rows, token_rows), 0)
    inputs_low = low(normalize(stacked, norm1_gain, norm1_bias))
    queries = low(low_back(jnp.dot(inputs_low[2 * segment:], query_weight, precision=HIGH)))
    queries = queries.reshape(segment, head_count, head_width)
    all_keys = low(low_back(jnp.dot(inputs_low, key_weight, precision=HIGH))).reshape(3 * segment, head_count, head_width)
    all_values = low(low_back(jnp.dot(inputs_low, value_weight, precision=HIGH))).reshape(3 * segment, head_count, head_width)
    allowed, distance = layout(0, 1, segment, first_slot)
    raw_scores = jnp.einsum('qhd,khd->hqk', queries, all_keys, precision=HIGH) * head_width ** (-0.5)
    raw_scores = raw_scores - slopes[:, None, None] * distance[None]
    scores = low_back(jnp.where(allowed[None], raw_scores, NEG))
    weights = jax.nn.softmax(scores, -1)
    mixture = jnp.einsum('hqk,khd->qhd', low(weights), all_values, precision=HIGH).reshape(segment, -1)
    mixture = low(low_back(mixture))
    residual = token_rows + low_back(jnp.dot(mixture, out_weight, precision=HIGH))
    normed_low = low(normalize(residual, norm2_gain, norm2_bias))
    pre_act = low_back(jnp.dot(normed_low, in_weight, precision=HIGH) + in_bias)
    act_low = low(activate(pre_act))
    output = residual + low_back(jnp.dot(act_low, hidden_weight, precision=HIGH) + hidden_bias)
    padded = jnp.concatenate((jnp.zeros((3 * NEWSLOTS - segment, D), jnp.float32), memory_rows), 0)
    windows = padded.reshape(NEWSLOTS, 3 * D)
    new_slots = jnp.dot(windows, compress_weight, precision=HIGH) + compress_bias
    return (output, new_slots)

def reference(tokens, memory, compressed, mask_start, norm1_gain, norm1_bias, query_weight, key_weight, value_weight, out_weight, slopes, norm2_gain, norm2_bias, in_weight, in_bias, hidden_weight, hidden_bias, compress_weight, compress_bias, grad_out, grad_compressed):
    params = (norm1_gain, norm1_bias, query_weight, key_weight, value_weight, out_weight, slopes, norm2_gain, norm2_bias, in_weight, in_bias, hidden_weight, hidden_bias, compress_weight, compress_bias)
    params = jax.tree.map(lambda leaf: leaf.astype(jnp.float32), params)

    def stream_step(totals, stream_item):
        token_rows, memory_rows, compressed_rows, first_slot, grad_rows, grad_slots = stream_item
        memory_f = memory_rows.astype(jnp.float32)
        compressed_f = compressed_rows.astype(jnp.float32)

        def forward(token_input, weight_input):
            return stream_layer(weight_input, token_input, memory_f, compressed_f, first_slot)
        outputs, pullback = jax.vjp(forward, token_rows.astype(jnp.float32), params)
        grad_input, grad_params = pullback((grad_rows.astype(jnp.float32), grad_slots.astype(jnp.float32)))
        totals = jax.tree.map(jnp.add, totals, grad_params)
        return (totals, (outputs[0].astype(jnp.bfloat16), outputs[1].astype(jnp.bfloat16), grad_input.astype(jnp.bfloat16)))
    zeros_start = jax.tree.map(jnp.zeros_like, params)
    totals, stream_outs = lax.scan(stream_step, zeros_start, (tokens, memory, compressed, mask_start, grad_out, grad_compressed))
    output, new_compressed, grad_tokens = stream_outs
    return (output, new_compressed, grad_tokens, totals[0], totals[1], totals[2], totals[3], totals[4], totals[5], totals[6], totals[7], totals[8], totals[9], totals[10], totals[11], totals[12], totals[13], totals[14])
```

```python
import functools

import jax
import jax.numpy as jnp
from jax import lax
from jax.experimental import pallas as pl
from jax.experimental.pallas import tpu as pltpu
from jax.sharding import PartitionSpec as P

EPS = 1e-05
NEG = -1e30
LOG2E = 1.4426950408889634
F32 = jnp.float32
BF16 = jnp.bfloat16


def dot(a, b, dims=((1,), (0,))):
    return lax.dot_general(a, b, (dims, ((), ())), preferred_element_type=F32)


def dot_nt(a, b):
    return dot(a, b, ((1,), (1,)))


def dot_tn(a, b):
    return dot(a, b, ((0,), (0,)))


def rows_stats(x):
    mean = jnp.mean(x, -1, keepdims=True)
    centered = x - mean
    rstd = lax.rsqrt(jnp.mean(centered * centered, -1, keepdims=True) + EPS)
    return centered * rstd, rstd


def norm_back(grad, gain, normed, rstd):
    dn = grad * gain
    return rstd * (
        dn
        - jnp.mean(dn, -1, keepdims=True)
        - normed * jnp.mean(dn * normed, -1, keepdims=True)
    )


TINY = pl.CostEstimate(flops=1000, bytes_accessed=1000, transcendentals=0)
PARAMS = pltpu.CompilerParams(vmem_limit_bytes=48 * 2**20)


def spec(shape, at=None):
    zeros = (0,) * len(shape)
    return pl.BlockSpec(shape, at if at is not None else (lambda *_: zeros))


def pieces_kernel(where, wq, wk, wv, wo, wi, first, second):
    size = wq.shape[1]
    first[:, :size] = wq[...]
    first[:, size : 2 * size] = wk[...]
    first[:, 2 * size :] = wv[...]
    second[:, : wo.shape[1]] = wo[...]
    second[:, wo.shape[1] :] = wi[...]


def pieces(where, share, wq, wk, wv, wo, wi):
    rows = wq.shape[0] // share
    cols = wq.shape[1] // 2
    wide = wi.shape[1] // 2
    half = spec((rows, cols), lambda i, w: (w[0], w[1]))
    return pl.pallas_call(
        pieces_kernel,
        grid_spec=pltpu.PrefetchScalarGridSpec(
            num_scalar_prefetch=1,
            grid=(1,),
            in_specs=[
                half,
                half,
                half,
                spec((rows, wo.shape[1]), lambda i, w: (w[0], 0)),
                spec((rows, wide), lambda i, w: (w[0], w[1])),
            ],
            out_specs=[spec((rows, 3 * cols)), spec((rows, wo.shape[1] + wide))],
        ),
        out_shape=[
            jax.ShapeDtypeStruct((rows, 3 * cols), BF16),
            jax.ShapeDtypeStruct((rows, wo.shape[1] + wide), BF16),
        ],
        compiler_params=PARAMS,
        cost_estimate=TINY,
        name="pieces",
    )(where, wq, wk, wv, wo, wi)


def project_kernel(where, comp, mem, tok, other, gain, shift, wq, wk, wv, mine, got, low, q, k, v, x):
    step = pl.program_id(0)
    rows = tok.shape[0]
    for at, own in enumerate((comp, mem, tok)):

        @pl.when(step == 2 * at)
        def _(own=own):
            x[...] = own[...].astype(F32)

        @pl.when(step == 2 * at + 1)
        def _(at=at):
            x[...] = other[at * rows : (at + 1) * rows, :].astype(F32)

    unit, _ = rows_stats(x[...])
    n = (unit * gain[...] + shift[...]).astype(BF16)
    low[...] = n
    half = n.shape[1] // 2
    upper = where[0] == 0
    n_own = jnp.where(upper, n[:, :half], n[:, half:])
    n_other = jnp.where(upper, n[:, half:], n[:, :half])
    even = where[1] == 0
    n_mine = jnp.where(even, n_other[:, : half // 2], n_other[:, half // 2 :])
    n_got = jnp.where(even, n_other[:, half // 2 :], n_other[:, : half // 2])
    cols = wq.shape[1]

    def product(weight, index):
        at = slice(index * cols, (index + 1) * cols)
        total = dot(n_own, weight[...]) + dot(n_mine, mine[:, at]) + dot(n_got, got[:, at])
        return total.astype(BF16)

    k[...] = product(wk, 1)
    v[...] = product(wv, 2)

    @pl.when(step >= 4)
    def _():
        q[...] = product(wq, 0)


def project(where, comp, mem, tok, other, gain, shift, wq, wk, wv, mine, got):
    rows, width = tok.shape
    cols = wq.shape[1] // 2
    half = spec((wq.shape[0], cols), lambda i, w: (0, w[0]))

    def by_step(size):
        return spec((rows, size), lambda i, w: (i, 0))

    return pl.pallas_call(
        project_kernel,
        grid_spec=pltpu.PrefetchScalarGridSpec(
            num_scalar_prefetch=1,
            grid=(6,),
            in_specs=[spec((rows, width))] * 3
            + [spec((3 * rows, width)), spec((1, width)), spec((1, width)), half, half, half]
            + [spec(mine.shape)] * 2,
            out_specs=[
                by_step(width),
                spec((rows, cols), lambda i, w: (jnp.maximum(i - 4, 0), 0)),
                by_step(cols),
                by_step(cols),
            ],
            scratch_shapes=[pltpu.VMEM((rows, width), F32)],
        ),
        out_shape=[
            jax.ShapeDtypeStruct((6 * rows, width), BF16),
            jax.ShapeDtypeStruct((2 * rows, cols), BF16),
            jax.ShapeDtypeStruct((6 * rows, cols), BF16),
            jax.ShapeDtypeStruct((6 * rows, cols), BF16),
        ],
        compiler_params=PARAMS,
        cost_estimate=TINY,
        name="project",
    )(where, comp, mem, tok, other, gain[None], shift[None], wq, wk, wv, mine, got)


def turn_kernel(*refs):
    half = len(refs) // 2
    for source, target in zip(refs[:half], refs[half:]):
        target[...] = source[...].astype(F32).T


def turned(*arrays):
    return pl.pallas_call(
        turn_kernel,
        out_shape=[jax.ShapeDtypeStruct(a.shape[::-1], F32) for a in arrays],
        compiler_params=PARAMS,
        cost_estimate=TINY,
        name="turn",
    )(*arrays)


def attend_kernel(chunk, scale, info, slopes, q, k, v, place, mix, lse):
    head = pl.program_id(0)
    slope = slopes[head] * LOG2E
    bias = place[0:1, :] * slope + place[1:2, :]
    key_place = place[0:1, :]
    keys = k.shape[0]
    rows = q.shape[0]
    tail = keys - rows
    for step in range(rows // chunk):
        at = pl.ds(step * chunk, chunk)
        first = info[step * chunk // (rows // 2)] + (step * chunk) % (rows // 2)
        query_place = (lax.broadcasted_iota(jnp.int32, (chunk, 1), 0) + first).astype(F32)
        scores = dot_nt(q[at, :], k[...]) * (scale * LOG2E) + bias
        recent = jnp.where(key_place[:, tail:] <= query_place, scores[:, tail:], NEG)
        scores = jnp.concatenate((scores[:, :tail], recent), 1)
        highest = jnp.max(scores, -1, keepdims=True)
        weights = jnp.exp2(scores - highest)
        total = jnp.sum(weights, -1, keepdims=True)
        low = (weights * (1.0 / total)).astype(BF16)
        mix[at, :] = dot(low, v[...]).astype(BF16)
        lse[0, at, :] = highest + jnp.log2(total)


def attend(info, slopes, q, k, v, place):
    rows, width = q.shape
    heads = slopes.shape[0]
    hw = width // heads
    keys = k.shape[0]
    return pl.pallas_call(
        functools.partial(attend_kernel, 128, hw**-0.5),
        grid=(heads,),
        in_specs=[
            pl.BlockSpec(memory_space=pltpu.SMEM),
            pl.BlockSpec(memory_space=pltpu.SMEM),
            pl.BlockSpec((rows, hw), lambda h: (0, h)),
            pl.BlockSpec((keys, hw), lambda h: (0, h)),
            pl.BlockSpec((keys, hw), lambda h: (0, h)),
            pl.BlockSpec((2, keys), lambda h: (0, 0)),
        ],
        out_specs=[
            pl.BlockSpec((rows, hw), lambda h: (0, h)),
            pl.BlockSpec((1, rows, 1), lambda h: (h, 0, 0)),
        ],
        out_shape=[
            jax.ShapeDtypeStruct((rows, width), BF16),
            jax.ShapeDtypeStruct((heads, rows, 1), F32),
        ],
        compiler_params=PARAMS,
        cost_estimate=TINY,
        name="attend",
    )(info, slopes, q, k, v, place)


def attend_back_kernel(chunk, scale, info, slopes, q, k, v, dm, place, lse, dq, dk, dv, slope_out, dk_sum, dv_sum):
    head = pl.program_id(0)
    slope = slopes[head] * LOG2E
    bias = place[0:1, :] * slope + place[1:2, :]
    key_place = place[0:1, :]
    keys = k.shape[0]
    rows = q.shape[0]
    tail = keys - rows
    columns = jnp.zeros((1, keys), F32)
    by_row = jnp.zeros((1, 1), F32)
    for step in range(rows // chunk):
        at = pl.ds(step * chunk, chunk)
        first = info[step * chunk // (rows // 2)] + (step * chunk) % (rows // 2)
        query_place = (lax.broadcasted_iota(jnp.int32, (chunk, 1), 0) + first).astype(F32)
        scores = dot_nt(q[at, :], k[...]) * (scale * LOG2E) + bias
        recent = jnp.where(key_place[:, tail:] <= query_place, scores[:, tail:], NEG)
        scores = jnp.concatenate((scores[:, :tail], recent), 1)
        weights = jnp.exp2(scores - lse[0, at, :])
        low = weights.astype(BF16)
        grads = dot_nt(dm[at, :], v[...])
        shift = jnp.sum(weights * grads, -1, keepdims=True)
        ds = (weights * (grads - shift)).astype(BF16)
        dq[at, :] = (dot(ds, k[...]) * scale).astype(BF16)
        dk_part = dot_tn(ds, q[at, :])
        dv_part = dot_tn(low, dm[at, :])
        if step == 0:
            dk_sum[...] = dk_part
            dv_sum[...] = dv_part
        else:
            dk_sum[...] += dk_part
            dv_sum[...] += dv_part
        wide = ds.astype(F32)
        columns += jnp.sum(wide, 0, keepdims=True)
        by_row += jnp.sum(jnp.sum(wide, -1, keepdims=True) * query_place, 0, keepdims=True)
    dk[...] = (dk_sum[...] * scale).astype(BF16)
    dv[...] = dv_sum[...].astype(BF16)
    total = jnp.sum(columns * key_place, -1, keepdims=True) - by_row
    slope_out[...] = jnp.broadcast_to(total.reshape(1, 1, 1), slope_out.shape)


def attend_back(info, slopes, q, k, v, dm, place, lse):
    rows, width = q.shape
    heads = slopes.shape[0]
    hw = width // heads
    keys = k.shape[0]
    by_rows = pl.BlockSpec((rows, hw), lambda h: (0, h))
    by_keys = pl.BlockSpec((keys, hw), lambda h: (0, h))
    return pl.pallas_call(
        functools.partial(attend_back_kernel, 128, hw**-0.5),
        grid=(heads,),
        in_specs=[
            pl.BlockSpec(memory_space=pltpu.SMEM),
            pl.BlockSpec(memory_space=pltpu.SMEM),
            by_rows,
            by_keys,
            by_keys,
            by_rows,
            pl.BlockSpec((2, keys), lambda h: (0, 0)),
            pl.BlockSpec((1, rows, 1), lambda h: (h, 0, 0)),
        ],
        out_specs=[by_rows, by_keys, by_keys, pl.BlockSpec((1, 8, 128), lambda h: (h, 0, 0))],
        out_shape=[
            jax.ShapeDtypeStruct((rows, width), BF16),
            jax.ShapeDtypeStruct((keys, width), BF16),
            jax.ShapeDtypeStruct((keys, width), BF16),
            jax.ShapeDtypeStruct((heads, 8, 128), F32),
        ],
        scratch_shapes=[pltpu.VMEM((keys, hw), F32), pltpu.VMEM((keys, hw), F32)],
        compiler_params=PARAMS,
        cost_estimate=TINY,
        name="attend_back",
    )(info, slopes, q, k, v, dm, place, lse)


def local(
    tokens,
    memory,
    compressed,
    mask_start,
    norm1_gain,
    norm1_bias,
    query_weight,
    key_weight,
    value_weight,
    out_weight,
    slopes,
    norm2_gain,
    norm2_bias,
    in_weight,
    in_bias,
    hidden_weight,
    hidden_bias,
    compress_weight,
    compress_bias,
    grad_out,
    grad_compressed,
):
    tokens, memory, compressed = tokens[0], memory[0], compressed[0]
    grad_out, grad_compressed = grad_out[0], grad_compressed[0]
    rows, width = tokens.shape
    heads = slopes.shape[0]
    own_heads = heads // 2
    dp = lax.axis_size("dp")
    levels = dp.bit_length() - 1
    d = lax.axis_index("dp")
    t = lax.axis_index("tm")
    segment = 2 * rows

    def swap(block):
        return lax.ppermute(block, "tm", [(0, 1), (1, 0)])

    def flip(level):
        return [(i, i ^ (1 << level)) for i in range(dp)]

    def after(array, *earlier):
        return lax.optimization_barrier((array,) + earlier)[0]

    def join(own, other, first):
        size = own.shape[0]
        both = jnp.concatenate((own, own), 0)
        return lax.dynamic_update_slice_in_dim(both, other, (1 - first) * size, 0)

    def natural_pair(mine, got):
        return join(mine, got, d & 1)

    def natural(own, other):
        return join(own, other, t)

    def half_of(array, index, axis):
        size = array.shape[axis] // 2
        return lax.dynamic_slice_in_dim(array, index * size, size, axis)

    sharing = min(levels, 4)
    mirrored = sum(((d >> level) & 1) << (sharing - 1 - level) for level in range(sharing))

    def grow(block, level):
        return join(block, lax.ppermute(block, "dp", flip(level)), (d >> level) & 1)

    class Shrink:
        def __init__(self, array, order, columns=False):
            blocks = dp // 2 if columns else dp
            self.array = array.reshape(blocks, array.shape[0] // blocks, array.shape[1])
            self.order = order
            self.columns = columns
            self.left = list(range(levels - 1 if columns else levels))
            self.step = 0
            self.parts = None

        def cut(self):
            if self.step == len(self.order):
                return self.array
            if self.parts is not None:
                return self.parts[1]
            level = self.order[self.step]
            bit = (d >> level) & 1
            if level in self.left:
                low = 1 << self.left.index(level)
                shape = self.array.shape
                split = self.array.reshape((shape[0] // (2 * low), 2, low) + shape[1:])
                self.parts = tuple(
                    lax.dynamic_index_in_dim(split, at, 1, keepdims=False).reshape(
                        (shape[0] // 2,) + shape[1:]
                    )
                    for at in (bit, 1 - bit)
                )
                self.left.remove(level)
            else:
                self.parts = tuple(half_of(self.array, at, 2) for at in (bit, 1 - bit))
            return self.parts[1]

        def add(self):
            if self.step == len(self.order):
                return self.array
            self.cut()
            keep, send = self.parts
            got = lax.ppermute(send, "dp", flip(self.order[self.step]))
            total = keep.astype(F32) + got.astype(F32)
            self.step += 1
            self.parts = None
            last = self.step == len(self.order) and not self.columns
            self.array = total if last else total.astype(BF16)
            return self.array

        def finish(self):
            while self.step < len(self.order):
                self.add()
            return self.array[0]

    sideways = list(range(levels))
    upward = [0] + list(range(2, levels)) + [1] if levels > 1 else [0]
    across = [0] + upward[1:2] + upward[-1:] + upward[2:-1] if levels > 2 else upward

    first, second = pieces(
        jnp.stack((mirrored, 1 - t)).astype(jnp.int32),
        1 << sharing,
        query_weight,
        key_weight,
        value_weight,
        out_weight,
        in_weight,
    )
    first, second = swap(first), swap(second)
    x_other = swap(jnp.concatenate((compressed, memory, tokens), 0))
    dc_other, dy_other = swap(grad_compressed), swap(grad_out)
    for level in reversed(range(1, sharing)):
        first = grow(first, level)
    first_got = lax.ppermute(first, "dp", flip(0))
    for level in reversed(range(min(2, sharing), sharing)):
        second = grow(second, level)
    second = after(second, first_got)
    for level in reversed(range(min(2, sharing))):
        second = grow(second, level)
    out_other = second[:, :width]
    in_full = natural(half_of(in_weight, t, 1), second[:, width:])
    bias_in = half_of(in_bias, t, 0)

    memory_other, tokens_other = x_other[rows : 2 * rows], x_other[2 * rows :]
    token_at = 2 * segment
    half_width = width // 2
    inputs_low, queries, keys, values = project(
        jnp.stack((t, d & 1)).astype(jnp.int32),
        compressed,
        memory,
        tokens,
        x_other,
        norm1_gain,
        norm1_bias,
        query_weight,
        key_weight,
        value_weight,
        first,
        first_got,
    )

    memory_full = natural(memory, memory_other)
    slots = 2 * grad_compressed.shape[0]
    lead = 3 * slots - segment
    padded = jnp.concatenate((jnp.zeros((lead, width), BF16), memory_full), 0)
    windows = half_of(padded.reshape(slots, 3 * width), t, 1)
    partial_c = dot(windows, compress_weight)
    away_c = half_of(partial_c, 1 - t, 0).astype(BF16)
    new_compressed = (
        half_of(partial_c, t, 0) + swap(away_c).astype(F32) + compress_bias
    ).astype(BF16)
    dc = natural(grad_compressed, dc_other)
    squeeze = Shrink(dot_tn(dc, windows).astype(BF16), sideways)

    index = jnp.arange(segment, dtype=jnp.int32)
    slot = jnp.where(index < rows, index + t * rows, index - rows + (1 - t) * rows)
    place = jnp.concatenate((-segment - 3 * (segment - slot), slot - segment, slot)).astype(F32)
    closed = jnp.where(slot >= mask_start[0], 0.0, NEG)
    closed = jnp.concatenate((closed, jnp.zeros((2 * segment,), F32)))
    place = jnp.stack((place, closed))
    info = jnp.stack((t * rows, (1 - t) * rows)).astype(jnp.int32)
    slopes_own = half_of(slopes, t, 0)
    squeeze.add()
    queries = after(queries, squeeze.cut(), away_c)
    mixture, lse = attend(info, slopes_own, queries, keys, values, place)
    mix_other = jnp.concatenate((swap(mixture[rows:]), swap(mixture[:rows])), 0)

    token_rows = jnp.concatenate((tokens, tokens_other), 0).astype(F32)
    residual = token_rows + (dot(mixture, out_weight) + dot(mix_other, out_other))
    unit2, rstd2 = rows_stats(residual)
    normed_low = (unit2 * norm2_gain + norm2_bias).astype(BF16)
    squeeze.add()
    normed_low = after(normed_low, squeeze.cut())
    dy = jnp.concatenate((grad_out, dy_other), 0)
    pre_act = dot(normed_low, in_full) + bias_in
    activated, act_back = jax.vjp(functools.partial(jax.nn.gelu, approximate=True), pre_act)
    act_low = activated.astype(BF16)
    grad_pre = act_back(dot_nt(dy, hidden_weight))[0].astype(BF16)
    partial_g2 = dot_nt(grad_pre, in_full)
    g2_low = partial_g2.astype(BF16)
    squeeze.add()
    hidden = Shrink(dot_tn(after(dy, g2_low, squeeze.cut()), act_low).astype(BF16), sideways)
    entry = Shrink(
        dot_tn(after(grad_pre, hidden.cut()), normed_low).astype(BF16), across, True
    )
    from_other = jnp.concatenate((swap(g2_low[rows:]), swap(g2_low[:rows])), 0)
    hidden.add()
    entry.add()
    partial_out = dot(act_low, hidden_weight)
    out_sent = after(partial_out[rows:].astype(BF16), entry.cut())
    output = (
        residual[:rows]
        + (partial_out[:rows] + swap(out_sent).astype(F32))
        + hidden_bias
    ).astype(BF16)

    from_other = after(from_other, hidden.cut(), entry.cut(), out_sent)
    grad_normed2 = partial_g2 + from_other.astype(F32)

    grad_residual = dy.astype(F32) + norm_back(grad_normed2, norm2_gain, unit2, rstd2)
    grad_res_low = grad_residual.astype(BF16)
    grad_mixture = dot_nt(grad_res_low, out_weight).astype(BF16)
    mix_out = Shrink(dot_tn(after(grad_res_low, grad_mixture), mixture).astype(BF16), sideways)
    grad_mixture = after(grad_mixture, mix_out.cut())
    dq, dk, dv, slope_parts = attend_back(
        info, slopes_own, queries, keys, values, grad_mixture, place, lse
    )
    blocks = dp // 2
    hidden.add()
    entry.add()
    dq, dk, dv = (after(a, hidden.cut(), entry.cut()) for a in (dq, dk, dv))
    trio = jnp.stack(
        [
            dot_tn(dv, inputs_low).astype(BF16),
            dot_tn(dk, inputs_low).astype(BF16),
            dot_tn(dq, inputs_low[token_at:]).astype(BF16),
        ]
    )
    trio = trio.reshape(3, blocks, half_width // blocks, width)
    trio = jnp.swapaxes(trio, 0, 1).reshape(blocks, -1, width)
    cut_at = trio.shape[1] // 2
    left = Shrink(trio[:, :cut_at].reshape(-1, width), sideways, True)
    right = Shrink(trio[:, cut_at:].reshape(-1, width), upward, True)
    left.cut()
    right.cut()

    weights_at = [half_of(w, t, 1) for w in (query_weight, key_weight, value_weight)]
    lower = natural_pair(first, first_got)
    wq, wk, wv = [
        natural(own, lower[:, i * half_width : (i + 1) * half_width])
        for i, own in enumerate(weights_at)
    ]
    dk = after(dk, left.cut(), right.cut())
    g1 = dot_nt(dk, wk) + dot_nt(dv, wv)
    g1_tok = g1[token_at:] + dot_nt(dq, wq)
    g1 = jnp.concatenate((g1[:token_at], g1_tok), 0)
    g1_away = g1_tok[rows:].astype(BF16)
    left.parts = (after(left.parts[0], g1_away), left.parts[1])
    g1_own = g1_tok[:rows] + swap(g1_away).astype(F32)
    stacked = jnp.concatenate(
        (compressed, x_other[:rows], memory, memory_other, tokens, tokens_other), 0
    )
    unit1, rstd1 = rows_stats(stacked.astype(F32))
    own_tokens = slice(token_at, token_at + rows)
    back1 = norm_back(g1_own, norm1_gain, unit1[own_tokens], rstd1[own_tokens])
    grad_tokens = (grad_residual[:rows] + back1).astype(BF16)

    def placed(part):
        zeros = jnp.zeros((2 * part.shape[0],), F32)
        return lax.dynamic_update_slice_in_dim(zeros, part, t * part.shape[0], 0)

    parts = (
        jnp.sum(grad_normed2[:rows] * unit2[:rows], 0),
        jnp.sum(grad_normed2[:rows], 0),
        placed(jnp.sum(grad_pre.astype(F32), 0)),
        jnp.sum(grad_out.astype(F32), 0),
        jnp.sum(grad_compressed.astype(F32), 0),
        jnp.sum(g1 * unit1, 0),
        jnp.sum(g1, 0),
        jnp.pad(placed(slope_parts[:, 0, 0]), (0, 1024 - heads)),
    )
    smalls = jnp.concatenate(parts).reshape(-1, 128)

    left.add()
    right.add()
    mix_out.add()
    smalls = after(smalls, left.cut(), right.cut())
    smalls = smalls + swap(smalls)
    groups = (hidden, entry, left, right, mix_out)
    for step in range(levels):
        sends = [group.cut() for group in groups]
        for group in groups:
            if group.parts is not None:
                group.parts = (after(group.parts[0], *sends), group.parts[1])
        smalls = smalls + lax.ppermute(smalls, "dp", flip(step))
        for group in groups:
            group.add()

    half = dp // 2
    route = []
    for i in range(dp):
        for j in range(2):
            route.append((2 * i + j, 2 * (j * half + i % half) + i // half))
    moved = [group.finish() for group in (left, right, entry)]
    sizes = [block.shape[0] for block in moved]
    moved = lax.ppermute(jnp.concatenate(moved, 0), ("dp", "tm"), route)
    part = half_width // blocks
    grad_value_w, grad_key_w, grad_query_w = [
        moved[i * part : (i + 1) * part].astype(F32).T for i in range(3)
    ]
    (grad_in_w,) = turned(moved[sizes[0] + sizes[1] :])
    grad_hidden_w, grad_out_w, grad_compress_w = [
        group.finish().T for group in (hidden, mix_out, squeeze)
    ]

    joined = smalls.reshape(-1)
    result, at = [], 0
    for entry_of in parts:
        result.append(joined[at : at + entry_of.shape[0]])
        at += entry_of.shape[0]
    gain2, bias2, in_b, hidden_b, compress_b, gain1, bias1, slope = result
    return (
        output[None],
        new_compressed[None],
        grad_tokens[None],
        gain1,
        bias1,
        grad_query_w,
        grad_key_w,
        grad_value_w,
        grad_out_w,
        slope[:heads],
        gain2,
        bias2,
        grad_in_w,
        in_b,
        grad_hidden_w,
        hidden_b,
        grad_compress_w,
        compress_b,
    )


def solution(mesh):
    split, whole, kept = P("dp", "tm", None), P(), P("tm", None)
    in_specs = (
        (split,) * 3
        + (P("dp"), whole, whole)
        + (kept,) * 4
        + (whole,) * 3
        + (kept, whole, kept, whole, kept, whole)
        + (split,) * 2
    )
    shared = P("tm", "dp")
    out_specs = (
        (split,) * 3
        + (whole,) * 2
        + (shared,) * 4
        + (whole,) * 3
        + (shared, whole, shared, whole, shared, whole)
    )
    return jax.shard_map(local, mesh=mesh, in_specs=in_specs, out_specs=out_specs, check_vma=False)
```

```python
import functools

import jax
import jax.numpy as jnp
from jax import lax
from jax.experimental import pallas as pl
from jax.experimental.pallas import tpu as pltpu
from jax.sharding import PartitionSpec as P

EPS = 1e-05
NEG = -1e30
LOG2E = 1.4426950408889634
F32 = jnp.float32
BF16 = jnp.bfloat16
TINY = pl.CostEstimate(flops=1000, bytes_accessed=1000, transcendentals=0)
LARGE = pl.CostEstimate(flops=20 * 10**9, bytes_accessed=10**6, transcendentals=0)
PARAMS = pltpu.CompilerParams(vmem_limit_bytes=52 * 2**20)


def dot(a, b, dims=((1,), (0,))):
    return lax.dot_general(a, b, (dims, ((), ())), preferred_element_type=F32)


def dot_nt(a, b):
    return dot(a, b, ((1,), (1,)))


def dot_tn(a, b):
    return dot(a, b, ((0,), (0,)))


def rows_stats(x):
    mean = jnp.mean(x, -1, keepdims=True)
    centered = x - mean
    rstd = lax.rsqrt(jnp.mean(centered * centered, -1, keepdims=True) + EPS)
    return centered * rstd, rstd


def norm_back(grad, gain, normed, rstd):
    dn = grad * gain
    return rstd * (
        dn
        - jnp.mean(dn, -1, keepdims=True)
        - normed * jnp.mean(dn * normed, -1, keepdims=True)
    )


def spec(shape, at=None):
    zeros = (0,) * len(shape)
    return pl.BlockSpec(shape, at if at is not None else (lambda *_: zeros))


def call(kernel, name, where, grid, ins, outs, scratch=(), cost=TINY):
    return pl.pallas_call(
        kernel,
        grid_spec=pltpu.PrefetchScalarGridSpec(
            num_scalar_prefetch=1,
            grid=grid,
            in_specs=[at for _, at in ins],
            out_specs=[at for _, _, at in outs],
            scratch_shapes=list(scratch),
        ),
        out_shape=[jax.ShapeDtypeStruct(shape, dtype) for shape, dtype, _ in outs],
        compiler_params=PARAMS,
        cost_estimate=cost,
        name=name,
    )(where, *[array for array, _ in ins])


def whole(array):
    return array, spec(array.shape)


def ordered(first, own, other, axis):
    return jnp.where(
        first, jnp.concatenate((own, other), axis), jnp.concatenate((other, own), axis)
    )


def place_pieces(where, parts, target, base=0, half=None):
    size = (half or target.shape[0]) // (where.shape[0] - 2)
    at = 0
    for part in parts:
        for block in range(part.shape[0] // size):
            row = pl.multiple_of(base + where[2 + at] * size, size)
            target[pl.ds(row, size), :] = part[block * size : (block + 1) * size, :]
            at += 1


def pieces_kernel(where, wq, wk, wv, wo, wi, first, second):
    size = wq.shape[1]
    first[:, :size] = wq[...]
    first[:, size : 2 * size] = wk[...]
    first[:, 2 * size :] = wv[...]
    second[:, : wo.shape[1]] = wo[...]
    second[:, wo.shape[1] :] = wi[...]


def pieces(where, share, wq, wk, wv, wo, wi):
    rows = wq.shape[0] // share
    cols = wq.shape[1] // 2
    wide = wi.shape[1] // 2
    half = spec((rows, cols), lambda i, w: (w[0], w[1]))
    return call(
        pieces_kernel,
        "pieces",
        where,
        (1,),
        [
            (wq, half),
            (wk, half),
            (wv, half),
            (wo, spec((rows, wo.shape[1]), lambda i, w: (w[0], 0))),
            (wi, spec((rows, wide), lambda i, w: (w[0], w[1]))),
        ],
        [
            ((rows, 3 * cols), BF16, spec((rows, 3 * cols))),
            ((rows, wo.shape[1] + wide), BF16, spec((rows, wo.shape[1] + wide))),
        ],
    )


def load_rows(step, x, comp, mem, tok, other):
    rows = tok.shape[0]
    sources = (
        comp,
        other.at[:rows, :],
        mem,
        other.at[rows : 2 * rows, :],
        tok,
        other.at[2 * rows :, :],
    )
    for at, source in enumerate(sources):

        @pl.when(step == at)
        def _(source=source):
            x[...] = source[...].astype(F32)


def project_kernel(
    where, comp, mem, tok, other, gain, shift, wq, wk, wv, mine, got, low, q, k, v, weights, x
):
    step = pl.program_id(0)
    load_rows(step, x, comp, mem, tok, other)
    half, cols = wq.shape

    @pl.when(step == 0)
    def _():
        own = pl.ds(pl.multiple_of(where[0] * half, half), half)
        for index, weight in enumerate((wq, wk, wv)):
            weights[own, index * cols : (index + 1) * cols] = weight[...]
        place_pieces(where, (mine, got), weights, (1 - where[0]) * half, half)

    unit, _ = rows_stats(x[...])
    n = (unit * gain[...] + shift[...]).astype(BF16)
    low[...] = n
    k[...] = dot(n, weights[:, cols : 2 * cols]).astype(BF16)
    v[...] = dot(n, weights[:, 2 * cols :]).astype(BF16)

    @pl.when(step >= 4)
    def _():
        q[...] = dot(n, weights[:, :cols]).astype(BF16)


def project(where, comp, mem, tok, other, gain, shift, wq, wk, wv, mine, got):
    rows, width = tok.shape
    cols = wq.shape[1] // 2
    half = spec((wq.shape[0], cols), lambda i, w: (0, w[0]))

    def by_step(size):
        return spec((rows, size), lambda i, w: (i, 0))

    return call(
        project_kernel,
        "project",
        where,
        (6,),
        [whole(a) for a in (comp, mem, tok, other, gain[None], shift[None])]
        + [(wq, half), (wk, half), (wv, half), whole(mine), whole(got)],
        [
            ((6 * rows, width), BF16, by_step(width)),
            ((2 * rows, cols), BF16, spec((rows, cols), lambda i, w: (jnp.maximum(i - 4, 0), 0))),
            ((6 * rows, cols), BF16, by_step(cols)),
            ((6 * rows, cols), BF16, by_step(cols)),
            ((width, 3 * cols), BF16, spec((width, 3 * cols))),
        ],
        [pltpu.VMEM((rows, width), F32)],
        cost=LARGE,
    )


def split_pairs(where, total, height, keep, send):
    pairs = total.reshape(total.shape[0] // (2 * height), 2, height, total.shape[1])
    even = where[1] == 0
    keep[...] = jnp.where(even, pairs[:, 0], pairs[:, 1]).astype(BF16)
    send[...] = jnp.where(even, pairs[:, 1], pairs[:, 0]).astype(BF16)


def squeeze_kernel(slots, where, mem, other, dc, dc_o, weight, stay, away, keep, send, dc_sum):
    t = where[0]
    dc_sum[...] = jnp.sum(dc[...].astype(F32), 0, keepdims=True)
    rows, width = mem.shape
    mem_o = other.at[rows : 2 * rows, :]
    padded = dc.shape[0]
    half = width // 2
    lead = 3 * 2 * slots - 2 * rows
    first = t == 0
    shape = (padded, rows)
    slot = lax.broadcasted_iota(jnp.int32, shape, 0)
    row = lax.broadcasted_iota(jnp.int32, shape, 1)
    mem_half = jnp.where(first, mem[:, :half], mem[:, half:])
    mem_o_half = jnp.where(first, mem_o[:, :half], mem_o[:, half:])

    def picked(slot_half, row_half, offset):
        place = 3 * (slot + slot_half * slots) + offset - lead
        hit = (place == row + row_half * rows) & (slot < slots)
        return jnp.where(hit, 1.0, 0.0).astype(BF16)

    def windows(slot_half):
        edge = dot(picked(slot_half, t, 2 * t), mem[...]) + dot(
            picked(slot_half, 1 - t, 2 * t), mem_o[...]
        )
        middle = dot(picked(slot_half, t, 1), mem_half) + dot(
            picked(slot_half, 1 - t, 1), mem_o_half
        )
        return ordered(first, edge, middle, 1).astype(BF16)

    both = jnp.concatenate((windows(t), windows(1 - t)), 0)
    slots_out = dot(both, weight[...])
    stay[...] = slots_out[:padded, :]
    away[...] = slots_out[padded:, :].astype(BF16)
    turned_dc = jnp.concatenate((dc[...], dc_o[...]), 0).T
    columns = both.shape[1]
    height = keep.shape[1]
    for at in range(0, columns, half):
        part = slice(at, at + half)
        total = dot(turned_dc, both[:, part])
        split_pairs(where, total, height, keep.at[:, :, part], send.at[:, :, part])


def squeeze_rows(where, dp, slots, mem, other, dc, dc_o, weight):
    padded, width = dc.shape
    half = ((dp // 2, width // dp, weight.shape[0]), BF16)
    ins = [whole(a) for a in (mem, other, dc, dc_o, weight)]
    return call(
        functools.partial(squeeze_kernel, slots),
        "squeeze",
        where,
        (1,),
        ins,
        [
            ((padded, width), F32, spec((padded, width))),
            ((padded, width), BF16, spec((padded, width))),
            half + (spec(half[0]),),
            half + (spec(half[0]),),
            ((1, width), F32, spec((1, width))),
        ],
    )


def masked_scores(place, slope, q, keys, scale, first, tail):
    bias = place[0:1, :] * slope + place[1:2, :]
    chunk = q.shape[0]
    query_place = (lax.broadcasted_iota(jnp.int32, (chunk, 1), 0) + first).astype(F32)
    scores = dot_nt(q, keys) * (scale * LOG2E) + bias
    recent = jnp.where(place[0:1, tail:] <= query_place, scores[:, tail:], NEG)
    return jnp.concatenate((scores[:, :tail], recent), 1), query_place


def attend_kernel(turn, scale, where, slopes, q, k, v, place, mix, lse):
    slope = slopes[pl.program_id(0)] * LOG2E
    rows = q.shape[0]
    first = jnp.abs(turn - where[0]) * rows
    scores, _ = masked_scores(place, slope, q[...], k[...], scale, first, k.shape[0] - 2 * rows)
    highest = jnp.max(scores, -1, keepdims=True)
    weights = jnp.exp2(scores - highest)
    total = jnp.sum(weights, -1, keepdims=True)
    mix[...] = (dot(weights.astype(BF16), v[...]) * (1.0 / total)).astype(BF16)
    lse[0] = highest + jnp.log2(total)


def attend(where, turn, slopes, q, k, v, place):
    rows, width = q.shape[0] // 2, q.shape[1]
    heads = slopes.shape[0]
    hw = width // heads
    keys = k.shape[0]
    by_head = spec((keys, hw), lambda h, w: (0, h))
    return call(
        functools.partial(attend_kernel, turn, hw**-0.5),
        "attend",
        where,
        (heads,),
        [
            (slopes, pl.BlockSpec(memory_space=pltpu.SMEM)),
            (q, spec((rows, hw), lambda h, w: (turn, h))),
            (k, by_head),
            (v, by_head),
            whole(place),
        ],
        [
            ((rows, width), BF16, spec((rows, hw), lambda h, w: (0, h))),
            ((heads, rows, 1), F32, spec((1, rows, 1), lambda h, w: (h, 0, 0))),
        ],
        cost=LARGE,
    )


def attend_back_kernel(
    chunk,
    scale,
    where,
    slopes,
    q,
    k,
    v,
    dm,
    place,
    lse_own,
    lse_other,
    dq,
    dk,
    dv,
    dq_turned,
    dk_turned,
    dv_turned,
    slope_out,
    dk_sum,
    dv_sum,
):
    slope = slopes[pl.program_id(0)] * LOG2E
    keys = k.shape[0]
    rows = q.shape[0]
    half = rows // 2
    columns = jnp.zeros((1, keys), F32)
    by_row = jnp.zeros((1, 1), F32)
    for step in range(rows // chunk):
        at = slice(step * chunk, (step + 1) * chunk)
        time_half = where[0] if step * chunk < half else 1 - where[0]
        scores, query_place = masked_scores(
            place,
            slope,
            q[at, :],
            k[...],
            scale,
            time_half * half + step * chunk % half,
            keys - rows,
        )
        weights = jnp.exp2(scores - (lse_own if step == 0 else lse_other)[0])
        low = weights.astype(BF16)
        grads = dot_nt(dm[at, :], v[...])
        shift = jnp.sum(weights * grads, -1, keepdims=True)
        ds = (weights * (grads - shift)).astype(BF16)
        dq_part = dot(ds, k[...]) * scale
        dq[at, :] = dq_part.astype(BF16)
        dq_turned[:, at] = dq_part.T.astype(BF16)
        dk_part = dot_tn(q[at, :], ds)
        dv_part = dot_tn(dm[at, :], low)
        if step == 0:
            dk_sum[...] = dk_part
            dv_sum[...] = dv_part
        else:
            dk_sum[...] += dk_part
            dv_sum[...] += dv_part
        wide = ds.astype(F32)
        columns += jnp.sum(wide, 0, keepdims=True)
        by_row += jnp.sum(jnp.sum(wide, -1, keepdims=True) * query_place, 0, keepdims=True)
    dk_all, dv_all = dk_sum[...] * scale, dv_sum[...]
    dk_turned[...] = dk_all.astype(BF16)
    dv_turned[...] = dv_all.astype(BF16)
    dk[...] = dk_all.T.astype(BF16)
    dv[...] = dv_all.T.astype(BF16)
    total = jnp.sum(columns * place[0:1, :], -1, keepdims=True) - by_row
    slope_out[...] = jnp.broadcast_to(total.reshape(1, 1, 1), slope_out.shape)


def attend_back(where, slopes, q, k, v, dm, place, lses):
    rows, width = q.shape
    heads = slopes.shape[0]
    hw = width // heads
    keys = k.shape[0]
    by_rows = spec((rows, hw), lambda h, w: (0, h))
    by_keys = spec((keys, hw), lambda h, w: (0, h))
    return call(
        functools.partial(attend_back_kernel, rows // 2, hw**-0.5),
        "attend_back",
        where,
        (heads,),
        [
            (slopes, pl.BlockSpec(memory_space=pltpu.SMEM)),
            (q, by_rows),
            (k, by_keys),
            (v, by_keys),
            (dm, by_rows),
            whole(place),
            (lses[0], spec((1, rows // 2, 1), lambda h, w: (h, 0, 0))),
            (lses[1], spec((1, rows // 2, 1), lambda h, w: (h, 0, 0))),
        ],
        [
            ((rows, width), BF16, by_rows),
            ((keys, width), BF16, by_keys),
            ((keys, width), BF16, by_keys),
            ((width, rows), BF16, spec((hw, rows), lambda h, w: (h, 0))),
            ((width, keys), BF16, spec((hw, keys), lambda h, w: (h, 0))),
            ((width, keys), BF16, spec((hw, keys), lambda h, w: (h, 0))),
            ((heads, 8, 128), F32, spec((1, 8, 128), lambda h, w: (h, 0, 0))),
        ],
        [pltpu.VMEM((hw, keys), F32), pltpu.VMEM((hw, keys), F32)],
        cost=LARGE,
    )


def gelu_pair(v):
    c = 0.7978845608028654
    inner = c * (v + 0.044715 * v * v * v)
    th = jnp.tanh(inner)
    slope = 0.5 * (1.0 + th) + 0.5 * v * (1.0 - th * th) * c * (1.0 + 3 * 0.044715 * v * v)
    return 0.5 * v * (1.0 + th), slope


def feed_kernel(
    where,
    mix,
    far,
    tok,
    wo,
    wo_mine,
    wo_got,
    gain,
    shift,
    dy,
    wi,
    wi_mine,
    wi_got,
    bias,
    wh,
    residual,
    normed,
    act,
    grad_pre,
    g2,
    sent,
    out,
    bias_sum,
    dy_sum,
    wo_far,
    weight,
    out_sum,
):
    step = pl.program_id(0)
    half = wi.shape[0]

    @pl.when(step == 0)
    def _():
        place_pieces(where, (wo_mine, wo_got), wo_far)
        dy_sum[...] = jnp.sum(dy[...].astype(F32), 0, keepdims=True)
        total = tok[...].astype(F32) + (dot(mix[...], wo[...]) + dot(far[...], wo_far[...]))
        residual[...] = total
        unit, _ = rows_stats(total)
        normed[...] = (unit * gain[...] + shift[...]).astype(BF16)

    weight[pl.ds(pl.multiple_of(where[0] * half, half), half), :] = wi[...]
    place_pieces(where, (wi_mine, wi_got), weight, (1 - where[0]) * half, half)
    pre = dot(normed[...], weight[...]) + bias[...]
    value, slope = gelu_pair(pre)
    low = value.astype(BF16)
    act[...] = low
    grad = (dot_nt(dy[...], wh[...]) * slope).astype(BF16)
    grad_pre[...] = grad
    bias_sum[...] = jnp.sum(grad.astype(F32), 0, keepdims=True)
    g2_part = dot_nt(grad, weight[...])
    out_part = dot(low, wh[...])

    @pl.when(step == 0)
    def _():
        g2[...] = g2_part
        out_sum[...] = out_part

    @pl.when(step > 0)
    def _():
        g2[...] += g2_part
        out_sum[...] += out_part

    @pl.when(step == pl.num_programs(0) - 1)
    def _():
        sent[...] = g2[...].astype(BF16)
        out[...] = out_sum[...].astype(out.dtype)


def feed(where, mix, far, tok, tok_at, wo, gain, shift, dy, wi, bias, wh, second, chunk, kept):
    rows, width = dy.shape
    hidden = wh.shape[0]
    steps = hidden // chunk
    mine, got = second
    by_cols = spec((rows, chunk), lambda j, w: (0, j))
    wo_part = spec((mine.shape[0], width), lambda j, w: (0, 0))
    wi_part = spec((mine.shape[0], chunk), lambda j, w: (0, width // chunk + j))

    def once(dtype):
        return (rows, width), dtype, spec((rows, width))

    return call(
        feed_kernel,
        "feed",
        where,
        (steps,),
        [
            whole(mix),
            whole(far),
            (tok, spec((rows, width), lambda j, w: (tok_at, 0))),
            whole(wo),
            (mine, wo_part),
            (got, wo_part),
            whole(gain[None]),
            whole(shift[None]),
            whole(dy),
            (wi, spec((wi.shape[0], chunk), lambda j, w: (0, w[0] * steps + j))),
            (mine, wi_part),
            (got, wi_part),
            (bias[None], spec((1, chunk), lambda j, w: (0, w[0] * steps + j))),
            (wh, spec((chunk, width), lambda j, w: (j, 0))),
        ],
        [
            once(F32),
            once(BF16),
            ((rows, hidden), BF16, by_cols),
            ((rows, hidden), BF16, by_cols),
            once(F32),
            once(BF16),
            once(kept),
            ((1, hidden), F32, spec((1, chunk), lambda j, w: (0, j))),
            ((1, width), F32, spec((1, width))),
        ],
        [
            pltpu.VMEM(wo.shape, BF16),
            pltpu.VMEM((width, chunk), BF16),
            pltpu.VMEM((rows, width), F32),
        ],        cost=LARGE,
    )


def hidden_grad_kernel(where, dy, dy_o, act, act_o, keep, send, turned, turned_o):
    @pl.when(pl.program_id(0) == 0)
    def _():
        turned[...] = dy[...].T
        turned_o[...] = dy_o[...].T

    total = dot(turned[...], act[...]) + dot(turned_o[...], act_o[...])
    split_pairs(where, total, keep.shape[1], keep, send)


def hidden_grad(where, dp, dys, acts, chunk):
    rows, width = dys[0].shape
    hidden = acts[0].shape[1]
    height = width // dp
    out = ((dp // 2, height, hidden), BF16, spec((dp // 2, height, chunk), lambda j, w: (0, 0, j)))
    by_cols = spec((rows, chunk), lambda j, w: (0, j))
    return call(
        hidden_grad_kernel,
        "hidden_grad",
        where,
        (hidden // chunk,),
        [whole(dys[0]), whole(dys[1]), (acts[0], by_cols), (acts[1], by_cols)],
        [out, out],
        [pltpu.VMEM((width, rows), BF16)] * 2,
    )


def entry_grad_kernel(where, grad, grad_o, normed, normed_o, keep, send, turned, turned_o):
    @pl.when(pl.program_id(0) == 0)
    def _():
        turned[...] = normed[...].T
        turned_o[...] = normed_o[...].T

    total = dot(turned[...], grad[...]) + dot(turned_o[...], grad_o[...])
    size = keep.shape[2]
    even = where[1] == 0
    for pair in range(keep.shape[0]):
        one = total[:, 2 * pair * size : (2 * pair + 1) * size]
        two = total[:, (2 * pair + 1) * size : (2 * pair + 2) * size]
        keep[pair] = jnp.where(even, one, two).astype(BF16)
        send[pair] = jnp.where(even, two, one).astype(BF16)


def entry_grad(where, dp, grads, norms, chunk):
    rows, width = norms[0].shape
    hidden = grads[0].shape[1]
    size = hidden // (dp // 2)
    chunk = max(chunk, 2 * size)
    pairs = chunk // (2 * size)
    out = ((dp // 4, width, size), BF16, spec((pairs, width, size), lambda j, w: (j, 0, 0)))
    by_cols = spec((rows, chunk), lambda j, w: (0, j))
    return call(
        entry_grad_kernel,
        "entry_grad",
        where,
        (hidden // chunk,),
        [(grads[0], by_cols), (grads[1], by_cols), whole(norms[0]), whole(norms[1])],
        [out, out],
        [pltpu.VMEM((width, rows), BF16)] * 2,
    )


def middle_kernel(
    where,
    g_own,
    g_other,
    got_own,
    got_other,
    residual_own,
    residual_other,
    gain,
    dy,
    dy_o,
    wo,
    mix_own,
    mix_other,
    grad_res,
    dm,
    sums,
    keep,
    send,
):
    rows = dy.shape[0]
    lows = []
    halves = ((g_own, got_own, dy, residual_own), (g_other, got_other, dy_o, residual_other))
    for at, (g, got, d, residual) in enumerate(halves):
        here = slice(at * rows, (at + 1) * rows)
        grad = g[...] + got[...].astype(F32)
        unit, rstd = rows_stats(residual[...])
        total = d[...].astype(F32) + norm_back(grad, gain[...], unit, rstd)
        low = total.astype(BF16)
        lows.append(low)
        dm[here, :] = dot_nt(low, wo[...]).astype(BF16)
        if at == 0:
            grad_res[...] = total
            sums[0:1, :] = jnp.sum(grad * unit, 0, keepdims=True)
            sums[1:2, :] = jnp.sum(grad, 0, keepdims=True)
    split_pairs(
        where, dot_tn(lows[0], mix_own[...]) + dot_tn(lows[1], mix_other[...]), keep.shape[1], keep, send
    )


def middle(where, dp, g, got, residuals, gain, dys, wo, mix):
    rows, width = dys[0].shape
    heads = wo.shape[0]
    half = ((dp // 2, width // dp, heads), BF16, spec((dp // 2, width // dp, heads)))
    return call(
        middle_kernel,
        "middle",
        where,
        (1,),
        [whole(a) for a in (*g, *got, *residuals, gain[None], *dys, wo, *mix)],
        [
            ((rows, width), F32, spec((rows, width))),
            ((2 * rows, heads), BF16, spec((2 * rows, heads))),
            ((8, width), F32, spec((8, width))),
            half,
            half,
        ],
        cost=LARGE,
    )


def trio_kernel(where, dq, dk, dv, low, left_keep, left_send, right_keep, right_send):
    side = pl.program_id(0)
    count = dq.shape[1]
    n = low[...]
    height = left_keep.shape[2]
    even = where[1] == 0
    for index, (grad, rows) in enumerate(((dq, n[n.shape[0] - count :]), (dk, n), (dv, n))):
        total = dot(grad[...], rows)
        pairs = total.reshape(total.shape[0] // (2 * height), 2, height, total.shape[1])
        stay = jnp.where(even, pairs[:, 0], pairs[:, 1]).astype(BF16)
        away = jnp.where(even, pairs[:, 1], pairs[:, 0]).astype(BF16)

        @pl.when(side == 0)
        def _():
            left_keep[:, index] = stay
            left_send[:, index] = away

        @pl.when(side == 1)
        def _():
            right_keep[:, index] = stay
            right_send[:, index] = away


def trio(where, dp, dq, dk, dv, low):
    cols, rows = dk.shape
    width = low.shape[1]
    blocks = dp // 2
    height = cols // blocks
    chunk = width // 4
    shape = (blocks // 2, 3, height, width // 2)
    block = (blocks // 2, 3, height, chunk)
    left = (shape, BF16, spec(block, lambda s, r, w: (0, 0, 0, jnp.where(s == 0, r, 1))))
    right = (shape, BF16, spec(block, lambda s, r, w: (0, 0, 0, jnp.where(s == 0, 0, r))))
    return call(
        trio_kernel,
        "trio",
        where,
        (2, 2),
        [
            whole(dq),
            whole(dk),
            whole(dv),
            (low, spec((rows, chunk), lambda s, r, w: (0, 2 * r + s))),
        ],
        [left, left, right, right],
    )


def inputs_kernel(
    where, comp, mem, tok, other, dq, dk, dv, weights, sums2, bias_sum, bias_sum_o, dy_sum, dc_sum, slope_parts, g_own, sent, sums, x
):
    step = pl.program_id(0)
    load_rows(step, x, comp, mem, tok, other)
    cols = dk.shape[1]
    g = dot_nt(dk[...], weights[:, cols : 2 * cols]) + dot_nt(dv[...], weights[:, 2 * cols :])
    unit, _ = rows_stats(x[...])

    def add_sums(total):
        gain = jnp.sum(total * unit, 0, keepdims=True)
        shift = jnp.sum(total, 0, keepdims=True)

        @pl.when(step == 0)
        def _():
            sums[8:9, :] = gain
            sums[9:10, :] = shift
            sums[0:2, :] = sums2[0:2, :]
            width = dy_sum.shape[1]
            first = where[0] == 0
            parts = bias_sum.shape[1] // width
            for part in range(parts):
                at = slice(part * width, (part + 1) * width)
                row = bias_sum[:, at] + bias_sum_o[:, at]
                sums[2 + part : 3 + part, :] = jnp.where(first, row, 0.0)
                at = 2 + parts + part
                sums[at : at + 1, :] = jnp.where(first, 0.0, row)
            sums[6:7, :] = dy_sum[...]
            sums[7:8, :] = dc_sum[...]
            lane = lax.broadcasted_iota(jnp.int32, (1, width), 1)
            own_heads = slope_parts.shape[0]
            slope = jnp.zeros((1, width), F32)
            for head in range(own_heads):
                here = lane == where[0] * own_heads + head
                slope += jnp.where(here, slope_parts[head, 0:1, 0:1], 0.0)
            sums[10:11, :] = slope
            sums[11:16, :] = jnp.zeros((5, width), F32)

        @pl.when(step > 0)
        def _():
            sums[8:9, :] += gain
            sums[9:10, :] += shift

    @pl.when(step < 4)
    def _():
        add_sums(g)

    @pl.when(step >= 4)
    def _():
        total = g + dot_nt(dq[...], weights[:, :cols])
        add_sums(total)

        @pl.when(step == 4)
        def _():
            g_own[...] = total

        @pl.when(step == 5)
        def _():
            sent[...] = total.astype(BF16)


def inputs_back(where, comp, mem, tok, other, dq, dk, dv, weights, small):
    rows, width = tok.shape
    cols = dk.shape[1]
    by_step = spec((rows, cols), lambda i, w: (i, 0))
    return call(
        inputs_kernel,
        "inputs_back",
        where,
        (6,),
        [whole(a) for a in (comp, mem, tok, other)]
        + [
            (dq, spec((rows, cols), lambda i, w: (jnp.maximum(i - 4, 0), 0))),
            (dk, by_step),
            (dv, by_step),
            whole(weights),
        ]
        + [whole(a) for a in small],
        [
            ((rows, width), F32, spec((rows, width))),
            ((rows, width), BF16, spec((rows, width))),
            ((16, width), F32, spec((16, width))),
        ],
        [pltpu.VMEM((rows, width), F32)],
    )


def local(
    tokens,
    memory,
    compressed,
    mask_start,
    norm1_gain,
    norm1_bias,
    query_weight,
    key_weight,
    value_weight,
    out_weight,
    slopes,
    norm2_gain,
    norm2_bias,
    in_weight,
    in_bias,
    hidden_weight,
    hidden_bias,
    compress_weight,
    compress_bias,
    grad_out,
    grad_compressed,
):
    tokens, memory, compressed = tokens[0], memory[0], compressed[0]
    grad_out, grad_compressed = grad_out[0], grad_compressed[0]
    rows, width = tokens.shape
    heads = slopes.shape[0]
    dp = lax.axis_size("dp")
    levels = dp.bit_length() - 1
    top = levels - 1
    d = lax.axis_index("dp")
    t = lax.axis_index("tm")
    segment = 2 * rows

    def swap(block):
        return lax.ppermute(block, "tm", [(0, 1), (1, 0)])

    def across(block, mask):
        return lax.ppermute(block, "dp", [(i, i ^ mask) for i in range(dp)])

    def after(array, *earlier):
        return lax.optimization_barrier((array,) + earlier)[0]

    def total_over(array, masks):
        def moved(mask):
            return lax.ppermute(array, ("dp", "tm"), [(i, i ^ mask) for i in range(2 * dp)])

        total = array
        if len(masks) > 0:
            total = total + moved(masks[0])
        if len(masks) > 1:
            total = total + (moved(masks[1]) + moved(masks[0] ^ masks[1]))
        return total

    def bit(level):
        return (d >> level) & 1

    class Shrink:
        def __init__(self, keep, send, order, columns=False, trade_axis=3):
            shape = keep.shape if keep.ndim == 4 else keep.shape[:1] + (1,) + keep.shape[1:]
            self.parts = keep.reshape(shape), send.reshape(shape)
            self.order = [0] + order
            self.trade_axis = trade_axis
            self.left = [level for level in range(1, top if columns else levels)]
            self.step = 0
            self.array = None

        def trade(self):
            axis = self.trade_axis
            size = self.array.shape[axis] // 2
            keep = lax.dynamic_slice_in_dim(self.array, t * size, size, axis)
            got = swap(lax.dynamic_slice_in_dim(self.array, (1 - t) * size, size, axis))
            same = bit(top) == t
            self.parts = jnp.where(same, keep, got), jnp.where(same, got, keep)

        def cut(self):
            if self.parts is not None:
                return self.parts[1]
            if self.step == len(self.order):
                return self.array
            level = self.order[self.step]
            if level in self.left:
                low = 1 << self.left.index(level)
                blocks, rest = self.array.shape[0], self.array.shape[1:]
                split = self.array.reshape((blocks // (2 * low), 2, low) + rest)
                self.parts = tuple(
                    lax.dynamic_index_in_dim(split, at, 1, keepdims=False).reshape(
                        (blocks // 2,) + rest
                    )
                    for at in (bit(level), 1 - bit(level))
                )
                self.left.remove(level)
            else:
                self.trade()
            return self.parts[1]

        def add(self):
            if self.step == len(self.order):
                return self.array
            self.cut()
            keep, send = self.parts
            got = across(send, 1 << self.order[self.step])
            self.step += 1
            total = keep.astype(F32) + got.astype(F32)
            last = self.step == len(self.order)
            self.array = total if last else total.astype(BF16)
            self.parts = None
            return self.array

        def wait(self, *earlier):
            if self.parts is not None:
                self.parts = after(self.parts[0], *earlier), self.parts[1]

        def finish(self):
            while self.step < len(self.order):
                self.add()
            return self.array[0]

    sideways = list(range(1, levels))
    upward = list(range(2, levels)) + [1] if levels > 1 else []
    between = upward[:1] + upward[-1:] + upward[1:-1] if levels > 2 else upward

    sharing = min(levels, 4)
    share = 1 << sharing
    ups = [z << 2 for z in range(1 << max(sharing - 2, 0))]
    offsets = [x + z for x in ((0, 2) if sharing > 1 else (0,)) for z in ups]
    low_bits = d & (share - 1)
    targets = [low_bits ^ off for off in offsets] + [low_bits ^ off ^ 1 for off in offsets]
    where = jnp.stack([t, bit(0)] + targets).astype(jnp.int32)

    def gather_up(piece):
        return jnp.concatenate([piece] + [across(piece, z) for z in ups[1:]], 0)

    def gather_side(block):
        return jnp.concatenate((block, across(block, 2)), 0) if sharing > 1 else block

    first, second = pieces(
        jnp.stack((low_bits, 1 - t)).astype(jnp.int32),
        share,
        query_weight,
        key_weight,
        value_weight,
        out_weight,
        in_weight,
    )
    first, second = swap(first), swap(second)
    slots = grad_compressed.shape[0]
    dc = jnp.pad(grad_compressed, ((0, -slots % 16), (0, 0)))
    x_other = swap(jnp.concatenate((compressed, memory, tokens), 0))
    first = gather_side(gather_up(first))
    first_got = across(first, 1)
    second_up = gather_up(second)
    second = gather_side(after(second_up, first))
    second_got = across(second, 1)
    dc_other, dy_other = swap(after(dc, x_other)), swap(after(grad_out, x_other))

    inputs_low, queries, keys, values, qkv = project(
        where,
        compressed,
        memory,
        tokens,
        x_other,
        after(norm1_gain, second),
        norm1_bias,
        query_weight,
        key_weight,
        value_weight,
        first,
        first_got,
    )

    index = jnp.arange(segment, dtype=jnp.int32)
    slot = jnp.where(index < rows, index + t * rows, index - rows + (1 - t) * rows)
    place = jnp.concatenate((-segment - 3 * (segment - slot), slot - segment, slot)).astype(F32)
    closed = jnp.where(slot >= mask_start[0], 0.0, NEG)
    closed = jnp.concatenate((closed, jnp.zeros((2 * segment,), F32)))
    place = jnp.stack((place, closed))
    own_heads = heads // 2
    slopes_own = lax.dynamic_slice_in_dim(slopes, t * own_heads, own_heads, 0)
    squeeze_stay, squeeze_away, keep, send, dc_sum = squeeze_rows(
        where, dp, slots, after(memory, queries), x_other, dc, dc_other, compress_weight
    )
    squeeze = Shrink(keep, send, sideways)
    queries = after(queries, squeeze_away)
    mix_other, lse_other = attend(where, 1, slopes_own, queries, keys, values, place)
    far_own = swap(mix_other)
    mix_own, lse_own = attend(
        where, 0, slopes_own, after(queries, mix_other), keys, values, place
    )
    far_other = swap(mix_own)
    dys = grad_out, dy_other
    mix = mix_own, mix_other
    chunk = in_weight.shape[1] // 8

    def feed_rows(mixed, far, tok, tok_at, dy, kept):
        return feed(
            where,
            mixed,
            far,
            tok,
            tok_at,
            out_weight,
            norm2_gain,
            norm2_bias,
            dy,
            in_weight,
            in_bias,
            hidden_weight,
            (second, second_got),
            chunk,
            kept,
        )

    squeeze.add()
    residual, normed, act, grad_pre, g_own, sent, out_own, bias_sum, dy_sum = feed_rows(
        after(mix_own, squeeze.cut()), far_own, tokens, 0, grad_out, F32
    )
    got_other = swap(sent)
    residual_o, normed_o, act_o, grad_pre_o, g_other, sent, out_sent, bias_sum_o, _ = feed_rows(
        after(mix_other, sent), far_other, x_other, 2, dy_other, BF16
    )
    got = swap(sent), got_other
    bias_sums = bias_sum, bias_sum_o
    squeeze.add()
    hidden = Shrink(
        *hidden_grad(where, dp, dys, (act, after(act_o, squeeze.cut())), chunk), sideways
    )
    entry = Shrink(
        *entry_grad(
            where, dp, (after(grad_pre, hidden.cut()), grad_pre_o), (normed, normed_o), chunk
        ),
        between,
        True,
        2,
    )
    entry_send = entry.cut()
    grad_residual, grad_mixture, sums2, keep, send = middle(
        where,
        dp,
        (after(g_own, entry_send), g_other),
        got,
        (residual, residual_o),
        norm2_gain,
        dys,
        out_weight,
        mix,
    )
    mix_out = Shrink(keep, send, sideways)
    out_got = swap(after(out_sent, grad_mixture))
    squeeze_got = swap(after(squeeze_away, grad_mixture))
    squeeze.add()
    hidden.add()
    entry.add()
    dq, dk, dv, dq_turned, dk_turned, dv_turned, slope_parts = attend_back(
        where,
        slopes_own,
        queries,
        keys,
        values,
        after(grad_mixture, hidden.cut(), entry.cut(), squeeze.cut()),
        place,
        (lse_own, lse_other),
    )
    output = (after(residual, dq) + (out_own + out_got.astype(F32)) + hidden_bias).astype(BF16)
    new_compressed = (
        after(squeeze_stay, dq)[:slots] + squeeze_got[:slots].astype(F32) + compress_bias
    ).astype(BF16)
    mix_out.wait(dq)
    left_keep, left_send, right_keep, right_send = trio(
        where, dp, dq_turned, dk_turned, dv_turned, inputs_low
    )
    left = Shrink(left_keep, left_send, sideways, True)
    right = Shrink(right_keep, right_send, upward, True)
    hidden.add()
    entry.add()
    left.wait(hidden.cut())
    right.wait(entry.cut())
    left.add()
    right.add()
    mix_out.add()
    squeeze.add()
    g1_own, g1_sent, smalls = inputs_back(
        where,
        compressed,
        memory,
        tokens,
        x_other,
        after(
            dq, left.cut(), right.cut(), hidden.cut(), entry.cut(), squeeze.array
        ),
        dk,
        dv,
        qkv,
        (sums2, *bias_sums, dy_sum, dc_sum, slope_parts),
    )
    left.wait(g1_sent)
    right.wait(g1_sent)
    left.add()
    right.add()
    smalls, g1_sent = (
        after(smalls, left.array, right.array),
        after(g1_sent, left.array, right.array),
    )
    groups = (hidden, entry, left, right, mix_out, squeeze)
    rounds = [(1, 2), (4,)] + [(8, 16)] + [(2 << level,) for level in range(4, levels)]
    rounds = [tuple(m for m in round_of if m <= dp) for round_of in rounds]
    for step in range(max(levels, len(rounds))):
        sends = [group.cut() for group in groups]
        for mask in rounds[step : step + 1]:
            smalls = total_over(after(smalls, *sends), mask)
        for group in groups:
            group.wait(*sends)
            group.add()

    g1 = g1_own + swap(g1_sent).astype(F32)
    unit1, rstd1 = rows_stats(tokens.astype(F32))
    grad_tokens = (grad_residual + norm_back(g1, norm1_gain, unit1, rstd1)).astype(BF16)

    trio_parts = jnp.concatenate((left.finish(), right.finish()), 2)
    grad_query_w, grad_key_w, grad_value_w = [trio_parts[i].T for i in range(3)]
    grad_in_w = entry.finish()[0]
    grad_hidden_w, grad_out_w, grad_compress_w = [
        group.finish()[0].T for group in (hidden, mix_out, squeeze)
    ]

    gain2, bias2, hidden_b, compress_b, gain1, bias1, slope = [
        smalls[i] for i in (0, 1, 6, 7, 8, 9, 10)
    ]
    in_b = smalls[2:6].reshape(-1)
    return (
        output[None],
        new_compressed[None],
        grad_tokens[None],
        gain1,
        bias1,
        grad_query_w,
        grad_key_w,
        grad_value_w,
        grad_out_w,
        slope[:heads],
        gain2,
        bias2,
        grad_in_w,
        in_b,
        grad_hidden_w,
        hidden_b,
        grad_compress_w,
        compress_b,
    )


def solution(mesh):
    split, whole, kept = P("dp", "tm", None), P(), P("tm", None)
    in_specs = (
        (split,) * 3
        + (P("dp"), whole, whole)
        + (kept,) * 4
        + (whole,) * 3
        + (kept, whole, kept, whole, kept, whole)
        + (split,) * 2
    )
    shared = P("tm", "dp")
    out_specs = (
        (split,) * 3
        + (whole,) * 2
        + (shared,) * 4
        + (whole,) * 3
        + (shared, whole, shared, whole, shared, whole)
    )
    return jax.shard_map(local, mesh=mesh, in_specs=in_specs, out_specs=out_specs, check_vma=False)
```

```python
import functools

import jax
import jax.numpy as jnp
from jax import lax
from jax.experimental import pallas as pl
from jax.experimental.pallas import tpu as pltpu
from jax.sharding import PartitionSpec as P

EPS = 1e-05
NEG = -1e30
LOG2E = 1.4426950408889634
F32 = jnp.float32
BF16 = jnp.bfloat16
TINY = pl.CostEstimate(flops=1000, bytes_accessed=1000, transcendentals=0)
LARGE = pl.CostEstimate(flops=20 * 10**9, bytes_accessed=10**6, transcendentals=0)
PARAMS = pltpu.CompilerParams(vmem_limit_bytes=52 * 2**20)


def dot(a, b, dims=((1,), (0,))):
    return lax.dot_general(a, b, (dims, ((), ())), preferred_element_type=F32)


def dot_nt(a, b):
    return dot(a, b, ((1,), (1,)))


def dot_tn(a, b):
    return dot(a, b, ((0,), (0,)))


def rows_stats(x):
    mean = jnp.mean(x, -1, keepdims=True)
    centered = x - mean
    rstd = lax.rsqrt(jnp.mean(centered * centered, -1, keepdims=True) + EPS)
    return centered * rstd, rstd


def norm_back(grad, gain, normed, rstd):
    dn = grad * gain
    return rstd * (
        dn
        - jnp.mean(dn, -1, keepdims=True)
        - normed * jnp.mean(dn * normed, -1, keepdims=True)
    )


def spec(shape, at=None):
    zeros = (0,) * len(shape)
    return pl.BlockSpec(shape, at if at is not None else (lambda *_: zeros))


def call(kernel, name, where, grid, ins, outs, scratch=(), cost=TINY, onto=None):
    onto = onto or {}
    count = len(ins)
    ins = list(ins) + [(array, pl.BlockSpec(memory_space=pl.ANY)) for array in onto.values()]

    def body(place, *refs):
        kernel(place, *refs[:count], *refs[len(ins) :])

    return pl.pallas_call(
        body,
        grid_spec=pltpu.PrefetchScalarGridSpec(
            num_scalar_prefetch=1,
            grid=grid,
            in_specs=[at for _, at in ins],
            out_specs=[at for _, _, at in outs],
            scratch_shapes=list(scratch),
        ),
        out_shape=[jax.ShapeDtypeStruct(shape, dtype) for shape, dtype, _ in outs],
        input_output_aliases={1 + count + i: out for i, out in enumerate(onto)},
        compiler_params=PARAMS,
        cost_estimate=cost,
        name=name,
    )(where, *[array for array, _ in ins])


def whole(array):
    return array, spec(array.shape)


def ordered(first, own, other, axis):
    return jnp.where(
        first, jnp.concatenate((own, other), axis), jnp.concatenate((other, own), axis)
    )


def place_pieces(where, parts, target, base=0, half=None):
    size = (half or target.shape[0]) // (where.shape[0] - 2)
    at = 0
    for part in parts:
        for block in range(part.shape[0] // size):
            row = pl.multiple_of(base + where[2 + at] * size, size)
            target[pl.ds(row, size), :] = part[block * size : (block + 1) * size, :]
            at += 1


def pieces_kernel(where, wq, wk, wv, wo, wi, first, second):
    size = wq.shape[1]
    first[:, :size] = wq[...]
    first[:, size : 2 * size] = wk[...]
    first[:, 2 * size :] = wv[...]
    second[:, : wo.shape[1]] = wo[...]
    second[:, wo.shape[1] :] = wi[...]


def pieces(where, share, wq, wk, wv, wo, wi):
    rows = wq.shape[0] // share
    cols = wq.shape[1] // 2
    wide = wi.shape[1] // 2
    half = spec((rows, cols), lambda i, w: (w[0], w[1]))
    return call(
        pieces_kernel,
        "pieces",
        where,
        (1,),
        [
            (wq, half),
            (wk, half),
            (wv, half),
            (wo, spec((rows, wo.shape[1]), lambda i, w: (w[0], 0))),
            (wi, spec((rows, wide), lambda i, w: (w[0], w[1]))),
        ],
        [
            ((rows, 3 * cols), BF16, spec((rows, 3 * cols))),
            ((rows, wo.shape[1] + wide), BF16, spec((rows, wo.shape[1] + wide))),
        ],
    )


def load_rows(step, x, comp, mem, tok, mem_o, comp_o, upper, lower):
    sources = (comp, comp_o, mem, mem_o, tok)
    for at, source in enumerate(sources):

        @pl.when(step == at)
        def _(source=source):
            x[...] = source[...].astype(F32)

    @pl.when(step == len(sources))
    def _():
        half = upper.shape[0]
        x[:half, :] = upper[...].astype(F32)
        x[half:, :] = lower[...].astype(F32)


def project_kernel(
    where,
    comp,
    mem,
    tok,
    mem_o,
    comp_o,
    upper,
    lower,
    gain,
    shift,
    wq,
    wk,
    wv,
    mine,
    got,
    low,
    q,
    k,
    v,
    weights,
    x,
):
    step = pl.program_id(0)
    load_rows(step, x, comp, mem, tok, mem_o, comp_o, upper, lower)
    half, cols = wq.shape

    @pl.when(step == 0)
    def _():
        own = pl.ds(pl.multiple_of(where[0] * half, half), half)
        for index, weight in enumerate((wq, wk, wv)):
            weights[own, index * cols : (index + 1) * cols] = weight[...]
        place_pieces(where, (mine, got), weights, (1 - where[0]) * half, half)

    unit, _ = rows_stats(x[...])
    n = (unit * gain[...] + shift[...]).astype(BF16)
    low[...] = n
    k[...] = dot(n, weights[:, cols : 2 * cols]).astype(BF16)
    v[...] = dot(n, weights[:, 2 * cols :]).astype(BF16)

    @pl.when(step >= 4)
    def _():
        q[...] = dot(n, weights[:, :cols]).astype(BF16)


def project(where, comp, mem, tok, mem_o, other, gain, shift, wq, wk, wv, mine, got):
    rows, width = tok.shape
    cols = wq.shape[1] // 2
    half = spec((wq.shape[0], cols), lambda i, w: (0, w[0]))

    def by_step(size):
        return spec((rows, size), lambda i, w: (i, 0))

    return call(
        project_kernel,
        "project",
        where,
        (6,),
        [whole(a) for a in (comp, mem, tok, mem_o, *other, gain[None], shift[None])]
        + [(wq, half), (wk, half), (wv, half), whole(mine), whole(got)],
        [
            ((6 * rows, width), BF16, by_step(width)),
            ((2 * rows, cols), BF16, spec((rows, cols), lambda i, w: (jnp.maximum(i - 4, 0), 0))),
            ((6 * rows, cols), BF16, by_step(cols)),
            ((6 * rows, cols), BF16, by_step(cols)),
            ((width, 3 * cols), BF16, spec((width, 3 * cols))),
        ],
        [pltpu.VMEM((rows, width), F32)],
        cost=LARGE,
    )


def split_pairs(where, total, height, keep, send):
    pairs = total.reshape(total.shape[0] // (2 * height), 2, height, total.shape[1])
    even = where[1] == 0
    keep[...] = jnp.where(even, pairs[:, 0], pairs[:, 1]).astype(BF16)
    send[...] = jnp.where(even, pairs[:, 1], pairs[:, 0]).astype(BF16)


def by_parity(where, total, height):
    pairs = total.reshape(total.shape[0] // (2 * height), 2, height, total.shape[1])
    even = where[1] == 0
    shape = (total.shape[0] // 2, total.shape[1])
    keep = jnp.where(even, pairs[:, 0], pairs[:, 1]).reshape(shape)
    return keep, jnp.where(even, pairs[:, 1], pairs[:, 0]).reshape(shape)


def squeeze_kernel(slots, where, mem, mem_o, dc, dc_o, weight, stay, away, keep, send, dc_sum):
    t = where[0]
    dc_sum[...] = jnp.sum(dc[...].astype(F32), 0, keepdims=True)
    rows, width = mem.shape
    padded = dc.shape[0]
    half = width // 2
    lead = 3 * 2 * slots - 2 * rows
    first = t == 0
    shape = (padded, rows)
    slot = lax.broadcasted_iota(jnp.int32, shape, 0)
    row = lax.broadcasted_iota(jnp.int32, shape, 1)
    mem_half = jnp.where(first, mem[:, :half], mem[:, half:])
    mem_o_half = jnp.where(first, mem_o[:, :half], mem_o[:, half:])

    def picked(slot_half, row_half, offset):
        place = 3 * (slot + slot_half * slots) + offset - lead
        hit = (place == row + row_half * rows) & (slot < slots)
        return jnp.where(hit, 1.0, 0.0).astype(BF16)

    def windows(slot_half):
        edge = dot(picked(slot_half, t, 2 * t), mem[...]) + dot(
            picked(slot_half, 1 - t, 2 * t), mem_o[...]
        )
        middle = dot(picked(slot_half, t, 1), mem_half) + dot(
            picked(slot_half, 1 - t, 1), mem_o_half
        )
        return ordered(first, edge, middle, 1).astype(BF16)

    both = jnp.concatenate((windows(t), windows(1 - t)), 0)
    slots_out = dot(both, weight[...])
    stay[...] = slots_out[:padded, :]
    away[...] = slots_out[padded:, :].astype(BF16)
    turned_dc = jnp.concatenate((dc[...], dc_o[...]), 0).T
    columns = both.shape[1]
    height = keep.shape[1]
    for at in range(0, columns, half):
        part = slice(at, at + half)
        total = dot(turned_dc, both[:, part])
        split_pairs(where, total, height, keep.at[:, :, part], send.at[:, :, part])


def squeeze_rows(where, dp, slots, mem, mem_o, dc, dc_o, weight):
    padded, width = dc.shape
    half = ((dp // 2, width // dp, weight.shape[0]), BF16)
    ins = [whole(a) for a in (mem, mem_o, dc, dc_o, weight)]
    return call(
        functools.partial(squeeze_kernel, slots),
        "squeeze",
        where,
        (1,),
        ins,
        [
            ((padded, width), F32, spec((padded, width))),
            ((padded, width), BF16, spec((padded, width))),
            half + (spec(half[0]),),
            half + (spec(half[0]),),
            ((1, width), F32, spec((1, width))),
        ],
        cost=LARGE,
    )


def masked_scores(place, slope, q, keys, scale, first, tail):
    bias = place[0:1, :] * slope + place[1:2, :]
    chunk = q.shape[0]
    query_place = (lax.broadcasted_iota(jnp.int32, (chunk, 1), 0) + first).astype(F32)
    scores = dot_nt(q, keys) * (scale * LOG2E) + bias
    recent = jnp.where(place[0:1, tail:] <= query_place, scores[:, tail:], NEG)
    return jnp.concatenate((scores[:, :tail], recent), 1), query_place


def attend_kernel(turn, scale, where, slopes, q, k, v, place, mix, lse):
    slope = slopes[pl.program_id(0)] * LOG2E
    rows = q.shape[0]
    first = jnp.abs(turn - where[0]) * rows
    scores, _ = masked_scores(place, slope, q[...], k[...], scale, first, k.shape[0] - 2 * rows)
    highest = jnp.max(scores, -1, keepdims=True)
    weights = jnp.exp2(scores - highest)
    total = jnp.sum(weights, -1, keepdims=True)
    mix[...] = (dot(weights.astype(BF16), v[...]) * (1.0 / total)).astype(BF16)
    lse[0] = highest + jnp.log2(total)


def attend(where, turn, slopes, q, k, v, place):
    rows, width = q.shape[0] // 2, q.shape[1]
    heads = slopes.shape[0]
    hw = width // heads
    keys = k.shape[0]
    by_head = spec((keys, hw), lambda h, w: (0, h))
    return call(
        functools.partial(attend_kernel, turn, hw**-0.5),
        "attend",
        where,
        (heads,),
        [
            (slopes, pl.BlockSpec(memory_space=pltpu.SMEM)),
            (q, spec((rows, hw), lambda h, w: (turn, h))),
            (k, by_head),
            (v, by_head),
            whole(place),
        ],
        [
            ((rows, width), BF16, spec((rows, hw), lambda h, w: (0, h))),
            ((heads, rows, 1), F32, spec((1, rows, 1), lambda h, w: (h, 0, 0))),
        ],
        cost=LARGE,
    )


def attend_back_kernel(
    chunk,
    scale,
    height,
    where,
    slopes,
    q,
    k,
    v,
    dm,
    place,
    lse_own,
    lse_other,
    dq,
    dk,
    dv,
    q_keep,
    q_send,
    kv_keep,
    kv_send,
    slope_out,
    dk_sum,
    dv_sum,
):
    slope = slopes[pl.program_id(0)] * LOG2E
    keys = k.shape[0]
    rows = q.shape[0]
    half = rows // 2
    columns = jnp.zeros((1, keys), F32)
    by_row = jnp.zeros((1, 1), F32)
    dq_parts = []
    for step in range(rows // chunk):
        at = slice(step * chunk, (step + 1) * chunk)
        time_half = where[0] if step * chunk < half else 1 - where[0]
        scores, query_place = masked_scores(
            place,
            slope,
            q[at, :],
            k[...],
            scale,
            time_half * half + step * chunk % half,
            keys - rows,
        )
        weights = jnp.exp2(scores - (lse_own if step == 0 else lse_other)[0])
        low = weights.astype(BF16)
        grads = dot_nt(dm[at, :], v[...])
        shift = jnp.sum(weights * grads, -1, keepdims=True)
        ds = (weights * (grads - shift)).astype(BF16)
        dq_part = dot(ds, k[...]) * scale
        dq[at, :] = dq_part.astype(BF16)
        dq_parts.append(dq_part.T)
        dk_part = dot_tn(q[at, :], ds)
        dv_part = dot_tn(dm[at, :], low)
        if step == 0:
            dk_sum[...] = dk_part
            dv_sum[...] = dv_part
        else:
            dk_sum[...] += dk_part
            dv_sum[...] += dv_part
        wide = ds.astype(F32)
        columns += jnp.sum(wide, 0, keepdims=True)
        by_row += jnp.sum(jnp.sum(wide, -1, keepdims=True) * query_place, 0, keepdims=True)
    dk_all, dv_all = dk_sum[...] * scale, dv_sum[...]
    dq_halves = by_parity(where, jnp.concatenate(dq_parts, 1), height)
    dk_halves, dv_halves = by_parity(where, dk_all, height), by_parity(where, dv_all, height)
    for q_part, kv_part, dq_half, dk_half, dv_half in zip(
        (q_keep, q_send), (kv_keep, kv_send), dq_halves, dk_halves, dv_halves
    ):
        blocks = [half.reshape(half.shape[0] // height, height, keys) for half in (dv_half, dk_half)]
        q_part[...] = dq_half.astype(BF16)
        kv_part[...] = jnp.stack(blocks, 1).reshape(kv_part.shape).astype(BF16)
    dk[...] = dk_all.T.astype(BF16)
    dv[...] = dv_all.T.astype(BF16)
    total = jnp.sum(columns * place[0:1, :], -1, keepdims=True) - by_row
    slope_out[...] = jnp.broadcast_to(total.reshape(1, 1, 1), slope_out.shape)


def attend_back(where, height, slopes, q, k, v, dm, place, lses):
    rows, width = q.shape
    heads = slopes.shape[0]
    hw = width // heads
    keys = k.shape[0]
    by_rows = spec((rows, hw), lambda h, w: (0, h))
    by_keys = spec((keys, hw), lambda h, w: (0, h))
    return call(
        functools.partial(attend_back_kernel, rows // 2, hw**-0.5, height),
        "attend_back",
        where,
        (heads,),
        [
            (slopes, pl.BlockSpec(memory_space=pltpu.SMEM)),
            (q, by_rows),
            (k, by_keys),
            (v, by_keys),
            (dm, by_rows),
            whole(place),
            (lses[0], spec((1, rows // 2, 1), lambda h, w: (h, 0, 0))),
            (lses[1], spec((1, rows // 2, 1), lambda h, w: (h, 0, 0))),
        ],
        [
            ((rows, width), BF16, by_rows),
            ((keys, width), BF16, by_keys),
            ((keys, width), BF16, by_keys),
            ((width // 2, rows), BF16, spec((hw // 2, rows), lambda h, w: (h, 0))),
            ((width // 2, rows), BF16, spec((hw // 2, rows), lambda h, w: (h, 0))),
            ((width, keys), BF16, spec((hw, keys), lambda h, w: (h, 0))),
            ((width, keys), BF16, spec((hw, keys), lambda h, w: (h, 0))),
            ((heads, 8, 128), F32, spec((1, 8, 128), lambda h, w: (h, 0, 0))),
        ],
        [pltpu.VMEM((hw, keys), F32), pltpu.VMEM((hw, keys), F32)],
    )


def gelu_pair(v):
    c = 0.7978845608028654
    inner = c * (v + 0.044715 * v * v * v)
    th = jnp.tanh(inner)
    slope = 0.5 * (1.0 + th) + 0.5 * v * (1.0 - th * th) * c * (1.0 + 3 * 0.044715 * v * v)
    return 0.5 * v * (1.0 + th), slope


def feed_kernel(height, block, where, *refs):
    (
        mix,
        far,
        tok,
        wo,
        wo_mine,
        wo_got,
        gain,
        shift,
        dy,
        wi,
        wi_mine,
        wi_got,
        bias,
        wh,
        residual,
        normed,
        act,
        grad_keep,
        grad_send,
        dy_keep,
        dy_send,
        g2,
        out,
        bias_sum,
        dy_sum,
        *sent,
        wo_far,
        weight,
        out_sum,
    ) = refs
    step = pl.program_id(0)
    half = wi.shape[0]

    @pl.when(step == 0)
    def _():
        place_pieces(where, (wo_mine, wo_got), wo_far)
        wide_dy = dy[...].astype(F32)
        dy_sum[...] = jnp.sum(wide_dy, 0, keepdims=True)
        dy_stay, dy_away = by_parity(where, wide_dy.T, height)
        dy_keep[...] = dy_stay.astype(BF16)
        dy_send[...] = dy_away.astype(BF16)
        total = tok[...].astype(F32) + (dot(mix[...], wo[...]) + dot(far[...], wo_far[...]))
        residual[...] = total
        unit, _ = rows_stats(total)
        normed[...] = (unit * gain[...] + shift[...]).astype(BF16)

    weight[pl.ds(pl.multiple_of(where[0] * half, half), half), :] = wi[...]
    place_pieces(where, (wi_mine, wi_got), weight, (1 - where[0]) * half, half)
    pre = dot(normed[...], weight[...]) + bias[...]
    value, slope = gelu_pair(pre)
    low = value.astype(BF16)
    act[...] = low
    grad = (dot_nt(dy[...], wh[...]) * slope).astype(BF16)
    blocks = [grad[:, at : at + block] for at in range(0, grad.shape[1], block)]
    evens, odds = jnp.concatenate(blocks[::2], 1), jnp.concatenate(blocks[1::2], 1)
    even = where[1] == 0
    grad_keep[...] = jnp.where(even, evens, odds)
    grad_send[...] = jnp.where(even, odds, evens)
    bias_sum[...] = jnp.sum(grad.astype(F32), 0, keepdims=True)
    g2_part = dot_nt(grad, weight[...])
    out_part = dot(low, wh[...])

    @pl.when(step == 0)
    def _():
        g2[...] = g2_part
        out_sum[...] = out_part

    @pl.when(step > 0)
    def _():
        g2[...] += g2_part
        out_sum[...] += out_part

    @pl.when(step == pl.num_programs(0) - 1)
    def _():
        first_row = 0
        for piece in sent:
            piece[...] = g2[first_row : first_row + piece.shape[0], :].astype(BF16)
            first_row += piece.shape[0]
        out[...] = out_sum[...].astype(out.dtype)


def feed(
    where, dp, turn, mix, far, tok, wo, gain, shift, dy, wi, bias, wh, second, chunk, kept, parts, onto
):
    rows, width = dy.shape
    hidden = wh.shape[0]
    steps = hidden // chunk
    mine, got = second
    by_cols = spec((rows, chunk), lambda j, w: (turn, j))
    by_half = spec((rows, chunk // 2), lambda j, w: (turn, j))
    half = (2 * rows, hidden // 2), BF16, by_half
    turned = (width // 2, 2 * rows), BF16, spec((width // 2, rows), lambda j, w: (0, turn))
    wo_part = spec((mine.shape[0], width), lambda j, w: (0, 0))
    wi_part = spec((mine.shape[0], chunk), lambda j, w: (0, width // chunk + j))

    def once(dtype):
        return (rows, width), dtype, spec((rows, width))

    return call(
        functools.partial(feed_kernel, width // dp, hidden // (dp // 2)),
        "feed",
        where,
        (steps,),
        [
            whole(mix),
            whole(far),
            whole(tok),
            whole(wo),
            (mine, wo_part),
            (got, wo_part),
            whole(gain[None]),
            whole(shift[None]),
            whole(dy),
            (wi, spec((wi.shape[0], chunk), lambda j, w: (0, w[0] * steps + j))),
            (mine, wi_part),
            (got, wi_part),
            (bias[None], spec((1, chunk), lambda j, w: (0, w[0] * steps + j))),
            (wh, spec((chunk, width), lambda j, w: (j, 0))),
        ],
        [
            once(F32),
            ((2 * rows, width), BF16, spec((rows, width), lambda j, w: (turn, 0))),
            ((2 * rows, hidden), BF16, by_cols),
            half,
            half,
            turned,
            turned,
            once(F32),
            once(kept),
            ((1, hidden), F32, spec((1, chunk), lambda j, w: (0, j))),
            ((1, width), F32, spec((1, width))),
        ]
        + [((rows // part, width), BF16, spec((rows // part, width))) for part in parts],
        [
            pltpu.VMEM(wo.shape, BF16),
            pltpu.VMEM((width, chunk), BF16),
            pltpu.VMEM((rows, width), F32),
        ],
        cost=LARGE,
        onto=onto,
    )


def middle_kernel(
    where,
    g_own,
    g_other,
    got_first,
    got_second,
    got_third,
    got_other,
    residual_own,
    residual_other,
    gain,
    dy,
    dy_o,
    wo,
    mix_own,
    mix_other,
    grad_res,
    dm,
    sums,
    keep,
    send,
):
    rows = dy.shape[0]
    lows = []
    got_own = jnp.concatenate((got_first[...], got_second[...], got_third[...]), 0)
    halves = ((g_own, got_own, dy, residual_own), (g_other, got_other, dy_o, residual_other))
    for at, (g, got, d, residual) in enumerate(halves):
        here = slice(at * rows, (at + 1) * rows)
        grad = g[...] + got[...].astype(F32)
        unit, rstd = rows_stats(residual[...])
        total = d[...].astype(F32) + norm_back(grad, gain[...], unit, rstd)
        low = total.astype(BF16)
        lows.append(low)
        dm[here, :] = dot_nt(low, wo[...]).astype(BF16)
        if at == 0:
            grad_res[...] = total
            sums[0:1, :] = jnp.sum(grad * unit, 0, keepdims=True)
            sums[1:2, :] = jnp.sum(grad, 0, keepdims=True)
    split_pairs(
        where, dot_tn(lows[0], mix_own[...]) + dot_tn(lows[1], mix_other[...]), keep.shape[1], keep, send
    )


def middle(where, dp, g, got, residuals, gain, dys, wo, mix):
    rows, width = dys[0].shape
    heads = wo.shape[0]
    half = ((dp // 2, width // dp, heads), BF16, spec((dp // 2, width // dp, heads)))
    return call(
        middle_kernel,
        "middle",
        where,
        (1,),
        [whole(a) for a in (*g, *got, *residuals, gain[None], *dys, wo, *mix)],
        [
            ((rows, width), F32, spec((rows, width))),
            ((2 * rows, heads), BF16, spec((2 * rows, heads))),
            ((8, width), F32, spec((8, width))),
            half,
            half,
        ],
    )


def inputs_kernel(
    where, comp, mem, tok, mem_o, comp_o, upper, lower, dq, dk, dv, weights, sums2, bias_sum, bias_sum_o, dy_sum, dc_sum, slope_parts, g_own, sent, sums, x
):
    step = pl.program_id(0)
    load_rows(step, x, comp, mem, tok, mem_o, comp_o, upper, lower)
    cols = dk.shape[1]
    g = dot_nt(dk[...], weights[:, cols : 2 * cols]) + dot_nt(dv[...], weights[:, 2 * cols :])
    unit, _ = rows_stats(x[...])

    def add_sums(total):
        gain = jnp.sum(total * unit, 0, keepdims=True)
        shift = jnp.sum(total, 0, keepdims=True)

        @pl.when(step == 0)
        def _():
            sums[8:9, :] = gain
            sums[9:10, :] = shift
            sums[0:2, :] = sums2[0:2, :]
            width = dy_sum.shape[1]
            first = where[0] == 0
            parts = bias_sum.shape[1] // width
            for part in range(parts):
                at = slice(part * width, (part + 1) * width)
                row = bias_sum[:, at] + bias_sum_o[:, at]
                sums[2 + part : 3 + part, :] = jnp.where(first, row, 0.0)
                at = 2 + parts + part
                sums[at : at + 1, :] = jnp.where(first, 0.0, row)
            sums[6:7, :] = dy_sum[...]
            sums[7:8, :] = dc_sum[...]
            lane = lax.broadcasted_iota(jnp.int32, (1, width), 1)
            own_heads = slope_parts.shape[0]
            slope = jnp.zeros((1, width), F32)
            for head in range(own_heads):
                here = lane == where[0] * own_heads + head
                slope += jnp.where(here, slope_parts[head, 0:1, 0:1], 0.0)
            sums[10:11, :] = slope
            sums[11:16, :] = jnp.zeros((5, width), F32)

        @pl.when(step > 0)
        def _():
            sums[8:9, :] += gain
            sums[9:10, :] += shift

    @pl.when(step < 4)
    def _():
        add_sums(g)

    @pl.when(step >= 4)
    def _():
        total = g + dot_nt(dq[...], weights[:, :cols])
        add_sums(total)

        @pl.when(step == 4)
        def _():
            g_own[...] = total

        @pl.when(step == 5)
        def _():
            sent[...] = total.astype(BF16)


def inputs_back(where, comp, mem, tok, mem_o, other, dq, dk, dv, weights, small):
    rows, width = tok.shape
    cols = dk.shape[1]
    by_step = spec((rows, cols), lambda i, w: (i, 0))
    return call(
        inputs_kernel,
        "inputs_back",
        where,
        (6,),
        [whole(a) for a in (comp, mem, tok, mem_o, *other)]
        + [
            (dq, spec((rows, cols), lambda i, w: (jnp.maximum(i - 4, 0), 0))),
            (dk, by_step),
            (dv, by_step),
            whole(weights),
        ]
        + [whole(a) for a in small],
        [
            ((rows, width), F32, spec((rows, width))),
            ((rows, width), BF16, spec((rows, width))),
            ((16, width), F32, spec((16, width))),
        ],
        [pltpu.VMEM((rows, width), F32)],
        cost=LARGE,
    )


def turn_kernel(source, target):
    target[...] = source[...].T


def turned(array):
    return pl.pallas_call(
        turn_kernel,
        out_shape=jax.ShapeDtypeStruct(array.shape[::-1], F32),
        compiler_params=PARAMS,
        cost_estimate=TINY,
        name="turn",
    )(array)


def local(
    tokens,
    memory,
    compressed,
    mask_start,
    norm1_gain,
    norm1_bias,
    query_weight,
    key_weight,
    value_weight,
    out_weight,
    slopes,
    norm2_gain,
    norm2_bias,
    in_weight,
    in_bias,
    hidden_weight,
    hidden_bias,
    compress_weight,
    compress_bias,
    grad_out,
    grad_compressed,
):
    tokens, memory, compressed = tokens[0], memory[0], compressed[0]
    grad_out, grad_compressed = grad_out[0], grad_compressed[0]
    rows, width = tokens.shape
    heads = slopes.shape[0]
    dp = lax.axis_size("dp")
    levels = dp.bit_length() - 1
    top = levels - 1
    d = lax.axis_index("dp")
    t = lax.axis_index("tm")
    segment = 2 * rows

    def swap(block):
        return lax.ppermute(block, "tm", [(0, 1), (1, 0)])

    def across(block, mask):
        return lax.ppermute(block, "dp", [(i, i ^ mask) for i in range(dp)])

    def after(array, *earlier):
        return lax.optimization_barrier((array,) + earlier)[0]

    def total_over(array, masks):
        def moved(mask):
            return lax.ppermute(array, ("dp", "tm"), [(i, i ^ mask) for i in range(2 * dp)])

        total = array
        if len(masks) > 0:
            total = total + moved(masks[0])
        if len(masks) > 1:
            total = total + (moved(masks[1]) + moved(masks[0] ^ masks[1]))
        return total

    def bit(level):
        return (d >> level) & 1

    class Shrink:
        def __init__(self, keep, send, order, columns=False, trade_axis=3):
            shape = keep.shape if keep.ndim == 4 else keep.shape[:1] + (1,) + keep.shape[1:]
            self.parts = keep.reshape(shape), send.reshape(shape)
            self.order = [0] + order
            self.trade_axis = trade_axis
            self.left = [level for level in range(1, top if columns else levels)]
            self.step = 0
            self.array = None
            self.got = None

        def trade(self):
            axis = self.trade_axis
            size = self.array.shape[axis] // 2
            keep = lax.dynamic_slice_in_dim(self.array, t * size, size, axis)
            got = swap(lax.dynamic_slice_in_dim(self.array, (1 - t) * size, size, axis))
            same = bit(top) == t
            self.parts = jnp.where(same, keep, got), jnp.where(same, got, keep)

        def cut(self):
            if self.parts is not None:
                return self.parts[1]
            if self.step == len(self.order):
                return self.array
            level = self.order[self.step]
            if level in self.left:
                low = 1 << self.left.index(level)
                blocks, rest = self.array.shape[0], self.array.shape[1:]
                split = self.array.reshape((blocks // (2 * low), 2, low) + rest)
                self.parts = tuple(
                    lax.dynamic_index_in_dim(split, at, 1, keepdims=False).reshape(
                        (blocks // 2,) + rest
                    )
                    for at in (bit(level), 1 - bit(level))
                )
                self.left.remove(level)
            else:
                self.trade()
            return self.parts[1]

        def add(self):
            if self.step == len(self.order):
                return self.array
            self.cut()
            keep, send = self.parts
            got = self.got if self.got is not None else across(send, 1 << self.order[self.step])
            self.got = None
            self.step += 1
            total = keep.astype(F32) + got.astype(F32)
            last = self.step == len(self.order)
            self.array = total if last else total.astype(BF16)
            self.parts = None
            return self.array

        def wait(self, *earlier):
            if self.parts is not None:
                self.parts = after(self.parts[0], *earlier), self.parts[1]

        def finish(self):
            while self.step < len(self.order):
                self.add()
            return self.array[0]

    def meet(groups, *earlier):
        gots = [across(group.cut(), 1 << group.order[group.step]) for group in groups]
        gots = lax.optimization_barrier(tuple(gots) + earlier)
        for group, got in zip(groups, gots):
            group.got = got
            group.add()

    sideways = list(range(1, levels))
    upward = list(range(2, levels)) + [1] if levels > 1 else []
    between = upward[:1] + upward[-1:] + upward[1:-1] if levels > 2 else upward

    sharing = min(levels, 4)
    share = 1 << sharing
    ups = [z << 2 for z in range(1 << max(sharing - 2, 0))]
    offsets = [x + z for x in ((0, 2) if sharing > 1 else (0,)) for z in ups]
    low_bits = d & (share - 1)
    targets = [low_bits ^ off for off in offsets] + [low_bits ^ off ^ 1 for off in offsets]
    where = jnp.stack([t, bit(0)] + targets).astype(jnp.int32)

    def gather_up(piece):
        return jnp.concatenate([piece] + [across(piece, z) for z in ups[1:]], 0)

    def gather_side(block):
        return jnp.concatenate((block, across(block, 2)), 0) if sharing > 1 else block

    first, second = pieces(
        jnp.stack((low_bits, 1 - t)).astype(jnp.int32),
        share,
        query_weight,
        key_weight,
        value_weight,
        out_weight,
        in_weight,
    )
    first, second = swap(first), swap(second)
    slots = grad_compressed.shape[0]
    dc = jnp.pad(grad_compressed, ((0, -slots % 16), (0, 0)))
    memory_other, dc_other = swap(memory), swap(dc)
    compressed_other = swap(after(compressed, memory_other))
    upper = swap(after(tokens[: rows // 2], compressed_other))
    lower = swap(after(tokens[rows // 2 :], upper))
    x_other = compressed_other, upper, lower
    first = gather_side(gather_up(first))
    first_got = across(first, 1)
    second = gather_side(gather_up(after(second, first)))
    second_got = across(second, 1)
    dy_other = swap(after(grad_out, lower))
    tokens_other = jnp.concatenate((upper, lower), 0)
    squeeze_stay, squeeze_away, keep, send, dc_sum = squeeze_rows(
        where, dp, slots, memory, memory_other, dc, dc_other, compress_weight
    )
    squeeze = Shrink(keep, send, sideways)

    inputs_low, queries, keys, values, qkv = project(
        where,
        compressed,
        memory,
        tokens,
        memory_other,
        x_other,
        after(norm1_gain, squeeze_away),
        norm1_bias,
        query_weight,
        key_weight,
        value_weight,
        first,
        first_got,
    )

    index = jnp.arange(segment, dtype=jnp.int32)
    slot = jnp.where(index < rows, index + t * rows, index - rows + (1 - t) * rows)
    place = jnp.concatenate((-segment - 3 * (segment - slot), slot - segment, slot)).astype(F32)
    closed = jnp.where(slot >= mask_start[0], 0.0, NEG)
    closed = jnp.concatenate((closed, jnp.zeros((2 * segment,), F32)))
    place = jnp.stack((place, closed))
    own_heads = heads // 2
    slopes_own = lax.dynamic_slice_in_dim(slopes, t * own_heads, own_heads, 0)
    queries = after(queries, second)
    mix_other, lse_other = attend(where, 1, slopes_own, queries, keys, values, place)
    far_own = swap(mix_other)
    mix_own, lse_own = attend(
        where, 0, slopes_own, after(queries, mix_other), keys, values, place
    )
    far_other = swap(mix_own)
    dys = grad_out, dy_other
    mix = mix_own, mix_other
    chunk = max(in_weight.shape[1] // 8, 2 * in_weight.shape[1] // dp)

    def feed_rows(turn, mixed, far, tok, dy, kept, parts, onto=None):
        return feed(
            where,
            dp,
            turn,
            mixed,
            far,
            tok,
            out_weight,
            norm2_gain,
            norm2_bias,
            dy,
            in_weight,
            in_bias,
            hidden_weight,
            (second, second_got),
            chunk,
            kept,
            parts,
            onto,
        )

    squeeze.add()
    residual, *half_filled, g_own, out_own, bias_sum, dy_sum, sent = feed_rows(
        0, after(mix_own, squeeze.cut()), far_own, tokens, grad_out, F32, (1,)
    )
    got_other = swap(sent)
    residual_o, *filled, g_other, out_sent, bias_sum_o, _, sent, near, rest = feed_rows(
        1,
        after(mix_other, sent),
        far_other,
        tokens_other,
        dy_other,
        BF16,
        (4, 4, 2),
        {1 + i: array for i, array in enumerate(half_filled)},
    )
    got_own = [swap(sent)]
    for piece in (near, rest):
        got_own.append(swap(after(piece, got_own[-1])))
    normed, act, grad_keep, grad_send, dy_keep, dy_send = filled
    bias_sums = bias_sum, bias_sum_o
    squeeze.wait(out_sent)
    squeeze.add()
    blocks = dp // 2

    def cut_rows(product, count):
        return product.astype(BF16).reshape(count, product.shape[0] // count, product.shape[1])

    hidden_send = dot(after(dy_send, squeeze.cut(), got_other), act).astype(BF16)
    entry_send = dot_tn(after(grad_send, hidden_send), normed).astype(BF16)
    hidden_keep = dot(after(dy_keep, entry_send), act).astype(BF16)
    entry_keep = dot_tn(after(grad_keep, hidden_keep), normed).astype(BF16)
    hidden = Shrink(cut_rows(hidden_keep, blocks), cut_rows(hidden_send, blocks), sideways)
    entry = Shrink(
        cut_rows(entry_keep, blocks // 2), cut_rows(entry_send, blocks // 2), between, True
    )
    hidden.add()
    entry.add()
    grad_residual, grad_mixture, sums2, keep, send = middle(
        where,
        dp,
        (after(g_own, hidden.cut(), entry.cut()), g_other),
        (*got_own, got_other),
        (residual, residual_o),
        norm2_gain,
        dys,
        out_weight,
        mix,
    )
    mix_out = Shrink(keep, send, sideways)
    out_got = swap(after(out_sent, grad_mixture))
    squeeze_got = swap(after(squeeze_away, grad_mixture))
    squeeze.add()
    height = key_weight.shape[1] // dp
    dq, dk, dv, q_keep, q_send, kv_keep, kv_send, slope_parts = attend_back(
        where,
        height,
        slopes_own,
        queries,
        keys,
        values,
        after(grad_mixture, squeeze.cut()),
        place,
        (lse_own, lse_other),
    )
    mix_out.wait(dq)

    def cut_heads(product):
        return product.reshape(blocks // 2, -1, height, width)

    kv_send = dot(kv_send, inputs_low).astype(BF16)
    tokens_low = inputs_low[2 * segment :]
    hidden.add()
    entry.add()
    kv_keep = dot(after(kv_keep, kv_send, hidden.cut(), entry.cut()), inputs_low).astype(BF16)
    left = Shrink(cut_heads(kv_keep), cut_heads(kv_send), sideways, True)
    mix_out.add()
    left.add()
    q_send = dot(after(q_send, left.cut()), tokens_low).astype(BF16)
    q_keep = dot(after(q_keep, q_send), tokens_low).astype(BF16)
    right = Shrink(cut_heads(q_keep), cut_heads(q_send), upward, True)
    right.add()
    squeeze.add()
    g1_own, g1_sent, smalls = inputs_back(
        where,
        compressed,
        memory,
        tokens,
        memory_other,
        x_other,
        after(
            dq,
            q_keep,
            left.cut(),
            right.cut(),
            hidden.cut(),
            entry.cut(),
            squeeze.array,
        ),
        dk,
        dv,
        qkv,
        (sums2, *bias_sums, dy_sum, dc_sum, slope_parts),
    )
    meet((left, right, hidden, entry), g1_sent)
    smalls = after(smalls, left.array, right.array, hidden.array, entry.array)
    mix_out.cut()
    mix_out.wait(left.array, right.array)
    mix_out.add()
    rounds = [(1, 2), (4,), (8, 16)] + [(2 << level,) for level in range(4, levels)]
    for masks in rounds:
        smalls = total_over(smalls, tuple(mask for mask in masks if mask <= dp))
        if masks[0] == 1:
            g1_sent = after(g1_sent, smalls)
            output = (after(residual, smalls) + (out_own + out_got.astype(F32)) + hidden_bias).astype(BF16)
            new_compressed = (
                after(squeeze_stay, smalls)[:slots] + squeeze_got[:slots].astype(F32) + compress_bias
            ).astype(BF16)
        smalls = after(smalls, left.add())
    g1 = g1_own + swap(g1_sent).astype(F32)
    unit1, rstd1 = rows_stats(tokens.astype(F32))
    grad_tokens = (grad_residual + norm_back(g1, norm1_gain, unit1, rstd1)).astype(BF16)

    grad_value_w, grad_key_w = [part.T for part in left.finish()]
    grad_query_w = right.finish()[0].T
    grad_in_w = turned(entry.finish()[0])
    grad_hidden_w, grad_out_w, grad_compress_w = [
        group.finish()[0].T for group in (hidden, mix_out, squeeze)
    ]
    gain2, bias2, hidden_b, compress_b, gain1, bias1, slope = [
        smalls[i] for i in (0, 1, 6, 7, 8, 9, 10)
    ]
    in_b = smalls[2:6].reshape(-1)
    return (
        output[None],
        new_compressed[None],
        grad_tokens[None],
        gain1,
        bias1,
        grad_query_w,
        grad_key_w,
        grad_value_w,
        grad_out_w,
        slope[:heads],
        gain2,
        bias2,
        grad_in_w,
        in_b,
        grad_hidden_w,
        hidden_b,
        grad_compress_w,
        compress_b,
    )


def solution(mesh):
    split, whole, kept = P("dp", "tm", None), P(), P("tm", None)
    in_specs = (
        (split,) * 3
        + (P("dp"), whole, whole)
        + (kept,) * 4
        + (whole,) * 3
        + (kept, whole, kept, whole, kept, whole)
        + (split,) * 2
    )
    shared = P("tm", "dp")
    out_specs = (
        (split,) * 3
        + (whole,) * 2
        + (shared,) * 4
        + (whole,) * 3
        + (shared, whole, shared, whole, shared, whole)
    )
    return jax.shard_map(local, mesh=mesh, in_specs=in_specs, out_specs=out_specs, check_vma=False)
```

```python
import functools

import jax
import jax.numpy as jnp
from jax import lax
from jax.experimental import pallas as pl
from jax.experimental.pallas import tpu as pltpu
from jax.sharding import PartitionSpec as P

EPS = 1e-05
NEG = -1e30
LOG2E = 1.4426950408889634
F32 = jnp.float32
BF16 = jnp.bfloat16
TINY = pl.CostEstimate(flops=1000, bytes_accessed=1000, transcendentals=0)
LARGE = pl.CostEstimate(flops=20 * 10**9, bytes_accessed=10**6, transcendentals=0)
PARAMS = pltpu.CompilerParams(vmem_limit_bytes=52 * 2**20)


def dot(a, b, dims=((1,), (0,))):
    return lax.dot_general(a, b, (dims, ((), ())), preferred_element_type=F32)


def dot_nt(a, b):
    return dot(a, b, ((1,), (1,)))


def dot_tn(a, b):
    return dot(a, b, ((0,), (0,)))


def rows_stats(x):
    mean = jnp.mean(x, -1, keepdims=True)
    centered = x - mean
    rstd = lax.rsqrt(jnp.mean(centered * centered, -1, keepdims=True) + EPS)
    return centered * rstd, rstd


def norm_back(grad, gain, normed, rstd):
    dn = grad * gain
    return rstd * (
        dn
        - jnp.mean(dn, -1, keepdims=True)
        - normed * jnp.mean(dn * normed, -1, keepdims=True)
    )


def spec(shape, at=None):
    zeros = (0,) * len(shape)
    return pl.BlockSpec(shape, at if at is not None else (lambda *_: zeros))


def call(kernel, name, where, grid, ins, outs, scratch=(), cost=TINY, onto=None):
    onto = onto or {}
    count = len(ins)
    ins = list(ins) + [(array, pl.BlockSpec(memory_space=pl.ANY)) for array in onto.values()]

    def body(place, *refs):
        kernel(place, *refs[:count], *refs[len(ins) :])

    return pl.pallas_call(
        body,
        grid_spec=pltpu.PrefetchScalarGridSpec(
            num_scalar_prefetch=1,
            grid=grid,
            in_specs=[at for _, at in ins],
            out_specs=[at for _, _, at in outs],
            scratch_shapes=list(scratch),
        ),
        out_shape=[jax.ShapeDtypeStruct(shape, dtype) for shape, dtype, _ in outs],
        input_output_aliases={1 + count + i: out for i, out in enumerate(onto)},
        compiler_params=PARAMS,
        cost_estimate=cost,
        name=name,
    )(where, *[array for array, _ in ins])


def whole(array):
    return array, spec(array.shape)


def ordered(first, own, other, axis):
    return jnp.where(
        first, jnp.concatenate((own, other), axis), jnp.concatenate((other, own), axis)
    )


def place_pieces(where, parts, target, base=0, half=None):
    size = (half or target.shape[0]) // (where.shape[0] - 2)
    at = 0
    for part in parts:
        for block in range(part.shape[0] // size):
            row = pl.multiple_of(base + where[2 + at] * size, size)
            target[pl.ds(row, size), :] = part[block * size : (block + 1) * size, :]
            at += 1


def pieces_kernel(where, wq, wk, wv, wo, wi, joined):
    size = wq.shape[1]
    first, second = joined.at[:, : 3 * size], joined.at[:, 3 * size :]
    first[:, :size] = wq[...]
    first[:, size : 2 * size] = wk[...]
    first[:, 2 * size :] = wv[...]
    second[:, : wo.shape[1]] = wo[...]
    second[:, wo.shape[1] :] = wi[...]


def pieces(where, share, wq, wk, wv, wo, wi):
    rows = wq.shape[0] // share
    cols = wq.shape[1] // 2
    wide = wi.shape[1] // 2
    half = spec((rows, cols), lambda i, w: (w[0], w[1]))
    return call(
        pieces_kernel,
        "pieces",
        where,
        (1,),
        [
            (wq, half),
            (wk, half),
            (wv, half),
            (wo, spec((rows, wo.shape[1]), lambda i, w: (w[0], 0))),
            (wi, spec((rows, wide), lambda i, w: (w[0], w[1]))),
        ],
        [
            (
                (rows, 3 * cols + wo.shape[1] + wide),
                BF16,
                spec((rows, 3 * cols + wo.shape[1] + wide)),
            )
        ],
    )


def load_rows(step, x, comp, mem, tok, other):
    rows = tok.shape[0]
    sources = (
        comp,
        other.at[:rows, :],
        mem,
        other.at[rows : 2 * rows, :],
        tok,
        other.at[2 * rows :, :],
    )
    for at, source in enumerate(sources):

        @pl.when(step == at)
        def _(source=source):
            x[...] = source[...].astype(F32)


def project_kernel(
    where,
    comp,
    mem,
    tok,
    other,
    gain,
    shift,
    wq,
    wk,
    wv,
    mine,
    got,
    low,
    q,
    k,
    v,
    weights,
    x,
):
    step = pl.program_id(0)
    load_rows(step, x, comp, mem, tok, other)
    half, cols = wq.shape

    @pl.when(step == 0)
    def _():
        own = pl.ds(pl.multiple_of(where[0] * half, half), half)
        for index, weight in enumerate((wq, wk, wv)):
            weights[own, index * cols : (index + 1) * cols] = weight[...]
        place_pieces(where, (mine, got), weights, (1 - where[0]) * half, half)

    unit, _ = rows_stats(x[...])
    n = (unit * gain[...] + shift[...]).astype(BF16)
    low[...] = n
    k[...] = dot(n, weights[:, cols : 2 * cols]).astype(BF16)
    v[...] = dot(n, weights[:, 2 * cols :]).astype(BF16)

    @pl.when(step >= 4)
    def _():
        q[...] = dot(n, weights[:, :cols]).astype(BF16)


def project(where, comp, mem, tok, other, gain, shift, wq, wk, wv, mine, got):
    rows, width = tok.shape
    cols = wq.shape[1] // 2
    half = spec((wq.shape[0], cols), lambda i, w: (0, w[0]))

    def by_step(size):
        return spec((rows, size), lambda i, w: (i, 0))

    return call(
        project_kernel,
        "project",
        where,
        (6,),
        [whole(a) for a in (comp, mem, tok, other, gain[None], shift[None])]
        + [(wq, half), (wk, half), (wv, half), whole(mine), whole(got)],
        [
            ((6 * rows, width), BF16, by_step(width)),
            ((2 * rows, cols), BF16, spec((rows, cols), lambda i, w: (jnp.maximum(i - 4, 0), 0))),
            ((6 * rows, cols), BF16, by_step(cols)),
            ((6 * rows, cols), BF16, by_step(cols)),
            ((width, 3 * cols), BF16, spec((width, 3 * cols))),
        ],
        [pltpu.VMEM((rows, width), F32)],
        cost=LARGE,
    )


def split_pairs(where, total, height, keep, send):
    pairs = total.reshape(total.shape[0] // (2 * height), 2, height, total.shape[1])
    even = where[1] == 0
    keep[...] = jnp.where(even, pairs[:, 0], pairs[:, 1]).astype(BF16)
    send[...] = jnp.where(even, pairs[:, 1], pairs[:, 0]).astype(BF16)


def by_parity(where, total, height):
    pairs = total.reshape(total.shape[0] // (2 * height), 2, height, total.shape[1])
    even = where[1] == 0
    shape = (total.shape[0] // 2, total.shape[1])
    keep = jnp.where(even, pairs[:, 0], pairs[:, 1]).reshape(shape)
    return keep, jnp.where(even, pairs[:, 1], pairs[:, 0]).reshape(shape)


def squeeze_kernel(slots, where, mem, other, dc, dc_o, weight, stay, away, keep, send, dc_sum):
    t = where[0]
    dc_sum[...] = jnp.sum(dc[...].astype(F32), 0, keepdims=True)
    rows, width = mem.shape
    mem_o = other.at[rows : 2 * rows, :]
    padded = dc.shape[0]
    half = width // 2
    lead = 3 * 2 * slots - 2 * rows
    first = t == 0
    shape = (padded, rows)
    slot = lax.broadcasted_iota(jnp.int32, shape, 0)
    row = lax.broadcasted_iota(jnp.int32, shape, 1)
    mem_half = jnp.where(first, mem[:, :half], mem[:, half:])
    mem_o_half = jnp.where(first, mem_o[:, :half], mem_o[:, half:])

    def picked(slot_half, row_half, offset):
        place = 3 * (slot + slot_half * slots) + offset - lead
        hit = (place == row + row_half * rows) & (slot < slots)
        return jnp.where(hit, 1.0, 0.0).astype(BF16)

    def windows(slot_half):
        edge = dot(picked(slot_half, t, 2 * t), mem[...]) + dot(
            picked(slot_half, 1 - t, 2 * t), mem_o[...]
        )
        middle = dot(picked(slot_half, t, 1), mem_half) + dot(
            picked(slot_half, 1 - t, 1), mem_o_half
        )
        return ordered(first, edge, middle, 1).astype(BF16)

    both = jnp.concatenate((windows(t), windows(1 - t)), 0)
    slots_out = dot(both, weight[...])
    stay[...] = slots_out[:padded, :]
    away[...] = slots_out[padded:, :].astype(BF16)
    turned_dc = jnp.concatenate((dc[...], dc_o[...]), 0).T
    columns = both.shape[1]
    height = keep.shape[1]
    for at in range(0, columns, half):
        part = slice(at, at + half)
        total = dot(turned_dc, both[:, part])
        split_pairs(where, total, height, keep.at[:, :, part], send.at[:, :, part])


def squeeze_rows(where, dp, slots, mem, other, dc, dc_o, weight):
    padded, width = dc.shape
    half = ((dp // 2, width // dp, weight.shape[0]), BF16)
    ins = [whole(a) for a in (mem, other, dc, dc_o, weight)]
    return call(
        functools.partial(squeeze_kernel, slots),
        "squeeze",
        where,
        (1,),
        ins,
        [
            ((padded, width), F32, spec((padded, width))),
            ((padded, width), BF16, spec((padded, width))),
            half + (spec(half[0]),),
            half + (spec(half[0]),),
            ((1, width), F32, spec((1, width))),
        ],
    )


def masked_scores(place, slope, q, keys, scale, first, tail):
    bias = place[0:1, :] * slope + place[1:2, :]
    chunk = q.shape[0]
    query_place = (lax.broadcasted_iota(jnp.int32, (chunk, 1), 0) + first).astype(F32)
    scores = dot_nt(q, keys) * (scale * LOG2E) + bias
    recent = jnp.where(place[0:1, tail:] <= query_place, scores[:, tail:], NEG)
    return jnp.concatenate((scores[:, :tail], recent), 1), query_place


def attend_kernel(turn, scale, where, slopes, q, k, v, place, mix, lse):
    slope = slopes[pl.program_id(0)] * LOG2E
    rows = q.shape[0]
    first = jnp.abs(turn - where[0]) * rows
    scores, _ = masked_scores(place, slope, q[...], k[...], scale, first, k.shape[0] - 2 * rows)
    highest = jnp.max(scores, -1, keepdims=True)
    weights = jnp.exp2(scores - highest)
    total = jnp.sum(weights, -1, keepdims=True)
    mix[...] = (dot(weights.astype(BF16), v[...]) * (1.0 / total)).astype(BF16)
    lse[0] = highest + jnp.log2(total)


def attend(where, turn, slopes, q, k, v, place):
    rows, width = q.shape[0] // 2, q.shape[1]
    heads = slopes.shape[0]
    hw = width // heads
    keys = k.shape[0]
    by_head = spec((keys, hw), lambda h, w: (0, h))
    return call(
        functools.partial(attend_kernel, turn, hw**-0.5),
        "attend",
        where,
        (heads,),
        [
            (slopes, pl.BlockSpec(memory_space=pltpu.SMEM)),
            (q, spec((rows, hw), lambda h, w: (turn, h))),
            (k, by_head),
            (v, by_head),
            whole(place),
        ],
        [
            ((rows, width), BF16, spec((rows, hw), lambda h, w: (0, h))),
            ((heads, rows, 1), F32, spec((1, rows, 1), lambda h, w: (h, 0, 0))),
        ],
        cost=LARGE,
    )


def attend_back_kernel(
    chunk,
    scale,
    height,
    where,
    slopes,
    q,
    k,
    v,
    dm,
    place,
    lse_own,
    lse_other,
    dq,
    dk,
    dv,
    all_keep,
    all_send,
    slope_out,
    dk_sum,
    dv_sum,
):
    slope = slopes[pl.program_id(0)] * LOG2E
    keys = k.shape[0]
    rows = q.shape[0]
    half = rows // 2
    columns = jnp.zeros((1, keys), F32)
    by_row = jnp.zeros((1, 1), F32)
    dq_parts = []
    for step in range(rows // chunk):
        at = slice(step * chunk, (step + 1) * chunk)
        time_half = where[0] if step * chunk < half else 1 - where[0]
        scores, query_place = masked_scores(
            place,
            slope,
            q[at, :],
            k[...],
            scale,
            time_half * half + step * chunk % half,
            keys - rows,
        )
        weights = jnp.exp2(scores - (lse_own if step == 0 else lse_other)[0])
        low = weights.astype(BF16)
        grads = dot_nt(dm[at, :], v[...])
        shift = jnp.sum(weights * grads, -1, keepdims=True)
        ds = (weights * (grads - shift)).astype(BF16)
        dq_part = dot(ds, k[...]) * scale
        dq[at, :] = dq_part.astype(BF16)
        dq_parts.append(dq_part.T)
        dk_part = dot_tn(q[at, :], ds)
        dv_part = dot_tn(dm[at, :], low)
        if step == 0:
            dk_sum[...] = dk_part
            dv_sum[...] = dv_part
        else:
            dk_sum[...] += dk_part
            dv_sum[...] += dv_part
        wide = ds.astype(F32)
        columns += jnp.sum(wide, 0, keepdims=True)
        by_row += jnp.sum(jnp.sum(wide, -1, keepdims=True) * query_place, 0, keepdims=True)
    dk_all, dv_all = dk_sum[...] * scale, dv_sum[...]
    dq_all = jnp.concatenate([jnp.zeros((dk_all.shape[0], keys - rows), F32)] + dq_parts, 1)
    halves = [by_parity(where, part, height) for part in (dq_all, dk_all, dv_all)]
    for target, parts in zip((all_keep, all_send), zip(*halves)):
        blocks = [part.reshape(part.shape[0] // height, height, keys) for part in parts]
        target[...] = jnp.stack(blocks, 1).reshape(target.shape).astype(BF16)
    dk[...] = dk_all.T.astype(BF16)
    dv[...] = dv_all.T.astype(BF16)
    total = jnp.sum(columns * place[0:1, :], -1, keepdims=True) - by_row
    slope_out[...] = jnp.broadcast_to(total.reshape(1, 1, 1), slope_out.shape)


def attend_back(where, height, slopes, q, k, v, dm, place, lses):
    rows, width = q.shape
    heads = slopes.shape[0]
    hw = width // heads
    keys = k.shape[0]
    by_rows = spec((rows, hw), lambda h, w: (0, h))
    by_keys = spec((keys, hw), lambda h, w: (0, h))
    return call(
        functools.partial(attend_back_kernel, rows // 2, hw**-0.5, height),
        "attend_back",
        where,
        (heads,),
        [
            (slopes, pl.BlockSpec(memory_space=pltpu.SMEM)),
            (q, by_rows),
            (k, by_keys),
            (v, by_keys),
            (dm, by_rows),
            whole(place),
            (lses[0], spec((1, rows // 2, 1), lambda h, w: (h, 0, 0))),
            (lses[1], spec((1, rows // 2, 1), lambda h, w: (h, 0, 0))),
        ],
        [
            ((rows, width), BF16, by_rows),
            ((keys, width), BF16, by_keys),
            ((keys, width), BF16, by_keys),
            ((3 * width // 2, keys), BF16, spec((3 * hw // 2, keys), lambda h, w: (h, 0))),
            ((3 * width // 2, keys), BF16, spec((3 * hw // 2, keys), lambda h, w: (h, 0))),
            ((heads, 8, 128), F32, spec((1, 8, 128), lambda h, w: (h, 0, 0))),
        ],
        [pltpu.VMEM((hw, keys), F32), pltpu.VMEM((hw, keys), F32)],
        cost=LARGE,
    )


def gelu_pair(v):
    c = 0.7978845608028654
    inner = c * (v + 0.044715 * v * v * v)
    th = jnp.tanh(inner)
    slope = 0.5 * (1.0 + th) + 0.5 * v * (1.0 - th * th) * c * (1.0 + 3 * 0.044715 * v * v)
    return 0.5 * v * (1.0 + th), slope


def feed_kernel(height, block, where, *refs):
    (
        mix,
        far,
        tok,
        wo,
        wo_mine,
        wo_got,
        gain,
        shift,
        dy,
        wi,
        wi_mine,
        wi_got,
        bias,
        wh,
        residual,
        normed,
        act,
        grad_keep,
        grad_send,
        dy_keep,
        dy_send,
        g2,
        out,
        bias_sum,
        dy_sum,
        *sent,
        wo_far,
        weight,
        out_sum,
    ) = refs
    step = pl.program_id(0)
    half = wi.shape[0]

    @pl.when(step == 0)
    def _():
        place_pieces(where, (wo_mine, wo_got), wo_far)
        wide_dy = dy[...].astype(F32)
        dy_sum[...] = jnp.sum(wide_dy, 0, keepdims=True)
        dy_stay, dy_away = by_parity(where, wide_dy.T, height)
        dy_keep[...] = dy_stay.astype(BF16)
        dy_send[...] = dy_away.astype(BF16)
        total = tok[...].astype(F32) + (dot(mix[...], wo[...]) + dot(far[...], wo_far[...]))
        residual[...] = total
        unit, _ = rows_stats(total)
        normed[...] = (unit * gain[...] + shift[...]).astype(BF16)

    weight[pl.ds(pl.multiple_of(where[0] * half, half), half), :] = wi[...]
    place_pieces(where, (wi_mine, wi_got), weight, (1 - where[0]) * half, half)
    pre = dot(normed[...], weight[...]) + bias[...]
    value, slope = gelu_pair(pre)
    low = value.astype(BF16)
    act[...] = low
    grad = (dot_nt(dy[...], wh[...]) * slope).astype(BF16)
    blocks = [grad[:, at : at + block] for at in range(0, grad.shape[1], block)]
    evens, odds = jnp.concatenate(blocks[::2], 1), jnp.concatenate(blocks[1::2], 1)
    even = where[1] == 0
    grad_keep[...] = jnp.where(even, evens, odds)
    grad_send[...] = jnp.where(even, odds, evens)
    bias_sum[...] = jnp.sum(grad.astype(F32), 0, keepdims=True)
    g2_part = dot_nt(grad, weight[...])
    out_part = dot(low, wh[...])

    @pl.when(step == 0)
    def _():
        g2[...] = g2_part
        out_sum[...] = out_part

    @pl.when(step > 0)
    def _():
        g2[...] += g2_part
        out_sum[...] += out_part

    @pl.when(step == pl.num_programs(0) - 1)
    def _():
        first_row = 0
        for piece in sent:
            piece[...] = g2[first_row : first_row + piece.shape[0], :].astype(BF16)
            first_row += piece.shape[0]
        out[...] = out_sum[...].astype(out.dtype)


def feed(
    where, dp, turn, mix, far, tok, wo, gain, shift, dy, wi, bias, wh, second, chunk, kept, parts, onto
):
    rows, width = dy.shape
    hidden = wh.shape[0]
    steps = hidden // chunk
    mine, got = second
    by_cols = spec((rows, chunk), lambda j, w: (turn, j))
    by_half = spec((rows, chunk // 2), lambda j, w: (turn, j))
    half = (2 * rows, hidden // 2), BF16, by_half
    turned = (width // 2, 2 * rows), BF16, spec((width // 2, rows), lambda j, w: (0, turn))
    wo_part = spec((mine.shape[0], width), lambda j, w: (0, 0))
    wi_part = spec((mine.shape[0], chunk), lambda j, w: (0, width // chunk + j))

    def once(dtype):
        return (rows, width), dtype, spec((rows, width))

    return call(
        functools.partial(feed_kernel, width // dp, hidden // (dp // 2)),
        "feed",
        where,
        (steps,),
        [
            whole(mix),
            whole(far),
            (tok, spec((rows, width), lambda j, w: (2 * turn, 0))),
            whole(wo),
            (mine, wo_part),
            (got, wo_part),
            whole(gain[None]),
            whole(shift[None]),
            whole(dy),
            (wi, spec((wi.shape[0], chunk), lambda j, w: (0, w[0] * steps + j))),
            (mine, wi_part),
            (got, wi_part),
            (bias[None], spec((1, chunk), lambda j, w: (0, w[0] * steps + j))),
            (wh, spec((chunk, width), lambda j, w: (j, 0))),
        ],
        [
            once(F32),
            ((2 * rows, width), BF16, spec((rows, width), lambda j, w: (turn, 0))),
            ((2 * rows, hidden), BF16, by_cols),
            half,
            half,
            turned,
            turned,
            once(F32),
            once(kept),
            ((1, hidden), F32, spec((1, chunk), lambda j, w: (0, j))),
            ((1, width), F32, spec((1, width))),
        ]
        + [((rows // part, width), BF16, spec((rows // part, width))) for part in parts],
        [
            pltpu.VMEM(wo.shape, BF16),
            pltpu.VMEM((width, chunk), BF16),
            pltpu.VMEM((rows, width), F32),
        ],
        cost=LARGE,
        onto=onto,
    )


def middle_kernel(
    where,
    g_own,
    g_other,
    got_own,
    got_other,
    residual_own,
    residual_other,
    gain,
    dy,
    dy_o,
    wo,
    mix_own,
    mix_other,
    bias_sum,
    bias_sum_o,
    dy_sum,
    dc_sum,
    grad_res,
    dm,
    sums,
    keep,
    send,
):
    rows = dy.shape[0]
    lows = []
    halves = ((g_own, got_own, dy, residual_own), (g_other, got_other, dy_o, residual_other))
    for at, (g, got, d, residual) in enumerate(halves):
        here = slice(at * rows, (at + 1) * rows)
        grad = g[...] + got[...].astype(F32)
        unit, rstd = rows_stats(residual[...])
        total = d[...].astype(F32) + norm_back(grad, gain[...], unit, rstd)
        low = total.astype(BF16)
        lows.append(low)
        dm[here, :] = dot_nt(low, wo[...]).astype(BF16)
        if at == 0:
            grad_res[...] = total
            small = [jnp.sum(grad * unit, 0, keepdims=True), jnp.sum(grad, 0, keepdims=True)]
    width = dy.shape[1]
    first = where[0] == 0
    parts = [slice(at, at + width) for at in range(0, bias_sum.shape[1], width)]
    downs = [bias_sum[:, part] + bias_sum_o[:, part] for part in parts]
    small += [jnp.where(first, down, 0.0) for down in downs]
    small += [jnp.where(first, 0.0, down) for down in downs]
    small += [dy_sum[...], dc_sum[...]]
    sums[...] = jnp.concatenate(small, 0)
    split_pairs(
        where, dot_tn(lows[0], mix_own[...]) + dot_tn(lows[1], mix_other[...]), keep.shape[1], keep, send
    )


def middle(where, dp, g, got, residuals, gain, dys, wo, mix, small):
    rows, width = dys[0].shape
    heads = wo.shape[0]
    half = ((dp // 2, width // dp, heads), BF16, spec((dp // 2, width // dp, heads)))
    return call(
        middle_kernel,
        "middle",
        where,
        (1,),
        [whole(a) for a in (*g, *got, *residuals, gain[None], *dys, wo, *mix, *small)],
        [
            ((rows, width), F32, spec((rows, width))),
            ((2 * rows, heads), BF16, spec((2 * rows, heads))),
            ((8, width), F32, spec((8, width))),
            half,
            half,
        ],
        cost=LARGE,
    )


def norm_sums(step, grad, x, sums):
    unit, _ = rows_stats(x)
    rows = jnp.sum(grad * unit, 0, keepdims=True), jnp.sum(grad, 0, keepdims=True)

    @pl.when(step == 0)
    def _():
        sums[0:1, :], sums[1:2, :] = rows

    @pl.when(step > 0)
    def _():
        sums[0:1, :] += rows[0]
        sums[1:2, :] += rows[1]


def tokens_kernel(where, tok, other, dq, dk, dv, weights, g_own, sent, sums):
    step = pl.program_id(0)
    cols = dq.shape[1]
    grad = (
        dot_nt(dq[...], weights[:, :cols])
        + dot_nt(dk[...], weights[:, cols : 2 * cols])
        + dot_nt(dv[...], weights[:, 2 * cols :])
    )
    x = jnp.where(step == 0, tok[...].astype(F32), other[...].astype(F32))
    norm_sums(step, grad, x, sums)

    @pl.when(step == 0)
    def _():
        g_own[...] = grad

    @pl.when(step == 1)
    def _():
        sent[...] = grad.astype(BF16)


def tokens_back(where, tok, other, dq, dk, dv, weights):
    rows, width = tok.shape
    cols = dk.shape[1]
    late = spec((rows, cols), lambda i, w: (4 + i, 0))
    return call(
        tokens_kernel,
        "tokens_back",
        where,
        (2,),
        [
            whole(tok),
            (other, spec((rows, width), lambda i, w: (2, 0))),
            (dq, spec((rows, cols), lambda i, w: (i, 0))),
            (dk, late),
            (dv, late),
            whole(weights),
        ],
        [
            ((rows, width), F32, spec((rows, width))),
            ((rows, width), BF16, spec((rows, width))),
            ((2, width), F32, spec((2, width))),
        ],
    )


def slots_kernel(
    where, comp, mem, other, dk, dv, weights, start, slope_parts, early, sums, total
):
    step = pl.program_id(0)
    cols = dk.shape[1]
    grad = dot_nt(dk[...], weights[:, cols : 2 * cols]) + dot_nt(dv[...], weights[:, 2 * cols :])
    own = jnp.where(step == 0, comp[...].astype(F32), mem[...].astype(F32))
    x = jnp.where(step % 2 == 0, own, other[...].astype(F32))
    norm_sums(step, grad, x, total)

    @pl.when(step == pl.num_programs(0) - 1)
    def _():
        width = comp.shape[1]
        lane = lax.broadcasted_iota(jnp.int32, (1, width), 1)
        own_heads = slope_parts.shape[0]
        slope = jnp.zeros((1, width), F32)
        for head in range(own_heads):
            here = lane == where[0] * own_heads + head
            slope += jnp.where(here, slope_parts[head, 0:1, 0:1], 0.0)
        sums[:8, :] = early[...]
        rest = (total[...] + start[...], slope, jnp.zeros((5, width), F32))
        sums[8:, :] = jnp.concatenate(rest, 0)


def slots_back(where, comp, mem, other, dk, dv, weights, start, slope_parts, early):
    rows, width = comp.shape
    cols = dk.shape[1]
    by_step = spec((rows, cols), lambda i, w: (i, 0))
    return call(
        slots_kernel,
        "slots_back",
        where,
        (4,),
        [
            whole(comp),
            whole(mem),
            (other, spec((rows, width), lambda i, w: (i // 2, 0))),
            (dk, by_step),
            (dv, by_step),
            whole(weights),
            whole(start),
            whole(slope_parts),
            whole(early),
        ],
        [((16, width), F32, spec((16, width)))],
        [pltpu.VMEM((2, width), F32)],
        cost=LARGE,
    )


def turn_kernel(source, target):
    target[...] = source[...].T


def turned(array):
    return pl.pallas_call(
        turn_kernel,
        out_shape=jax.ShapeDtypeStruct(array.shape[::-1], F32),
        compiler_params=PARAMS,
        cost_estimate=TINY,
        name="turn",
    )(array)


def local(
    tokens,
    memory,
    compressed,
    mask_start,
    norm1_gain,
    norm1_bias,
    query_weight,
    key_weight,
    value_weight,
    out_weight,
    slopes,
    norm2_gain,
    norm2_bias,
    in_weight,
    in_bias,
    hidden_weight,
    hidden_bias,
    compress_weight,
    compress_bias,
    grad_out,
    grad_compressed,
):
    tokens, memory, compressed = tokens[0], memory[0], compressed[0]
    grad_out, grad_compressed = grad_out[0], grad_compressed[0]
    rows, width = tokens.shape
    heads = slopes.shape[0]
    dp = lax.axis_size("dp")
    levels = dp.bit_length() - 1
    top = levels - 1
    d = lax.axis_index("dp")
    t = lax.axis_index("tm")
    segment = 2 * rows

    def swap(block):
        return lax.ppermute(block, "tm", [(0, 1), (1, 0)])

    def across(block, mask):
        return lax.ppermute(block, "dp", [(i, i ^ mask) for i in range(dp)])

    def after(array, *earlier):
        return lax.optimization_barrier((array,) + earlier)[0]

    def bit(level):
        return (d >> level) & 1

    class Shrink:
        def __init__(self, keep, send, order, columns=False):
            shape = keep.shape if keep.ndim == 4 else keep.shape[:1] + (1,) + keep.shape[1:]
            self.pending = keep.reshape(shape), send.reshape(shape), 1
            self.order = [0] + order
            self.left = [level for level in range(1, top if columns else levels)]
            self.step = 0
            self.array = None

        def cut(self):
            if self.pending is not None:
                return self.pending[1]
            if self.step == len(self.order):
                return self.array
            level = self.order[self.step]
            if level in self.left:
                low = 1 << self.left.index(level)
                blocks, rest = self.array.shape[0], self.array.shape[1:]
                split = self.array.reshape((blocks // (2 * low), 2, low) + rest)
                keep, send = [
                    lax.dynamic_index_in_dim(split, at, 1, keepdims=False).reshape(
                        (blocks // 2,) + rest
                    )
                    for at in (bit(level), 1 - bit(level))
                ]
                self.left.remove(level)
                self.pending = keep, send, 1 << level
            else:
                size = self.array.shape[3] // 2
                keep, send = [
                    lax.dynamic_slice_in_dim(self.array, at * size, size, 3) for at in (t, 1 - t)
                ]
                self.pending = keep, send, 0
            return send

        def move(self):
            send = self.cut()
            return across(send, self.pending[2]) if self.pending[2] else swap(send)

        def take(self, got):
            keep, _, mask = self.pending
            if mask == 0:
                same = bit(top) == t
                self.pending = jnp.where(same, keep, got), jnp.where(same, got, keep), 1 << top
                return self.pending[1]
            self.step += 1
            total = keep.astype(F32) + got.astype(F32)
            last = self.step == len(self.order)
            self.array = total if last else total.astype(BF16)
            self.pending = None
            return self.array

        def add(self):
            if self.step == len(self.order):
                return self.array
            self.cut()
            if self.pending[2] == 0:
                self.take(self.move())
            return self.take(self.move())

        def wait(self, *earlier):
            if self.pending is not None:
                self.pending = (after(self.pending[0], *earlier),) + self.pending[1:]

        def finish(self):
            while self.step < len(self.order):
                self.add()
            return self.array[0]

    def meet(groups, *others):
        groups = [group for group in groups if group.step < len(group.order)]
        got = lax.optimization_barrier(tuple(group.move() for group in groups) + others)
        for group, block in zip(groups, got):
            group.take(block)
        for group in groups:
            group.cut()
        return got[len(groups) :]

    sideways = list(range(1, levels))
    upward = list(range(2, levels)) + [1] if levels > 1 else []
    between = upward[:1] + upward[-1:] + upward[1:-1] if levels > 2 else upward

    sharing = min(levels, 4)
    share = 1 << sharing
    ups = [z << 2 for z in range(1 << max(sharing - 2, 0))]
    offsets = [x + z for x in ((0, 2) if sharing > 1 else (0,)) for z in ups]
    low_bits = d & (share - 1)
    targets = [low_bits ^ off for off in offsets] + [low_bits ^ off ^ 1 for off in offsets]
    where = jnp.stack([t, bit(0)] + targets).astype(jnp.int32)

    def gather_up(piece):
        return jnp.concatenate([piece] + [across(piece, z) for z in ups[1:]], 0)

    def gather_side(block):
        return jnp.concatenate((block, across(block, 2)), 0) if sharing > 1 else block

    (joined,) = pieces(
        jnp.stack((low_bits, 1 - t)).astype(jnp.int32),
        share,
        query_weight,
        key_weight,
        value_weight,
        out_weight,
        in_weight,
    )
    joined = swap(joined)
    first_size = 3 * query_weight.shape[1] // 2
    first, second = joined[:, :first_size], joined[:, first_size:]
    slots = grad_compressed.shape[0]
    dc = jnp.pad(grad_compressed, ((0, -slots % 16), (0, 0)))
    x_other = swap(jnp.concatenate((compressed, memory, tokens), 0))
    first = gather_side(gather_up(first))
    first_got = across(first, 1)
    second = gather_side(gather_up(after(second, first)))
    second_got = across(second, 1)
    dc_other, dy_other = swap(after(dc, x_other)), swap(after(grad_out, x_other))

    inputs_low, queries, keys, values, qkv = project(
        where,
        compressed,
        memory,
        tokens,
        x_other,
        norm1_gain,
        norm1_bias,
        query_weight,
        key_weight,
        value_weight,
        first,
        first_got,
    )

    index = jnp.arange(segment, dtype=jnp.int32)
    slot = jnp.where(index < rows, index + t * rows, index - rows + (1 - t) * rows)
    place = jnp.concatenate((-segment - 3 * (segment - slot), slot - segment, slot)).astype(F32)
    closed = jnp.where(slot >= mask_start[0], 0.0, NEG)
    closed = jnp.concatenate((closed, jnp.zeros((2 * segment,), F32)))
    place = jnp.stack((place, closed))
    own_heads = heads // 2
    slopes_own = lax.dynamic_slice_in_dim(slopes, t * own_heads, own_heads, 0)
    queries = after(queries, second)
    mix_other, lse_other = attend(where, 1, slopes_own, queries, keys, values, place)
    far_own = swap(mix_other)
    squeeze_stay, squeeze_away, keep, send, dc_sum = squeeze_rows(
        where, dp, slots, after(memory, mix_other), x_other, dc, dc_other, compress_weight
    )
    squeeze = Shrink(keep, send, sideways)
    squeeze_got = swap(squeeze_away)
    mix_own, lse_own = attend(
        where, 0, slopes_own, after(queries, squeeze_away), keys, values, place
    )
    far_other = swap(mix_own)
    dys = grad_out, dy_other
    mix = mix_own, mix_other
    chunk = max(in_weight.shape[1] // 8, 2 * in_weight.shape[1] // dp)

    def feed_rows(turn, mixed, far, tok, dy, kept, parts, onto=None):
        return feed(
            where,
            dp,
            turn,
            mixed,
            far,
            tok,
            out_weight,
            norm2_gain,
            norm2_bias,
            dy,
            in_weight,
            in_bias,
            hidden_weight,
            (second, second_got),
            chunk,
            kept,
            parts,
            onto,
        )

    squeeze.add()
    residual, *half_filled, g_own, out_own, bias_sum, dy_sum, sent = feed_rows(
        0, after(mix_own, squeeze.cut()), far_own, tokens, grad_out, F32, (1,)
    )
    got_other = swap(sent)
    residual_o, *filled, g_other, out_sent, bias_sum_o, _, sent = feed_rows(
        1,
        after(mix_other, sent, squeeze_got),
        far_other,
        x_other,
        dy_other,
        BF16,
        (1,),
        {1 + i: array for i, array in enumerate(half_filled)},
    )
    got = swap(sent), got_other
    normed, act, grad_keep, grad_send, dy_keep, dy_send = filled
    squeeze.wait(out_sent)
    squeeze.add()
    blocks = dp // 2

    def cut_rows(product, count):
        return product.astype(BF16).reshape(count, product.shape[0] // count, product.shape[1])

    hidden_send = dot(after(dy_send, squeeze.cut(), got_other), act).astype(BF16)
    entry_send = dot_tn(after(grad_send, hidden_send), normed).astype(BF16)
    hidden_keep = dot(after(dy_keep, entry_send), act).astype(BF16)
    entry_keep = dot_tn(after(grad_keep, hidden_keep), normed).astype(BF16)
    hidden = Shrink(cut_rows(hidden_keep, blocks), cut_rows(hidden_send, blocks), sideways)
    entry = Shrink(
        cut_rows(entry_keep, blocks // 2), cut_rows(entry_send, blocks // 2), between, True
    )
    grad_residual, grad_mixture, early, keep, send = middle(
        where,
        dp,
        (after(g_own, entry_keep), g_other),
        got,
        (residual, residual_o),
        norm2_gain,
        dys,
        out_weight,
        mix,
        (bias_sum, bias_sum_o, dy_sum, dc_sum),
    )
    mix_out = Shrink(keep, send, sideways)
    out_got = swap(after(out_sent, grad_mixture))
    squeeze.add()
    hidden.add()
    entry.add()
    height = key_weight.shape[1] // dp
    dq, dk, dv, all_keep, all_send, slope_parts = attend_back(
        where,
        height,
        slopes_own,
        queries,
        keys,
        values,
        after(grad_mixture, hidden.cut(), entry.cut(), squeeze.array),
        place,
        (lse_own, lse_other),
    )
    mix_out.wait(dq)

    def cut_heads(product):
        return product.reshape(blocks // 2, -1, height, width)

    all_send = dot(after(all_send, out_got), inputs_low).astype(BF16)
    hidden.add()
    entry.add()
    all_keep = dot(
        after(all_keep, all_send, hidden.cut(), entry.cut()), inputs_low
    ).astype(BF16)
    left = Shrink(cut_heads(all_keep), cut_heads(all_send), sideways, True)
    mix_out.add()
    left.add()
    mix_out.cut()
    mix_out.wait(left.cut())
    mix_out.add()
    squeeze.add()
    g1_own, g1_sent, token_sums = tokens_back(
        where,
        tokens,
        x_other,
        after(dq, left.cut(), hidden.cut(), entry.cut(), mix_out.cut(), squeeze.array),
        dk,
        dv,
        qkv,
    )
    g1_got = swap(g1_sent)
    mix_out.wait(g1_sent)
    mix_out.add()
    (smalls,) = slots_back(
        where,
        compressed,
        memory,
        x_other,
        after(dk, mix_out.cut()),
        dv,
        qkv,
        token_sums,
        slope_parts,
        early,
    )

    def joint(array, mask):
        return lax.ppermute(array, ("dp", "tm"), [(i, i ^ mask) for i in range(2 * dp)])

    smalls, g1_got = meet((left, hidden, entry, mix_out), smalls, g1_got)
    groups = (left, hidden, entry, mix_out, squeeze)
    masks = [1 << at for at in range(levels + 1)]
    while masks:
        sends = [group.cut() for group in groups]
        smalls = after(smalls, *sends)
        if len(masks) > 1 and len(masks) % 2:
            smalls = smalls + joint(smalls, masks.pop(0))
        smalls, got = meet(groups, smalls, joint(smalls, masks.pop(0)))
        smalls = smalls + got
    output = (after(residual, sends[0]) + (out_own + out_got.astype(F32)) + hidden_bias).astype(
        BF16
    )
    new_compressed = (
        after(squeeze_stay, sends[0])[:slots] + squeeze_got[:slots].astype(F32) + compress_bias
    ).astype(BF16)
    g1 = g1_own + g1_got.astype(F32)
    unit1, rstd1 = rows_stats(tokens.astype(F32))
    grad_tokens = (grad_residual + norm_back(g1, norm1_gain, unit1, rstd1)).astype(BF16)

    grad_query_w, grad_key_w, grad_value_w = [part.T for part in left.finish()]
    grad_in_w = turned(entry.finish()[0])
    grad_hidden_w, grad_out_w, grad_compress_w = [
        group.finish()[0].T for group in (hidden, mix_out, squeeze)
    ]
    gain2, bias2, hidden_b, compress_b, gain1, bias1, slope = [
        smalls[i] for i in (0, 1, 6, 7, 8, 9, 10)
    ]
    in_b = smalls[2:6].reshape(-1)
    return (
        output[None],
        new_compressed[None],
        grad_tokens[None],
        gain1,
        bias1,
        grad_query_w,
        grad_key_w,
        grad_value_w,
        grad_out_w,
        slope[:heads],
        gain2,
        bias2,
        grad_in_w,
        in_b,
        grad_hidden_w,
        hidden_b,
        grad_compress_w,
        compress_b,
    )


def solution(mesh):
    split, whole, kept = P("dp", "tm", None), P(), P("tm", None)
    in_specs = (
        (split,) * 3
        + (P("dp"), whole, whole)
        + (kept,) * 4
        + (whole,) * 3
        + (kept, whole, kept, whole, kept, whole)
        + (split,) * 2
    )
    shared = P("tm", "dp")
    out_specs = (
        (split,) * 3
        + (whole,) * 2
        + (shared,) * 4
        + (whole,) * 3
        + (shared, whole, shared, whole, shared, whole)
    )
    return jax.shard_map(local, mesh=mesh, in_specs=in_specs, out_specs=out_specs, check_vma=False)
```

```python
import functools

import jax
import jax.numpy as jnp
from jax import lax
from jax.experimental import pallas as pl
from jax.experimental.pallas import tpu as pltpu
from jax.sharding import PartitionSpec as P

EPS = 1e-05
NEG = -1e30
LOG2E = 1.4426950408889634
F32 = jnp.float32
BF16 = jnp.bfloat16
TINY = pl.CostEstimate(flops=1000, bytes_accessed=1000, transcendentals=0)
LARGE = pl.CostEstimate(flops=20 * 10**9, bytes_accessed=10**6, transcendentals=0)
PARAMS = pltpu.CompilerParams(vmem_limit_bytes=52 * 2**20)


def dot(a, b, dims=((1,), (0,))):
    return lax.dot_general(a, b, (dims, ((), ())), preferred_element_type=F32)


def dot_nt(a, b):
    return dot(a, b, ((1,), (1,)))


def dot_tn(a, b):
    return dot(a, b, ((0,), (0,)))


def rows_stats(x):
    mean = jnp.mean(x, -1, keepdims=True)
    centered = x - mean
    rstd = lax.rsqrt(jnp.mean(centered * centered, -1, keepdims=True) + EPS)
    return centered * rstd, rstd


def norm_back(grad, gain, normed, rstd):
    dn = grad * gain
    return rstd * (
        dn
        - jnp.mean(dn, -1, keepdims=True)
        - normed * jnp.mean(dn * normed, -1, keepdims=True)
    )


def spec(shape, at=None):
    zeros = (0,) * len(shape)
    return pl.BlockSpec(shape, at if at is not None else (lambda *_: zeros))


def call(kernel, name, where, grid, ins, outs, scratch=(), cost=TINY, onto=None):
    onto = onto or {}
    count = len(ins)
    ins = list(ins) + [(array, pl.BlockSpec(memory_space=pl.ANY)) for array in onto.values()]

    def body(place, *refs):
        kernel(place, *refs[:count], *refs[len(ins) :])

    return pl.pallas_call(
        body,
        grid_spec=pltpu.PrefetchScalarGridSpec(
            num_scalar_prefetch=1,
            grid=grid,
            in_specs=[at for _, at in ins],
            out_specs=[at for _, _, at in outs],
            scratch_shapes=list(scratch),
        ),
        out_shape=[jax.ShapeDtypeStruct(shape, dtype) for shape, dtype, _ in outs],
        input_output_aliases={1 + count + i: out for i, out in enumerate(onto)},
        compiler_params=PARAMS,
        cost_estimate=cost,
        name=name,
    )(where, *[array for array, _ in ins])


def whole(array):
    return array, spec(array.shape)


def ordered(first, own, other, axis):
    return jnp.where(
        first, jnp.concatenate((own, other), axis), jnp.concatenate((other, own), axis)
    )


def place_pieces(where, parts, target, base=0, half=None):
    size = (half or target.shape[0]) // (where.shape[0] - 2)
    at = 0
    for part in parts:
        for block in range(part.shape[0] // size):
            row = pl.multiple_of(base + where[2 + at] * size, size)
            target[pl.ds(row, size), :] = part[block * size : (block + 1) * size, :]
            at += 1


def pieces_kernel(where, wq, wk, wv, wo, wi, joined):
    size = wq.shape[1]
    first, second = joined.at[:, : 3 * size], joined.at[:, 3 * size :]
    first[:, :size] = wq[...]
    first[:, size : 2 * size] = wk[...]
    first[:, 2 * size :] = wv[...]
    second[:, : wo.shape[1]] = wo[...]
    second[:, wo.shape[1] :] = wi[...]


def pieces(where, share, wq, wk, wv, wo, wi):
    rows = wq.shape[0] // share
    cols = wq.shape[1] // 2
    wide = wi.shape[1] // 2
    half = spec((rows, cols), lambda i, w: (w[0], w[1]))
    return call(
        pieces_kernel,
        "pieces",
        where,
        (1,),
        [
            (wq, half),
            (wk, half),
            (wv, half),
            (wo, spec((rows, wo.shape[1]), lambda i, w: (w[0], 0))),
            (wi, spec((rows, wide), lambda i, w: (w[0], w[1]))),
        ],
        [
            (
                (rows, 3 * cols + wo.shape[1] + wide),
                BF16,
                spec((rows, 3 * cols + wo.shape[1] + wide)),
            )
        ],
    )


def load_rows(step, x, comp, mem, tok, other):
    rows = tok.shape[0]
    sources = (
        comp,
        other.at[:rows, :],
        mem,
        other.at[rows : 2 * rows, :],
        tok,
        other.at[2 * rows :, :],
    )
    for at, source in enumerate(sources):

        @pl.when(step == at)
        def _(source=source):
            x[...] = source[...].astype(F32)


def project_kernel(
    where,
    comp,
    mem,
    tok,
    other,
    gain,
    shift,
    wq,
    wk,
    wv,
    mine,
    got,
    low,
    q,
    k,
    v,
    weights,
    x,
):
    step = pl.program_id(0)
    load_rows(step, x, comp, mem, tok, other)
    half, cols = wq.shape

    @pl.when(step == 0)
    def _():
        own = pl.ds(pl.multiple_of(where[0] * half, half), half)
        for index, weight in enumerate((wq, wk, wv)):
            weights[own, index * cols : (index + 1) * cols] = weight[...]
        place_pieces(where, (mine, got), weights, (1 - where[0]) * half, half)

    unit, _ = rows_stats(x[...])
    n = (unit * gain[...] + shift[...]).astype(BF16)
    low[...] = n
    k[...] = dot(n, weights[:, cols : 2 * cols]).astype(BF16)
    v[...] = dot(n, weights[:, 2 * cols :]).astype(BF16)

    @pl.when(step >= 4)
    def _():
        q[...] = dot(n, weights[:, :cols]).astype(BF16)


def project(where, comp, mem, tok, other, gain, shift, wq, wk, wv, mine, got):
    rows, width = tok.shape
    cols = wq.shape[1] // 2
    half = spec((wq.shape[0], cols), lambda i, w: (0, w[0]))

    def by_step(size):
        return spec((rows, size), lambda i, w: (i, 0))

    return call(
        project_kernel,
        "project",
        where,
        (6,),
        [whole(a) for a in (comp, mem, tok, other, gain[None], shift[None])]
        + [(wq, half), (wk, half), (wv, half), whole(mine), whole(got)],
        [
            ((6 * rows, width), BF16, by_step(width)),
            ((2 * rows, cols), BF16, spec((rows, cols), lambda i, w: (jnp.maximum(i - 4, 0), 0))),
            ((6 * rows, cols), BF16, by_step(cols)),
            ((6 * rows, cols), BF16, by_step(cols)),
            ((width, 3 * cols), BF16, spec((width, 3 * cols))),
        ],
        [pltpu.VMEM((rows, width), F32)],
        cost=LARGE,
    )


def split_pairs(where, total, height, keep, send):
    pairs = total.reshape(total.shape[0] // (2 * height), 2, height, total.shape[1])
    even = where[1] == 0
    keep[...] = jnp.where(even, pairs[:, 0], pairs[:, 1]).astype(BF16)
    send[...] = jnp.where(even, pairs[:, 1], pairs[:, 0]).astype(BF16)


def by_parity(where, total, height):
    pairs = total.reshape(total.shape[0] // (2 * height), 2, height, total.shape[1])
    even = where[1] == 0
    shape = (total.shape[0] // 2, total.shape[1])
    keep = jnp.where(even, pairs[:, 0], pairs[:, 1]).reshape(shape)
    return keep, jnp.where(even, pairs[:, 1], pairs[:, 0]).reshape(shape)


def squeeze_kernel(slots, where, mem, other, dc, dc_o, weight, stay, away, keep, send, dc_sum):
    t = where[0]
    dc_sum[...] = jnp.sum(dc[...].astype(F32), 0, keepdims=True)
    rows, width = mem.shape
    mem_o = other.at[rows : 2 * rows, :]
    padded = dc.shape[0]
    half = width // 2
    lead = 3 * 2 * slots - 2 * rows
    first = t == 0
    shape = (padded, rows)
    slot = lax.broadcasted_iota(jnp.int32, shape, 0)
    row = lax.broadcasted_iota(jnp.int32, shape, 1)
    mem_half = jnp.where(first, mem[:, :half], mem[:, half:])
    mem_o_half = jnp.where(first, mem_o[:, :half], mem_o[:, half:])

    def picked(slot_half, row_half, offset):
        place = 3 * (slot + slot_half * slots) + offset - lead
        hit = (place == row + row_half * rows) & (slot < slots)
        return jnp.where(hit, 1.0, 0.0).astype(BF16)

    def windows(slot_half):
        edge = dot(picked(slot_half, t, 2 * t), mem[...]) + dot(
            picked(slot_half, 1 - t, 2 * t), mem_o[...]
        )
        middle = dot(picked(slot_half, t, 1), mem_half) + dot(
            picked(slot_half, 1 - t, 1), mem_o_half
        )
        return ordered(first, edge, middle, 1).astype(BF16)

    both = jnp.concatenate((windows(t), windows(1 - t)), 0)
    slots_out = dot(both, weight[...])
    stay[...] = slots_out[:padded, :]
    away[...] = slots_out[padded:, :].astype(BF16)
    turned_dc = jnp.concatenate((dc[...], dc_o[...]), 0).T
    columns = both.shape[1]
    height = keep.shape[1]
    for at in range(0, columns, half):
        part = slice(at, at + half)
        total = dot(turned_dc, both[:, part])
        split_pairs(where, total, height, keep.at[:, :, part], send.at[:, :, part])


def squeeze_rows(where, dp, slots, mem, other, dc, dc_o, weight):
    padded, width = dc.shape
    half = ((dp // 2, width // dp, weight.shape[0]), BF16)
    ins = [whole(a) for a in (mem, other, dc, dc_o, weight)]
    return call(
        functools.partial(squeeze_kernel, slots),
        "squeeze",
        where,
        (1,),
        ins,
        [
            ((padded, width), F32, spec((padded, width))),
            ((padded, width), BF16, spec((padded, width))),
            half + (spec(half[0]),),
            half + (spec(half[0]),),
            ((1, width), F32, spec((1, width))),
        ],
    )


def masked_scores(place, slope, q, keys, scale, first, tail):
    bias = place[0:1, :] * slope + place[1:2, :]
    chunk = q.shape[0]
    query_place = (lax.broadcasted_iota(jnp.int32, (chunk, 1), 0) + first).astype(F32)
    scores = dot_nt(q, keys) * (scale * LOG2E) + bias
    recent = jnp.where(place[0:1, tail:] <= query_place, scores[:, tail:], NEG)
    return jnp.concatenate((scores[:, :tail], recent), 1), query_place


def attend_kernel(turn, scale, where, slopes, q, k, v, place, mix, lse):
    slope = slopes[pl.program_id(0)] * LOG2E
    rows = q.shape[0]
    first = jnp.abs(turn - where[0]) * rows
    scores, _ = masked_scores(place, slope, q[...], k[...], scale, first, k.shape[0] - 2 * rows)
    highest = jnp.max(scores, -1, keepdims=True)
    weights = jnp.exp2(scores - highest)
    total = jnp.sum(weights, -1, keepdims=True)
    mix[...] = (dot(weights.astype(BF16), v[...]) * (1.0 / total)).astype(BF16)
    lse[0] = highest + jnp.log2(total)


def attend(where, turn, slopes, q, k, v, place):
    rows, width = q.shape[0] // 2, q.shape[1]
    heads = slopes.shape[0]
    hw = width // heads
    keys = k.shape[0]
    by_head = spec((keys, hw), lambda h, w: (0, h))
    return call(
        functools.partial(attend_kernel, turn, hw**-0.5),
        "attend",
        where,
        (heads,),
        [
            (slopes, pl.BlockSpec(memory_space=pltpu.SMEM)),
            (q, spec((rows, hw), lambda h, w: (turn, h))),
            (k, by_head),
            (v, by_head),
            whole(place),
        ],
        [
            ((rows, width), BF16, spec((rows, hw), lambda h, w: (0, h))),
            ((heads, rows, 1), F32, spec((1, rows, 1), lambda h, w: (h, 0, 0))),
        ],
        cost=LARGE,
    )


def attend_back_kernel(
    chunk,
    scale,
    height,
    where,
    slopes,
    q,
    k,
    v,
    dm,
    place,
    lse_own,
    lse_other,
    dq,
    dk,
    dv,
    all_keep,
    all_send,
    slope_out,
    dk_sum,
    dv_sum,
):
    slope = slopes[pl.program_id(0)] * LOG2E
    keys = k.shape[0]
    rows = q.shape[0]
    half = rows // 2
    columns = jnp.zeros((1, keys), F32)
    by_row = jnp.zeros((1, 1), F32)
    dq_parts = []
    for step in range(rows // chunk):
        at = slice(step * chunk, (step + 1) * chunk)
        time_half = where[0] if step * chunk < half else 1 - where[0]
        scores, query_place = masked_scores(
            place,
            slope,
            q[at, :],
            k[...],
            scale,
            time_half * half + step * chunk % half,
            keys - rows,
        )
        weights = jnp.exp2(scores - (lse_own if step == 0 else lse_other)[0])
        low = weights.astype(BF16)
        grads = dot_nt(dm[at, :], v[...])
        shift = jnp.sum(weights * grads, -1, keepdims=True)
        ds = (weights * (grads - shift)).astype(BF16)
        dq_part = dot(ds, k[...]) * scale
        dq[at, :] = dq_part.astype(BF16)
        dq_parts.append(dq_part.T)
        dk_part = dot_tn(q[at, :], ds)
        dv_part = dot_tn(dm[at, :], low)
        if step == 0:
            dk_sum[...] = dk_part
            dv_sum[...] = dv_part
        else:
            dk_sum[...] += dk_part
            dv_sum[...] += dv_part
        wide = ds.astype(F32)
        columns += jnp.sum(wide, 0, keepdims=True)
        by_row += jnp.sum(jnp.sum(wide, -1, keepdims=True) * query_place, 0, keepdims=True)
    dk_all, dv_all = dk_sum[...] * scale, dv_sum[...]
    dq_all = jnp.concatenate([jnp.zeros((dk_all.shape[0], keys - rows), F32)] + dq_parts, 1)
    halves = [by_parity(where, part, height) for part in (dq_all, dk_all, dv_all)]
    for target, parts in zip((all_keep, all_send), zip(*halves)):
        blocks = [part.reshape(part.shape[0] // height, height, keys) for part in parts]
        target[...] = jnp.stack(blocks, 1).reshape(target.shape).astype(BF16)
    dk[...] = dk_all.T.astype(BF16)
    dv[...] = dv_all.T.astype(BF16)
    total = jnp.sum(columns * place[0:1, :], -1, keepdims=True) - by_row
    slope_out[...] = jnp.broadcast_to(total.reshape(1, 1, 1), slope_out.shape)


def attend_back(where, height, slopes, q, k, v, dm, place, lses):
    rows, width = q.shape
    heads = slopes.shape[0]
    hw = width // heads
    keys = k.shape[0]
    by_rows = spec((rows, hw), lambda h, w: (0, h))
    by_keys = spec((keys, hw), lambda h, w: (0, h))
    return call(
        functools.partial(attend_back_kernel, rows // 2, hw**-0.5, height),
        "attend_back",
        where,
        (heads,),
        [
            (slopes, pl.BlockSpec(memory_space=pltpu.SMEM)),
            (q, by_rows),
            (k, by_keys),
            (v, by_keys),
            (dm, by_rows),
            whole(place),
            (lses[0], spec((1, rows // 2, 1), lambda h, w: (h, 0, 0))),
            (lses[1], spec((1, rows // 2, 1), lambda h, w: (h, 0, 0))),
        ],
        [
            ((rows, width), BF16, by_rows),
            ((keys, width), BF16, by_keys),
            ((keys, width), BF16, by_keys),
            ((3 * width // 2, keys), BF16, spec((3 * hw // 2, keys), lambda h, w: (h, 0))),
            ((3 * width // 2, keys), BF16, spec((3 * hw // 2, keys), lambda h, w: (h, 0))),
            ((heads, 8, 128), F32, spec((1, 8, 128), lambda h, w: (h, 0, 0))),
        ],
        [pltpu.VMEM((hw, keys), F32), pltpu.VMEM((hw, keys), F32)],
        cost=LARGE,
    )


def gelu_pair(v):
    c = 0.7978845608028654
    inner = c * (v + 0.044715 * v * v * v)
    th = jnp.tanh(inner)
    slope = 0.5 * (1.0 + th) + 0.5 * v * (1.0 - th * th) * c * (1.0 + 3 * 0.044715 * v * v)
    return 0.5 * v * (1.0 + th), slope


def feed_kernel(height, block, where, *refs):
    (
        mix,
        far,
        tok,
        wo,
        wo_mine,
        wo_got,
        gain,
        shift,
        dy,
        wi,
        wi_mine,
        wi_got,
        bias,
        wh,
        residual,
        normed,
        act,
        grad_keep,
        grad_send,
        dy_keep,
        dy_send,
        g2,
        bias_sum,
        dy_sum,
        *sent,
        wo_far,
        weight,
    ) = refs
    step = pl.program_id(0)
    half = wi.shape[0]

    @pl.when(step == 0)
    def _():
        place_pieces(where, (wo_mine, wo_got), wo_far)
        wide_dy = dy[...].astype(F32)
        dy_sum[...] = jnp.sum(wide_dy, 0, keepdims=True)
        dy_stay, dy_away = by_parity(where, wide_dy.T, height)
        dy_keep[...] = dy_stay.astype(BF16)
        dy_send[...] = dy_away.astype(BF16)
        total = tok[...].astype(F32) + (dot(mix[...], wo[...]) + dot(far[...], wo_far[...]))
        residual[...] = total
        unit, _ = rows_stats(total)
        normed[...] = (unit * gain[...] + shift[...]).astype(BF16)

    weight[pl.ds(pl.multiple_of(where[0] * half, half), half), :] = wi[...]
    place_pieces(where, (wi_mine, wi_got), weight, (1 - where[0]) * half, half)
    pre = dot(normed[...], weight[...]) + bias[...]
    value, slope = gelu_pair(pre)
    low = value.astype(BF16)
    act[...] = low
    grad = (dot_nt(dy[...], wh[...]) * slope).astype(BF16)
    blocks = [grad[:, at : at + block] for at in range(0, grad.shape[1], block)]
    evens, odds = jnp.concatenate(blocks[::2], 1), jnp.concatenate(blocks[1::2], 1)
    even = where[1] == 0
    grad_keep[...] = jnp.where(even, evens, odds)
    grad_send[...] = jnp.where(even, odds, evens)
    bias_sum[...] = jnp.sum(grad.astype(F32), 0, keepdims=True)
    g2_part = dot_nt(grad, weight[...])

    @pl.when(step == 0)
    def _():
        g2[...] = g2_part

    @pl.when(step > 0)
    def _():
        g2[...] += g2_part

    @pl.when(step == pl.num_programs(0) - 1)
    def _():
        first_row = 0
        for piece in sent:
            piece[...] = g2[first_row : first_row + piece.shape[0], :].astype(BF16)
            first_row += piece.shape[0]


def feed(
    where, dp, turn, mix, far, tok, wo, gain, shift, dy, wi, bias, wh, second, chunk, parts, onto
):
    rows, width = dy.shape
    hidden = wh.shape[0]
    steps = hidden // chunk
    mine, got = second
    by_cols = spec((rows, chunk), lambda j, w: (turn, j))
    by_half = spec((rows, chunk // 2), lambda j, w: (turn, j))
    half = (2 * rows, hidden // 2), BF16, by_half
    turned = (width // 2, 2 * rows), BF16, spec((width // 2, rows), lambda j, w: (0, turn))
    wo_part = spec((mine.shape[0], width), lambda j, w: (0, 0))
    wi_part = spec((mine.shape[0], chunk), lambda j, w: (0, width // chunk + j))

    def once(dtype):
        return (rows, width), dtype, spec((rows, width))

    return call(
        functools.partial(feed_kernel, width // dp, hidden // (dp // 2)),
        "feed",
        where,
        (steps,),
        [
            whole(mix),
            whole(far),
            (tok, spec((rows, width), lambda j, w: (2 * turn, 0))),
            whole(wo),
            (mine, wo_part),
            (got, wo_part),
            whole(gain[None]),
            whole(shift[None]),
            whole(dy),
            (wi, spec((wi.shape[0], chunk), lambda j, w: (0, w[0] * steps + j))),
            (mine, wi_part),
            (got, wi_part),
            (bias[None], spec((1, chunk), lambda j, w: (0, w[0] * steps + j))),
            (wh, spec((chunk, width), lambda j, w: (j, 0))),
        ],
        [
            once(F32),
            ((2 * rows, width), BF16, spec((rows, width), lambda j, w: (turn, 0))),
            ((2 * rows, hidden), BF16, by_cols),
            half,
            half,
            turned,
            turned,
            once(F32),
            ((1, hidden), F32, spec((1, chunk), lambda j, w: (0, j))),
            ((1, width), F32, spec((1, width))),
        ]
        + [((rows // part, width), BF16, spec((rows // part, width))) for part in parts],
        [
            pltpu.VMEM(wo.shape, BF16),
            pltpu.VMEM((width, chunk), BF16),
        ],
        cost=LARGE,
        onto=onto,
    )


def middle_kernel(
    where,
    g_own,
    g_other,
    got_own,
    got_other,
    residual_own,
    residual_other,
    gain,
    dy,
    dy_o,
    wo,
    mix_own,
    mix_other,
    bias_sum,
    bias_sum_o,
    dy_sum,
    dc_sum,
    grad_res,
    dm,
    sums,
    keep,
    send,
):
    rows = dy.shape[0]
    lows = []
    halves = ((g_own, got_own, dy, residual_own), (g_other, got_other, dy_o, residual_other))
    for at, (g, got, d, residual) in enumerate(halves):
        here = slice(at * rows, (at + 1) * rows)
        grad = g[...] + got[...].astype(F32)
        unit, rstd = rows_stats(residual[...])
        total = d[...].astype(F32) + norm_back(grad, gain[...], unit, rstd)
        low = total.astype(BF16)
        lows.append(low)
        dm[here, :] = dot_nt(low, wo[...]).astype(BF16)
        if at == 0:
            grad_res[...] = total
            small = [jnp.sum(grad * unit, 0, keepdims=True), jnp.sum(grad, 0, keepdims=True)]
    width = dy.shape[1]
    first = where[0] == 0
    parts = [slice(at, at + width) for at in range(0, bias_sum.shape[1], width)]
    downs = [bias_sum[:, part] + bias_sum_o[:, part] for part in parts]
    small += [jnp.where(first, down, 0.0) for down in downs]
    small += [jnp.where(first, 0.0, down) for down in downs]
    small += [dy_sum[...], dc_sum[...]]
    sums[...] = jnp.concatenate(small, 0)
    split_pairs(
        where, dot_tn(lows[0], mix_own[...]) + dot_tn(lows[1], mix_other[...]), keep.shape[1], keep, send
    )


def middle(where, dp, g, got, residuals, gain, dys, wo, mix, small):
    rows, width = dys[0].shape
    heads = wo.shape[0]
    half = ((dp // 2, width // dp, heads), BF16, spec((dp // 2, width // dp, heads)))
    return call(
        middle_kernel,
        "middle",
        where,
        (1,),
        [whole(a) for a in (*g, *got, *residuals, gain[None], *dys, wo, *mix, *small)],
        [
            ((rows, width), F32, spec((rows, width))),
            ((2 * rows, heads), BF16, spec((2 * rows, heads))),
            ((8, width), F32, spec((8, width))),
            half,
            half,
        ],
        cost=LARGE,
    )


def norm_sums(step, grad, x, sums):
    unit, _ = rows_stats(x)
    rows = jnp.sum(grad * unit, 0, keepdims=True), jnp.sum(grad, 0, keepdims=True)

    @pl.when(step == 0)
    def _():
        sums[0:1, :], sums[1:2, :] = rows

    @pl.when(step > 0)
    def _():
        sums[0:1, :] += rows[0]
        sums[1:2, :] += rows[1]


def tokens_kernel(where, tok, other, dq, dk, dv, weights, g_own, sent, sums):
    step = pl.program_id(0)
    cols = dq.shape[1]
    grad = (
        dot_nt(dq[...], weights[:, :cols])
        + dot_nt(dk[...], weights[:, cols : 2 * cols])
        + dot_nt(dv[...], weights[:, 2 * cols :])
    )
    x = jnp.where(step == 0, tok[...].astype(F32), other[...].astype(F32))
    norm_sums(step, grad, x, sums)

    @pl.when(step == 0)
    def _():
        g_own[...] = grad

    @pl.when(step == 1)
    def _():
        sent[...] = grad.astype(BF16)


def tokens_back(where, tok, other, dq, dk, dv, weights):
    rows, width = tok.shape
    cols = dk.shape[1]
    late = spec((rows, cols), lambda i, w: (4 + i, 0))
    return call(
        tokens_kernel,
        "tokens_back",
        where,
        (2,),
        [
            whole(tok),
            (other, spec((rows, width), lambda i, w: (2, 0))),
            (dq, spec((rows, cols), lambda i, w: (i, 0))),
            (dk, late),
            (dv, late),
            whole(weights),
        ],
        [
            ((rows, width), F32, spec((rows, width))),
            ((rows, width), BF16, spec((rows, width))),
            ((2, width), F32, spec((2, width))),
        ],
    )


def slots_kernel(
    where, comp, mem, other, dk, dv, weights, start, slope_parts, early, sums, total
):
    step = pl.program_id(0)
    cols = dk.shape[1]
    grad = dot_nt(dk[...], weights[:, cols : 2 * cols]) + dot_nt(dv[...], weights[:, 2 * cols :])
    own = jnp.where(step == 0, comp[...].astype(F32), mem[...].astype(F32))
    x = jnp.where(step % 2 == 0, own, other[...].astype(F32))
    norm_sums(step, grad, x, total)

    @pl.when(step == pl.num_programs(0) - 1)
    def _():
        width = comp.shape[1]
        lane = lax.broadcasted_iota(jnp.int32, (1, width), 1)
        own_heads = slope_parts.shape[0]
        slope = jnp.zeros((1, width), F32)
        for head in range(own_heads):
            here = lane == where[0] * own_heads + head
            slope += jnp.where(here, slope_parts[head, 0:1, 0:1], 0.0)
        sums[:8, :] = early[...]
        rest = (total[...] + start[...], slope, jnp.zeros((5, width), F32))
        sums[8:, :] = jnp.concatenate(rest, 0)


def slots_back(where, comp, mem, other, dk, dv, weights, start, slope_parts, early):
    rows, width = comp.shape
    cols = dk.shape[1]
    by_step = spec((rows, cols), lambda i, w: (i, 0))
    return call(
        slots_kernel,
        "slots_back",
        where,
        (4,),
        [
            whole(comp),
            whole(mem),
            (other, spec((rows, width), lambda i, w: (i // 2, 0))),
            (dk, by_step),
            (dv, by_step),
            whole(weights),
            whole(start),
            whole(slope_parts),
            whole(early),
        ],
        [((16, width), F32, spec((16, width)))],
        [pltpu.VMEM((2, width), F32)],
        cost=LARGE,
    )


def turn_kernel(source, target):
    target[...] = source[...].T


def turned(array):
    return pl.pallas_call(
        turn_kernel,
        out_shape=jax.ShapeDtypeStruct(array.shape[::-1], F32),
        compiler_params=PARAMS,
        cost_estimate=TINY,
        name="turn",
    )(array)


def local(
    tokens,
    memory,
    compressed,
    mask_start,
    norm1_gain,
    norm1_bias,
    query_weight,
    key_weight,
    value_weight,
    out_weight,
    slopes,
    norm2_gain,
    norm2_bias,
    in_weight,
    in_bias,
    hidden_weight,
    hidden_bias,
    compress_weight,
    compress_bias,
    grad_out,
    grad_compressed,
):
    tokens, memory, compressed = tokens[0], memory[0], compressed[0]
    grad_out, grad_compressed = grad_out[0], grad_compressed[0]
    rows, width = tokens.shape
    heads = slopes.shape[0]
    dp = lax.axis_size("dp")
    levels = dp.bit_length() - 1
    top = levels - 1
    d = lax.axis_index("dp")
    t = lax.axis_index("tm")
    segment = 2 * rows

    def swap(block):
        return lax.ppermute(block, "tm", [(0, 1), (1, 0)])

    def across(block, mask):
        return lax.ppermute(block, "dp", [(i, i ^ mask) for i in range(dp)])

    def after(array, *earlier):
        return lax.optimization_barrier((array,) + earlier)[0]

    def bit(level):
        return (d >> level) & 1

    class Shrink:
        def __init__(self, keep, send, order, columns=False):
            shape = keep.shape if keep.ndim == 4 else keep.shape[:1] + (1,) + keep.shape[1:]
            self.pending = keep.reshape(shape), send.reshape(shape), 1
            self.order = [0] + order
            self.left = [level for level in range(1, top if columns else levels)]
            self.step = 0
            self.array = None

        def cut(self):
            if self.pending is not None:
                return self.pending[1]
            if self.step == len(self.order):
                return self.array
            level = self.order[self.step]
            if level in self.left:
                low = 1 << self.left.index(level)
                blocks, rest = self.array.shape[0], self.array.shape[1:]
                split = self.array.reshape((blocks // (2 * low), 2, low) + rest)
                keep, send = [
                    lax.dynamic_index_in_dim(split, at, 1, keepdims=False).reshape(
                        (blocks // 2,) + rest
                    )
                    for at in (bit(level), 1 - bit(level))
                ]
                self.left.remove(level)
                self.pending = keep, send, 1 << level
            else:
                size = self.array.shape[3] // 2
                keep, send = [
                    lax.dynamic_slice_in_dim(self.array, at * size, size, 3) for at in (t, 1 - t)
                ]
                self.pending = keep, send, 0
            return send

        def move(self):
            send = self.cut()
            return across(send, self.pending[2]) if self.pending[2] else swap(send)

        def take(self, got):
            keep, _, mask = self.pending
            if mask == 0:
                same = bit(top) == t
                self.pending = jnp.where(same, keep, got), jnp.where(same, got, keep), 1 << top
                return self.pending[1]
            self.step += 1
            total = keep.astype(F32) + got.astype(F32)
            last = self.step == len(self.order)
            self.array = total if last else total.astype(BF16)
            self.pending = None
            return self.array

        def add(self):
            if self.step == len(self.order):
                return self.array
            self.cut()
            if self.pending[2] == 0:
                self.take(self.move())
            return self.take(self.move())

        def wait(self, *earlier):
            if self.pending is not None:
                self.pending = (after(self.pending[0], *earlier),) + self.pending[1:]

        def finish(self):
            while self.step < len(self.order):
                self.add()
            return self.array[0]

    def meet(groups, *others):
        groups = [group for group in groups if group.step < len(group.order)]
        got = lax.optimization_barrier(tuple(group.move() for group in groups) + others)
        for group, block in zip(groups, got):
            group.take(block)
        for group in groups:
            group.cut()
        return got[len(groups) :]

    sideways = list(range(1, levels))
    upward = list(range(2, levels)) + [1] if levels > 1 else []
    between = upward[:1] + upward[-1:] + upward[1:-1] if levels > 2 else upward

    sharing = min(levels, 4)
    share = 1 << sharing
    ups = [z << 2 for z in range(1 << max(sharing - 2, 0))]
    offsets = [x + z for x in ((0, 2) if sharing > 1 else (0,)) for z in ups]
    low_bits = d & (share - 1)
    targets = [low_bits ^ off for off in offsets] + [low_bits ^ off ^ 1 for off in offsets]
    where = jnp.stack([t, bit(0)] + targets).astype(jnp.int32)

    def gather_up(piece):
        return jnp.concatenate([piece] + [across(piece, z) for z in ups[1:]], 0)

    def gather_side(block):
        return jnp.concatenate((block, across(block, 2)), 0) if sharing > 1 else block

    (joined,) = pieces(
        jnp.stack((low_bits, 1 - t)).astype(jnp.int32),
        share,
        query_weight,
        key_weight,
        value_weight,
        out_weight,
        in_weight,
    )
    joined = swap(joined)
    first_size = 3 * query_weight.shape[1] // 2
    first, second = joined[:, :first_size], joined[:, first_size:]
    slots = grad_compressed.shape[0]
    dc = jnp.pad(grad_compressed, ((0, -slots % 16), (0, 0)))
    x_other = swap(jnp.concatenate((compressed, memory, tokens), 0))
    first = gather_side(gather_up(first))
    first_got = across(first, 1)
    second = gather_side(gather_up(after(second, first)))
    second_got = across(second, 1)
    dc_other, dy_other = swap(after(dc, x_other)), swap(after(grad_out, x_other))

    inputs_low, queries, keys, values, qkv = project(
        where,
        compressed,
        memory,
        tokens,
        x_other,
        norm1_gain,
        norm1_bias,
        query_weight,
        key_weight,
        value_weight,
        first,
        first_got,
    )

    index = jnp.arange(segment, dtype=jnp.int32)
    slot = jnp.where(index < rows, index + t * rows, index - rows + (1 - t) * rows)
    place = jnp.concatenate((-segment - 3 * (segment - slot), slot - segment, slot)).astype(F32)
    closed = jnp.where(slot >= mask_start[0], 0.0, NEG)
    closed = jnp.concatenate((closed, jnp.zeros((2 * segment,), F32)))
    place = jnp.stack((place, closed))
    own_heads = heads // 2
    slopes_own = lax.dynamic_slice_in_dim(slopes, t * own_heads, own_heads, 0)
    queries = after(queries, second)
    mix_other, lse_other = attend(where, 1, slopes_own, queries, keys, values, place)
    far_own = swap(mix_other)
    squeeze_stay, squeeze_away, keep, send, dc_sum = squeeze_rows(
        where, dp, slots, after(memory, mix_other), x_other, dc, dc_other, compress_weight
    )
    squeeze = Shrink(keep, send, sideways)
    squeeze_got = swap(squeeze_away)
    mix_own, lse_own = attend(
        where, 0, slopes_own, after(queries, squeeze_away), keys, values, place
    )
    far_other = swap(mix_own)
    dys = grad_out, dy_other
    mix = mix_own, mix_other
    chunk = max(in_weight.shape[1] // 8, 2 * in_weight.shape[1] // dp)

    def feed_rows(turn, mixed, far, tok, dy, parts, onto=None):
        return feed(
            where,
            dp,
            turn,
            mixed,
            far,
            tok,
            out_weight,
            norm2_gain,
            norm2_bias,
            dy,
            in_weight,
            in_bias,
            hidden_weight,
            (second, second_got),
            chunk,
            parts,
            onto,
        )

    squeeze.add()
    residual, *half_filled, g_own, bias_sum, dy_sum, sent = feed_rows(
        0, after(mix_own, squeeze.cut()), far_own, tokens, grad_out, (1,)
    )
    got_other = swap(sent)
    residual_o, *filled, g_other, bias_sum_o, _, sent = feed_rows(
        1,
        after(mix_other, sent, squeeze_got),
        far_other,
        x_other,
        dy_other,
        (1,),
        {1 + i: array for i, array in enumerate(half_filled)},
    )
    got = swap(sent), got_other
    normed, act, grad_keep, grad_send, dy_keep, dy_send = filled
    squeeze.wait(sent)
    squeeze.add()
    blocks = dp // 2

    def cut_rows(product, count):
        return product.astype(BF16).reshape(count, product.shape[0] // count, product.shape[1])

    hidden_send = dot(after(dy_send, squeeze.cut(), got_other), act).astype(BF16)
    entry_send = dot_tn(after(grad_send, hidden_send), normed).astype(BF16)
    hidden_keep = dot(after(dy_keep, entry_send), act).astype(BF16)
    entry_keep = dot_tn(after(grad_keep, hidden_keep), normed).astype(BF16)
    hidden = Shrink(cut_rows(hidden_keep, blocks), cut_rows(hidden_send, blocks), sideways)
    entry = Shrink(
        cut_rows(entry_keep, blocks // 2), cut_rows(entry_send, blocks // 2), between, True
    )
    got = after(got[0], entry_keep), got[1]
    grad_residual, grad_mixture, early, keep, send = middle(
        where,
        dp,
        (after(g_own, entry_keep), g_other),
        got,
        (residual, residual_o),
        norm2_gain,
        dys,
        out_weight,
        mix,
        (bias_sum, bias_sum_o, dy_sum, dc_sum),
    )
    mix_out = Shrink(keep, send, sideways)
    squeeze.add()
    hidden.add()
    entry.add()
    height = key_weight.shape[1] // dp
    dq, dk, dv, all_keep, all_send, slope_parts = attend_back(
        where,
        height,
        slopes_own,
        queries,
        keys,
        values,
        after(grad_mixture, hidden.cut(), entry.cut(), squeeze.array),
        place,
        (lse_own, lse_other),
    )
    mix_out.wait(dq)

    def cut_heads(product):
        return product.reshape(blocks // 2, -1, height, width)

    all_send = dot(all_send, inputs_low).astype(BF16)
    all_keep = dot(after(all_keep, all_send), inputs_low).astype(BF16)
    hidden.add()
    entry.add()
    left = Shrink(cut_heads(all_keep), cut_heads(all_send), sideways, True)
    mix_out.add()
    left.add()
    mix_out.cut()
    mix_out.wait(left.cut())
    mix_out.add()
    squeeze.add()
    g1_own, g1_sent, token_sums = tokens_back(
        where,
        tokens,
        x_other,
        after(dq, left.cut(), hidden.cut(), entry.cut(), mix_out.cut(), squeeze.array),
        dk,
        dv,
        qkv,
    )
    g1_got = swap(g1_sent)
    mix_out.wait(g1_sent)
    mix_out.add()
    (smalls,) = slots_back(
        where,
        compressed,
        memory,
        x_other,
        after(dk, mix_out.cut()),
        dv,
        qkv,
        token_sums,
        slope_parts,
        early,
    )

    def joint(array, mask):
        return lax.ppermute(array, ("dp", "tm"), [(i, i ^ mask) for i in range(2 * dp)])

    out_part = dot(after(act, smalls), hidden_weight)
    out_own, out_sent = out_part[:rows], out_part[rows:].astype(BF16)
    smalls, g1_got, out_sent = meet((left, hidden, entry, mix_out), smalls, g1_got, out_sent)
    out_got = swap(out_sent)
    groups = (left, hidden, entry, mix_out, squeeze)
    masks = [1 << at for at in range(levels + 1)]
    while masks:
        sends = [group.cut() for group in groups]
        smalls = after(smalls, *sends)
        if len(masks) > 1 and len(masks) % 2:
            smalls = smalls + joint(smalls, masks.pop(0))
        smalls, got = meet(groups, smalls, joint(smalls, masks.pop(0)))
        smalls = smalls + got
    output = (residual + (out_own + out_got.astype(F32)) + hidden_bias).astype(BF16)
    new_compressed = (
        after(squeeze_stay, sends[0])[:slots] + squeeze_got[:slots].astype(F32) + compress_bias
    ).astype(BF16)
    g1 = g1_own + g1_got.astype(F32)
    unit1, rstd1 = rows_stats(tokens.astype(F32))
    grad_tokens = (grad_residual + norm_back(g1, norm1_gain, unit1, rstd1)).astype(BF16)

    grad_query_w, grad_key_w, grad_value_w = [part.T for part in left.finish()]
    grad_in_w = turned(entry.finish()[0])
    grad_hidden_w, grad_out_w, grad_compress_w = [
        group.finish()[0].T for group in (hidden, mix_out, squeeze)
    ]
    gain2, bias2, hidden_b, compress_b, gain1, bias1, slope = [
        smalls[i] for i in (0, 1, 6, 7, 8, 9, 10)
    ]
    in_b = smalls[2:6].reshape(-1)
    return (
        output[None],
        new_compressed[None],
        grad_tokens[None],
        gain1,
        bias1,
        grad_query_w,
        grad_key_w,
        grad_value_w,
        grad_out_w,
        slope[:heads],
        gain2,
        bias2,
        grad_in_w,
        in_b,
        grad_hidden_w,
        hidden_b,
        grad_compress_w,
        compress_b,
    )


def solution(mesh):
    split, whole, kept = P("dp", "tm", None), P(), P("tm", None)
    in_specs = (
        (split,) * 3
        + (P("dp"), whole, whole)
        + (kept,) * 4
        + (whole,) * 3
        + (kept, whole, kept, whole, kept, whole)
        + (split,) * 2
    )
    shared = P("tm", "dp")
    out_specs = (
        (split,) * 3
        + (whole,) * 2
        + (shared,) * 4
        + (whole,) * 3
        + (shared, whole, shared, whole, shared, whole)
    )
    return jax.shard_map(local, mesh=mesh, in_specs=in_specs, out_specs=out_specs, check_vma=False)
```

```python
import functools

import jax
import jax.numpy as jnp
from jax import lax
from jax.experimental import pallas as pl
from jax.experimental.pallas import tpu as pltpu
from jax.sharding import PartitionSpec as P

EPS = 1e-05
NEG = -1e30
LOG2E = 1.4426950408889634
F32 = jnp.float32
BF16 = jnp.bfloat16
TINY = pl.CostEstimate(flops=1000, bytes_accessed=1000, transcendentals=0)
LARGE = pl.CostEstimate(flops=20 * 10**9, bytes_accessed=10**6, transcendentals=0)
PARAMS = pltpu.CompilerParams(vmem_limit_bytes=52 * 2**20)


def dot(a, b, dims=((1,), (0,))):
    return lax.dot_general(a, b, (dims, ((), ())), preferred_element_type=F32)


def dot_nt(a, b):
    return dot(a, b, ((1,), (1,)))


def dot_tn(a, b):
    return dot(a, b, ((0,), (0,)))


def rows_stats(x):
    mean = jnp.mean(x, -1, keepdims=True)
    centered = x - mean
    rstd = lax.rsqrt(jnp.mean(centered * centered, -1, keepdims=True) + EPS)
    return centered * rstd, rstd


def norm_back(grad, gain, normed, rstd):
    dn = grad * gain
    return rstd * (
        dn
        - jnp.mean(dn, -1, keepdims=True)
        - normed * jnp.mean(dn * normed, -1, keepdims=True)
    )


def spec(shape, at=None):
    zeros = (0,) * len(shape)
    return pl.BlockSpec(shape, at if at is not None else (lambda *_: zeros))


def call(kernel, name, where, grid, ins, outs, scratch=(), cost=TINY, onto=None):
    onto = onto or {}
    count = len(ins)
    ins = list(ins) + [(array, pl.BlockSpec(memory_space=pl.ANY)) for array in onto.values()]

    def body(place, *refs):
        kernel(place, *refs[:count], *refs[len(ins) :])

    return pl.pallas_call(
        body,
        grid_spec=pltpu.PrefetchScalarGridSpec(
            num_scalar_prefetch=1,
            grid=grid,
            in_specs=[at for _, at in ins],
            out_specs=[at for _, _, at in outs],
            scratch_shapes=list(scratch),
        ),
        out_shape=[jax.ShapeDtypeStruct(shape, dtype) for shape, dtype, _ in outs],
        input_output_aliases={1 + count + i: out for i, out in enumerate(onto)},
        compiler_params=PARAMS,
        cost_estimate=cost,
        name=name,
    )(where, *[array for array, _ in ins])


def whole(array):
    return array, spec(array.shape)


def ordered(first, own, other, axis):
    return jnp.where(
        first, jnp.concatenate((own, other), axis), jnp.concatenate((other, own), axis)
    )


def place_pieces(where, parts, target, base=0, half=None):
    size = (half or target.shape[0]) // (where.shape[0] - 2)
    at = 0
    for part in parts:
        for block in range(part.shape[0] // size):
            row = pl.multiple_of(base + where[2 + at] * size, size)
            target[pl.ds(row, size), :] = part[block * size : (block + 1) * size, :]
            at += 1


def pieces_kernel(where, wq, wk, wv, wo, wi, joined):
    size = wq.shape[1]
    first, second = joined.at[:, : 3 * size], joined.at[:, 3 * size :]
    first[:, :size] = wq[...]
    first[:, size : 2 * size] = wk[...]
    first[:, 2 * size :] = wv[...]
    second[:, : wo.shape[1]] = wo[...]
    second[:, wo.shape[1] :] = wi[...]


def pieces(where, share, wq, wk, wv, wo, wi):
    rows = wq.shape[0] // share
    cols = wq.shape[1] // 2
    wide = wi.shape[1] // 2
    half = spec((rows, cols), lambda i, w: (w[0], w[1]))
    return call(
        pieces_kernel,
        "pieces",
        where,
        (1,),
        [
            (wq, half),
            (wk, half),
            (wv, half),
            (wo, spec((rows, wo.shape[1]), lambda i, w: (w[0], 0))),
            (wi, spec((rows, wide), lambda i, w: (w[0], w[1]))),
        ],
        [
            (
                (rows, 3 * cols + wo.shape[1] + wide),
                BF16,
                spec((rows, 3 * cols + wo.shape[1] + wide)),
            )
        ],
    )


def load_rows(step, x, comp, mem, tok, other):
    rows = tok.shape[0]
    sources = (
        comp,
        other.at[:rows, :],
        mem,
        other.at[rows : 2 * rows, :],
        tok,
        other.at[2 * rows :, :],
    )
    for at, source in enumerate(sources):

        @pl.when(step == at)
        def _(source=source):
            x[...] = source[...].astype(F32)


def project_kernel(
    where,
    comp,
    mem,
    tok,
    other,
    gain,
    shift,
    wq,
    wk,
    wv,
    mine,
    got,
    low,
    q,
    k,
    v,
    weights,
    x,
):
    step = pl.program_id(0)
    load_rows(step, x, comp, mem, tok, other)
    half, cols = wq.shape

    @pl.when(step == 0)
    def _():
        own = pl.ds(pl.multiple_of(where[0] * half, half), half)
        for index, weight in enumerate((wq, wk, wv)):
            weights[own, index * cols : (index + 1) * cols] = weight[...]
        place_pieces(where, (mine, got), weights, (1 - where[0]) * half, half)

    unit, _ = rows_stats(x[...])
    n = (unit * gain[...] + shift[...]).astype(BF16)
    low[...] = n
    k[...] = dot(n, weights[:, cols : 2 * cols]).astype(BF16)
    v[...] = dot(n, weights[:, 2 * cols :]).astype(BF16)

    @pl.when(step >= 4)
    def _():
        q[...] = dot(n, weights[:, :cols]).astype(BF16)


def project(where, comp, mem, tok, other, gain, shift, wq, wk, wv, mine, got):
    rows, width = tok.shape
    cols = wq.shape[1] // 2
    half = spec((wq.shape[0], cols), lambda i, w: (0, w[0]))

    def by_step(size):
        return spec((rows, size), lambda i, w: (i, 0))

    return call(
        project_kernel,
        "project",
        where,
        (6,),
        [whole(a) for a in (comp, mem, tok, other, gain[None], shift[None])]
        + [(wq, half), (wk, half), (wv, half), whole(mine), whole(got)],
        [
            ((6 * rows, width), BF16, by_step(width)),
            ((2 * rows, cols), BF16, spec((rows, cols), lambda i, w: (jnp.maximum(i - 4, 0), 0))),
            ((6 * rows, cols), BF16, by_step(cols)),
            ((6 * rows, cols), BF16, by_step(cols)),
            ((width, 3 * cols), BF16, spec((width, 3 * cols))),
        ],
        [pltpu.VMEM((rows, width), F32)],
        cost=LARGE,
    )


def split_pairs(where, total, height, keep, send):
    pairs = total.reshape(total.shape[0] // (2 * height), 2, height, total.shape[1])
    even = where[1] == 0
    keep[...] = jnp.where(even, pairs[:, 0], pairs[:, 1]).astype(BF16)
    send[...] = jnp.where(even, pairs[:, 1], pairs[:, 0]).astype(BF16)


def by_parity(where, total, height):
    pairs = total.reshape(total.shape[0] // (2 * height), 2, height, total.shape[1])
    even = where[1] == 0
    shape = (total.shape[0] // 2, total.shape[1])
    keep = jnp.where(even, pairs[:, 0], pairs[:, 1]).reshape(shape)
    return keep, jnp.where(even, pairs[:, 1], pairs[:, 0]).reshape(shape)


def squeeze_kernel(slots, where, mem, other, dc, dc_o, weight, stay, away, keep, send, dc_sum):
    t = where[0]
    dc_sum[...] = jnp.sum(dc[...].astype(F32), 0, keepdims=True)
    rows, width = mem.shape
    mem_o = other.at[rows : 2 * rows, :]
    padded = dc.shape[0]
    half = width // 2
    lead = 3 * 2 * slots - 2 * rows
    first = t == 0
    shape = (padded, rows)
    slot = lax.broadcasted_iota(jnp.int32, shape, 0)
    row = lax.broadcasted_iota(jnp.int32, shape, 1)
    mem_half = jnp.where(first, mem[:, :half], mem[:, half:])
    mem_o_half = jnp.where(first, mem_o[:, :half], mem_o[:, half:])

    def picked(slot_half, row_half, offset):
        place = 3 * (slot + slot_half * slots) + offset - lead
        hit = (place == row + row_half * rows) & (slot < slots)
        return jnp.where(hit, 1.0, 0.0).astype(BF16)

    def windows(slot_half):
        edge = dot(picked(slot_half, t, 2 * t), mem[...]) + dot(
            picked(slot_half, 1 - t, 2 * t), mem_o[...]
        )
        middle = dot(picked(slot_half, t, 1), mem_half) + dot(
            picked(slot_half, 1 - t, 1), mem_o_half
        )
        return ordered(first, edge, middle, 1).astype(BF16)

    both = jnp.concatenate((windows(t), windows(1 - t)), 0)
    slots_out = dot(both, weight[...])
    stay[...] = slots_out[:padded, :]
    away[...] = slots_out[padded:, :].astype(BF16)
    turned_dc = jnp.concatenate((dc[...], dc_o[...]), 0).T
    columns = both.shape[1]
    height = keep.shape[1]
    for at in range(0, columns, half):
        part = slice(at, at + half)
        total = dot(turned_dc, both[:, part])
        split_pairs(where, total, height, keep.at[:, :, part], send.at[:, :, part])


def squeeze_rows(where, dp, slots, mem, other, dc, dc_o, weight):
    padded, width = dc.shape
    half = ((dp // 2, width // dp, weight.shape[0]), BF16)
    ins = [whole(a) for a in (mem, other, dc, dc_o, weight)]
    return call(
        functools.partial(squeeze_kernel, slots),
        "squeeze",
        where,
        (1,),
        ins,
        [
            ((padded, width), F32, spec((padded, width))),
            ((padded, width), BF16, spec((padded, width))),
            half + (spec(half[0]),),
            half + (spec(half[0]),),
            ((1, width), F32, spec((1, width))),
        ],
    )


def masked_scores(place, slope, q, keys, scale, first, tail):
    bias = place[0:1, :] * slope + place[1:2, :]
    chunk = q.shape[0]
    query_place = (lax.broadcasted_iota(jnp.int32, (chunk, 1), 0) + first).astype(F32)
    scores = dot_nt(q, keys) * (scale * LOG2E) + bias
    recent = jnp.where(place[0:1, tail:] <= query_place, scores[:, tail:], NEG)
    return jnp.concatenate((scores[:, :tail], recent), 1), query_place


def attend_kernel(turn, scale, where, slopes, q, k, v, place, mix, lse):
    slope = slopes[pl.program_id(0)] * LOG2E
    rows = q.shape[0]
    first = jnp.abs(turn - where[0]) * rows
    scores, _ = masked_scores(place, slope, q[...], k[...], scale, first, k.shape[0] - 2 * rows)
    highest = jnp.max(scores, -1, keepdims=True)
    weights = jnp.exp2(scores - highest)
    total = jnp.sum(weights, -1, keepdims=True)
    mix[...] = (dot(weights.astype(BF16), v[...]) * (1.0 / total)).astype(BF16)
    lse[0] = highest + jnp.log2(total)


def attend(where, turn, slopes, q, k, v, place):
    rows, width = q.shape[0] // 2, q.shape[1]
    heads = slopes.shape[0]
    hw = width // heads
    keys = k.shape[0]
    by_head = spec((keys, hw), lambda h, w: (0, h))
    return call(
        functools.partial(attend_kernel, turn, hw**-0.5),
        "attend",
        where,
        (heads,),
        [
            (slopes, pl.BlockSpec(memory_space=pltpu.SMEM)),
            (q, spec((rows, hw), lambda h, w: (turn, h))),
            (k, by_head),
            (v, by_head),
            whole(place),
        ],
        [
            ((rows, width), BF16, spec((rows, hw), lambda h, w: (0, h))),
            ((heads, rows, 1), F32, spec((1, rows, 1), lambda h, w: (h, 0, 0))),
        ],
        cost=LARGE,
    )


def attend_back_kernel(
    chunk,
    scale,
    height,
    where,
    slopes,
    q,
    k,
    v,
    dm,
    place,
    lse_own,
    lse_other,
    dq,
    dk,
    dv,
    all_keep,
    all_send,
    slope_out,
    dk_sum,
    dv_sum,
):
    slope = slopes[pl.program_id(0)] * LOG2E
    keys = k.shape[0]
    rows = q.shape[0]
    half = rows // 2
    columns = jnp.zeros((1, keys), F32)
    by_row = jnp.zeros((1, 1), F32)
    dq_parts = []
    for step in range(rows // chunk):
        at = slice(step * chunk, (step + 1) * chunk)
        time_half = where[0] if step * chunk < half else 1 - where[0]
        scores, query_place = masked_scores(
            place,
            slope,
            q[at, :],
            k[...],
            scale,
            time_half * half + step * chunk % half,
            keys - rows,
        )
        weights = jnp.exp2(scores - (lse_own if step == 0 else lse_other)[0])
        low = weights.astype(BF16)
        grads = dot_nt(dm[at, :], v[...])
        shift = jnp.sum(weights * grads, -1, keepdims=True)
        ds = (weights * (grads - shift)).astype(BF16)
        dq_part = dot(ds, k[...]) * scale
        dq[at, :] = dq_part.astype(BF16)
        dq_parts.append(dq_part.T)
        dk_part = dot_tn(q[at, :], ds)
        dv_part = dot_tn(dm[at, :], low)
        if step == 0:
            dk_sum[...] = dk_part
            dv_sum[...] = dv_part
        else:
            dk_sum[...] += dk_part
            dv_sum[...] += dv_part
        wide = ds.astype(F32)
        columns += jnp.sum(wide, 0, keepdims=True)
        by_row += jnp.sum(jnp.sum(wide, -1, keepdims=True) * query_place, 0, keepdims=True)
    dk_all, dv_all = dk_sum[...] * scale, dv_sum[...]
    dq_all = jnp.concatenate([jnp.zeros((dk_all.shape[0], keys - rows), F32)] + dq_parts, 1)
    halves = [by_parity(where, part, height) for part in (dq_all, dk_all, dv_all)]
    for target, parts in zip((all_keep, all_send), zip(*halves)):
        blocks = [part.reshape(part.shape[0] // height, height, keys) for part in parts]
        target[...] = jnp.stack(blocks, 1).reshape(target.shape).astype(BF16)
    dk[...] = dk_all.T.astype(BF16)
    dv[...] = dv_all.T.astype(BF16)
    total = jnp.sum(columns * place[0:1, :], -1, keepdims=True) - by_row
    slope_out[...] = jnp.broadcast_to(total.reshape(1, 1, 1), slope_out.shape)


def attend_back(where, height, slopes, q, k, v, dm, place, lses):
    rows, width = q.shape
    heads = slopes.shape[0]
    hw = width // heads
    keys = k.shape[0]
    by_rows = spec((rows, hw), lambda h, w: (0, h))
    by_keys = spec((keys, hw), lambda h, w: (0, h))
    return call(
        functools.partial(attend_back_kernel, rows // 2, hw**-0.5, height),
        "attend_back",
        where,
        (heads,),
        [
            (slopes, pl.BlockSpec(memory_space=pltpu.SMEM)),
            (q, by_rows),
            (k, by_keys),
            (v, by_keys),
            (dm, by_rows),
            whole(place),
            (lses[0], spec((1, rows // 2, 1), lambda h, w: (h, 0, 0))),
            (lses[1], spec((1, rows // 2, 1), lambda h, w: (h, 0, 0))),
        ],
        [
            ((rows, width), BF16, by_rows),
            ((keys, width), BF16, by_keys),
            ((keys, width), BF16, by_keys),
            ((3 * width // 2, keys), BF16, spec((3 * hw // 2, keys), lambda h, w: (h, 0))),
            ((3 * width // 2, keys), BF16, spec((3 * hw // 2, keys), lambda h, w: (h, 0))),
            ((heads, 8, 128), F32, spec((1, 8, 128), lambda h, w: (h, 0, 0))),
        ],
        [pltpu.VMEM((hw, keys), F32), pltpu.VMEM((hw, keys), F32)],
        cost=LARGE,
    )


def gelu_pair(v):
    c = 0.7978845608028654
    inner = c * (v + 0.044715 * v * v * v)
    th = jnp.tanh(inner)
    slope = 0.5 * (1.0 + th) + 0.5 * v * (1.0 - th * th) * c * (1.0 + 3 * 0.044715 * v * v)
    return 0.5 * v * (1.0 + th), slope


def feed_kernel(height, block, where, *refs):
    (
        mix,
        far,
        tok,
        wo,
        wo_mine,
        wo_got,
        gain,
        shift,
        dy,
        wi,
        wi_mine,
        wi_got,
        bias,
        wh,
        residual,
        normed,
        act,
        grad_keep,
        grad_send,
        dy_keep,
        dy_send,
        g2,
        bias_sum,
        dy_sum,
        *sent,
        wo_far,
        weight,
    ) = refs
    step = pl.program_id(0)
    half = wi.shape[0]

    @pl.when(step == 0)
    def _():
        place_pieces(where, (wo_mine, wo_got), wo_far)
        wide_dy = dy[...].astype(F32)
        dy_sum[...] = jnp.sum(wide_dy, 0, keepdims=True)
        dy_stay, dy_away = by_parity(where, wide_dy.T, height)
        dy_keep[...] = dy_stay.astype(BF16)
        dy_send[...] = dy_away.astype(BF16)
        total = tok[...].astype(F32) + (dot(mix[...], wo[...]) + dot(far[...], wo_far[...]))
        residual[...] = total
        unit, _ = rows_stats(total)
        normed[...] = (unit * gain[...] + shift[...]).astype(BF16)

    weight[pl.ds(pl.multiple_of(where[0] * half, half), half), :] = wi[...]
    place_pieces(where, (wi_mine, wi_got), weight, (1 - where[0]) * half, half)
    pre = dot(normed[...], weight[...]) + bias[...]
    value, slope = gelu_pair(pre)
    low = value.astype(BF16)
    act[...] = low
    grad = (dot_nt(dy[...], wh[...]) * slope).astype(BF16)
    blocks = [grad[:, at : at + block] for at in range(0, grad.shape[1], block)]
    evens, odds = jnp.concatenate(blocks[::2], 1), jnp.concatenate(blocks[1::2], 1)
    even = where[1] == 0
    grad_keep[...] = jnp.where(even, evens, odds)
    grad_send[...] = jnp.where(even, odds, evens)
    bias_sum[...] = jnp.sum(grad.astype(F32), 0, keepdims=True)
    g2_part = dot_nt(grad, weight[...])

    @pl.when(step == 0)
    def _():
        g2[...] = g2_part

    @pl.when(step > 0)
    def _():
        g2[...] += g2_part

    @pl.when(step == pl.num_programs(0) - 1)
    def _():
        first_row = 0
        for piece in sent:
            piece[...] = g2[first_row : first_row + piece.shape[0], :].astype(BF16)
            first_row += piece.shape[0]


def feed(
    where, dp, turn, mix, far, tok, wo, gain, shift, dy, wi, bias, wh, second, chunk, parts, onto
):
    rows, width = dy.shape
    hidden = wh.shape[0]
    steps = hidden // chunk
    mine, got = second
    by_cols = spec((rows, chunk), lambda j, w: (turn, j))
    by_half = spec((rows, chunk // 2), lambda j, w: (turn, j))
    half = (2 * rows, hidden // 2), BF16, by_half
    turned = (width // 2, 2 * rows), BF16, spec((width // 2, rows), lambda j, w: (0, turn))
    wo_part = spec((mine.shape[0], width), lambda j, w: (0, 0))
    wi_part = spec((mine.shape[0], chunk), lambda j, w: (0, width // chunk + j))

    def once(dtype):
        return (rows, width), dtype, spec((rows, width))

    return call(
        functools.partial(feed_kernel, width // dp, hidden // (dp // 2)),
        "feed",
        where,
        (steps,),
        [
            whole(mix),
            whole(far),
            (tok, spec((rows, width), lambda j, w: (2 * turn, 0))),
            whole(wo),
            (mine, wo_part),
            (got, wo_part),
            whole(gain[None]),
            whole(shift[None]),
            whole(dy),
            (wi, spec((wi.shape[0], chunk), lambda j, w: (0, w[0] * steps + j))),
            (mine, wi_part),
            (got, wi_part),
            (bias[None], spec((1, chunk), lambda j, w: (0, w[0] * steps + j))),
            (wh, spec((chunk, width), lambda j, w: (j, 0))),
        ],
        [
            once(F32),
            ((2 * rows, width), BF16, spec((rows, width), lambda j, w: (turn, 0))),
            ((2 * rows, hidden), BF16, by_cols),
            half,
            half,
            turned,
            turned,
            once(F32),
            ((1, hidden), F32, spec((1, chunk), lambda j, w: (0, j))),
            ((1, width), F32, spec((1, width))),
        ]
        + [((rows // part, width), BF16, spec((rows // part, width))) for part in parts],
        [
            pltpu.VMEM(wo.shape, BF16),
            pltpu.VMEM((width, chunk), BF16),
        ],
        cost=LARGE,
        onto=onto,
    )


def middle_kernel(
    where,
    g_own,
    g_other,
    got_own,
    got_other,
    residual_own,
    residual_other,
    gain,
    dy,
    dy_o,
    wo,
    mix_own,
    mix_other,
    bias_sum,
    bias_sum_o,
    dy_sum,
    dc_sum,
    grad_res,
    dm,
    sums,
    keep,
    send,
):
    rows = dy.shape[0]
    lows = []
    halves = ((g_own, got_own, dy, residual_own), (g_other, got_other, dy_o, residual_other))
    for at, (g, got, d, residual) in enumerate(halves):
        here = slice(at * rows, (at + 1) * rows)
        grad = g[...] + got[...].astype(F32)
        unit, rstd = rows_stats(residual[...])
        total = d[...].astype(F32) + norm_back(grad, gain[...], unit, rstd)
        low = total.astype(BF16)
        lows.append(low)
        dm[here, :] = dot_nt(low, wo[...]).astype(BF16)
        if at == 0:
            grad_res[...] = total
            small = [jnp.sum(grad * unit, 0, keepdims=True), jnp.sum(grad, 0, keepdims=True)]
    width = dy.shape[1]
    first = where[0] == 0
    parts = [slice(at, at + width) for at in range(0, bias_sum.shape[1], width)]
    downs = [bias_sum[:, part] + bias_sum_o[:, part] for part in parts]
    small += [jnp.where(first, down, 0.0) for down in downs]
    small += [jnp.where(first, 0.0, down) for down in downs]
    small += [dy_sum[...], dc_sum[...]]
    sums[...] = jnp.concatenate(small, 0)
    split_pairs(
        where, dot_tn(lows[0], mix_own[...]) + dot_tn(lows[1], mix_other[...]), keep.shape[1], keep, send
    )


def middle(where, dp, g, got, residuals, gain, dys, wo, mix, small):
    rows, width = dys[0].shape
    heads = wo.shape[0]
    half = ((dp // 2, width // dp, heads), BF16, spec((dp // 2, width // dp, heads)))
    return call(
        middle_kernel,
        "middle",
        where,
        (1,),
        [whole(a) for a in (*g, *got, *residuals, gain[None], *dys, wo, *mix, *small)],
        [
            ((rows, width), F32, spec((rows, width))),
            ((2 * rows, heads), BF16, spec((2 * rows, heads))),
            ((8, width), F32, spec((8, width))),
            half,
            half,
        ],
        cost=LARGE,
    )


def norm_sums(step, grad, x, sums):
    unit, _ = rows_stats(x)
    rows = jnp.sum(grad * unit, 0, keepdims=True), jnp.sum(grad, 0, keepdims=True)

    @pl.when(step == 0)
    def _():
        sums[0:1, :], sums[1:2, :] = rows

    @pl.when(step > 0)
    def _():
        sums[0:1, :] += rows[0]
        sums[1:2, :] += rows[1]


def tokens_kernel(where, tok, other, dq, dk, dv, weights, g_own, sent, sums):
    step = pl.program_id(0)
    cols = dq.shape[1]
    grad = (
        dot_nt(dq[...], weights[:, :cols])
        + dot_nt(dk[...], weights[:, cols : 2 * cols])
        + dot_nt(dv[...], weights[:, 2 * cols :])
    )
    x = jnp.where(step == 0, tok[...].astype(F32), other[...].astype(F32))
    norm_sums(step, grad, x, sums)

    @pl.when(step == 0)
    def _():
        g_own[...] = grad

    @pl.when(step == 1)
    def _():
        sent[...] = grad.astype(BF16)


def tokens_back(where, tok, other, dq, dk, dv, weights):
    rows, width = tok.shape
    cols = dk.shape[1]
    late = spec((rows, cols), lambda i, w: (4 + i, 0))
    return call(
        tokens_kernel,
        "tokens_back",
        where,
        (2,),
        [
            whole(tok),
            (other, spec((rows, width), lambda i, w: (2, 0))),
            (dq, spec((rows, cols), lambda i, w: (i, 0))),
            (dk, late),
            (dv, late),
            whole(weights),
        ],
        [
            ((rows, width), F32, spec((rows, width))),
            ((rows, width), BF16, spec((rows, width))),
            ((2, width), F32, spec((2, width))),
        ],
    )


def slots_kernel(
    where, comp, mem, other, dk, dv, weights, start, slope_parts, early, sums, total
):
    step = pl.program_id(0)
    cols = dk.shape[1]
    grad = dot_nt(dk[...], weights[:, cols : 2 * cols]) + dot_nt(dv[...], weights[:, 2 * cols :])
    own = jnp.where(step == 0, comp[...].astype(F32), mem[...].astype(F32))
    x = jnp.where(step % 2 == 0, own, other[...].astype(F32))
    norm_sums(step, grad, x, total)

    @pl.when(step == pl.num_programs(0) - 1)
    def _():
        width = comp.shape[1]
        lane = lax.broadcasted_iota(jnp.int32, (1, width), 1)
        own_heads = slope_parts.shape[0]
        slope = jnp.zeros((1, width), F32)
        for head in range(own_heads):
            here = lane == where[0] * own_heads + head
            slope += jnp.where(here, slope_parts[head, 0:1, 0:1], 0.0)
        sums[:8, :] = early[...]
        rest = (total[...] + start[...], slope, jnp.zeros((5, width), F32))
        sums[8:, :] = jnp.concatenate(rest, 0)


def slots_back(where, comp, mem, other, dk, dv, weights, start, slope_parts, early):
    rows, width = comp.shape
    cols = dk.shape[1]
    by_step = spec((rows, cols), lambda i, w: (i, 0))
    return call(
        slots_kernel,
        "slots_back",
        where,
        (4,),
        [
            whole(comp),
            whole(mem),
            (other, spec((rows, width), lambda i, w: (i // 2, 0))),
            (dk, by_step),
            (dv, by_step),
            whole(weights),
            whole(start),
            whole(slope_parts),
            whole(early),
        ],
        [((16, width), F32, spec((16, width)))],
        [pltpu.VMEM((2, width), F32)],
        cost=LARGE,
    )


def turn_kernel(source, target):
    target[...] = source[...].T


def turned(array):
    return pl.pallas_call(
        turn_kernel,
        out_shape=jax.ShapeDtypeStruct(array.shape[::-1], F32),
        compiler_params=PARAMS,
        cost_estimate=TINY,
        name="turn",
    )(array)


def local(
    tokens,
    memory,
    compressed,
    mask_start,
    norm1_gain,
    norm1_bias,
    query_weight,
    key_weight,
    value_weight,
    out_weight,
    slopes,
    norm2_gain,
    norm2_bias,
    in_weight,
    in_bias,
    hidden_weight,
    hidden_bias,
    compress_weight,
    compress_bias,
    grad_out,
    grad_compressed,
):
    tokens, memory, compressed = tokens[0], memory[0], compressed[0]
    grad_out, grad_compressed = grad_out[0], grad_compressed[0]
    rows, width = tokens.shape
    heads = slopes.shape[0]
    dp = lax.axis_size("dp")
    levels = dp.bit_length() - 1
    top = levels - 1
    d = lax.axis_index("dp")
    t = lax.axis_index("tm")
    segment = 2 * rows

    def swap(block):
        return lax.ppermute(block, "tm", [(0, 1), (1, 0)])

    def across(block, mask):
        return lax.ppermute(block, "dp", [(i, i ^ mask) for i in range(dp)])

    def after(array, *earlier):
        return lax.optimization_barrier((array,) + earlier)[0]

    def bit(level):
        return (d >> level) & 1

    class Shrink:
        def __init__(self, keep, send, order, columns=False):
            shape = keep.shape if keep.ndim == 4 else keep.shape[:1] + (1,) + keep.shape[1:]
            self.pending = keep.reshape(shape), send.reshape(shape), 1
            self.order = [0] + order
            self.left = [level for level in range(1, top if columns else levels)]
            self.step = 0
            self.array = None

        def cut(self):
            if self.pending is not None:
                return self.pending[1]
            if self.step == len(self.order):
                return self.array
            level = self.order[self.step]
            if level in self.left:
                low = 1 << self.left.index(level)
                blocks, rest = self.array.shape[0], self.array.shape[1:]
                split = self.array.reshape((blocks // (2 * low), 2, low) + rest)
                keep, send = [
                    lax.dynamic_index_in_dim(split, at, 1, keepdims=False).reshape(
                        (blocks // 2,) + rest
                    )
                    for at in (bit(level), 1 - bit(level))
                ]
                self.left.remove(level)
                self.pending = keep, send, 1 << level
            else:
                size = self.array.shape[3] // 2
                keep, send = [
                    lax.dynamic_slice_in_dim(self.array, at * size, size, 3) for at in (t, 1 - t)
                ]
                self.pending = keep, send, 0
            return send

        def move(self):
            send = self.cut()
            return across(send, self.pending[2]) if self.pending[2] else swap(send)

        def take(self, got):
            keep, _, mask = self.pending
            if mask == 0:
                same = bit(top) == t
                self.pending = jnp.where(same, keep, got), jnp.where(same, got, keep), 1 << top
                return self.pending[1]
            self.step += 1
            total = keep.astype(F32) + got.astype(F32)
            last = self.step == len(self.order)
            self.array = total if last else total.astype(BF16)
            self.pending = None
            return self.array

        def add(self):
            if self.step == len(self.order):
                return self.array
            self.cut()
            if self.pending[2] == 0:
                self.take(self.move())
            return self.take(self.move())

        def wait(self, *earlier):
            if self.pending is not None:
                self.pending = (after(self.pending[0], *earlier),) + self.pending[1:]

        def hold(self, *earlier):
            keep, send, mask = self.pending
            self.pending = keep, after(send, *earlier), mask

        def finish(self):
            while self.step < len(self.order):
                self.add()
            return self.array[0]

    def meet(groups, *others):
        groups = [group for group in groups if group.step < len(group.order)]
        got = lax.optimization_barrier(tuple(group.move() for group in groups) + others)
        for group, block in zip(groups, got):
            group.take(block)
        for group in groups:
            group.cut()
        return got[len(groups) :]

    sideways = list(range(1, levels))
    upward = list(range(2, levels)) + [1] if levels > 1 else []
    between = upward[:1] + upward[-1:] + upward[1:-1] if levels > 2 else upward

    sharing = min(levels, 4)
    share = 1 << sharing
    ups = [z << 2 for z in range(1 << max(sharing - 2, 0))]
    offsets = [x + z for x in ((0, 2) if sharing > 1 else (0,)) for z in ups]
    low_bits = d & (share - 1)
    targets = [low_bits ^ off for off in offsets] + [low_bits ^ off ^ 1 for off in offsets]
    where = jnp.stack([t, bit(0)] + targets).astype(jnp.int32)

    def gather_up(piece):
        return jnp.concatenate([piece] + [across(piece, z) for z in ups[1:]], 0)

    def gather_side(block):
        return jnp.concatenate((block, across(block, 2)), 0) if sharing > 1 else block

    (joined,) = pieces(
        jnp.stack((low_bits, 1 - t)).astype(jnp.int32),
        share,
        query_weight,
        key_weight,
        value_weight,
        out_weight,
        in_weight,
    )
    joined = swap(joined)
    first_size = 3 * query_weight.shape[1] // 2
    first, second = joined[:, :first_size], joined[:, first_size:]
    slots = grad_compressed.shape[0]
    dc = jnp.pad(grad_compressed, ((0, -slots % 16), (0, 0)))
    x_other = swap(jnp.concatenate((compressed, memory, tokens), 0))
    first = gather_side(gather_up(first))
    first_got = across(first, 1)
    second = gather_side(gather_up(after(second, first)))
    second_got = across(second, 1)
    dc_other, dy_other = swap(after(dc, x_other)), swap(after(grad_out, x_other))

    inputs_low, queries, keys, values, qkv = project(
        where,
        compressed,
        memory,
        tokens,
        x_other,
        norm1_gain,
        norm1_bias,
        query_weight,
        key_weight,
        value_weight,
        first,
        first_got,
    )

    index = jnp.arange(segment, dtype=jnp.int32)
    slot = jnp.where(index < rows, index + t * rows, index - rows + (1 - t) * rows)
    place = jnp.concatenate((-segment - 3 * (segment - slot), slot - segment, slot)).astype(F32)
    closed = jnp.where(slot >= mask_start[0], 0.0, NEG)
    closed = jnp.concatenate((closed, jnp.zeros((2 * segment,), F32)))
    place = jnp.stack((place, closed))
    own_heads = heads // 2
    slopes_own = lax.dynamic_slice_in_dim(slopes, t * own_heads, own_heads, 0)
    queries = after(queries, second)
    mix_other, lse_other = attend(where, 1, slopes_own, queries, keys, values, place)
    far_own = swap(mix_other)
    squeeze_stay, squeeze_away, keep, send, dc_sum = squeeze_rows(
        where, dp, slots, after(memory, mix_other), x_other, dc, dc_other, compress_weight
    )
    squeeze = Shrink(keep, send, sideways)
    squeeze_got = swap(squeeze_away)
    mix_own, lse_own = attend(
        where, 0, slopes_own, after(queries, squeeze_away), keys, values, place
    )
    far_other = swap(mix_own)
    dys = grad_out, dy_other
    mix = mix_own, mix_other
    chunk = max(in_weight.shape[1] // 8, 2 * in_weight.shape[1] // dp)

    def feed_rows(turn, mixed, far, tok, dy, parts, onto=None):
        return feed(
            where,
            dp,
            turn,
            mixed,
            far,
            tok,
            out_weight,
            norm2_gain,
            norm2_bias,
            dy,
            in_weight,
            in_bias,
            hidden_weight,
            (second, second_got),
            chunk,
            parts,
            onto,
        )

    squeeze.add()
    residual, *half_filled, g_own, bias_sum, dy_sum, sent = feed_rows(
        0, after(mix_own, squeeze.cut()), far_own, tokens, grad_out, (1,)
    )
    got_other = swap(sent)
    residual_o, *filled, g_other, bias_sum_o, _, sent = feed_rows(
        1,
        after(mix_other, sent, squeeze_got),
        far_other,
        x_other,
        dy_other,
        (1,),
        {1 + i: array for i, array in enumerate(half_filled)},
    )
    got = swap(sent), got_other
    normed, act, grad_keep, grad_send, dy_keep, dy_send = filled
    blocks = dp // 2

    def cut_rows(product, count):
        return product.astype(BF16).reshape(count, product.shape[0] // count, product.shape[1])

    hidden_send = dot(after(dy_send, got_other), act).astype(BF16)
    entry_send = dot_tn(after(grad_send, hidden_send), normed).astype(BF16)
    hidden_keep = dot(after(dy_keep, entry_send), act).astype(BF16)
    entry_keep = dot_tn(after(grad_keep, hidden_keep), normed).astype(BF16)
    hidden = Shrink(cut_rows(hidden_keep, blocks), cut_rows(hidden_send, blocks), sideways)
    entry = Shrink(
        cut_rows(entry_keep, blocks // 2), cut_rows(entry_send, blocks // 2), between, True
    )
    got = after(got[0], entry_keep), got[1]
    grad_residual, grad_mixture, early, keep, send = middle(
        where,
        dp,
        (after(g_own, entry_keep), g_other),
        got,
        (residual, residual_o),
        norm2_gain,
        dys,
        out_weight,
        mix,
        (bias_sum, bias_sum_o, dy_sum, dc_sum),
    )
    mix_out = Shrink(keep, send, sideways)
    hidden.add()
    entry.add()
    height = key_weight.shape[1] // dp
    dq, dk, dv, all_keep, all_send, slope_parts = attend_back(
        where,
        height,
        slopes_own,
        queries,
        keys,
        values,
        after(grad_mixture, hidden.cut(), entry.cut()),
        place,
        (lse_own, lse_other),
    )
    mix_out.wait(dq)

    def cut_heads(product):
        return product.reshape(blocks // 2, -1, height, width)

    all_send = dot(all_send, inputs_low).astype(BF16)
    all_keep = dot(after(all_keep, all_send), inputs_low).astype(BF16)
    hidden.add()
    entry.add()
    left = Shrink(cut_heads(all_keep), cut_heads(all_send), sideways, True)
    mix_out.add()
    left.add()
    mix_out.cut()
    mix_out.wait(left.cut())
    mix_out.add()
    squeeze.wait(left.cut())
    squeeze.add()
    g1_own, g1_sent, token_sums = tokens_back(
        where,
        tokens,
        x_other,
        after(dq, left.cut(), hidden.cut(), entry.array, mix_out.cut(), squeeze.cut()),
        dk,
        dv,
        qkv,
    )
    g1_got = swap(g1_sent)
    entry.cut()
    entry.hold(g1_sent)
    mix_out.wait(g1_sent)
    mix_out.add()
    (smalls,) = slots_back(
        where,
        compressed,
        memory,
        x_other,
        after(dk, mix_out.cut(), entry.cut()),
        dv,
        qkv,
        token_sums,
        slope_parts,
        early,
    )

    def joint(array, mask):
        return lax.ppermute(array, ("dp", "tm"), [(i, i ^ mask) for i in range(2 * dp)])

    hidden.wait(smalls)
    hidden.add()
    out_part = dot(after(act, smalls, hidden.cut()), hidden_weight)
    out_own, out_sent = out_part[:rows], out_part[rows:].astype(BF16)
    smalls, g1_got, out_sent = meet((left, mix_out, squeeze), smalls, g1_got, out_sent)
    out_got = swap(out_sent)
    groups = (left, hidden, entry, mix_out, squeeze)
    masks = [1 << at for at in range(levels + 1)]
    while masks:
        sends = [group.cut() for group in groups]
        smalls = after(smalls, *sends)
        if len(masks) > 1 and len(masks) % 2:
            smalls = smalls + joint(smalls, masks.pop(0))
        smalls, got = meet(groups, smalls, joint(smalls, masks.pop(0)))
        smalls = smalls + got
    output = (residual + (out_own + out_got.astype(F32)) + hidden_bias).astype(BF16)
    new_compressed = (
        after(squeeze_stay, sends[0])[:slots] + squeeze_got[:slots].astype(F32) + compress_bias
    ).astype(BF16)
    g1 = g1_own + g1_got.astype(F32)
    unit1, rstd1 = rows_stats(tokens.astype(F32))
    grad_tokens = (grad_residual + norm_back(g1, norm1_gain, unit1, rstd1)).astype(BF16)

    grad_query_w, grad_key_w, grad_value_w = [part.T for part in left.finish()]
    grad_in_w = turned(entry.finish()[0])
    grad_hidden_w, grad_out_w, grad_compress_w = [
        group.finish()[0].T for group in (hidden, mix_out, squeeze)
    ]
    gain2, bias2, hidden_b, compress_b, gain1, bias1, slope = [
        smalls[i] for i in (0, 1, 6, 7, 8, 9, 10)
    ]
    in_b = smalls[2:6].reshape(-1)
    return (
        output[None],
        new_compressed[None],
        grad_tokens[None],
        gain1,
        bias1,
        grad_query_w,
        grad_key_w,
        grad_value_w,
        grad_out_w,
        slope[:heads],
        gain2,
        bias2,
        grad_in_w,
        in_b,
        grad_hidden_w,
        hidden_b,
        grad_compress_w,
        compress_b,
    )


def solution(mesh):
    split, whole, kept = P("dp", "tm", None), P(), P("tm", None)
    in_specs = (
        (split,) * 3
        + (P("dp"), whole, whole)
        + (kept,) * 4
        + (whole,) * 3
        + (kept, whole, kept, whole, kept, whole)
        + (split,) * 2
    )
    shared = P("tm", "dp")
    out_specs = (
        (split,) * 3
        + (whole,) * 2
        + (shared,) * 4
        + (whole,) * 3
        + (shared, whole, shared, whole, shared, whole)
    )
    return jax.shard_map(local, mesh=mesh, in_specs=in_specs, out_specs=out_specs, check_vma=False)
```

```python
import functools

import jax
import jax.numpy as jnp
from jax import lax
from jax.experimental import pallas as pl
from jax.experimental.pallas import tpu as pltpu
from jax.sharding import PartitionSpec as P

EPS = 1e-05
NEG = -1e30
LOG2E = 1.4426950408889634
F32 = jnp.float32
BF16 = jnp.bfloat16
TINY = pl.CostEstimate(flops=1000, bytes_accessed=1000, transcendentals=0)
LARGE = pl.CostEstimate(flops=20 * 10**9, bytes_accessed=10**6, transcendentals=0)
PARAMS = pltpu.CompilerParams(vmem_limit_bytes=52 * 2**20)


def dot(a, b, dims=((1,), (0,))):
    return lax.dot_general(a, b, (dims, ((), ())), preferred_element_type=F32)


def dot_nt(a, b):
    return dot(a, b, ((1,), (1,)))


def dot_tn(a, b):
    return dot(a, b, ((0,), (0,)))


def rows_stats(x):
    mean = jnp.mean(x, -1, keepdims=True)
    centered = x - mean
    rstd = lax.rsqrt(jnp.mean(centered * centered, -1, keepdims=True) + EPS)
    return centered * rstd, rstd


def norm_back(grad, gain, normed, rstd):
    dn = grad * gain
    return rstd * (
        dn
        - jnp.mean(dn, -1, keepdims=True)
        - normed * jnp.mean(dn * normed, -1, keepdims=True)
    )


def spec(shape, at=None):
    zeros = (0,) * len(shape)
    return pl.BlockSpec(shape, at if at is not None else (lambda *_: zeros))


def call(kernel, name, where, grid, ins, outs, scratch=(), cost=TINY, onto=None):
    onto = onto or {}
    count = len(ins)
    ins = list(ins) + [(array, pl.BlockSpec(memory_space=pl.ANY)) for array in onto.values()]

    def body(place, *refs):
        kernel(place, *refs[:count], *refs[len(ins) :])

    return pl.pallas_call(
        body,
        grid_spec=pltpu.PrefetchScalarGridSpec(
            num_scalar_prefetch=1,
            grid=grid,
            in_specs=[at for _, at in ins],
            out_specs=[at for _, _, at in outs],
            scratch_shapes=list(scratch),
        ),
        out_shape=[jax.ShapeDtypeStruct(shape, dtype) for shape, dtype, _ in outs],
        input_output_aliases={1 + count + i: out for i, out in enumerate(onto)},
        compiler_params=PARAMS,
        cost_estimate=cost,
        name=name,
    )(where, *[array for array, _ in ins])


def whole(array):
    return array, spec(array.shape)


def ordered(first, own, other, axis):
    return jnp.where(
        first, jnp.concatenate((own, other), axis), jnp.concatenate((other, own), axis)
    )


def place_pieces(where, parts, target, base=0, half=None):
    size = (half or target.shape[0]) // (where.shape[0] - 2)
    at = 0
    for part in parts:
        for block in range(part.shape[0] // size):
            row = pl.multiple_of(base + where[2 + at] * size, size)
            target[pl.ds(row, size), :] = part[block * size : (block + 1) * size, :]
            at += 1


def pieces_kernel(where, wq, wk, wv, wo, wi, joined):
    size = wq.shape[1]
    first, second = joined.at[:, : 3 * size], joined.at[:, 3 * size :]
    first[:, :size] = wq[...]
    first[:, size : 2 * size] = wk[...]
    first[:, 2 * size :] = wv[...]
    second[:, : wo.shape[1]] = wo[...]
    second[:, wo.shape[1] :] = wi[...]


def pieces(where, share, wq, wk, wv, wo, wi):
    rows = wq.shape[0] // share
    cols = wq.shape[1] // 2
    wide = wi.shape[1] // 2
    half = spec((rows, cols), lambda i, w: (w[0], w[1]))
    return call(
        pieces_kernel,
        "pieces",
        where,
        (1,),
        [
            (wq, half),
            (wk, half),
            (wv, half),
            (wo, spec((rows, wo.shape[1]), lambda i, w: (w[0], 0))),
            (wi, spec((rows, wide), lambda i, w: (w[0], w[1]))),
        ],
        [
            (
                (rows, 3 * cols + wo.shape[1] + wide),
                BF16,
                spec((rows, 3 * cols + wo.shape[1] + wide)),
            )
        ],
    )


def project_rows(x, gain, shift, weights, low, q, k, v):
    cols = k.shape[1]
    unit, _ = rows_stats(x)
    n = (unit * gain[...] + shift[...]).astype(BF16)
    low[...] = n
    k[...] = dot(n, weights[:, cols : 2 * cols]).astype(BF16)
    v[...] = dot(n, weights[:, 2 * cols :]).astype(BF16)

    @pl.when(pl.program_id(0) == 2)
    def _():
        q[...] = dot(n, weights[:, :cols]).astype(BF16)


def project_own_kernel(
    where, comp, mem, tok, gain, shift, wq, wk, wv, mine, got, low, q, k, v, weights, x
):
    step = pl.program_id(0)
    half, cols = wq.shape
    for at, source in enumerate((comp, mem, tok)):

        @pl.when(step == at)
        def _(source=source):
            x[...] = source[...].astype(F32)

    @pl.when(step == 0)
    def _():
        own = pl.ds(pl.multiple_of(where[0] * half, half), half)
        for index, weight in enumerate((wq, wk, wv)):
            weights[own, index * cols : (index + 1) * cols] = weight[...]
        place_pieces(where, (mine, got), weights, (1 - where[0]) * half, half)

    project_rows(x[...], gain, shift, weights, low, q, k, v)


def project_other_kernel(where, other, gain, shift, weights, low, q, k, v):
    project_rows(other[...].astype(F32), gain, shift, weights, low, q, k, v)


def project_outs(rows, width, cols, turn):
    def by_step(size):
        return (6 * rows, size), BF16, spec((rows, size), lambda i, w: (2 * i + turn, 0))

    query = (2 * rows, cols), BF16, spec((rows, cols), lambda i, w: (turn, 0))
    return [by_step(width), query, by_step(cols), by_step(cols)]


def project_own(where, comp, mem, tok, gain, shift, wq, wk, wv, mine, got):
    rows, width = tok.shape
    cols = wq.shape[1] // 2
    half = spec((wq.shape[0], cols), lambda i, w: (0, w[0]))
    return call(
        project_own_kernel,
        "project_own",
        where,
        (3,),
        [whole(a) for a in (comp, mem, tok, gain[None], shift[None])]
        + [(wq, half), (wk, half), (wv, half), whole(mine), whole(got)],
        project_outs(rows, width, cols, 0)
        + [((width, 3 * cols), BF16, spec((width, 3 * cols)))],
        [pltpu.VMEM((rows, width), F32)],
        cost=LARGE,
    )


def project_other(where, other, gain, shift, weights, filled):
    rows, width = other.shape[0] // 3, other.shape[1]
    return call(
        project_other_kernel,
        "project_other",
        where,
        (3,),
        [(other, spec((rows, width), lambda i, w: (i, 0)))]
        + [whole(a) for a in (gain[None], shift[None], weights)],
        project_outs(rows, width, weights.shape[1] // 3, 1),
        cost=LARGE,
        onto=dict(enumerate(filled)),
    )


def split_pairs(where, total, height, keep, send):
    pairs = total.reshape(total.shape[0] // (2 * height), 2, height, total.shape[1])
    even = where[1] == 0
    keep[...] = jnp.where(even, pairs[:, 0], pairs[:, 1]).astype(BF16)
    send[...] = jnp.where(even, pairs[:, 1], pairs[:, 0]).astype(BF16)


def by_parity(where, total, height):
    pairs = total.reshape(total.shape[0] // (2 * height), 2, height, total.shape[1])
    even = where[1] == 0
    shape = (total.shape[0] // 2, total.shape[1])
    keep = jnp.where(even, pairs[:, 0], pairs[:, 1]).reshape(shape)
    return keep, jnp.where(even, pairs[:, 1], pairs[:, 0]).reshape(shape)


def squeeze_kernel(slots, where, mem, other, dc, dc_o, weight, stay, away, keep, send, dc_sum):
    t = where[0]
    dc_sum[...] = jnp.sum(dc[...].astype(F32), 0, keepdims=True)
    rows, width = mem.shape
    mem_o = other.at[rows : 2 * rows, :]
    padded = dc.shape[0]
    half = width // 2
    lead = 3 * 2 * slots - 2 * rows
    first = t == 0
    shape = (padded, rows)
    slot = lax.broadcasted_iota(jnp.int32, shape, 0)
    row = lax.broadcasted_iota(jnp.int32, shape, 1)
    mem_half = jnp.where(first, mem[:, :half], mem[:, half:])
    mem_o_half = jnp.where(first, mem_o[:, :half], mem_o[:, half:])

    def picked(slot_half, row_half, offset):
        place = 3 * (slot + slot_half * slots) + offset - lead
        hit = (place == row + row_half * rows) & (slot < slots)
        return jnp.where(hit, 1.0, 0.0).astype(BF16)

    def windows(slot_half):
        edge = dot(picked(slot_half, t, 2 * t), mem[...]) + dot(
            picked(slot_half, 1 - t, 2 * t), mem_o[...]
        )
        middle = dot(picked(slot_half, t, 1), mem_half) + dot(
            picked(slot_half, 1 - t, 1), mem_o_half
        )
        return ordered(first, edge, middle, 1).astype(BF16)

    both = jnp.concatenate((windows(t), windows(1 - t)), 0)
    slots_out = dot(both, weight[...])
    stay[...] = slots_out[:padded, :]
    away[...] = slots_out[padded:, :].astype(BF16)
    turned_dc = jnp.concatenate((dc[...], dc_o[...]), 0).T
    columns = both.shape[1]
    height = keep.shape[1]
    for at in range(0, columns, half):
        part = slice(at, at + half)
        total = dot(turned_dc, both[:, part])
        split_pairs(where, total, height, keep.at[:, :, part], send.at[:, :, part])


def squeeze_rows(where, dp, slots, mem, other, dc, dc_o, weight):
    padded, width = dc.shape
    half = ((dp // 2, width // dp, weight.shape[0]), BF16)
    ins = [whole(a) for a in (mem, other, dc, dc_o, weight)]
    return call(
        functools.partial(squeeze_kernel, slots),
        "squeeze",
        where,
        (1,),
        ins,
        [
            ((padded, width), F32, spec((padded, width))),
            ((padded, width), BF16, spec((padded, width))),
            half + (spec(half[0]),),
            half + (spec(half[0]),),
            ((1, width), F32, spec((1, width))),
        ],
    )


def masked_scores(place, slope, q, keys, scale, first, tail):
    bias = place[0:1, :] * slope + place[1:2, :]
    chunk = q.shape[0]
    query_place = (lax.broadcasted_iota(jnp.int32, (chunk, 1), 0) + first).astype(F32)
    scores = dot_nt(q, keys) * (scale * LOG2E) + bias
    recent = jnp.where(place[0:1, tail:] <= query_place, scores[:, tail:], NEG)
    return jnp.concatenate((scores[:, :tail], recent), 1), query_place


def attend_kernel(turn, scale, where, slopes, q, k, v, place, mix, lse):
    slope = slopes[pl.program_id(0)] * LOG2E
    rows = q.shape[0]
    first = jnp.abs(turn - where[0]) * rows
    scores, _ = masked_scores(place, slope, q[...], k[...], scale, first, k.shape[0] - 2 * rows)
    highest = jnp.max(scores, -1, keepdims=True)
    weights = jnp.exp2(scores - highest)
    total = jnp.sum(weights, -1, keepdims=True)
    mix[...] = (dot(weights.astype(BF16), v[...]) * (1.0 / total)).astype(BF16)
    lse[0] = highest + jnp.log2(total)


def attend(where, turn, slopes, q, k, v, place):
    rows, width = q.shape[0] // 2, q.shape[1]
    heads = slopes.shape[0]
    hw = width // heads
    keys = k.shape[0]
    by_head = spec((keys, hw), lambda h, w: (0, h))
    return call(
        functools.partial(attend_kernel, turn, hw**-0.5),
        "attend",
        where,
        (heads,),
        [
            (slopes, pl.BlockSpec(memory_space=pltpu.SMEM)),
            (q, spec((rows, hw), lambda h, w: (turn, h))),
            (k, by_head),
            (v, by_head),
            whole(place),
        ],
        [
            ((rows, width), BF16, spec((rows, hw), lambda h, w: (0, h))),
            ((heads, rows, 1), F32, spec((1, rows, 1), lambda h, w: (h, 0, 0))),
        ],
        cost=LARGE,
    )


def attend_back_kernel(
    chunk,
    scale,
    height,
    where,
    slopes,
    q,
    k,
    v,
    dm,
    place,
    lse_own,
    lse_other,
    dq,
    dk,
    dv,
    all_keep,
    all_send,
    slope_out,
    dk_sum,
    dv_sum,
):
    slope = slopes[pl.program_id(0)] * LOG2E
    keys = k.shape[0]
    rows = q.shape[0]
    half = rows // 2
    columns = jnp.zeros((1, keys), F32)
    by_row = jnp.zeros((1, 1), F32)
    dq_parts = []
    for step in range(rows // chunk):
        at = slice(step * chunk, (step + 1) * chunk)
        time_half = where[0] if step * chunk < half else 1 - where[0]
        scores, query_place = masked_scores(
            place,
            slope,
            q[at, :],
            k[...],
            scale,
            time_half * half + step * chunk % half,
            keys - rows,
        )
        weights = jnp.exp2(scores - (lse_own if step == 0 else lse_other)[0])
        low = weights.astype(BF16)
        grads = dot_nt(dm[at, :], v[...])
        shift = jnp.sum(weights * grads, -1, keepdims=True)
        ds = (weights * (grads - shift)).astype(BF16)
        dq_part = dot(ds, k[...]) * scale
        dq[at, :] = dq_part.astype(BF16)
        dq_parts.append(dq_part.T)
        dk_part = dot_tn(q[at, :], ds)
        dv_part = dot_tn(dm[at, :], low)
        if step == 0:
            dk_sum[...] = dk_part
            dv_sum[...] = dv_part
        else:
            dk_sum[...] += dk_part
            dv_sum[...] += dv_part
        wide = ds.astype(F32)
        columns += jnp.sum(wide, 0, keepdims=True)
        by_row += jnp.sum(jnp.sum(wide, -1, keepdims=True) * query_place, 0, keepdims=True)
    dk_all, dv_all = dk_sum[...] * scale, dv_sum[...]
    dq_all = jnp.concatenate([jnp.zeros((dk_all.shape[0], keys - rows), F32)] + dq_parts, 1)
    halves = [by_parity(where, part, height) for part in (dq_all, dk_all, dv_all)]
    for target, parts in zip((all_keep, all_send), zip(*halves)):
        blocks = [part.reshape(part.shape[0] // height, height, keys) for part in parts]
        target[...] = jnp.stack(blocks, 1).reshape(target.shape).astype(BF16)
    dk[...] = dk_all.T.astype(BF16)
    dv[...] = dv_all.T.astype(BF16)
    total = jnp.sum(columns * place[0:1, :], -1, keepdims=True) - by_row
    slope_out[...] = jnp.broadcast_to(total.reshape(1, 1, 1), slope_out.shape)


def attend_back(where, height, slopes, q, k, v, dm, place, lses):
    rows, width = q.shape
    heads = slopes.shape[0]
    hw = width // heads
    keys = k.shape[0]
    by_rows = spec((rows, hw), lambda h, w: (0, h))
    by_keys = spec((keys, hw), lambda h, w: (0, h))
    return call(
        functools.partial(attend_back_kernel, rows // 2, hw**-0.5, height),
        "attend_back",
        where,
        (heads,),
        [
            (slopes, pl.BlockSpec(memory_space=pltpu.SMEM)),
            (q, by_rows),
            (k, by_keys),
            (v, by_keys),
            (dm, by_rows),
            whole(place),
            (lses[0], spec((1, rows // 2, 1), lambda h, w: (h, 0, 0))),
            (lses[1], spec((1, rows // 2, 1), lambda h, w: (h, 0, 0))),
        ],
        [
            ((rows, width), BF16, by_rows),
            ((keys, width), BF16, by_keys),
            ((keys, width), BF16, by_keys),
            ((3 * width // 2, keys), BF16, spec((3 * hw // 2, keys), lambda h, w: (h, 0))),
            ((3 * width // 2, keys), BF16, spec((3 * hw // 2, keys), lambda h, w: (h, 0))),
            ((heads, 8, 128), F32, spec((1, 8, 128), lambda h, w: (h, 0, 0))),
        ],
        [pltpu.VMEM((hw, keys), F32), pltpu.VMEM((hw, keys), F32)],
        cost=LARGE,
    )


def gelu_pair(v):
    c = 0.7978845608028654
    inner = c * (v + 0.044715 * v * v * v)
    th = jnp.tanh(inner)
    slope = 0.5 * (1.0 + th) + 0.5 * v * (1.0 - th * th) * c * (1.0 + 3 * 0.044715 * v * v)
    return 0.5 * v * (1.0 + th), slope


def feed_kernel(height, block, where, *refs):
    (
        mix,
        far,
        tok,
        wo,
        wo_mine,
        wo_got,
        gain,
        shift,
        dy,
        wi,
        wi_mine,
        wi_got,
        bias,
        wh,
        residual,
        normed,
        act,
        grad_keep,
        grad_send,
        dy_keep,
        dy_send,
        g2,
        bias_sum,
        dy_sum,
        *sent,
        wo_far,
        weight,
    ) = refs
    step = pl.program_id(0)
    half = wi.shape[0]

    @pl.when(step == 0)
    def _():
        place_pieces(where, (wo_mine, wo_got), wo_far)
        wide_dy = dy[...].astype(F32)
        dy_sum[...] = jnp.sum(wide_dy, 0, keepdims=True)
        dy_stay, dy_away = by_parity(where, wide_dy.T, height)
        dy_keep[...] = dy_stay.astype(BF16)
        dy_send[...] = dy_away.astype(BF16)
        total = tok[...].astype(F32) + (dot(mix[...], wo[...]) + dot(far[...], wo_far[...]))
        residual[...] = total
        unit, _ = rows_stats(total)
        normed[...] = (unit * gain[...] + shift[...]).astype(BF16)

    weight[pl.ds(pl.multiple_of(where[0] * half, half), half), :] = wi[...]
    place_pieces(where, (wi_mine, wi_got), weight, (1 - where[0]) * half, half)
    pre = dot(normed[...], weight[...]) + bias[...]
    value, slope = gelu_pair(pre)
    low = value.astype(BF16)
    act[...] = low
    grad = (dot_nt(dy[...], wh[...]) * slope).astype(BF16)
    blocks = [grad[:, at : at + block] for at in range(0, grad.shape[1], block)]
    evens, odds = jnp.concatenate(blocks[::2], 1), jnp.concatenate(blocks[1::2], 1)
    even = where[1] == 0
    grad_keep[...] = jnp.where(even, evens, odds)
    grad_send[...] = jnp.where(even, odds, evens)
    bias_sum[...] = jnp.sum(grad.astype(F32), 0, keepdims=True)
    g2_part = dot_nt(grad, weight[...])

    @pl.when(step == 0)
    def _():
        g2[...] = g2_part

    @pl.when(step > 0)
    def _():
        g2[...] += g2_part

    @pl.when(step == pl.num_programs(0) - 1)
    def _():
        first_row = 0
        for piece in sent:
            piece[...] = g2[first_row : first_row + piece.shape[0], :].astype(BF16)
            first_row += piece.shape[0]


def feed(
    where, dp, turn, mix, far, tok, wo, gain, shift, dy, wi, bias, wh, second, chunk, parts, onto
):
    rows, width = dy.shape
    hidden = wh.shape[0]
    steps = hidden // chunk
    mine, got = second
    by_cols = spec((rows, chunk), lambda j, w: (turn, j))
    by_half = spec((rows, chunk // 2), lambda j, w: (turn, j))
    half = (2 * rows, hidden // 2), BF16, by_half
    turned = (width // 2, 2 * rows), BF16, spec((width // 2, rows), lambda j, w: (0, turn))
    wo_part = spec((mine.shape[0], width), lambda j, w: (0, 0))
    wi_part = spec((mine.shape[0], chunk), lambda j, w: (0, width // chunk + j))

    def once(dtype):
        return (rows, width), dtype, spec((rows, width))

    return call(
        functools.partial(feed_kernel, width // dp, hidden // (dp // 2)),
        "feed",
        where,
        (steps,),
        [
            whole(mix),
            whole(far),
            (tok, spec((rows, width), lambda j, w: (2 * turn, 0))),
            whole(wo),
            (mine, wo_part),
            (got, wo_part),
            whole(gain[None]),
            whole(shift[None]),
            whole(dy),
            (wi, spec((wi.shape[0], chunk), lambda j, w: (0, w[0] * steps + j))),
            (mine, wi_part),
            (got, wi_part),
            (bias[None], spec((1, chunk), lambda j, w: (0, w[0] * steps + j))),
            (wh, spec((chunk, width), lambda j, w: (j, 0))),
        ],
        [
            once(F32),
            ((2 * rows, width), BF16, spec((rows, width), lambda j, w: (turn, 0))),
            ((2 * rows, hidden), BF16, by_cols),
            half,
            half,
            turned,
            turned,
            once(F32),
            ((1, hidden), F32, spec((1, chunk), lambda j, w: (0, j))),
            ((1, width), F32, spec((1, width))),
        ]
        + [((rows // part, width), BF16, spec((rows // part, width))) for part in parts],
        [
            pltpu.VMEM(wo.shape, BF16),
            pltpu.VMEM((width, chunk), BF16),
        ],
        cost=LARGE,
        onto=onto,
    )


def middle_kernel(
    where,
    g_own,
    g_other,
    got_own,
    got_other,
    residual_own,
    residual_other,
    gain,
    dy,
    dy_o,
    wo,
    mix_own,
    mix_other,
    bias_sum,
    bias_sum_o,
    dy_sum,
    dc_sum,
    grad_res,
    dm,
    sums,
    keep,
    send,
):
    rows = dy.shape[0]
    lows = []
    halves = ((g_own, got_own, dy, residual_own), (g_other, got_other, dy_o, residual_other))
    for at, (g, got, d, residual) in enumerate(halves):
        here = slice(at * rows, (at + 1) * rows)
        grad = g[...] + got[...].astype(F32)
        unit, rstd = rows_stats(residual[...])
        total = d[...].astype(F32) + norm_back(grad, gain[...], unit, rstd)
        low = total.astype(BF16)
        lows.append(low)
        dm[here, :] = dot_nt(low, wo[...]).astype(BF16)
        if at == 0:
            grad_res[...] = total
            small = [jnp.sum(grad * unit, 0, keepdims=True), jnp.sum(grad, 0, keepdims=True)]
    width = dy.shape[1]
    first = where[0] == 0
    parts = [slice(at, at + width) for at in range(0, bias_sum.shape[1], width)]
    downs = [bias_sum[:, part] + bias_sum_o[:, part] for part in parts]
    small += [jnp.where(first, down, 0.0) for down in downs]
    small += [jnp.where(first, 0.0, down) for down in downs]
    small += [dy_sum[...], dc_sum[...]]
    sums[...] = jnp.concatenate(small, 0)
    split_pairs(
        where, dot_tn(lows[0], mix_own[...]) + dot_tn(lows[1], mix_other[...]), keep.shape[1], keep, send
    )


def middle(where, dp, g, got, residuals, gain, dys, wo, mix, small):
    rows, width = dys[0].shape
    heads = wo.shape[0]
    half = ((dp // 2, width // dp, heads), BF16, spec((dp // 2, width // dp, heads)))
    return call(
        middle_kernel,
        "middle",
        where,
        (1,),
        [whole(a) for a in (*g, *got, *residuals, gain[None], *dys, wo, *mix, *small)],
        [
            ((rows, width), F32, spec((rows, width))),
            ((2 * rows, heads), BF16, spec((2 * rows, heads))),
            ((8, width), F32, spec((8, width))),
            half,
            half,
        ],
        cost=LARGE,
    )


def norm_sums(step, grad, x, sums):
    unit, _ = rows_stats(x)
    rows = jnp.sum(grad * unit, 0, keepdims=True), jnp.sum(grad, 0, keepdims=True)

    @pl.when(step == 0)
    def _():
        sums[0:1, :], sums[1:2, :] = rows

    @pl.when(step > 0)
    def _():
        sums[0:1, :] += rows[0]
        sums[1:2, :] += rows[1]


def tokens_kernel(where, tok, other, dq, dk, dv, weights, g_own, sent, sums):
    step = pl.program_id(0)
    cols = dq.shape[1]
    grad = (
        dot_nt(dq[...], weights[:, :cols])
        + dot_nt(dk[...], weights[:, cols : 2 * cols])
        + dot_nt(dv[...], weights[:, 2 * cols :])
    )
    x = jnp.where(step == 0, tok[...].astype(F32), other[...].astype(F32))
    norm_sums(step, grad, x, sums)

    @pl.when(step == 0)
    def _():
        g_own[...] = grad

    @pl.when(step == 1)
    def _():
        sent[...] = grad.astype(BF16)


def tokens_back(where, tok, other, dq, dk, dv, weights):
    rows, width = tok.shape
    cols = dk.shape[1]
    late = spec((rows, cols), lambda i, w: (4 + i, 0))
    return call(
        tokens_kernel,
        "tokens_back",
        where,
        (2,),
        [
            whole(tok),
            (other, spec((rows, width), lambda i, w: (2, 0))),
            (dq, spec((rows, cols), lambda i, w: (i, 0))),
            (dk, late),
            (dv, late),
            whole(weights),
        ],
        [
            ((rows, width), F32, spec((rows, width))),
            ((rows, width), BF16, spec((rows, width))),
            ((2, width), F32, spec((2, width))),
        ],
    )


def slots_kernel(
    where, comp, mem, other, dk, dv, weights, start, slope_parts, early, sums, total
):
    step = pl.program_id(0)
    cols = dk.shape[1]
    grad = dot_nt(dk[...], weights[:, cols : 2 * cols]) + dot_nt(dv[...], weights[:, 2 * cols :])
    own = jnp.where(step == 0, comp[...].astype(F32), mem[...].astype(F32))
    x = jnp.where(step % 2 == 0, own, other[...].astype(F32))
    norm_sums(step, grad, x, total)

    @pl.when(step == pl.num_programs(0) - 1)
    def _():
        width = comp.shape[1]
        lane = lax.broadcasted_iota(jnp.int32, (1, width), 1)
        own_heads = slope_parts.shape[0]
        slope = jnp.zeros((1, width), F32)
        for head in range(own_heads):
            here = lane == where[0] * own_heads + head
            slope += jnp.where(here, slope_parts[head, 0:1, 0:1], 0.0)
        sums[:8, :] = early[...]
        rest = (total[...] + start[...], slope, jnp.zeros((5, width), F32))
        sums[8:, :] = jnp.concatenate(rest, 0)


def slots_back(where, comp, mem, other, dk, dv, weights, start, slope_parts, early):
    rows, width = comp.shape
    cols = dk.shape[1]
    by_step = spec((rows, cols), lambda i, w: (i, 0))
    return call(
        slots_kernel,
        "slots_back",
        where,
        (4,),
        [
            whole(comp),
            whole(mem),
            (other, spec((rows, width), lambda i, w: (i // 2, 0))),
            (dk, by_step),
            (dv, by_step),
            whole(weights),
            whole(start),
            whole(slope_parts),
            whole(early),
        ],
        [((16, width), F32, spec((16, width)))],
        [pltpu.VMEM((2, width), F32)],
        cost=LARGE,
    )


def turn_kernel(source, target):
    target[...] = source[...].T


def turned(array):
    return pl.pallas_call(
        turn_kernel,
        out_shape=jax.ShapeDtypeStruct(array.shape[::-1], F32),
        compiler_params=PARAMS,
        cost_estimate=TINY,
        name="turn",
    )(array)


def local(
    tokens,
    memory,
    compressed,
    mask_start,
    norm1_gain,
    norm1_bias,
    query_weight,
    key_weight,
    value_weight,
    out_weight,
    slopes,
    norm2_gain,
    norm2_bias,
    in_weight,
    in_bias,
    hidden_weight,
    hidden_bias,
    compress_weight,
    compress_bias,
    grad_out,
    grad_compressed,
):
    tokens, memory, compressed = tokens[0], memory[0], compressed[0]
    grad_out, grad_compressed = grad_out[0], grad_compressed[0]
    rows, width = tokens.shape
    heads = slopes.shape[0]
    dp = lax.axis_size("dp")
    levels = dp.bit_length() - 1
    top = levels - 1
    d = lax.axis_index("dp")
    t = lax.axis_index("tm")
    segment = 2 * rows

    def swap(block):
        return lax.ppermute(block, "tm", [(0, 1), (1, 0)])

    def across(block, mask):
        return lax.ppermute(block, "dp", [(i, i ^ mask) for i in range(dp)])

    def after(array, *earlier):
        return lax.optimization_barrier((array,) + earlier)[0]

    def bit(level):
        return (d >> level) & 1

    class Shrink:
        def __init__(self, keep, send, order, columns=False):
            shape = keep.shape if keep.ndim == 4 else keep.shape[:1] + (1,) + keep.shape[1:]
            self.pending = keep.reshape(shape), send.reshape(shape), 1
            self.order = [0] + order
            self.left = [level for level in range(1, top if columns else levels)]
            self.step = 0
            self.array = None

        def cut(self):
            if self.pending is not None:
                return self.pending[1]
            if self.step == len(self.order):
                return self.array
            level = self.order[self.step]
            if level in self.left:
                low = 1 << self.left.index(level)
                blocks, rest = self.array.shape[0], self.array.shape[1:]
                split = self.array.reshape((blocks // (2 * low), 2, low) + rest)
                keep, send = [
                    lax.dynamic_index_in_dim(split, at, 1, keepdims=False).reshape(
                        (blocks // 2,) + rest
                    )
                    for at in (bit(level), 1 - bit(level))
                ]
                self.left.remove(level)
                self.pending = keep, send, 1 << level
            else:
                size = self.array.shape[3] // 2
                keep, send = [
                    lax.dynamic_slice_in_dim(self.array, at * size, size, 3) for at in (t, 1 - t)
                ]
                self.pending = keep, send, 0
            return send

        def move(self):
            send = self.cut()
            return across(send, self.pending[2]) if self.pending[2] else swap(send)

        def take(self, got):
            keep, _, mask = self.pending
            if mask == 0:
                same = bit(top) == t
                self.pending = jnp.where(same, keep, got), jnp.where(same, got, keep), 1 << top
                return self.pending[1]
            self.step += 1
            total = keep.astype(F32) + got.astype(F32)
            last = self.step == len(self.order)
            self.array = total if last else total.astype(BF16)
            self.pending = None
            return self.array

        def add(self):
            if self.step == len(self.order):
                return self.array
            self.cut()
            if self.pending[2] == 0:
                self.take(self.move())
            return self.take(self.move())

        def wait(self, *earlier):
            if self.pending is not None:
                self.pending = (after(self.pending[0], *earlier),) + self.pending[1:]

        def finish(self):
            while self.step < len(self.order):
                self.add()
            return self.array[0]

    def meet(groups, *others):
        groups = [group for group in groups if group.step < len(group.order)]
        got = lax.optimization_barrier(tuple(group.move() for group in groups) + others)
        for group, block in zip(groups, got):
            group.take(block)
        for group in groups:
            group.cut()
        return got[len(groups) :]

    sideways = list(range(1, levels))
    upward = list(range(2, levels)) + [1] if levels > 1 else []
    between = upward[:1] + upward[-1:] + upward[1:-1] if levels > 2 else upward

    sharing = min(levels, 4)
    share = 1 << sharing
    ups = [z << 2 for z in range(1 << max(sharing - 2, 0))]
    offsets = [x + z for x in ((0, 2) if sharing > 1 else (0,)) for z in ups]
    low_bits = d & (share - 1)
    targets = [low_bits ^ off for off in offsets] + [low_bits ^ off ^ 1 for off in offsets]
    where = jnp.stack([t, bit(0)] + targets).astype(jnp.int32)

    def gather_up(piece):
        return jnp.concatenate([piece] + [across(piece, z) for z in ups[1:]], 0)

    def gather_side(block):
        return jnp.concatenate((block, across(block, 2)), 0) if sharing > 1 else block

    (joined,) = pieces(
        jnp.stack((low_bits, 1 - t)).astype(jnp.int32),
        share,
        query_weight,
        key_weight,
        value_weight,
        out_weight,
        in_weight,
    )
    joined = swap(joined)
    first_size = 3 * query_weight.shape[1] // 2
    first, second = joined[:, :first_size], joined[:, first_size:]
    slots = grad_compressed.shape[0]
    dc = jnp.pad(grad_compressed, ((0, -slots % 16), (0, 0)))
    x_other = swap(jnp.concatenate((compressed, memory, tokens), 0))
    first = gather_side(gather_up(first))
    first_got = across(first, 1)
    second_up = gather_up(after(second, first_got))
    second = gather_side(second_up)
    second_got = across(second, 1)

    *filled, qkv = project_own(
        where,
        compressed,
        memory,
        tokens,
        norm1_gain,
        norm1_bias,
        query_weight,
        key_weight,
        value_weight,
        first,
        first_got,
    )
    inputs_low, queries, keys, values = project_other(
        where, x_other, norm1_gain, norm1_bias, qkv, filled
    )
    dc_other = swap(after(dc, queries))

    index = jnp.arange(segment, dtype=jnp.int32)
    slot = jnp.where(index < rows, index + t * rows, index - rows + (1 - t) * rows)
    place = jnp.concatenate((-segment - 3 * (segment - slot), slot - segment, slot)).astype(F32)
    closed = jnp.where(slot >= mask_start[0], 0.0, NEG)
    closed = jnp.concatenate((closed, jnp.zeros((2 * segment,), F32)))
    place = jnp.stack((place, closed))
    own_heads = heads // 2
    slopes_own = lax.dynamic_slice_in_dim(slopes, t * own_heads, own_heads, 0)
    mix_other, lse_other = attend(
        where, 1, slopes_own, after(queries, second_up), keys, values, place
    )
    far_own = swap(mix_other)
    dy_other = swap(after(grad_out, mix_other))
    squeeze_stay, squeeze_away, keep, send, dc_sum = squeeze_rows(
        where, dp, slots, after(memory, mix_other), x_other, dc, dc_other, compress_weight
    )
    squeeze = Shrink(keep, send, sideways)
    squeeze_got = swap(squeeze_away)
    mix_own, lse_own = attend(
        where, 0, slopes_own, after(queries, squeeze_away), keys, values, place
    )
    far_other = swap(mix_own)
    dys = grad_out, dy_other
    mix = mix_own, mix_other
    chunk = max(in_weight.shape[1] // 8, 2 * in_weight.shape[1] // dp)

    def feed_rows(turn, mixed, far, tok, dy, parts, onto=None):
        return feed(
            where,
            dp,
            turn,
            mixed,
            far,
            tok,
            out_weight,
            norm2_gain,
            norm2_bias,
            dy,
            in_weight,
            in_bias,
            hidden_weight,
            (second, second_got),
            chunk,
            parts,
            onto,
        )

    squeeze.add()
    residual, *half_filled, g_own, bias_sum, dy_sum, sent = feed_rows(
        0, after(mix_own, squeeze.cut()), far_own, tokens, grad_out, (1,)
    )
    got_other = swap(sent)
    residual_o, *filled, g_other, bias_sum_o, _, sent = feed_rows(
        1,
        after(mix_other, sent, squeeze_got),
        far_other,
        x_other,
        dy_other,
        (1,),
        {1 + i: array for i, array in enumerate(half_filled)},
    )
    got = swap(sent), got_other
    normed, act, grad_keep, grad_send, dy_keep, dy_send = filled
    squeeze.wait(sent, got_other)
    squeeze.add()
    blocks = dp // 2

    def cut_rows(product, count):
        return product.astype(BF16).reshape(count, product.shape[0] // count, product.shape[1])

    hidden_send = dot(after(dy_send, squeeze.cut(), got_other), act).astype(BF16)
    entry_send = dot_tn(after(grad_send, hidden_send), normed).astype(BF16)
    hidden_keep = dot(after(dy_keep, entry_send), act).astype(BF16)
    entry_keep = dot_tn(after(grad_keep, hidden_keep), normed).astype(BF16)
    hidden = Shrink(cut_rows(hidden_keep, blocks), cut_rows(hidden_send, blocks), sideways)
    entry = Shrink(
        cut_rows(entry_keep, blocks // 2), cut_rows(entry_send, blocks // 2), between, True
    )
    got = after(got[0], entry_keep), got[1]
    grad_residual, grad_mixture, early, keep, send = middle(
        where,
        dp,
        (after(g_own, entry_keep), g_other),
        got,
        (residual, residual_o),
        norm2_gain,
        dys,
        out_weight,
        mix,
        (bias_sum, bias_sum_o, dy_sum, dc_sum),
    )
    mix_out = Shrink(keep, send, sideways)
    squeeze.add()
    hidden.add()
    entry.add()
    height = key_weight.shape[1] // dp
    dq, dk, dv, all_keep, all_send, slope_parts = attend_back(
        where,
        height,
        slopes_own,
        queries,
        keys,
        values,
        after(grad_mixture, hidden.cut(), entry.cut(), squeeze.array),
        place,
        (lse_own, lse_other),
    )
    mix_out.wait(dq)

    def cut_heads(product):
        return product.reshape(blocks // 2, -1, height, width)

    all_send = dot(all_send, inputs_low).astype(BF16)
    all_keep = dot(after(all_keep, all_send), inputs_low).astype(BF16)
    hidden.add()
    entry.add()
    left = Shrink(cut_heads(all_keep), cut_heads(all_send), sideways, True)
    mix_out.add()
    left.add()
    mix_out.cut()
    mix_out.wait(left.cut())
    mix_out.add()
    squeeze.add()
    g1_own, g1_sent, token_sums = tokens_back(
        where,
        tokens,
        x_other,
        after(dq, left.cut(), hidden.cut(), entry.cut(), mix_out.cut(), squeeze.array),
        dk,
        dv,
        qkv,
    )
    g1_got = swap(g1_sent)
    mix_out.wait(g1_sent)
    mix_out.add()
    (smalls,) = slots_back(
        where,
        compressed,
        memory,
        x_other,
        after(dk, mix_out.cut()),
        dv,
        qkv,
        token_sums,
        slope_parts,
        early,
    )

    def joint(array, mask):
        return lax.ppermute(array, ("dp", "tm"), [(i, i ^ mask) for i in range(2 * dp)])

    out_part = dot(after(act, smalls), hidden_weight)
    out_own, out_sent = out_part[:rows], out_part[rows:].astype(BF16)
    smalls, g1_got, out_sent = meet((left, hidden, entry, mix_out), smalls, g1_got, out_sent)
    out_got = swap(out_sent)
    groups = (left, hidden, entry, mix_out, squeeze)
    masks = [1 << at for at in range(levels + 1)]
    while masks:
        sends = [group.cut() for group in groups]
        smalls = after(smalls, *sends)
        if len(masks) > 1 and len(masks) % 2:
            smalls = smalls + joint(smalls, masks.pop(0))
        smalls, got = meet(groups, smalls, joint(smalls, masks.pop(0)))
        smalls = smalls + got
    output = (residual + (out_own + out_got.astype(F32)) + hidden_bias).astype(BF16)
    new_compressed = (
        after(squeeze_stay, sends[0])[:slots] + squeeze_got[:slots].astype(F32) + compress_bias
    ).astype(BF16)
    g1 = g1_own + g1_got.astype(F32)
    unit1, rstd1 = rows_stats(tokens.astype(F32))
    grad_tokens = (grad_residual + norm_back(g1, norm1_gain, unit1, rstd1)).astype(BF16)

    grad_query_w, grad_key_w, grad_value_w = [part.T for part in left.finish()]
    grad_in_w = turned(entry.finish()[0])
    grad_hidden_w, grad_out_w, grad_compress_w = [
        group.finish()[0].T for group in (hidden, mix_out, squeeze)
    ]
    gain2, bias2, hidden_b, compress_b, gain1, bias1, slope = [
        smalls[i] for i in (0, 1, 6, 7, 8, 9, 10)
    ]
    in_b = smalls[2:6].reshape(-1)
    return (
        output[None],
        new_compressed[None],
        grad_tokens[None],
        gain1,
        bias1,
        grad_query_w,
        grad_key_w,
        grad_value_w,
        grad_out_w,
        slope[:heads],
        gain2,
        bias2,
        grad_in_w,
        in_b,
        grad_hidden_w,
        hidden_b,
        grad_compress_w,
        compress_b,
    )


def solution(mesh):
    split, whole, kept = P("dp", "tm", None), P(), P("tm", None)
    in_specs = (
        (split,) * 3
        + (P("dp"), whole, whole)
        + (kept,) * 4
        + (whole,) * 3
        + (kept, whole, kept, whole, kept, whole)
        + (split,) * 2
    )
    shared = P("tm", "dp")
    out_specs = (
        (split,) * 3
        + (whole,) * 2
        + (shared,) * 4
        + (whole,) * 3
        + (shared, whole, shared, whole, shared, whole)
    )
    return jax.shard_map(local, mesh=mesh, in_specs=in_specs, out_specs=out_specs, check_vma=False)
```

```python
import functools

import jax
import jax.numpy as jnp
from jax import lax
from jax.experimental import pallas as pl
from jax.experimental.pallas import tpu as pltpu
from jax.sharding import PartitionSpec as P

EPS = 1e-05
NEG = -1e30
LOG2E = 1.4426950408889634
F32 = jnp.float32
BF16 = jnp.bfloat16
TINY = pl.CostEstimate(flops=1000, bytes_accessed=1000, transcendentals=0)
LARGE = pl.CostEstimate(flops=20 * 10**9, bytes_accessed=10**6, transcendentals=0)
PARAMS = pltpu.CompilerParams(vmem_limit_bytes=52 * 2**20)


def dot(a, b, dims=((1,), (0,))):
    return lax.dot_general(a, b, (dims, ((), ())), preferred_element_type=F32)


def dot_nt(a, b):
    return dot(a, b, ((1,), (1,)))


def dot_tn(a, b):
    return dot(a, b, ((0,), (0,)))


def rows_stats(x):
    mean = jnp.mean(x, -1, keepdims=True)
    centered = x - mean
    rstd = lax.rsqrt(jnp.mean(centered * centered, -1, keepdims=True) + EPS)
    return centered * rstd, rstd


def norm_back(grad, gain, normed, rstd):
    dn = grad * gain
    return rstd * (
        dn
        - jnp.mean(dn, -1, keepdims=True)
        - normed * jnp.mean(dn * normed, -1, keepdims=True)
    )


def spec(shape, at=None):
    zeros = (0,) * len(shape)
    return pl.BlockSpec(shape, at if at is not None else (lambda *_: zeros))


def call(kernel, name, where, grid, ins, outs, scratch=(), cost=TINY, onto=None):
    onto = onto or {}
    count = len(ins)
    ins = list(ins) + [(array, pl.BlockSpec(memory_space=pl.ANY)) for array in onto.values()]

    def body(place, *refs):
        kernel(place, *refs[:count], *refs[len(ins) :])

    return pl.pallas_call(
        body,
        grid_spec=pltpu.PrefetchScalarGridSpec(
            num_scalar_prefetch=1,
            grid=grid,
            in_specs=[at for _, at in ins],
            out_specs=[at for _, _, at in outs],
            scratch_shapes=list(scratch),
        ),
        out_shape=[jax.ShapeDtypeStruct(shape, dtype) for shape, dtype, _ in outs],
        input_output_aliases={1 + count + i: out for i, out in enumerate(onto)},
        compiler_params=PARAMS,
        cost_estimate=cost,
        name=name,
    )(where, *[array for array, _ in ins])


def whole(array):
    return array, spec(array.shape)


def ordered(first, own, other, axis):
    return jnp.where(
        first, jnp.concatenate((own, other), axis), jnp.concatenate((other, own), axis)
    )


def place_pieces(where, parts, target, base=0, half=None):
    size = (half or target.shape[0]) // (where.shape[0] - 2)
    at = 0
    for part in parts:
        for block in range(part.shape[0] // size):
            row = pl.multiple_of(base + where[2 + at] * size, size)
            target[pl.ds(row, size), :] = part[block * size : (block + 1) * size, :]
            at += 1


def pieces_kernel(where, wq, wk, wv, wo, wi, joined):
    size = wq.shape[1]
    first, second = joined.at[:, : 3 * size], joined.at[:, 3 * size :]
    first[:, :size] = wq[...]
    first[:, size : 2 * size] = wk[...]
    first[:, 2 * size :] = wv[...]
    second[:, : wo.shape[1]] = wo[...]
    second[:, wo.shape[1] :] = wi[...]


def pieces(where, share, wq, wk, wv, wo, wi):
    rows = wq.shape[0] // share
    cols = wq.shape[1] // 2
    wide = wi.shape[1] // 2
    half = spec((rows, cols), lambda i, w: (w[0], w[1]))
    return call(
        pieces_kernel,
        "pieces",
        where,
        (1,),
        [
            (wq, half),
            (wk, half),
            (wv, half),
            (wo, spec((rows, wo.shape[1]), lambda i, w: (w[0], 0))),
            (wi, spec((rows, wide), lambda i, w: (w[0], w[1]))),
        ],
        [
            (
                (rows, 3 * cols + wo.shape[1] + wide),
                BF16,
                spec((rows, 3 * cols + wo.shape[1] + wide)),
            )
        ],
    )


def project_rows(x, gain, shift, weights, low, q, k, v):
    cols = k.shape[1]
    unit, _ = rows_stats(x)
    n = (unit * gain[...] + shift[...]).astype(BF16)
    low[...] = n
    k[...] = dot(n, weights[:, cols : 2 * cols]).astype(BF16)
    v[...] = dot(n, weights[:, 2 * cols :]).astype(BF16)

    @pl.when(pl.program_id(0) == 2)
    def _():
        q[...] = dot(n, weights[:, :cols]).astype(BF16)


def project_own_kernel(
    where, comp, mem, tok, gain, shift, wq, wk, wv, mine, got, low, q, k, v, weights, x
):
    step = pl.program_id(0)
    half, cols = wq.shape
    for at, source in enumerate((comp, mem, tok)):

        @pl.when(step == at)
        def _(source=source):
            x[...] = source[...].astype(F32)

    @pl.when(step == 0)
    def _():
        own = pl.ds(pl.multiple_of(where[0] * half, half), half)
        for index, weight in enumerate((wq, wk, wv)):
            weights[own, index * cols : (index + 1) * cols] = weight[...]
        place_pieces(where, (mine, got), weights, (1 - where[0]) * half, half)

    project_rows(x[...], gain, shift, weights, low, q, k, v)


def project_other_kernel(where, other, gain, shift, weights, low, q, k, v):
    project_rows(other[...].astype(F32), gain, shift, weights, low, q, k, v)


def project_outs(rows, width, cols, turn):
    def by_step(size):
        return (6 * rows, size), BF16, spec((rows, size), lambda i, w: (2 * i + turn, 0))

    query = (2 * rows, cols), BF16, spec((rows, cols), lambda i, w: (turn, 0))
    return [by_step(width), query, by_step(cols), by_step(cols)]


def project_own(where, comp, mem, tok, gain, shift, wq, wk, wv, mine, got):
    rows, width = tok.shape
    cols = wq.shape[1] // 2
    half = spec((wq.shape[0], cols), lambda i, w: (0, w[0]))
    return call(
        project_own_kernel,
        "project_own",
        where,
        (3,),
        [whole(a) for a in (comp, mem, tok, gain[None], shift[None])]
        + [(wq, half), (wk, half), (wv, half), whole(mine), whole(got)],
        project_outs(rows, width, cols, 0)
        + [((width, 3 * cols), BF16, spec((width, 3 * cols)))],
        [pltpu.VMEM((rows, width), F32)],
        cost=LARGE,
    )


def project_other(where, other, gain, shift, weights, filled):
    rows, width = other.shape[0] // 3, other.shape[1]
    return call(
        project_other_kernel,
        "project_other",
        where,
        (3,),
        [(other, spec((rows, width), lambda i, w: (i, 0)))]
        + [whole(a) for a in (gain[None], shift[None], weights)],
        project_outs(rows, width, weights.shape[1] // 3, 1),
        cost=LARGE,
        onto=dict(enumerate(filled)),
    )


def split_pairs(where, total, height, keep, send):
    pairs = total.reshape(total.shape[0] // (2 * height), 2, height, total.shape[1])
    even = where[1] == 0
    keep[...] = jnp.where(even, pairs[:, 0], pairs[:, 1]).astype(BF16)
    send[...] = jnp.where(even, pairs[:, 1], pairs[:, 0]).astype(BF16)


def by_parity(where, total, height):
    pairs = total.reshape(total.shape[0] // (2 * height), 2, height, total.shape[1])
    even = where[1] == 0
    shape = (total.shape[0] // 2, total.shape[1])
    keep = jnp.where(even, pairs[:, 0], pairs[:, 1]).reshape(shape)
    return keep, jnp.where(even, pairs[:, 1], pairs[:, 0]).reshape(shape)


def squeeze_kernel(slots, where, mem, other, dc, dc_o, weight, stay, away, keep, send, dc_sum):
    t = where[0]
    dc_sum[...] = jnp.sum(dc[...].astype(F32), 0, keepdims=True)
    rows, width = mem.shape
    mem_o = other.at[rows : 2 * rows, :]
    padded = dc.shape[0]
    half = width // 2
    lead = 3 * 2 * slots - 2 * rows
    first = t == 0
    shape = (padded, rows)
    slot = lax.broadcasted_iota(jnp.int32, shape, 0)
    row = lax.broadcasted_iota(jnp.int32, shape, 1)
    mem_half = jnp.where(first, mem[:, :half], mem[:, half:])
    mem_o_half = jnp.where(first, mem_o[:, :half], mem_o[:, half:])

    def picked(slot_half, row_half, offset):
        place = 3 * (slot + slot_half * slots) + offset - lead
        hit = (place == row + row_half * rows) & (slot < slots)
        return jnp.where(hit, 1.0, 0.0).astype(BF16)

    def windows(slot_half):
        edge = dot(picked(slot_half, t, 2 * t), mem[...]) + dot(
            picked(slot_half, 1 - t, 2 * t), mem_o[...]
        )
        middle = dot(picked(slot_half, t, 1), mem_half) + dot(
            picked(slot_half, 1 - t, 1), mem_o_half
        )
        return ordered(first, edge, middle, 1).astype(BF16)

    both = jnp.concatenate((windows(t), windows(1 - t)), 0)
    slots_out = dot(both, weight[...])
    stay[...] = slots_out[:padded, :]
    away[...] = slots_out[padded:, :].astype(BF16)
    turned_dc = jnp.concatenate((dc[...], dc_o[...]), 0).T
    columns = both.shape[1]
    height = keep.shape[1]
    for at in range(0, columns, half):
        part = slice(at, at + half)
        total = dot(turned_dc, both[:, part])
        split_pairs(where, total, height, keep.at[:, :, part], send.at[:, :, part])


def squeeze_rows(where, dp, slots, mem, other, dc, dc_o, weight):
    padded, width = dc.shape
    half = ((dp // 2, width // dp, weight.shape[0]), BF16)
    ins = [whole(a) for a in (mem, other, dc, dc_o, weight)]
    return call(
        functools.partial(squeeze_kernel, slots),
        "squeeze",
        where,
        (1,),
        ins,
        [
            ((padded, width), F32, spec((padded, width))),
            ((padded, width), BF16, spec((padded, width))),
            half + (spec(half[0]),),
            half + (spec(half[0]),),
            ((1, width), F32, spec((1, width))),
        ],
    )


def masked_scores(place, slope, q, keys, scale, first, tail):
    bias = place[0:1, :] * slope + place[1:2, :]
    chunk = q.shape[0]
    query_place = (lax.broadcasted_iota(jnp.int32, (chunk, 1), 0) + first).astype(F32)
    scores = dot_nt(q, keys) * (scale * LOG2E) + bias
    recent = jnp.where(place[0:1, tail:] <= query_place, scores[:, tail:], NEG)
    return jnp.concatenate((scores[:, :tail], recent), 1), query_place


def attend_kernel(turn, scale, where, slopes, q, k, v, place, mix, lse):
    slope = slopes[pl.program_id(0)] * LOG2E
    rows = q.shape[0]
    first = jnp.abs(turn - where[0]) * rows
    scores, _ = masked_scores(place, slope, q[...], k[...], scale, first, k.shape[0] - 2 * rows)
    highest = jnp.max(scores, -1, keepdims=True)
    weights = jnp.exp2(scores - highest)
    total = jnp.sum(weights, -1, keepdims=True)
    mix[...] = (dot(weights.astype(BF16), v[...]) * (1.0 / total)).astype(BF16)
    lse[0] = highest + jnp.log2(total)


def attend(where, turn, slopes, q, k, v, place):
    rows, width = q.shape[0] // 2, q.shape[1]
    heads = slopes.shape[0]
    hw = width // heads
    keys = k.shape[0]
    by_head = spec((keys, hw), lambda h, w: (0, h))
    return call(
        functools.partial(attend_kernel, turn, hw**-0.5),
        "attend",
        where,
        (heads,),
        [
            (slopes, pl.BlockSpec(memory_space=pltpu.SMEM)),
            (q, spec((rows, hw), lambda h, w: (turn, h))),
            (k, by_head),
            (v, by_head),
            whole(place),
        ],
        [
            ((rows, width), BF16, spec((rows, hw), lambda h, w: (0, h))),
            ((heads, rows, 1), F32, spec((1, rows, 1), lambda h, w: (h, 0, 0))),
        ],
        cost=LARGE,
    )


def attend_back_kernel(
    chunk,
    scale,
    height,
    where,
    slopes,
    q,
    k,
    v,
    dm,
    place,
    lse_own,
    lse_other,
    dq,
    dk,
    dv,
    all_keep,
    all_send,
    slope_out,
    dk_sum,
    dv_sum,
):
    slope = slopes[pl.program_id(0)] * LOG2E
    keys = k.shape[0]
    rows = q.shape[0]
    half = rows // 2
    columns = jnp.zeros((1, keys), F32)
    by_row = jnp.zeros((1, 1), F32)
    dq_parts = []
    for step in range(rows // chunk):
        at = slice(step * chunk, (step + 1) * chunk)
        time_half = where[0] if step * chunk < half else 1 - where[0]
        scores, query_place = masked_scores(
            place,
            slope,
            q[at, :],
            k[...],
            scale,
            time_half * half + step * chunk % half,
            keys - rows,
        )
        weights = jnp.exp2(scores - (lse_own if step == 0 else lse_other)[0])
        low = weights.astype(BF16)
        grads = dot_nt(dm[at, :], v[...])
        shift = jnp.sum(weights * grads, -1, keepdims=True)
        ds = (weights * (grads - shift)).astype(BF16)
        dq_part = dot(ds, k[...]) * scale
        dq[at, :] = dq_part.astype(BF16)
        dq_parts.append(dq_part.T)
        dk_part = dot_tn(q[at, :], ds)
        dv_part = dot_tn(dm[at, :], low)
        if step == 0:
            dk_sum[...] = dk_part
            dv_sum[...] = dv_part
        else:
            dk_sum[...] += dk_part
            dv_sum[...] += dv_part
        wide = ds.astype(F32)
        columns += jnp.sum(wide, 0, keepdims=True)
        by_row += jnp.sum(jnp.sum(wide, -1, keepdims=True) * query_place, 0, keepdims=True)
    dk_all, dv_all = dk_sum[...] * scale, dv_sum[...]
    dq_all = jnp.concatenate([jnp.zeros((dk_all.shape[0], keys - rows), F32)] + dq_parts, 1)
    halves = [by_parity(where, part, height) for part in (dq_all, dk_all, dv_all)]
    for target, parts in zip((all_keep, all_send), zip(*halves)):
        blocks = [part.reshape(part.shape[0] // height, height, keys) for part in parts]
        target[...] = jnp.stack(blocks, 1).reshape(target.shape).astype(BF16)
    dk[...] = dk_all.T.astype(BF16)
    dv[...] = dv_all.T.astype(BF16)
    total = jnp.sum(columns * place[0:1, :], -1, keepdims=True) - by_row
    slope_out[...] = jnp.broadcast_to(total.reshape(1, 1, 1), slope_out.shape)


def attend_back(where, height, slopes, q, k, v, dm, place, lses):
    rows, width = q.shape
    heads = slopes.shape[0]
    hw = width // heads
    keys = k.shape[0]
    by_rows = spec((rows, hw), lambda h, w: (0, h))
    by_keys = spec((keys, hw), lambda h, w: (0, h))
    return call(
        functools.partial(attend_back_kernel, rows // 2, hw**-0.5, height),
        "attend_back",
        where,
        (heads,),
        [
            (slopes, pl.BlockSpec(memory_space=pltpu.SMEM)),
            (q, by_rows),
            (k, by_keys),
            (v, by_keys),
            (dm, by_rows),
            whole(place),
            (lses[0], spec((1, rows // 2, 1), lambda h, w: (h, 0, 0))),
            (lses[1], spec((1, rows // 2, 1), lambda h, w: (h, 0, 0))),
        ],
        [
            ((rows, width), BF16, by_rows),
            ((keys, width), BF16, by_keys),
            ((keys, width), BF16, by_keys),
            ((3 * width // 2, keys), BF16, spec((3 * hw // 2, keys), lambda h, w: (h, 0))),
            ((3 * width // 2, keys), BF16, spec((3 * hw // 2, keys), lambda h, w: (h, 0))),
            ((heads, 8, 128), F32, spec((1, 8, 128), lambda h, w: (h, 0, 0))),
        ],
        [pltpu.VMEM((hw, keys), F32), pltpu.VMEM((hw, keys), F32)],
        cost=LARGE,
    )


def gelu_pair(v):
    c = 0.7978845608028654
    inner = c * (v + 0.044715 * v * v * v)
    th = jnp.tanh(inner)
    slope = 0.5 * (1.0 + th) + 0.5 * v * (1.0 - th * th) * c * (1.0 + 3 * 0.044715 * v * v)
    return 0.5 * v * (1.0 + th), slope


def feed_kernel(height, block, where, *refs):
    (
        mix,
        far,
        tok,
        wo,
        wo_mine,
        wo_got,
        gain,
        shift,
        dy,
        wi,
        wi_mine,
        wi_got,
        bias,
        wh,
        residual,
        normed,
        act,
        grad_keep,
        grad_send,
        dy_keep,
        dy_send,
        g2,
        bias_sum,
        dy_sum,
        *sent,
        wo_far,
        weight,
    ) = refs
    step = pl.program_id(0)
    half = wi.shape[0]

    @pl.when(step == 0)
    def _():
        place_pieces(where, (wo_mine, wo_got), wo_far)
        wide_dy = dy[...].astype(F32)
        dy_sum[...] = jnp.sum(wide_dy, 0, keepdims=True)
        dy_stay, dy_away = by_parity(where, wide_dy.T, height)
        dy_keep[...] = dy_stay.astype(BF16)
        dy_send[...] = dy_away.astype(BF16)
        total = tok[...].astype(F32) + (dot(mix[...], wo[...]) + dot(far[...], wo_far[...]))
        residual[...] = total
        unit, _ = rows_stats(total)
        normed[...] = (unit * gain[...] + shift[...]).astype(BF16)

    weight[pl.ds(pl.multiple_of(where[0] * half, half), half), :] = wi[...]
    place_pieces(where, (wi_mine, wi_got), weight, (1 - where[0]) * half, half)
    pre = dot(normed[...], weight[...]) + bias[...]
    value, slope = gelu_pair(pre)
    low = value.astype(BF16)
    act[...] = low
    grad = (dot_nt(dy[...], wh[...]) * slope).astype(BF16)
    blocks = [grad[:, at : at + block] for at in range(0, grad.shape[1], block)]
    evens, odds = jnp.concatenate(blocks[::2], 1), jnp.concatenate(blocks[1::2], 1)
    even = where[1] == 0
    grad_keep[...] = jnp.where(even, evens, odds)
    grad_send[...] = jnp.where(even, odds, evens)
    bias_sum[...] = jnp.sum(grad.astype(F32), 0, keepdims=True)
    g2_part = dot_nt(grad, weight[...])

    @pl.when(step == 0)
    def _():
        g2[...] = g2_part

    @pl.when(step > 0)
    def _():
        g2[...] += g2_part

    @pl.when(step == pl.num_programs(0) - 1)
    def _():
        first_row = 0
        for piece in sent:
            piece[...] = g2[first_row : first_row + piece.shape[0], :].astype(BF16)
            first_row += piece.shape[0]


def feed(
    where, dp, turn, mix, far, tok, wo, gain, shift, dy, wi, bias, wh, second, chunk, parts, onto
):
    rows, width = dy.shape
    hidden = wh.shape[0]
    steps = hidden // chunk
    mine, got = second
    by_cols = spec((rows, chunk), lambda j, w: (turn, j))
    by_half = spec((rows, chunk // 2), lambda j, w: (turn, j))
    half = (2 * rows, hidden // 2), BF16, by_half
    turned = (width // 2, 2 * rows), BF16, spec((width // 2, rows), lambda j, w: (0, turn))
    wo_part = spec((mine.shape[0], width), lambda j, w: (0, 0))
    wi_part = spec((mine.shape[0], chunk), lambda j, w: (0, width // chunk + j))

    def once(dtype):
        return (rows, width), dtype, spec((rows, width))

    return call(
        functools.partial(feed_kernel, width // dp, hidden // (dp // 2)),
        "feed",
        where,
        (steps,),
        [
            whole(mix),
            whole(far),
            (tok, spec((rows, width), lambda j, w: (2 * turn, 0))),
            whole(wo),
            (mine, wo_part),
            (got, wo_part),
            whole(gain[None]),
            whole(shift[None]),
            whole(dy),
            (wi, spec((wi.shape[0], chunk), lambda j, w: (0, w[0] * steps + j))),
            (mine, wi_part),
            (got, wi_part),
            (bias[None], spec((1, chunk), lambda j, w: (0, w[0] * steps + j))),
            (wh, spec((chunk, width), lambda j, w: (j, 0))),
        ],
        [
            once(F32),
            ((2 * rows, width), BF16, spec((rows, width), lambda j, w: (turn, 0))),
            ((2 * rows, hidden), BF16, by_cols),
            half,
            half,
            turned,
            turned,
            once(F32),
            ((1, hidden), F32, spec((1, chunk), lambda j, w: (0, j))),
            ((1, width), F32, spec((1, width))),
        ]
        + [((rows // part, width), BF16, spec((rows // part, width))) for part in parts],
        [
            pltpu.VMEM(wo.shape, BF16),
            pltpu.VMEM((width, chunk), BF16),
        ],
        cost=LARGE,
        onto=onto,
    )


def middle_kernel(
    where,
    g_own,
    g_other,
    got_own,
    got_other,
    residual_own,
    residual_other,
    gain,
    dy,
    dy_o,
    wo,
    mix_own,
    mix_other,
    bias_sum,
    bias_sum_o,
    dy_sum,
    dc_sum,
    grad_res,
    dm,
    sums,
    keep,
    send,
):
    rows = dy.shape[0]
    lows = []
    halves = ((g_own, got_own, dy, residual_own), (g_other, got_other, dy_o, residual_other))
    for at, (g, got, d, residual) in enumerate(halves):
        here = slice(at * rows, (at + 1) * rows)
        grad = g[...] + got[...].astype(F32)
        unit, rstd = rows_stats(residual[...])
        total = d[...].astype(F32) + norm_back(grad, gain[...], unit, rstd)
        low = total.astype(BF16)
        lows.append(low)
        dm[here, :] = dot_nt(low, wo[...]).astype(BF16)
        if at == 0:
            grad_res[...] = total
            small = [jnp.sum(grad * unit, 0, keepdims=True), jnp.sum(grad, 0, keepdims=True)]
    width = dy.shape[1]
    first = where[0] == 0
    parts = [slice(at, at + width) for at in range(0, bias_sum.shape[1], width)]
    downs = [bias_sum[:, part] + bias_sum_o[:, part] for part in parts]
    small += [jnp.where(first, down, 0.0) for down in downs]
    small += [jnp.where(first, 0.0, down) for down in downs]
    small += [dy_sum[...], dc_sum[...]]
    sums[...] = jnp.concatenate(small, 0)
    split_pairs(
        where, dot_tn(lows[0], mix_own[...]) + dot_tn(lows[1], mix_other[...]), keep.shape[1], keep, send
    )


def middle(where, dp, g, got, residuals, gain, dys, wo, mix, small):
    rows, width = dys[0].shape
    heads = wo.shape[0]
    half = ((dp // 2, width // dp, heads), BF16, spec((dp // 2, width // dp, heads)))
    return call(
        middle_kernel,
        "middle",
        where,
        (1,),
        [whole(a) for a in (*g, *got, *residuals, gain[None], *dys, wo, *mix, *small)],
        [
            ((rows, width), F32, spec((rows, width))),
            ((2 * rows, heads), BF16, spec((2 * rows, heads))),
            ((8, width), F32, spec((8, width))),
            half,
            half,
        ],
        cost=LARGE,
    )


def norm_sums(step, grad, x, sums):
    unit, _ = rows_stats(x)
    rows = jnp.sum(grad * unit, 0, keepdims=True), jnp.sum(grad, 0, keepdims=True)

    @pl.when(step == 0)
    def _():
        sums[0:1, :], sums[1:2, :] = rows

    @pl.when(step > 0)
    def _():
        sums[0:1, :] += rows[0]
        sums[1:2, :] += rows[1]


def tokens_kernel(where, tok, other, dq, dk, dv, weights, g_own, sent, sums):
    step = pl.program_id(0)
    cols = dq.shape[1]
    grad = (
        dot_nt(dq[...], weights[:, :cols])
        + dot_nt(dk[...], weights[:, cols : 2 * cols])
        + dot_nt(dv[...], weights[:, 2 * cols :])
    )
    x = jnp.where(step == 0, tok[...].astype(F32), other[...].astype(F32))
    norm_sums(step, grad, x, sums)

    @pl.when(step == 0)
    def _():
        g_own[...] = grad

    @pl.when(step == 1)
    def _():
        sent[...] = grad.astype(BF16)


def tokens_back(where, tok, other, dq, dk, dv, weights):
    rows, width = tok.shape
    cols = dk.shape[1]
    late = spec((rows, cols), lambda i, w: (4 + i, 0))
    return call(
        tokens_kernel,
        "tokens_back",
        where,
        (2,),
        [
            whole(tok),
            (other, spec((rows, width), lambda i, w: (2, 0))),
            (dq, spec((rows, cols), lambda i, w: (i, 0))),
            (dk, late),
            (dv, late),
            whole(weights),
        ],
        [
            ((rows, width), F32, spec((rows, width))),
            ((rows, width), BF16, spec((rows, width))),
            ((2, width), F32, spec((2, width))),
        ],
    )


def slots_kernel(
    where, comp, mem, other, dk, dv, weights, start, slope_parts, early, sums, total
):
    step = pl.program_id(0)
    cols = dk.shape[1]
    grad = dot_nt(dk[...], weights[:, cols : 2 * cols]) + dot_nt(dv[...], weights[:, 2 * cols :])
    own = jnp.where(step == 0, comp[...].astype(F32), mem[...].astype(F32))
    x = jnp.where(step % 2 == 0, own, other[...].astype(F32))
    norm_sums(step, grad, x, total)

    @pl.when(step == pl.num_programs(0) - 1)
    def _():
        width = comp.shape[1]
        lane = lax.broadcasted_iota(jnp.int32, (1, width), 1)
        own_heads = slope_parts.shape[0]
        slope = jnp.zeros((1, width), F32)
        for head in range(own_heads):
            here = lane == where[0] * own_heads + head
            slope += jnp.where(here, slope_parts[head, 0:1, 0:1], 0.0)
        sums[:8, :] = early[...]
        rest = (total[...] + start[...], slope, jnp.zeros((5, width), F32))
        sums[8:, :] = jnp.concatenate(rest, 0)


def slots_back(where, comp, mem, other, dk, dv, weights, start, slope_parts, early):
    rows, width = comp.shape
    cols = dk.shape[1]
    by_step = spec((rows, cols), lambda i, w: (i, 0))
    return call(
        slots_kernel,
        "slots_back",
        where,
        (4,),
        [
            whole(comp),
            whole(mem),
            (other, spec((rows, width), lambda i, w: (i // 2, 0))),
            (dk, by_step),
            (dv, by_step),
            whole(weights),
            whole(start),
            whole(slope_parts),
            whole(early),
        ],
        [((16, width), F32, spec((16, width)))],
        [pltpu.VMEM((2, width), F32)],
        cost=LARGE,
    )


def turn_kernel(source, target):
    target[...] = source[...].T


def turned(array):
    return pl.pallas_call(
        turn_kernel,
        out_shape=jax.ShapeDtypeStruct(array.shape[::-1], F32),
        compiler_params=PARAMS,
        cost_estimate=TINY,
        name="turn",
    )(array)


def local(
    tokens,
    memory,
    compressed,
    mask_start,
    norm1_gain,
    norm1_bias,
    query_weight,
    key_weight,
    value_weight,
    out_weight,
    slopes,
    norm2_gain,
    norm2_bias,
    in_weight,
    in_bias,
    hidden_weight,
    hidden_bias,
    compress_weight,
    compress_bias,
    grad_out,
    grad_compressed,
):
    tokens, memory, compressed = tokens[0], memory[0], compressed[0]
    grad_out, grad_compressed = grad_out[0], grad_compressed[0]
    rows, width = tokens.shape
    heads = slopes.shape[0]
    dp = lax.axis_size("dp")
    levels = dp.bit_length() - 1
    top = levels - 1
    d = lax.axis_index("dp")
    t = lax.axis_index("tm")
    segment = 2 * rows

    def swap(block):
        return lax.ppermute(block, "tm", [(0, 1), (1, 0)])

    def across(block, mask):
        return lax.ppermute(block, "dp", [(i, i ^ mask) for i in range(dp)])

    def after(array, *earlier):
        return lax.optimization_barrier((array,) + earlier)[0]

    def bit(level):
        return (d >> level) & 1

    class Shrink:
        def __init__(self, keep, send, order, columns=False):
            shape = keep.shape if keep.ndim == 4 else keep.shape[:1] + (1,) + keep.shape[1:]
            self.pending = keep.reshape(shape), send.reshape(shape), 1
            self.order = [0] + order
            self.left = [level for level in range(1, top if columns else levels)]
            self.step = 0
            self.array = None

        def cut(self):
            if self.pending is not None:
                return self.pending[1]
            if self.step == len(self.order):
                return self.array
            level = self.order[self.step]
            if level in self.left:
                low = 1 << self.left.index(level)
                blocks, rest = self.array.shape[0], self.array.shape[1:]
                split = self.array.reshape((blocks // (2 * low), 2, low) + rest)
                keep, send = [
                    lax.dynamic_index_in_dim(split, at, 1, keepdims=False).reshape(
                        (blocks // 2,) + rest
                    )
                    for at in (bit(level), 1 - bit(level))
                ]
                self.left.remove(level)
                self.pending = keep, send, 1 << level
            else:
                size = self.array.shape[3] // 2
                keep, send = [
                    lax.dynamic_slice_in_dim(self.array, at * size, size, 3) for at in (t, 1 - t)
                ]
                self.pending = keep, send, 0
            return send

        def move(self):
            send = self.cut()
            return across(send, self.pending[2]) if self.pending[2] else swap(send)

        def take(self, got):
            keep, _, mask = self.pending
            if mask == 0:
                same = bit(top) == t
                self.pending = jnp.where(same, keep, got), jnp.where(same, got, keep), 1 << top
                return self.pending[1]
            self.step += 1
            total = keep.astype(F32) + got.astype(F32)
            last = self.step == len(self.order)
            self.array = total if last else total.astype(BF16)
            self.pending = None
            return self.array

        def add(self):
            if self.step == len(self.order):
                return self.array
            self.cut()
            if self.pending[2] == 0:
                self.take(self.move())
            return self.take(self.move())

        def wait(self, *earlier):
            if self.pending is not None:
                self.pending = (after(self.pending[0], *earlier),) + self.pending[1:]

        def finish(self):
            while self.step < len(self.order):
                self.add()
            return self.array[0]

    def meet(groups, *others):
        groups = [group for group in groups if group.step < len(group.order)]
        got = lax.optimization_barrier(tuple(group.move() for group in groups) + others)
        for group, block in zip(groups, got):
            group.take(block)
        for group in groups:
            group.cut()
        return got[len(groups) :]

    sideways = list(range(1, levels))
    upward = list(range(2, levels)) + [1] if levels > 1 else []
    between = upward[:1] + upward[-1:] + upward[1:-1] if levels > 2 else upward

    sharing = min(levels, 4)
    share = 1 << sharing
    ups = [z << 2 for z in range(1 << max(sharing - 2, 0))]
    offsets = [x + z for x in ((0, 2) if sharing > 1 else (0,)) for z in ups]
    low_bits = d & (share - 1)
    targets = [low_bits ^ off for off in offsets] + [low_bits ^ off ^ 1 for off in offsets]
    where = jnp.stack([t, bit(0)] + targets).astype(jnp.int32)

    def gather_up(piece):
        return jnp.concatenate([piece] + [across(piece, z) for z in ups[1:]], 0)

    def gather_side(block):
        return jnp.concatenate((block, across(block, 2)), 0) if sharing > 1 else block

    (joined,) = pieces(
        jnp.stack((low_bits, 1 - t)).astype(jnp.int32),
        share,
        query_weight,
        key_weight,
        value_weight,
        out_weight,
        in_weight,
    )
    joined = swap(joined)
    first_size = 3 * query_weight.shape[1] // 2
    first, second = joined[:, :first_size], joined[:, first_size:]
    slots = grad_compressed.shape[0]
    dc = jnp.pad(grad_compressed, ((0, -slots % 16), (0, 0)))
    x_other = swap(jnp.concatenate((compressed, memory, tokens), 0))
    first = gather_side(gather_up(first))
    first_got = across(first, 1)
    second_up = gather_up(after(second, first_got))
    second = gather_side(second_up)
    second_got = across(second, 1)

    *filled, qkv = project_own(
        where,
        compressed,
        memory,
        tokens,
        norm1_gain,
        norm1_bias,
        query_weight,
        key_weight,
        value_weight,
        first,
        first_got,
    )
    inputs_low, queries, keys, values = project_other(
        where, x_other, norm1_gain, norm1_bias, qkv, filled
    )
    dc_other = swap(after(dc, queries))

    index = jnp.arange(segment, dtype=jnp.int32)
    slot = jnp.where(index < rows, index + t * rows, index - rows + (1 - t) * rows)
    place = jnp.concatenate((-segment - 3 * (segment - slot), slot - segment, slot)).astype(F32)
    closed = jnp.where(slot >= mask_start[0], 0.0, NEG)
    closed = jnp.concatenate((closed, jnp.zeros((2 * segment,), F32)))
    place = jnp.stack((place, closed))
    own_heads = heads // 2
    slopes_own = lax.dynamic_slice_in_dim(slopes, t * own_heads, own_heads, 0)
    mix_other, lse_other = attend(
        where, 1, slopes_own, after(queries, second_up), keys, values, place
    )
    far_own = swap(mix_other)
    dy_other = swap(after(grad_out, mix_other))
    squeeze_stay, squeeze_away, keep, send, dc_sum = squeeze_rows(
        where, dp, slots, after(memory, mix_other), x_other, dc, dc_other, compress_weight
    )
    squeeze = Shrink(keep, send, sideways)
    squeeze_got = swap(squeeze_away)
    mix_own, lse_own = attend(
        where, 0, slopes_own, after(queries, squeeze_away), keys, values, place
    )
    far_other = swap(mix_own)
    dys = grad_out, dy_other
    mix = mix_own, mix_other
    chunk = max(in_weight.shape[1] // 8, 2 * in_weight.shape[1] // dp)

    def feed_rows(turn, mixed, far, tok, dy, parts, onto=None):
        return feed(
            where,
            dp,
            turn,
            mixed,
            far,
            tok,
            out_weight,
            norm2_gain,
            norm2_bias,
            dy,
            in_weight,
            in_bias,
            hidden_weight,
            (second, second_got),
            chunk,
            parts,
            onto,
        )

    squeeze.add()
    residual, *half_filled, g_own, bias_sum, dy_sum, sent = feed_rows(
        0, after(mix_own, squeeze.cut()), far_own, tokens, grad_out, (1,)
    )
    got_other = swap(sent)
    residual_o, *filled, g_other, bias_sum_o, _, sent = feed_rows(
        1,
        after(mix_other, sent, squeeze_got),
        far_other,
        x_other,
        dy_other,
        (1,),
        {1 + i: array for i, array in enumerate(half_filled)},
    )
    got = swap(sent), got_other
    normed, act, grad_keep, grad_send, dy_keep, dy_send = filled
    squeeze.wait(sent, got_other)
    squeeze.add()
    blocks = dp // 2

    def cut_rows(product, count):
        return product.astype(BF16).reshape(count, product.shape[0] // count, product.shape[1])

    hidden_send = dot(after(dy_send, squeeze.cut(), got_other), act).astype(BF16)
    entry_send = dot_tn(after(grad_send, hidden_send), normed).astype(BF16)
    hidden_keep = dot(after(dy_keep, entry_send), act).astype(BF16)
    entry_keep = dot_tn(after(grad_keep, hidden_keep), normed).astype(BF16)
    hidden = Shrink(cut_rows(hidden_keep, blocks), cut_rows(hidden_send, blocks), sideways)
    entry = Shrink(
        cut_rows(entry_keep, blocks // 2), cut_rows(entry_send, blocks // 2), between, True
    )
    got = after(got[0], entry_keep), got[1]
    grad_residual, grad_mixture, early, keep, send = middle(
        where,
        dp,
        (after(g_own, entry_keep), g_other),
        got,
        (residual, residual_o),
        norm2_gain,
        dys,
        out_weight,
        mix,
        (bias_sum, bias_sum_o, dy_sum, dc_sum),
    )
    mix_out = Shrink(keep, send, sideways)
    squeeze.add()
    hidden.add()
    entry.add()
    height = key_weight.shape[1] // dp
    dq, dk, dv, all_keep, all_send, slope_parts = attend_back(
        where,
        height,
        slopes_own,
        queries,
        keys,
        values,
        after(grad_mixture, hidden.cut(), entry.cut(), squeeze.array),
        place,
        (lse_own, lse_other),
    )
    mix_out.wait(dq)

    def cut_heads(product):
        return product.reshape(blocks // 2, -1, height, width)

    all_send = dot(all_send, inputs_low).astype(BF16)
    all_keep = dot(after(all_keep, all_send), inputs_low).astype(BF16)
    hidden.add()
    entry.add()
    left = Shrink(cut_heads(all_keep), cut_heads(all_send), sideways, True)
    mix_out.add()
    left.add()
    mix_out.cut()
    mix_out.wait(left.cut())
    mix_out.add()
    squeeze.add()
    g1_own, g1_sent, token_sums = tokens_back(
        where,
        tokens,
        x_other,
        after(dq, left.cut(), hidden.cut(), entry.cut(), mix_out.cut(), squeeze.array),
        dk,
        dv,
        qkv,
    )
    g1_got = swap(g1_sent)
    mix_out.wait(g1_sent)
    mix_out.add()
    for group in (hidden, entry):
        group.wait(g1_sent)
        group.add()
    (smalls,) = slots_back(
        where,
        compressed,
        memory,
        x_other,
        after(dk, mix_out.cut(), hidden.cut(), entry.cut()),
        dv,
        qkv,
        token_sums,
        slope_parts,
        early,
    )

    def joint(array, mask):
        return lax.ppermute(array, ("dp", "tm"), [(i, i ^ mask) for i in range(2 * dp)])

    smalls, g1_got = meet((left, hidden, entry, mix_out), smalls, g1_got)
    groups = (left, hidden, entry, mix_out, squeeze)
    masks = [1 << at for at in range(levels + 1)]
    out_part = None
    while masks:
        sends = [group.cut() for group in groups]
        smalls = after(smalls, *sends)
        if len(masks) > 1 and len(masks) % 2:
            smalls = smalls + joint(smalls, masks.pop(0))
        others = smalls, joint(smalls, masks.pop(0))
        if out_part is None:
            out_part = dot(after(act, *sends), hidden_weight)
            smalls, got, out_sent = meet(groups, *others, out_part[rows:].astype(BF16))
            out_got = swap(out_sent)
        else:
            smalls, got = meet(groups, *others)
        smalls = smalls + got
    output = (residual + (out_part[:rows] + out_got.astype(F32)) + hidden_bias).astype(BF16)
    new_compressed = (
        after(squeeze_stay, sends[0])[:slots] + squeeze_got[:slots].astype(F32) + compress_bias
    ).astype(BF16)
    g1 = g1_own + g1_got.astype(F32)
    unit1, rstd1 = rows_stats(tokens.astype(F32))
    grad_tokens = (grad_residual + norm_back(g1, norm1_gain, unit1, rstd1)).astype(BF16)

    grad_query_w, grad_key_w, grad_value_w = [part.T for part in left.finish()]
    grad_in_w = turned(entry.finish()[0])
    grad_hidden_w, grad_out_w, grad_compress_w = [
        group.finish()[0].T for group in (hidden, mix_out, squeeze)
    ]
    gain2, bias2, hidden_b, compress_b, gain1, bias1, slope = [
        smalls[i] for i in (0, 1, 6, 7, 8, 9, 10)
    ]
    in_b = smalls[2:6].reshape(-1)
    return (
        output[None],
        new_compressed[None],
        grad_tokens[None],
        gain1,
        bias1,
        grad_query_w,
        grad_key_w,
        grad_value_w,
        grad_out_w,
        slope[:heads],
        gain2,
        bias2,
        grad_in_w,
        in_b,
        grad_hidden_w,
        hidden_b,
        grad_compress_w,
        compress_b,
    )


def solution(mesh):
    split, whole, kept = P("dp", "tm", None), P(), P("tm", None)
    in_specs = (
        (split,) * 3
        + (P("dp"), whole, whole)
        + (kept,) * 4
        + (whole,) * 3
        + (kept, whole, kept, whole, kept, whole)
        + (split,) * 2
    )
    shared = P("tm", "dp")
    out_specs = (
        (split,) * 3
        + (whole,) * 2
        + (shared,) * 4
        + (whole,) * 3
        + (shared, whole, shared, whole, shared, whole)
    )
    return jax.shard_map(local, mesh=mesh, in_specs=in_specs, out_specs=out_specs, check_vma=False)
```

```python
import functools

import jax
import jax.numpy as jnp
from jax import lax
from jax.experimental import pallas as pl
from jax.experimental.pallas import tpu as pltpu
from jax.sharding import PartitionSpec as P

EPS = 1e-05
NEG = -1e30
LOG2E = 1.4426950408889634
F32 = jnp.float32
BF16 = jnp.bfloat16
TINY = pl.CostEstimate(flops=1000, bytes_accessed=1000, transcendentals=0)
LARGE = pl.CostEstimate(flops=20 * 10**9, bytes_accessed=10**6, transcendentals=0)
PARAMS = pltpu.CompilerParams(vmem_limit_bytes=32 * 2**20)


def dot(a, b, dims=((1,), (0,))):
    return lax.dot_general(a, b, (dims, ((), ())), preferred_element_type=F32)


def dot_nt(a, b):
    return dot(a, b, ((1,), (1,)))


def dot_tn(a, b):
    return dot(a, b, ((0,), (0,)))


def rows_stats(x):
    mean = jnp.mean(x, -1, keepdims=True)
    centered = x - mean
    rstd = lax.rsqrt(jnp.mean(centered * centered, -1, keepdims=True) + EPS)
    return centered * rstd, rstd


def norm_back(grad, gain, normed, rstd):
    dn = grad * gain
    return rstd * (
        dn
        - jnp.mean(dn, -1, keepdims=True)
        - normed * jnp.mean(dn * normed, -1, keepdims=True)
    )


def spec(shape, at=None):
    zeros = (0,) * len(shape)
    return pl.BlockSpec(shape, at if at is not None else (lambda *_: zeros))


def call(kernel, name, where, grid, ins, outs, scratch=(), cost=TINY, onto=None):
    onto = onto or {}
    count = len(ins)
    ins = list(ins) + [(array, pl.BlockSpec(memory_space=pl.ANY)) for array in onto.values()]

    def body(place, *refs):
        kernel(place, *refs[:count], *refs[len(ins) :])

    return pl.pallas_call(
        body,
        grid_spec=pltpu.PrefetchScalarGridSpec(
            num_scalar_prefetch=1,
            grid=grid,
            in_specs=[at for _, at in ins],
            out_specs=[at for _, _, at in outs],
            scratch_shapes=list(scratch),
        ),
        out_shape=[jax.ShapeDtypeStruct(shape, dtype) for shape, dtype, _ in outs],
        input_output_aliases={1 + count + i: out for i, out in enumerate(onto)},
        compiler_params=PARAMS,
        cost_estimate=cost,
        name=name,
    )(where, *[array for array, _ in ins])


def whole(array):
    return array, spec(array.shape)


def ordered(first, own, other, axis):
    return jnp.where(
        first, jnp.concatenate((own, other), axis), jnp.concatenate((other, own), axis)
    )


def place_pieces(where, parts, target, base=0, half=None):
    size = (half or target.shape[0]) // (where.shape[0] - 2)
    at = 0
    for part in parts:
        for block in range(part.shape[0] // size):
            row = pl.multiple_of(base + where[2 + at] * size, size)
            target[pl.ds(row, size), :] = part[block * size : (block + 1) * size, :]
            at += 1


def pieces_kernel(where, wq, wk, wv, wo, wi, joined):
    size = wq.shape[1]
    first, second = joined.at[:, : 3 * size], joined.at[:, 3 * size :]
    first[:, :size] = wq[...]
    first[:, size : 2 * size] = wk[...]
    first[:, 2 * size :] = wv[...]
    second[:, : wo.shape[1]] = wo[...]
    second[:, wo.shape[1] :] = wi[...]


def pieces(where, share, wq, wk, wv, wo, wi):
    rows = wq.shape[0] // share
    cols = wq.shape[1] // 2
    wide = wi.shape[1] // 2
    half = spec((rows, cols), lambda i, w: (w[0], w[1]))
    return call(
        pieces_kernel,
        "pieces",
        where,
        (1,),
        [
            (wq, half),
            (wk, half),
            (wv, half),
            (wo, spec((rows, wo.shape[1]), lambda i, w: (w[0], 0))),
            (wi, spec((rows, wide), lambda i, w: (w[0], w[1]))),
        ],
        [
            (
                (rows, 3 * cols + wo.shape[1] + wide),
                BF16,
                spec((rows, 3 * cols + wo.shape[1] + wide)),
            )
        ],
    )


def project_rows(x, gain, shift, weights, low, q, k, v):
    cols = k.shape[1]
    unit, _ = rows_stats(x)
    n = (unit * gain[...] + shift[...]).astype(BF16)
    low[...] = n
    k[...] = dot(n, weights[:, cols : 2 * cols]).astype(BF16)
    v[...] = dot(n, weights[:, 2 * cols :]).astype(BF16)

    @pl.when(pl.program_id(0) == 2)
    def _():
        q[...] = dot(n, weights[:, :cols]).astype(BF16)


def project_own_kernel(
    where, comp, mem, tok, gain, shift, wq, wk, wv, mine, got, low, q, k, v, weights, x
):
    step = pl.program_id(0)
    half, cols = wq.shape
    for at, source in enumerate((comp, mem, tok)):

        @pl.when(step == at)
        def _(source=source):
            x[...] = source[...].astype(F32)

    @pl.when(step == 0)
    def _():
        own = pl.ds(pl.multiple_of(where[0] * half, half), half)
        for index, weight in enumerate((wq, wk, wv)):
            weights[own, index * cols : (index + 1) * cols] = weight[...]
        place_pieces(where, (mine, got), weights, (1 - where[0]) * half, half)

    project_rows(x[...], gain, shift, weights, low, q, k, v)


def project_other_kernel(where, other, gain, shift, weights, low, q, k, v):
    project_rows(other[...].astype(F32), gain, shift, weights, low, q, k, v)


def project_outs(rows, width, cols, turn):
    def by_step(size):
        return (6 * rows, size), BF16, spec((rows, size), lambda i, w: (2 * i + turn, 0))

    query = (2 * rows, cols), BF16, spec((rows, cols), lambda i, w: (turn, 0))
    return [by_step(width), query, by_step(cols), by_step(cols)]


def project_own(where, comp, mem, tok, gain, shift, wq, wk, wv, mine, got):
    rows, width = tok.shape
    cols = wq.shape[1] // 2
    half = spec((wq.shape[0], cols), lambda i, w: (0, w[0]))
    return call(
        project_own_kernel,
        "project_own",
        where,
        (3,),
        [whole(a) for a in (comp, mem, tok, gain[None], shift[None])]
        + [(wq, half), (wk, half), (wv, half), whole(mine), whole(got)],
        project_outs(rows, width, cols, 0)
        + [((width, 3 * cols), BF16, spec((width, 3 * cols)))],
        [pltpu.VMEM((rows, width), F32)],
        cost=LARGE,
    )


def project_other(where, other, gain, shift, weights, filled):
    rows, width = other.shape[0] // 3, other.shape[1]
    return call(
        project_other_kernel,
        "project_other",
        where,
        (3,),
        [(other, spec((rows, width), lambda i, w: (i, 0)))]
        + [whole(a) for a in (gain[None], shift[None], weights)],
        project_outs(rows, width, weights.shape[1] // 3, 1),
        cost=LARGE,
        onto=dict(enumerate(filled)),
    )


def split_pairs(where, total, height, keep, send):
    pairs = total.reshape(total.shape[0] // (2 * height), 2, height, total.shape[1])
    even = where[1] == 0
    keep[...] = jnp.where(even, pairs[:, 0], pairs[:, 1]).astype(BF16)
    send[...] = jnp.where(even, pairs[:, 1], pairs[:, 0]).astype(BF16)


def by_parity(where, total, height):
    pairs = total.reshape(total.shape[0] // (2 * height), 2, height, total.shape[1])
    even = where[1] == 0
    shape = (total.shape[0] // 2, total.shape[1])
    keep = jnp.where(even, pairs[:, 0], pairs[:, 1]).reshape(shape)
    return keep, jnp.where(even, pairs[:, 1], pairs[:, 0]).reshape(shape)


def squeeze_kernel(slots, where, mem, other, dc, dc_o, weight, stay, away, keep, send, dc_sum):
    t = where[0]
    dc_sum[...] = jnp.sum(dc[...].astype(F32), 0, keepdims=True)
    rows, width = mem.shape
    mem_o = other.at[rows : 2 * rows, :]
    padded = dc.shape[0]
    half = width // 2
    lead = 3 * 2 * slots - 2 * rows
    first = t == 0
    shape = (padded, rows)
    slot = lax.broadcasted_iota(jnp.int32, shape, 0)
    row = lax.broadcasted_iota(jnp.int32, shape, 1)
    mem_half = jnp.where(first, mem[:, :half], mem[:, half:])
    mem_o_half = jnp.where(first, mem_o[:, :half], mem_o[:, half:])

    def picked(slot_half, row_half, offset):
        place = 3 * (slot + slot_half * slots) + offset - lead
        hit = (place == row + row_half * rows) & (slot < slots)
        return jnp.where(hit, 1.0, 0.0).astype(BF16)

    def windows(slot_half):
        edge = dot(picked(slot_half, t, 2 * t), mem[...]) + dot(
            picked(slot_half, 1 - t, 2 * t), mem_o[...]
        )
        middle = dot(picked(slot_half, t, 1), mem_half) + dot(
            picked(slot_half, 1 - t, 1), mem_o_half
        )
        return ordered(first, edge, middle, 1).astype(BF16)

    both = jnp.concatenate((windows(t), windows(1 - t)), 0)
    slots_out = dot(both, weight[...])
    stay[...] = slots_out[:padded, :]
    away[...] = slots_out[padded:, :].astype(BF16)
    turned_dc = jnp.concatenate((dc[...], dc_o[...]), 0).T
    columns = both.shape[1]
    height = keep.shape[1]
    for at in range(0, columns, half):
        part = slice(at, at + half)
        total = dot(turned_dc, both[:, part])
        split_pairs(where, total, height, keep.at[:, :, part], send.at[:, :, part])


def squeeze_rows(where, dp, slots, mem, other, dc, dc_o, weight):
    padded, width = dc.shape
    half = ((dp // 2, width // dp, weight.shape[0]), BF16)
    ins = [whole(a) for a in (mem, other, dc, dc_o, weight)]
    return call(
        functools.partial(squeeze_kernel, slots),
        "squeeze",
        where,
        (1,),
        ins,
        [
            ((padded, width), F32, spec((padded, width))),
            ((padded, width), BF16, spec((padded, width))),
            half + (spec(half[0]),),
            half + (spec(half[0]),),
            ((1, width), F32, spec((1, width))),
        ],
    )


def masked_scores(place, slope, q, keys, scale, first, tail):
    bias = place[0:1, :] * slope + place[1:2, :]
    chunk = q.shape[0]
    query_place = (lax.broadcasted_iota(jnp.int32, (chunk, 1), 0) + first).astype(F32)
    scores = dot_nt(q, keys) * (scale * LOG2E) + bias
    recent = jnp.where(place[0:1, tail:] <= query_place, scores[:, tail:], NEG)
    return jnp.concatenate((scores[:, :tail], recent), 1), query_place


def attend_kernel(turn, scale, where, slopes, q, k, v, place, mix, lse):
    slope = slopes[pl.program_id(0)] * LOG2E
    rows = q.shape[0]
    first = jnp.abs(turn - where[0]) * rows
    scores, _ = masked_scores(place, slope, q[...], k[...], scale, first, k.shape[0] - 2 * rows)
    highest = jnp.max(scores, -1, keepdims=True)
    weights = jnp.exp2(scores - highest)
    total = jnp.sum(weights, -1, keepdims=True)
    mix[...] = (dot(weights.astype(BF16), v[...]) * (1.0 / total)).astype(BF16)
    lse[0] = highest + jnp.log2(total)


def attend(where, turn, slopes, q, k, v, place):
    rows, width = q.shape[0] // 2, q.shape[1]
    heads = slopes.shape[0]
    hw = width // heads
    keys = k.shape[0]
    by_head = spec((keys, hw), lambda h, w: (0, h))
    return call(
        functools.partial(attend_kernel, turn, hw**-0.5),
        "attend",
        where,
        (heads,),
        [
            (slopes, pl.BlockSpec(memory_space=pltpu.SMEM)),
            (q, spec((rows, hw), lambda h, w: (turn, h))),
            (k, by_head),
            (v, by_head),
            whole(place),
        ],
        [
            ((rows, width), BF16, spec((rows, hw), lambda h, w: (0, h))),
            ((heads, rows, 1), F32, spec((1, rows, 1), lambda h, w: (h, 0, 0))),
        ],
        cost=LARGE,
    )


def attend_back_kernel(
    chunk,
    scale,
    height,
    where,
    slopes,
    q,
    k,
    v,
    dm,
    place,
    lse_own,
    lse_other,
    dq,
    dk,
    dv,
    all_keep,
    all_send,
    slope_out,
    dk_sum,
    dv_sum,
):
    slope = slopes[pl.program_id(0)] * LOG2E
    keys = k.shape[0]
    rows = q.shape[0]
    half = rows // 2
    columns = jnp.zeros((1, keys), F32)
    by_row = jnp.zeros((1, 1), F32)
    dq_parts = []
    for step in range(rows // chunk):
        at = slice(step * chunk, (step + 1) * chunk)
        time_half = where[0] if step * chunk < half else 1 - where[0]
        scores, query_place = masked_scores(
            place,
            slope,
            q[at, :],
            k[...],
            scale,
            time_half * half + step * chunk % half,
            keys - rows,
        )
        weights = jnp.exp2(scores - (lse_own if step == 0 else lse_other)[0])
        low = weights.astype(BF16)
        grads = dot_nt(dm[at, :], v[...])
        shift = jnp.sum(weights * grads, -1, keepdims=True)
        ds = (weights * (grads - shift)).astype(BF16)
        dq_part = dot(ds, k[...]) * scale
        dq[at, :] = dq_part.astype(BF16)
        dq_parts.append(dq_part.T)
        dk_part = dot_tn(q[at, :], ds)
        dv_part = dot_tn(dm[at, :], low)
        if step == 0:
            dk_sum[...] = dk_part
            dv_sum[...] = dv_part
        else:
            dk_sum[...] += dk_part
            dv_sum[...] += dv_part
        wide = ds.astype(F32)
        columns += jnp.sum(wide, 0, keepdims=True)
        by_row += jnp.sum(jnp.sum(wide, -1, keepdims=True) * query_place, 0, keepdims=True)
    dk_all, dv_all = dk_sum[...] * scale, dv_sum[...]
    dq_all = jnp.concatenate([jnp.zeros((dk_all.shape[0], keys - rows), F32)] + dq_parts, 1)
    halves = [by_parity(where, part, height) for part in (dq_all, dk_all, dv_all)]
    for target, parts in zip((all_keep, all_send), zip(*halves)):
        blocks = [part.reshape(part.shape[0] // height, height, keys) for part in parts]
        target[...] = jnp.stack(blocks, 1).reshape(target.shape).astype(BF16)
    dk[...] = dk_all.T.astype(BF16)
    dv[...] = dv_all.T.astype(BF16)
    total = jnp.sum(columns * place[0:1, :], -1, keepdims=True) - by_row
    slope_out[...] = jnp.broadcast_to(total.reshape(1, 1, 1), slope_out.shape)


def attend_back(where, height, slopes, q, k, v, dm, place, lses):
    rows, width = q.shape
    heads = slopes.shape[0]
    hw = width // heads
    keys = k.shape[0]
    by_rows = spec((rows, hw), lambda h, w: (0, h))
    by_keys = spec((keys, hw), lambda h, w: (0, h))
    return call(
        functools.partial(attend_back_kernel, rows // 2, hw**-0.5, height),
        "attend_back",
        where,
        (heads,),
        [
            (slopes, pl.BlockSpec(memory_space=pltpu.SMEM)),
            (q, by_rows),
            (k, by_keys),
            (v, by_keys),
            (dm, by_rows),
            whole(place),
            (lses[0], spec((1, rows // 2, 1), lambda h, w: (h, 0, 0))),
            (lses[1], spec((1, rows // 2, 1), lambda h, w: (h, 0, 0))),
        ],
        [
            ((rows, width), BF16, by_rows),
            ((keys, width), BF16, by_keys),
            ((keys, width), BF16, by_keys),
            ((3 * width // 2, keys), BF16, spec((3 * hw // 2, keys), lambda h, w: (h, 0))),
            ((3 * width // 2, keys), BF16, spec((3 * hw // 2, keys), lambda h, w: (h, 0))),
            ((heads, 8, 128), F32, spec((1, 8, 128), lambda h, w: (h, 0, 0))),
        ],
        [pltpu.VMEM((hw, keys), F32), pltpu.VMEM((hw, keys), F32)],
        cost=LARGE,
    )


def gelu_pair(v):
    c = 0.7978845608028654
    inner = c * (v + 0.044715 * v * v * v)
    th = jnp.tanh(inner)
    slope = 0.5 * (1.0 + th) + 0.5 * v * (1.0 - th * th) * c * (1.0 + 3 * 0.044715 * v * v)
    return 0.5 * v * (1.0 + th), slope


def feed_kernel(height, block, where, *refs):
    (
        mix,
        far,
        tok,
        wo,
        wo_mine,
        wo_got,
        gain,
        shift,
        dy,
        wi,
        wi_mine,
        wi_got,
        bias,
        wh,
        residual,
        normed,
        act,
        grad_keep,
        grad_send,
        dy_keep,
        dy_send,
        g2,
        bias_sum,
        dy_sum,
        *sent,
        wo_far,
        weight,
    ) = refs
    step = pl.program_id(0)
    half = wi.shape[0]

    @pl.when(step == 0)
    def _():
        place_pieces(where, (wo_mine, wo_got), wo_far)
        wide_dy = dy[...].astype(F32)
        dy_sum[...] = jnp.sum(wide_dy, 0, keepdims=True)
        dy_stay, dy_away = by_parity(where, wide_dy.T, height)
        dy_keep[...] = dy_stay.astype(BF16)
        dy_send[...] = dy_away.astype(BF16)
        total = tok[...].astype(F32) + (dot(mix[...], wo[...]) + dot(far[...], wo_far[...]))
        residual[...] = total
        unit, _ = rows_stats(total)
        normed[...] = (unit * gain[...] + shift[...]).astype(BF16)

    weight[pl.ds(pl.multiple_of(where[0] * half, half), half), :] = wi[...]
    place_pieces(where, (wi_mine, wi_got), weight, (1 - where[0]) * half, half)
    pre = dot(normed[...], weight[...]) + bias[...]
    value, slope = gelu_pair(pre)
    low = value.astype(BF16)
    act[...] = low
    grad = (dot_nt(dy[...], wh[...]) * slope).astype(BF16)
    blocks = [grad[:, at : at + block] for at in range(0, grad.shape[1], block)]
    evens, odds = jnp.concatenate(blocks[::2], 1), jnp.concatenate(blocks[1::2], 1)
    even = where[1] == 0
    grad_keep[...] = jnp.where(even, evens, odds)
    grad_send[...] = jnp.where(even, odds, evens)
    bias_sum[...] = jnp.sum(grad.astype(F32), 0, keepdims=True)
    g2_part = dot_nt(grad, weight[...])

    @pl.when(step == 0)
    def _():
        g2[...] = g2_part

    @pl.when(step > 0)
    def _():
        g2[...] += g2_part

    @pl.when(step == pl.num_programs(0) - 1)
    def _():
        first_row = 0
        for piece in sent:
            piece[...] = g2[first_row : first_row + piece.shape[0], :].astype(BF16)
            first_row += piece.shape[0]


def feed(
    where, dp, turn, mix, far, tok, wo, gain, shift, dy, wi, bias, wh, second, chunk, parts, onto
):
    rows, width = dy.shape
    hidden = wh.shape[0]
    steps = hidden // chunk
    mine, got = second
    by_cols = spec((rows, chunk), lambda j, w: (turn, j))
    by_half = spec((rows, chunk // 2), lambda j, w: (turn, j))
    half = (2 * rows, hidden // 2), BF16, by_half
    turned = (width // 2, 2 * rows), BF16, spec((width // 2, rows), lambda j, w: (0, turn))
    wo_part = spec((mine.shape[0], width), lambda j, w: (0, 0))
    wi_part = spec((mine.shape[0], chunk), lambda j, w: (0, width // chunk + j))

    def once(dtype):
        return (rows, width), dtype, spec((rows, width))

    return call(
        functools.partial(feed_kernel, width // dp, hidden // (dp // 2)),
        "feed",
        where,
        (steps,),
        [
            whole(mix),
            whole(far),
            (tok, spec((rows, width), lambda j, w: (2 * turn, 0))),
            whole(wo),
            (mine, wo_part),
            (got, wo_part),
            whole(gain[None]),
            whole(shift[None]),
            whole(dy),
            (wi, spec((wi.shape[0], chunk), lambda j, w: (0, w[0] * steps + j))),
            (mine, wi_part),
            (got, wi_part),
            (bias[None], spec((1, chunk), lambda j, w: (0, w[0] * steps + j))),
            (wh, spec((chunk, width), lambda j, w: (j, 0))),
        ],
        [
            once(F32),
            ((2 * rows, width), BF16, spec((rows, width), lambda j, w: (turn, 0))),
            ((2 * rows, hidden), BF16, by_cols),
            half,
            half,
            turned,
            turned,
            once(F32),
            ((1, hidden), F32, spec((1, chunk), lambda j, w: (0, j))),
            ((1, width), F32, spec((1, width))),
        ]
        + [((rows // part, width), BF16, spec((rows // part, width))) for part in parts],
        [
            pltpu.VMEM(wo.shape, BF16),
            pltpu.VMEM((width, chunk), BF16),
        ],
        cost=LARGE,
        onto=onto,
    )


def middle_kernel(
    where,
    g_own,
    g_other,
    got_own,
    got_other,
    residual_own,
    residual_other,
    gain,
    dy,
    dy_o,
    wo,
    mix_own,
    mix_other,
    bias_sum,
    bias_sum_o,
    dy_sum,
    dc_sum,
    grad_res,
    dm,
    sums,
    keep,
    send,
):
    rows = dy.shape[0]
    lows = []
    halves = ((g_own, got_own, dy, residual_own), (g_other, got_other, dy_o, residual_other))
    for at, (g, got, d, residual) in enumerate(halves):
        here = slice(at * rows, (at + 1) * rows)
        grad = g[...] + got[...].astype(F32)
        unit, rstd = rows_stats(residual[...])
        total = d[...].astype(F32) + norm_back(grad, gain[...], unit, rstd)
        low = total.astype(BF16)
        lows.append(low)
        dm[here, :] = dot_nt(low, wo[...]).astype(BF16)
        if at == 0:
            grad_res[...] = total
            small = [jnp.sum(grad * unit, 0, keepdims=True), jnp.sum(grad, 0, keepdims=True)]
    width = dy.shape[1]
    first = where[0] == 0
    parts = [slice(at, at + width) for at in range(0, bias_sum.shape[1], width)]
    downs = [bias_sum[:, part] + bias_sum_o[:, part] for part in parts]
    small += [jnp.where(first, down, 0.0) for down in downs]
    small += [jnp.where(first, 0.0, down) for down in downs]
    small += [dy_sum[...], dc_sum[...]]
    sums[...] = jnp.concatenate(small, 0)
    split_pairs(
        where, dot_tn(lows[0], mix_own[...]) + dot_tn(lows[1], mix_other[...]), keep.shape[1], keep, send
    )


def middle(where, dp, g, got, residuals, gain, dys, wo, mix, small):
    rows, width = dys[0].shape
    heads = wo.shape[0]
    half = ((dp // 2, width // dp, heads), BF16, spec((dp // 2, width // dp, heads)))
    return call(
        middle_kernel,
        "middle",
        where,
        (1,),
        [whole(a) for a in (*g, *got, *residuals, gain[None], *dys, wo, *mix, *small)],
        [
            ((rows, width), F32, spec((rows, width))),
            ((2 * rows, heads), BF16, spec((2 * rows, heads))),
            ((8, width), F32, spec((8, width))),
            half,
            half,
        ],
        cost=LARGE,
    )


def norm_sums(step, grad, x, sums):
    unit, _ = rows_stats(x)
    rows = jnp.sum(grad * unit, 0, keepdims=True), jnp.sum(grad, 0, keepdims=True)

    @pl.when(step == 0)
    def _():
        sums[0:1, :], sums[1:2, :] = rows

    @pl.when(step > 0)
    def _():
        sums[0:1, :] += rows[0]
        sums[1:2, :] += rows[1]


def tokens_kernel(where, tok, other, dq, dk, dv, weights, g_own, sent, sums):
    step = pl.program_id(0)
    cols = dq.shape[1]
    grad = (
        dot_nt(dq[...], weights[:, :cols])
        + dot_nt(dk[...], weights[:, cols : 2 * cols])
        + dot_nt(dv[...], weights[:, 2 * cols :])
    )
    x = jnp.where(step == 0, tok[...].astype(F32), other[...].astype(F32))
    norm_sums(step, grad, x, sums)

    @pl.when(step == 0)
    def _():
        g_own[...] = grad

    @pl.when(step == 1)
    def _():
        sent[...] = grad.astype(BF16)


def tokens_back(where, tok, other, dq, dk, dv, weights):
    rows, width = tok.shape
    cols = dk.shape[1]
    late = spec((rows, cols), lambda i, w: (4 + i, 0))
    return call(
        tokens_kernel,
        "tokens_back",
        where,
        (2,),
        [
            whole(tok),
            (other, spec((rows, width), lambda i, w: (2, 0))),
            (dq, spec((rows, cols), lambda i, w: (i, 0))),
            (dk, late),
            (dv, late),
            whole(weights),
        ],
        [
            ((rows, width), F32, spec((rows, width))),
            ((rows, width), BF16, spec((rows, width))),
            ((2, width), F32, spec((2, width))),
        ],
    )


def slots_kernel(
    where, comp, mem, other, dk, dv, weights, start, slope_parts, early, sums, total
):
    step = pl.program_id(0)
    cols = dk.shape[1]
    grad = dot_nt(dk[...], weights[:, cols : 2 * cols]) + dot_nt(dv[...], weights[:, 2 * cols :])
    own = jnp.where(step == 0, comp[...].astype(F32), mem[...].astype(F32))
    x = jnp.where(step % 2 == 0, own, other[...].astype(F32))
    norm_sums(step, grad, x, total)

    @pl.when(step == pl.num_programs(0) - 1)
    def _():
        width = comp.shape[1]
        lane = lax.broadcasted_iota(jnp.int32, (1, width), 1)
        own_heads = slope_parts.shape[0]
        slope = jnp.zeros((1, width), F32)
        for head in range(own_heads):
            here = lane == where[0] * own_heads + head
            slope += jnp.where(here, slope_parts[head, 0:1, 0:1], 0.0)
        sums[:8, :] = early[...]
        rest = (total[...] + start[...], slope, jnp.zeros((5, width), F32))
        sums[8:, :] = jnp.concatenate(rest, 0)


def slots_back(where, comp, mem, other, dk, dv, weights, start, slope_parts, early):
    rows, width = comp.shape
    cols = dk.shape[1]
    by_step = spec((rows, cols), lambda i, w: (i, 0))
    return call(
        slots_kernel,
        "slots_back",
        where,
        (4,),
        [
            whole(comp),
            whole(mem),
            (other, spec((rows, width), lambda i, w: (i // 2, 0))),
            (dk, by_step),
            (dv, by_step),
            whole(weights),
            whole(start),
            whole(slope_parts),
            whole(early),
        ],
        [((16, width), F32, spec((16, width)))],
        [pltpu.VMEM((2, width), F32)],
        cost=LARGE,
    )


def turn_kernel(source, target):
    target[...] = source[...].T


def turned(array):
    return pl.pallas_call(
        turn_kernel,
        out_shape=jax.ShapeDtypeStruct(array.shape[::-1], F32),
        compiler_params=PARAMS,
        cost_estimate=TINY,
        name="turn",
    )(array)


def local(
    tokens,
    memory,
    compressed,
    mask_start,
    norm1_gain,
    norm1_bias,
    query_weight,
    key_weight,
    value_weight,
    out_weight,
    slopes,
    norm2_gain,
    norm2_bias,
    in_weight,
    in_bias,
    hidden_weight,
    hidden_bias,
    compress_weight,
    compress_bias,
    grad_out,
    grad_compressed,
):
    tokens, memory, compressed = tokens[0], memory[0], compressed[0]
    grad_out, grad_compressed = grad_out[0], grad_compressed[0]
    rows, width = tokens.shape
    heads = slopes.shape[0]
    dp = lax.axis_size("dp")
    levels = dp.bit_length() - 1
    top = levels - 1
    d = lax.axis_index("dp")
    t = lax.axis_index("tm")
    segment = 2 * rows

    def swap(block):
        return lax.ppermute(block, "tm", [(0, 1), (1, 0)])

    def across(block, mask):
        return lax.ppermute(block, "dp", [(i, i ^ mask) for i in range(dp)])

    def after(array, *earlier):
        return lax.optimization_barrier((array,) + earlier)[0]

    def bit(level):
        return (d >> level) & 1

    class Shrink:
        def __init__(self, keep, send, order, columns=False):
            shape = keep.shape if keep.ndim == 4 else keep.shape[:1] + (1,) + keep.shape[1:]
            self.pending = keep.reshape(shape), send.reshape(shape), 1
            self.order = [0] + order
            self.left = [level for level in range(1, top if columns else levels)]
            self.step = 0
            self.array = None

        def cut(self):
            if self.pending is not None:
                return self.pending[1]
            if self.step == len(self.order):
                return self.array
            level = self.order[self.step]
            if level in self.left:
                low = 1 << self.left.index(level)
                blocks, rest = self.array.shape[0], self.array.shape[1:]
                split = self.array.reshape((blocks // (2 * low), 2, low) + rest)
                keep, send = [
                    lax.dynamic_index_in_dim(split, at, 1, keepdims=False).reshape(
                        (blocks // 2,) + rest
                    )
                    for at in (bit(level), 1 - bit(level))
                ]
                self.left.remove(level)
                self.pending = keep, send, 1 << level
            else:
                size = self.array.shape[3] // 2
                keep, send = [
                    lax.dynamic_slice_in_dim(self.array, at * size, size, 3) for at in (t, 1 - t)
                ]
                self.pending = keep, send, 0
            return send

        def move(self):
            send = self.cut()
            return across(send, self.pending[2]) if self.pending[2] else swap(send)

        def take(self, got):
            keep, _, mask = self.pending
            if mask == 0:
                same = bit(top) == t
                self.pending = jnp.where(same, keep, got), jnp.where(same, got, keep), 1 << top
                return self.pending[1]
            self.step += 1
            total = keep.astype(F32) + got.astype(F32)
            last = self.step == len(self.order)
            self.array = total if last else total.astype(BF16)
            self.pending = None
            return self.array

        def add(self):
            if self.step == len(self.order):
                return self.array
            self.cut()
            if self.pending[2] == 0:
                self.take(self.move())
            return self.take(self.move())

        def wait(self, *earlier):
            if self.pending is not None:
                self.pending = (after(self.pending[0], *earlier),) + self.pending[1:]

        def finish(self):
            while self.step < len(self.order):
                self.add()
            return self.array[0]

    def meet(groups, *others):
        groups = [group for group in groups if group.step < len(group.order)]
        got = lax.optimization_barrier(tuple(group.move() for group in groups) + others)
        for group, block in zip(groups, got):
            group.take(block)
        for group in groups:
            group.cut()
        return got[len(groups) :]

    sideways = list(range(1, levels))
    upward = list(range(2, levels)) + [1] if levels > 1 else []
    between = upward[:1] + upward[-1:] + upward[1:-1] if levels > 2 else upward

    sharing = min(levels, 4)
    share = 1 << sharing
    ups = [z << 2 for z in range(1 << max(sharing - 2, 0))]
    offsets = [x + z for x in ((0, 2) if sharing > 1 else (0,)) for z in ups]
    low_bits = d & (share - 1)
    targets = [low_bits ^ off for off in offsets] + [low_bits ^ off ^ 1 for off in offsets]
    where = jnp.stack([t, bit(0)] + targets).astype(jnp.int32)

    def gather_up(piece):
        return jnp.concatenate([piece] + [across(piece, z) for z in ups[1:]], 0)

    def gather_side(block):
        return jnp.concatenate((block, across(block, 2)), 0) if sharing > 1 else block

    (joined,) = pieces(
        jnp.stack((low_bits, 1 - t)).astype(jnp.int32),
        share,
        query_weight,
        key_weight,
        value_weight,
        out_weight,
        in_weight,
    )
    joined = swap(joined)
    first_size = 3 * query_weight.shape[1] // 2
    first, second = joined[:, :first_size], joined[:, first_size:]
    slots = grad_compressed.shape[0]
    dc = jnp.pad(grad_compressed, ((0, -slots % 16), (0, 0)))
    x_other = swap(jnp.concatenate((compressed, memory, tokens), 0))
    first = gather_side(gather_up(first))
    first_got = across(first, 1)
    second_up = gather_up(after(second, first_got))
    second = gather_side(second_up)
    second_got = across(second, 1)

    *filled, qkv = project_own(
        where,
        compressed,
        memory,
        tokens,
        norm1_gain,
        norm1_bias,
        query_weight,
        key_weight,
        value_weight,
        first,
        first_got,
    )
    inputs_low, queries, keys, values = project_other(
        where, x_other, norm1_gain, norm1_bias, qkv, filled
    )
    dc_other = swap(after(dc, queries))

    index = jnp.arange(segment, dtype=jnp.int32)
    slot = jnp.where(index < rows, index + t * rows, index - rows + (1 - t) * rows)
    place = jnp.concatenate((-segment - 3 * (segment - slot), slot - segment, slot)).astype(F32)
    closed = jnp.where(slot >= mask_start[0], 0.0, NEG)
    closed = jnp.concatenate((closed, jnp.zeros((2 * segment,), F32)))
    place = jnp.stack((place, closed))
    own_heads = heads // 2
    slopes_own = lax.dynamic_slice_in_dim(slopes, t * own_heads, own_heads, 0)
    mix_other, lse_other = attend(
        where, 1, slopes_own, after(queries, second_up), keys, values, place
    )
    far_own = swap(mix_other)
    dy_other = swap(after(grad_out, mix_other))
    squeeze_stay, squeeze_away, keep, send, dc_sum = squeeze_rows(
        where, dp, slots, after(memory, mix_other), x_other, dc, dc_other, compress_weight
    )
    squeeze = Shrink(keep, send, sideways)
    squeeze_got = swap(squeeze_away)
    mix_own, lse_own = attend(
        where, 0, slopes_own, after(queries, squeeze_away), keys, values, place
    )
    far_other = swap(mix_own)
    dys = grad_out, dy_other
    mix = mix_own, mix_other
    chunk = max(in_weight.shape[1] // 8, 2 * in_weight.shape[1] // dp)

    def feed_rows(turn, mixed, far, tok, dy, parts, onto=None):
        return feed(
            where,
            dp,
            turn,
            mixed,
            far,
            tok,
            out_weight,
            norm2_gain,
            norm2_bias,
            dy,
            in_weight,
            in_bias,
            hidden_weight,
            (second, second_got),
            chunk,
            parts,
            onto,
        )

    squeeze.add()
    residual, *half_filled, g_own, bias_sum, dy_sum, sent = feed_rows(
        0, after(mix_own, squeeze.cut()), far_own, tokens, grad_out, (1,)
    )
    got_other = swap(sent)
    residual_o, *filled, g_other, bias_sum_o, _, sent = feed_rows(
        1,
        after(mix_other, sent, squeeze_got),
        far_other,
        x_other,
        dy_other,
        (1,),
        {1 + i: array for i, array in enumerate(half_filled)},
    )
    got = swap(sent), got_other
    normed, act, grad_keep, grad_send, dy_keep, dy_send = filled
    squeeze.wait(sent, got_other)
    squeeze.add()
    blocks = dp // 2

    def cut_rows(product, count):
        return product.astype(BF16).reshape(count, product.shape[0] // count, product.shape[1])

    hidden_send = dot(after(dy_send, squeeze.cut(), got_other), act).astype(BF16)
    entry_send = dot_tn(after(grad_send, hidden_send), normed).astype(BF16)
    hidden_keep = dot(after(dy_keep, entry_send), act).astype(BF16)
    entry_keep = dot_tn(after(grad_keep, hidden_keep), normed).astype(BF16)
    hidden = Shrink(cut_rows(hidden_keep, blocks), cut_rows(hidden_send, blocks), sideways)
    entry = Shrink(
        cut_rows(entry_keep, blocks // 2), cut_rows(entry_send, blocks // 2), between, True
    )
    got = after(got[0], entry_keep), got[1]
    grad_residual, grad_mixture, early, keep, send = middle(
        where,
        dp,
        (after(g_own, entry_keep), g_other),
        got,
        (residual, residual_o),
        norm2_gain,
        dys,
        out_weight,
        mix,
        (bias_sum, bias_sum_o, dy_sum, dc_sum),
    )
    mix_out = Shrink(keep, send, sideways)
    squeeze.add()
    hidden.add()
    entry.add()
    height = key_weight.shape[1] // dp
    dq, dk, dv, all_keep, all_send, slope_parts = attend_back(
        where,
        height,
        slopes_own,
        queries,
        keys,
        values,
        after(grad_mixture, hidden.cut(), entry.cut(), squeeze.cut()),
        place,
        (lse_own, lse_other),
    )
    mix_out.wait(dq)

    def cut_heads(product):
        return product.reshape(blocks // 2, -1, height, width)

    all_send = dot(all_send, inputs_low).astype(BF16)
    all_keep = dot(after(all_keep, all_send), inputs_low).astype(BF16)
    hidden.add()
    entry.add()
    left = Shrink(cut_heads(all_keep), cut_heads(all_send), sideways, True)
    mix_out.add()
    left.add()
    mix_out.cut()
    mix_out.wait(left.cut())
    mix_out.add()
    squeeze.cut()
    squeeze.wait(dq)
    squeeze.add()
    g1_own, g1_sent, token_sums = tokens_back(
        where,
        tokens,
        x_other,
        after(dq, left.cut(), hidden.cut(), entry.cut(), mix_out.cut(), squeeze.array),
        dk,
        dv,
        qkv,
    )
    g1_got = swap(g1_sent)
    mix_out.wait(g1_sent)
    mix_out.add()
    for group in (hidden, entry):
        group.wait(g1_sent)
        group.add()
    (smalls,) = slots_back(
        where,
        compressed,
        memory,
        x_other,
        after(dk, mix_out.cut(), hidden.cut(), entry.cut()),
        dv,
        qkv,
        token_sums,
        slope_parts,
        early,
    )

    def joint(array, mask):
        return lax.ppermute(array, ("dp", "tm"), [(i, i ^ mask) for i in range(2 * dp)])

    smalls, g1_got = meet((left, hidden, entry, mix_out), smalls, g1_got)
    groups = (left, hidden, entry, mix_out, squeeze)
    masks = [1 << at for at in range(levels + 1)]
    out_part = None
    while masks:
        sends = [group.cut() for group in groups]
        smalls = after(smalls, *sends)
        if len(masks) > 1 and len(masks) % 2:
            smalls = smalls + joint(smalls, masks.pop(0))
        others = smalls, joint(smalls, masks.pop(0))
        if out_part is None:
            out_part = dot(after(act, *sends), hidden_weight)
            smalls, got, out_sent = meet(groups, *others, out_part[rows:].astype(BF16))
            out_got = swap(out_sent)
        else:
            smalls, got = meet(groups, *others)
        smalls = smalls + got
    output = (residual + (out_part[:rows] + out_got.astype(F32)) + hidden_bias).astype(BF16)
    new_compressed = (
        after(squeeze_stay, sends[0])[:slots] + squeeze_got[:slots].astype(F32) + compress_bias
    ).astype(BF16)
    g1 = g1_own + g1_got.astype(F32)
    unit1, rstd1 = rows_stats(tokens.astype(F32))
    grad_tokens = (grad_residual + norm_back(g1, norm1_gain, unit1, rstd1)).astype(BF16)

    grad_query_w, grad_key_w, grad_value_w = [part.T for part in left.finish()]
    grad_in_w = turned(entry.finish()[0])
    grad_hidden_w, grad_out_w, grad_compress_w = [
        group.finish()[0].T for group in (hidden, mix_out, squeeze)
    ]
    gain2, bias2, hidden_b, compress_b, gain1, bias1, slope = [
        smalls[i] for i in (0, 1, 6, 7, 8, 9, 10)
    ]
    in_b = smalls[2:6].reshape(-1)
    return (
        output[None],
        new_compressed[None],
        grad_tokens[None],
        gain1,
        bias1,
        grad_query_w,
        grad_key_w,
        grad_value_w,
        grad_out_w,
        slope[:heads],
        gain2,
        bias2,
        grad_in_w,
        in_b,
        grad_hidden_w,
        hidden_b,
        grad_compress_w,
        compress_b,
    )


def solution(mesh):
    split, whole, kept = P("dp", "tm", None), P(), P("tm", None)
    in_specs = (
        (split,) * 3
        + (P("dp"), whole, whole)
        + (kept,) * 4
        + (whole,) * 3
        + (kept, whole, kept, whole, kept, whole)
        + (split,) * 2
    )
    shared = P("tm", "dp")
    out_specs = (
        (split,) * 3
        + (whole,) * 2
        + (shared,) * 4
        + (whole,) * 3
        + (shared, whole, shared, whole, shared, whole)
    )
    return jax.shard_map(local, mesh=mesh, in_specs=in_specs, out_specs=out_specs, check_vma=False)
```

```python
import functools

import jax
import jax.numpy as jnp
from jax import lax
from jax.experimental import pallas as pl
from jax.experimental.pallas import tpu as pltpu
from jax.sharding import PartitionSpec as P

EPS = 1e-05
NEG = -1e30
LOG2E = 1.4426950408889634
F32 = jnp.float32
BF16 = jnp.bfloat16
TINY = pl.CostEstimate(flops=1000, bytes_accessed=1000, transcendentals=0)
LARGE = pl.CostEstimate(flops=20 * 10**9, bytes_accessed=10**6, transcendentals=0)
PARAMS = pltpu.CompilerParams(vmem_limit_bytes=32 * 2**20)
WIDE = pltpu.CompilerParams(vmem_limit_bytes=56 * 2**20)


def dot(a, b, dims=((1,), (0,))):
    return lax.dot_general(a, b, (dims, ((), ())), preferred_element_type=F32)


def dot_nt(a, b):
    return dot(a, b, ((1,), (1,)))


def dot_tn(a, b):
    return dot(a, b, ((0,), (0,)))


def rows_stats(x):
    mean = jnp.mean(x, -1, keepdims=True)
    centered = x - mean
    rstd = lax.rsqrt(jnp.mean(centered * centered, -1, keepdims=True) + EPS)
    return centered * rstd, rstd


def norm_back(grad, gain, normed, rstd):
    dn = grad * gain
    return rstd * (
        dn
        - jnp.mean(dn, -1, keepdims=True)
        - normed * jnp.mean(dn * normed, -1, keepdims=True)
    )


def spec(shape, at=None):
    zeros = (0,) * len(shape)
    return pl.BlockSpec(shape, at if at is not None else (lambda *_: zeros))


def call(
    kernel, name, where, grid, ins, outs, scratch=(), cost=TINY, onto=None, params=PARAMS
):
    onto = onto or {}
    count = len(ins)
    ins = list(ins) + [(array, pl.BlockSpec(memory_space=pl.ANY)) for array in onto.values()]

    def body(place, *refs):
        kernel(place, *refs[:count], *refs[len(ins) :])

    return pl.pallas_call(
        body,
        grid_spec=pltpu.PrefetchScalarGridSpec(
            num_scalar_prefetch=1,
            grid=grid,
            in_specs=[at for _, at in ins],
            out_specs=[at for _, _, at in outs],
            scratch_shapes=list(scratch),
        ),
        out_shape=[jax.ShapeDtypeStruct(shape, dtype) for shape, dtype, _ in outs],
        input_output_aliases={1 + count + i: out for i, out in enumerate(onto)},
        compiler_params=params,
        cost_estimate=cost,
        name=name,
    )(where, *[array for array, _ in ins])


def whole(array):
    return array, spec(array.shape)


def ordered(first, own, other, axis):
    return jnp.where(
        first, jnp.concatenate((own, other), axis), jnp.concatenate((other, own), axis)
    )


def place_pieces(where, parts, target, base=0, half=None):
    size = (half or target.shape[0]) // (where.shape[0] - 2)
    at = 0
    for part in parts:
        for block in range(part.shape[0] // size):
            row = pl.multiple_of(base + where[2 + at] * size, size)
            target[pl.ds(row, size), :] = part[block * size : (block + 1) * size, :]
            at += 1


def pieces_kernel(where, wq, wk, wv, wo, wi, joined):
    size = wq.shape[1]
    first, second = joined.at[:, : 3 * size], joined.at[:, 3 * size :]
    first[:, :size] = wq[...]
    first[:, size : 2 * size] = wk[...]
    first[:, 2 * size :] = wv[...]
    second[:, : wo.shape[1]] = wo[...]
    second[:, wo.shape[1] :] = wi[...]


def pieces(where, share, wq, wk, wv, wo, wi):
    rows = wq.shape[0] // share
    cols = wq.shape[1] // 2
    wide = wi.shape[1] // 2
    half = spec((rows, cols), lambda i, w: (w[0], w[1]))
    return call(
        pieces_kernel,
        "pieces",
        where,
        (1,),
        [
            (wq, half),
            (wk, half),
            (wv, half),
            (wo, spec((rows, wo.shape[1]), lambda i, w: (w[0], 0))),
            (wi, spec((rows, wide), lambda i, w: (w[0], w[1]))),
        ],
        [
            (
                (rows, 3 * cols + wo.shape[1] + wide),
                BF16,
                spec((rows, 3 * cols + wo.shape[1] + wide)),
            )
        ],
        params=WIDE,
    )


def project_rows(x, gain, shift, weights, low, q, k, v):
    cols = k.shape[1]
    unit, _ = rows_stats(x)
    n = (unit * gain[...] + shift[...]).astype(BF16)
    low[...] = n
    k[...] = dot(n, weights[:, cols : 2 * cols]).astype(BF16)
    v[...] = dot(n, weights[:, 2 * cols :]).astype(BF16)

    @pl.when(pl.program_id(0) == 2)
    def _():
        q[...] = dot(n, weights[:, :cols]).astype(BF16)


def project_own_kernel(
    where, comp, mem, tok, gain, shift, wq, wk, wv, mine, got, low, q, k, v, weights, x
):
    step = pl.program_id(0)
    half, cols = wq.shape
    for at, source in enumerate((comp, mem, tok)):

        @pl.when(step == at)
        def _(source=source):
            x[...] = source[...].astype(F32)

    @pl.when(step == 0)
    def _():
        own = pl.ds(pl.multiple_of(where[0] * half, half), half)
        for index, weight in enumerate((wq, wk, wv)):
            weights[own, index * cols : (index + 1) * cols] = weight[...]
        place_pieces(where, (mine, got), weights, (1 - where[0]) * half, half)

    project_rows(x[...], gain, shift, weights, low, q, k, v)


def project_other_kernel(where, other, gain, shift, weights, low, q, k, v):
    project_rows(other[...].astype(F32), gain, shift, weights, low, q, k, v)


def project_outs(rows, width, cols, turn):
    def by_step(size):
        return (6 * rows, size), BF16, spec((rows, size), lambda i, w: (2 * i + turn, 0))

    query = (2 * rows, cols), BF16, spec((rows, cols), lambda i, w: (turn, 0))
    return [by_step(width), query, by_step(cols), by_step(cols)]


def project_own(where, comp, mem, tok, gain, shift, wq, wk, wv, mine, got):
    rows, width = tok.shape
    cols = wq.shape[1] // 2
    half = spec((wq.shape[0], cols), lambda i, w: (0, w[0]))
    return call(
        project_own_kernel,
        "project_own",
        where,
        (3,),
        [whole(a) for a in (comp, mem, tok, gain[None], shift[None])]
        + [(wq, half), (wk, half), (wv, half), whole(mine), whole(got)],
        project_outs(rows, width, cols, 0)
        + [((width, 3 * cols), BF16, spec((width, 3 * cols)))],
        [pltpu.VMEM((rows, width), F32)],
        cost=LARGE,
        params=WIDE,
    )


def project_other(where, other, gain, shift, weights, filled):
    rows, width = other.shape[0] // 3, other.shape[1]
    return call(
        project_other_kernel,
        "project_other",
        where,
        (3,),
        [(other, spec((rows, width), lambda i, w: (i, 0)))]
        + [whole(a) for a in (gain[None], shift[None], weights)],
        project_outs(rows, width, weights.shape[1] // 3, 1),
        cost=LARGE,
        onto=dict(enumerate(filled)),
    )


def split_pairs(where, total, height, keep, send):
    pairs = total.reshape(total.shape[0] // (2 * height), 2, height, total.shape[1])
    even = where[1] == 0
    keep[...] = jnp.where(even, pairs[:, 0], pairs[:, 1]).astype(BF16)
    send[...] = jnp.where(even, pairs[:, 1], pairs[:, 0]).astype(BF16)


def by_parity(where, total, height):
    pairs = total.reshape(total.shape[0] // (2 * height), 2, height, total.shape[1])
    even = where[1] == 0
    shape = (total.shape[0] // 2, total.shape[1])
    keep = jnp.where(even, pairs[:, 0], pairs[:, 1]).reshape(shape)
    return keep, jnp.where(even, pairs[:, 1], pairs[:, 0]).reshape(shape)


def squeeze_kernel(slots, where, mem, other, dc, dc_o, weight, stay, away, keep, send, dc_sum):
    t = where[0]
    dc_sum[...] = jnp.sum(dc[...].astype(F32), 0, keepdims=True)
    rows, width = mem.shape
    mem_o = other.at[rows : 2 * rows, :]
    padded = dc.shape[0]
    half = width // 2
    lead = 3 * 2 * slots - 2 * rows
    first = t == 0
    shape = (padded, rows)
    slot = lax.broadcasted_iota(jnp.int32, shape, 0)
    row = lax.broadcasted_iota(jnp.int32, shape, 1)
    mem_half = jnp.where(first, mem[:, :half], mem[:, half:])
    mem_o_half = jnp.where(first, mem_o[:, :half], mem_o[:, half:])

    def picked(slot_half, row_half, offset):
        place = 3 * (slot + slot_half * slots) + offset - lead
        hit = (place == row + row_half * rows) & (slot < slots)
        return jnp.where(hit, 1.0, 0.0).astype(BF16)

    def windows(slot_half):
        edge = dot(picked(slot_half, t, 2 * t), mem[...]) + dot(
            picked(slot_half, 1 - t, 2 * t), mem_o[...]
        )
        middle = dot(picked(slot_half, t, 1), mem_half) + dot(
            picked(slot_half, 1 - t, 1), mem_o_half
        )
        return ordered(first, edge, middle, 1).astype(BF16)

    both = jnp.concatenate((windows(t), windows(1 - t)), 0)
    slots_out = dot(both, weight[...])
    stay[...] = slots_out[:padded, :]
    away[...] = slots_out[padded:, :].astype(BF16)
    turned_dc = jnp.concatenate((dc[...], dc_o[...]), 0).T
    columns = both.shape[1]
    height = keep.shape[1]
    for at in range(0, columns, half):
        part = slice(at, at + half)
        total = dot(turned_dc, both[:, part])
        split_pairs(where, total, height, keep.at[:, :, part], send.at[:, :, part])


def squeeze_rows(where, dp, slots, mem, other, dc, dc_o, weight):
    padded, width = dc.shape
    half = ((dp // 2, width // dp, weight.shape[0]), BF16)
    ins = [whole(a) for a in (mem, other, dc, dc_o, weight)]
    return call(
        functools.partial(squeeze_kernel, slots),
        "squeeze",
        where,
        (1,),
        ins,
        [
            ((padded, width), F32, spec((padded, width))),
            ((padded, width), BF16, spec((padded, width))),
            half + (spec(half[0]),),
            half + (spec(half[0]),),
            ((1, width), F32, spec((1, width))),
        ],
    )


def masked_scores(place, slope, q, keys, scale, first, tail):
    bias = place[0:1, :] * slope + place[1:2, :]
    chunk = q.shape[0]
    query_place = (lax.broadcasted_iota(jnp.int32, (chunk, 1), 0) + first).astype(F32)
    scores = dot_nt(q, keys) * (scale * LOG2E) + bias
    recent = jnp.where(place[0:1, tail:] <= query_place, scores[:, tail:], NEG)
    return jnp.concatenate((scores[:, :tail], recent), 1), query_place


def attend_kernel(turn, scale, where, slopes, q, k, v, place, mix, lse):
    slope = slopes[pl.program_id(0)] * LOG2E
    rows = q.shape[0]
    first = jnp.abs(turn - where[0]) * rows
    scores, _ = masked_scores(place, slope, q[...], k[...], scale, first, k.shape[0] - 2 * rows)
    highest = jnp.max(scores, -1, keepdims=True)
    weights = jnp.exp2(scores - highest)
    total = jnp.sum(weights, -1, keepdims=True)
    mix[...] = (dot(weights.astype(BF16), v[...]) * (1.0 / total)).astype(BF16)
    lse[0] = highest + jnp.log2(total)


def attend(where, turn, slopes, q, k, v, place):
    rows, width = q.shape[0] // 2, q.shape[1]
    heads = slopes.shape[0]
    hw = width // heads
    keys = k.shape[0]
    by_head = spec((keys, hw), lambda h, w: (0, h))
    return call(
        functools.partial(attend_kernel, turn, hw**-0.5),
        "attend",
        where,
        (heads,),
        [
            (slopes, pl.BlockSpec(memory_space=pltpu.SMEM)),
            (q, spec((rows, hw), lambda h, w: (turn, h))),
            (k, by_head),
            (v, by_head),
            whole(place),
        ],
        [
            ((rows, width), BF16, spec((rows, hw), lambda h, w: (0, h))),
            ((heads, rows, 1), F32, spec((1, rows, 1), lambda h, w: (h, 0, 0))),
        ],
        cost=LARGE,
    )


def attend_back_kernel(
    chunk,
    scale,
    height,
    where,
    slopes,
    q,
    k,
    v,
    dm,
    place,
    lse_own,
    lse_other,
    dq,
    dk,
    dv,
    all_keep,
    all_send,
    slope_out,
    dk_sum,
    dv_sum,
):
    slope = slopes[pl.program_id(0)] * LOG2E
    keys = k.shape[0]
    rows = q.shape[0]
    half = rows // 2
    columns = jnp.zeros((1, keys), F32)
    by_row = jnp.zeros((1, 1), F32)
    dq_parts = []
    for step in range(rows // chunk):
        at = slice(step * chunk, (step + 1) * chunk)
        time_half = where[0] if step * chunk < half else 1 - where[0]
        scores, query_place = masked_scores(
            place,
            slope,
            q[at, :],
            k[...],
            scale,
            time_half * half + step * chunk % half,
            keys - rows,
        )
        weights = jnp.exp2(scores - (lse_own if step == 0 else lse_other)[0])
        low = weights.astype(BF16)
        grads = dot_nt(dm[at, :], v[...])
        shift = jnp.sum(weights * grads, -1, keepdims=True)
        ds = (weights * (grads - shift)).astype(BF16)
        dq_part = dot(ds, k[...]) * scale
        dq[at, :] = dq_part.astype(BF16)
        dq_parts.append(dq_part.T)
        dk_part = dot_tn(q[at, :], ds)
        dv_part = dot_tn(dm[at, :], low)
        if step == 0:
            dk_sum[...] = dk_part
            dv_sum[...] = dv_part
        else:
            dk_sum[...] += dk_part
            dv_sum[...] += dv_part
        wide = ds.astype(F32)
        columns += jnp.sum(wide, 0, keepdims=True)
        by_row += jnp.sum(jnp.sum(wide, -1, keepdims=True) * query_place, 0, keepdims=True)
    dk_all, dv_all = dk_sum[...] * scale, dv_sum[...]
    dq_all = jnp.concatenate([jnp.zeros((dk_all.shape[0], keys - rows), F32)] + dq_parts, 1)
    halves = [by_parity(where, part, height) for part in (dq_all, dk_all, dv_all)]
    for target, parts in zip((all_keep, all_send), zip(*halves)):
        blocks = [part.reshape(part.shape[0] // height, height, keys) for part in parts]
        target[...] = jnp.stack(blocks, 1).reshape(target.shape).astype(BF16)
    dk[...] = dk_all.T.astype(BF16)
    dv[...] = dv_all.T.astype(BF16)
    total = jnp.sum(columns * place[0:1, :], -1, keepdims=True) - by_row
    slope_out[...] = jnp.broadcast_to(total.reshape(1, 1, 1), slope_out.shape)


def attend_back(where, height, slopes, q, k, v, dm, place, lses):
    rows, width = q.shape
    heads = slopes.shape[0]
    hw = width // heads
    keys = k.shape[0]
    by_rows = spec((rows, hw), lambda h, w: (0, h))
    by_keys = spec((keys, hw), lambda h, w: (0, h))
    return call(
        functools.partial(attend_back_kernel, rows // 2, hw**-0.5, height),
        "attend_back",
        where,
        (heads,),
        [
            (slopes, pl.BlockSpec(memory_space=pltpu.SMEM)),
            (q, by_rows),
            (k, by_keys),
            (v, by_keys),
            (dm, by_rows),
            whole(place),
            (lses[0], spec((1, rows // 2, 1), lambda h, w: (h, 0, 0))),
            (lses[1], spec((1, rows // 2, 1), lambda h, w: (h, 0, 0))),
        ],
        [
            ((rows, width), BF16, by_rows),
            ((keys, width), BF16, by_keys),
            ((keys, width), BF16, by_keys),
            ((3 * width // 2, keys), BF16, spec((3 * hw // 2, keys), lambda h, w: (h, 0))),
            ((3 * width // 2, keys), BF16, spec((3 * hw // 2, keys), lambda h, w: (h, 0))),
            ((heads, 8, 128), F32, spec((1, 8, 128), lambda h, w: (h, 0, 0))),
        ],
        [pltpu.VMEM((hw, keys), F32), pltpu.VMEM((hw, keys), F32)],
        cost=LARGE,
    )


def gelu_pair(v):
    c = 0.7978845608028654
    inner = c * (v + 0.044715 * v * v * v)
    th = jnp.tanh(inner)
    slope = 0.5 * (1.0 + th) + 0.5 * v * (1.0 - th * th) * c * (1.0 + 3 * 0.044715 * v * v)
    return 0.5 * v * (1.0 + th), slope


def feed_kernel(height, block, where, *refs):
    (
        mix,
        far,
        tok,
        wo,
        wo_mine,
        wo_got,
        gain,
        shift,
        dy,
        wi,
        wi_mine,
        wi_got,
        bias,
        wh,
        residual,
        normed,
        act,
        grad_keep,
        grad_send,
        dy_keep,
        dy_send,
        g2,
        bias_sum,
        dy_sum,
        *sent,
        wo_far,
        weight,
    ) = refs
    step = pl.program_id(0)
    half = wi.shape[0]

    @pl.when(step == 0)
    def _():
        place_pieces(where, (wo_mine, wo_got), wo_far)
        wide_dy = dy[...].astype(F32)
        dy_sum[...] = jnp.sum(wide_dy, 0, keepdims=True)
        dy_stay, dy_away = by_parity(where, wide_dy.T, height)
        dy_keep[...] = dy_stay.astype(BF16)
        dy_send[...] = dy_away.astype(BF16)
        total = tok[...].astype(F32) + (dot(mix[...], wo[...]) + dot(far[...], wo_far[...]))
        residual[...] = total
        unit, _ = rows_stats(total)
        normed[...] = (unit * gain[...] + shift[...]).astype(BF16)

    weight[pl.ds(pl.multiple_of(where[0] * half, half), half), :] = wi[...]
    place_pieces(where, (wi_mine, wi_got), weight, (1 - where[0]) * half, half)
    pre = dot(normed[...], weight[...]) + bias[...]
    value, slope = gelu_pair(pre)
    low = value.astype(BF16)
    act[...] = low
    grad = (dot_nt(dy[...], wh[...]) * slope).astype(BF16)
    blocks = [grad[:, at : at + block] for at in range(0, grad.shape[1], block)]
    evens, odds = jnp.concatenate(blocks[::2], 1), jnp.concatenate(blocks[1::2], 1)
    even = where[1] == 0
    grad_keep[...] = jnp.where(even, evens, odds)
    grad_send[...] = jnp.where(even, odds, evens)
    bias_sum[...] = jnp.sum(grad.astype(F32), 0, keepdims=True)
    g2_part = dot_nt(grad, weight[...])

    @pl.when(step == 0)
    def _():
        g2[...] = g2_part

    @pl.when(step > 0)
    def _():
        g2[...] += g2_part

    @pl.when(step == pl.num_programs(0) - 1)
    def _():
        first_row = 0
        for piece in sent:
            piece[...] = g2[first_row : first_row + piece.shape[0], :].astype(BF16)
            first_row += piece.shape[0]


def feed(
    where, dp, turn, mix, far, tok, wo, gain, shift, dy, wi, bias, wh, second, chunk, parts, onto
):
    rows, width = dy.shape
    hidden = wh.shape[0]
    steps = hidden // chunk
    mine, got = second
    by_cols = spec((rows, chunk), lambda j, w: (turn, j))
    by_half = spec((rows, chunk // 2), lambda j, w: (turn, j))
    half = (2 * rows, hidden // 2), BF16, by_half
    turned = (width // 2, 2 * rows), BF16, spec((width // 2, rows), lambda j, w: (0, turn))
    wo_part = spec((mine.shape[0], width), lambda j, w: (0, 0))
    wi_part = spec((mine.shape[0], chunk), lambda j, w: (0, width // chunk + j))

    def once(dtype):
        return (rows, width), dtype, spec((rows, width))

    return call(
        functools.partial(feed_kernel, width // dp, hidden // (dp // 2)),
        "feed",
        where,
        (steps,),
        [
            whole(mix),
            whole(far),
            (tok, spec((rows, width), lambda j, w: (2 * turn, 0))),
            whole(wo),
            (mine, wo_part),
            (got, wo_part),
            whole(gain[None]),
            whole(shift[None]),
            whole(dy),
            (wi, spec((wi.shape[0], chunk), lambda j, w: (0, w[0] * steps + j))),
            (mine, wi_part),
            (got, wi_part),
            (bias[None], spec((1, chunk), lambda j, w: (0, w[0] * steps + j))),
            (wh, spec((chunk, width), lambda j, w: (j, 0))),
        ],
        [
            once(F32),
            ((2 * rows, width), BF16, spec((rows, width), lambda j, w: (turn, 0))),
            ((2 * rows, hidden), BF16, by_cols),
            half,
            half,
            turned,
            turned,
            once(F32),
            ((1, hidden), F32, spec((1, chunk), lambda j, w: (0, j))),
            ((1, width), F32, spec((1, width))),
        ]
        + [((rows // part, width), BF16, spec((rows // part, width))) for part in parts],
        [
            pltpu.VMEM(wo.shape, BF16),
            pltpu.VMEM((width, chunk), BF16),
        ],
        cost=LARGE,
        onto=onto,
    )


def middle_kernel(
    where,
    g_own,
    g_other,
    got_own,
    got_other,
    residual_own,
    residual_other,
    gain,
    dy,
    dy_o,
    wo,
    mix_own,
    mix_other,
    bias_sum,
    bias_sum_o,
    dy_sum,
    dc_sum,
    grad_res,
    dm,
    sums,
    keep,
    send,
):
    rows = dy.shape[0]
    lows = []
    halves = ((g_own, got_own, dy, residual_own), (g_other, got_other, dy_o, residual_other))
    for at, (g, got, d, residual) in enumerate(halves):
        here = slice(at * rows, (at + 1) * rows)
        grad = g[...] + got[...].astype(F32)
        unit, rstd = rows_stats(residual[...])
        total = d[...].astype(F32) + norm_back(grad, gain[...], unit, rstd)
        low = total.astype(BF16)
        lows.append(low)
        dm[here, :] = dot_nt(low, wo[...]).astype(BF16)
        if at == 0:
            grad_res[...] = total
            small = [jnp.sum(grad * unit, 0, keepdims=True), jnp.sum(grad, 0, keepdims=True)]
    width = dy.shape[1]
    first = where[0] == 0
    parts = [slice(at, at + width) for at in range(0, bias_sum.shape[1], width)]
    downs = [bias_sum[:, part] + bias_sum_o[:, part] for part in parts]
    small += [jnp.where(first, down, 0.0) for down in downs]
    small += [jnp.where(first, 0.0, down) for down in downs]
    small += [dy_sum[...], dc_sum[...]]
    sums[...] = jnp.concatenate(small, 0)
    split_pairs(
        where, dot_tn(lows[0], mix_own[...]) + dot_tn(lows[1], mix_other[...]), keep.shape[1], keep, send
    )


def middle(where, dp, g, got, residuals, gain, dys, wo, mix, small):
    rows, width = dys[0].shape
    heads = wo.shape[0]
    half = ((dp // 2, width // dp, heads), BF16, spec((dp // 2, width // dp, heads)))
    return call(
        middle_kernel,
        "middle",
        where,
        (1,),
        [whole(a) for a in (*g, *got, *residuals, gain[None], *dys, wo, *mix, *small)],
        [
            ((rows, width), F32, spec((rows, width))),
            ((2 * rows, heads), BF16, spec((2 * rows, heads))),
            ((8, width), F32, spec((8, width))),
            half,
            half,
        ],
        cost=LARGE,
    )


def norm_sums(step, grad, x, sums):
    unit, _ = rows_stats(x)
    rows = jnp.sum(grad * unit, 0, keepdims=True), jnp.sum(grad, 0, keepdims=True)

    @pl.when(step == 0)
    def _():
        sums[0:1, :], sums[1:2, :] = rows

    @pl.when(step > 0)
    def _():
        sums[0:1, :] += rows[0]
        sums[1:2, :] += rows[1]


def tokens_kernel(where, tok, other, dq, dk, dv, weights, g_own, sent, sums):
    step = pl.program_id(0)
    cols = dq.shape[1]
    grad = (
        dot_nt(dq[...], weights[:, :cols])
        + dot_nt(dk[...], weights[:, cols : 2 * cols])
        + dot_nt(dv[...], weights[:, 2 * cols :])
    )
    x = jnp.where(step == 0, tok[...].astype(F32), other[...].astype(F32))
    norm_sums(step, grad, x, sums)

    @pl.when(step == 0)
    def _():
        g_own[...] = grad

    @pl.when(step == 1)
    def _():
        sent[...] = grad.astype(BF16)


def tokens_back(where, tok, other, dq, dk, dv, weights):
    rows, width = tok.shape
    cols = dk.shape[1]
    late = spec((rows, cols), lambda i, w: (4 + i, 0))
    return call(
        tokens_kernel,
        "tokens_back",
        where,
        (2,),
        [
            whole(tok),
            (other, spec((rows, width), lambda i, w: (2, 0))),
            (dq, spec((rows, cols), lambda i, w: (i, 0))),
            (dk, late),
            (dv, late),
            whole(weights),
        ],
        [
            ((rows, width), F32, spec((rows, width))),
            ((rows, width), BF16, spec((rows, width))),
            ((2, width), F32, spec((2, width))),
        ],
    )


def slots_kernel(
    where, comp, mem, other, dk, dv, weights, start, slope_parts, early, sums, total
):
    step = pl.program_id(0)
    cols = dk.shape[1]
    grad = dot_nt(dk[...], weights[:, cols : 2 * cols]) + dot_nt(dv[...], weights[:, 2 * cols :])
    own = jnp.where(step == 0, comp[...].astype(F32), mem[...].astype(F32))
    x = jnp.where(step % 2 == 0, own, other[...].astype(F32))
    norm_sums(step, grad, x, total)

    @pl.when(step == pl.num_programs(0) - 1)
    def _():
        width = comp.shape[1]
        lane = lax.broadcasted_iota(jnp.int32, (1, width), 1)
        own_heads = slope_parts.shape[0]
        slope = jnp.zeros((1, width), F32)
        for head in range(own_heads):
            here = lane == where[0] * own_heads + head
            slope += jnp.where(here, slope_parts[head, 0:1, 0:1], 0.0)
        sums[:8, :] = early[...]
        rest = (total[...] + start[...], slope, jnp.zeros((5, width), F32))
        sums[8:, :] = jnp.concatenate(rest, 0)


def slots_back(where, comp, mem, other, dk, dv, weights, start, slope_parts, early):
    rows, width = comp.shape
    cols = dk.shape[1]
    by_step = spec((rows, cols), lambda i, w: (i, 0))
    return call(
        slots_kernel,
        "slots_back",
        where,
        (4,),
        [
            whole(comp),
            whole(mem),
            (other, spec((rows, width), lambda i, w: (i // 2, 0))),
            (dk, by_step),
            (dv, by_step),
            whole(weights),
            whole(start),
            whole(slope_parts),
            whole(early),
        ],
        [((16, width), F32, spec((16, width)))],
        [pltpu.VMEM((2, width), F32)],
        cost=LARGE,
    )


def turn_kernel(source, target):
    target[...] = source[...].T


def turned(array):
    return pl.pallas_call(
        turn_kernel,
        out_shape=jax.ShapeDtypeStruct(array.shape[::-1], F32),
        compiler_params=PARAMS,
        cost_estimate=TINY,
        name="turn",
    )(array)


def local(
    tokens,
    memory,
    compressed,
    mask_start,
    norm1_gain,
    norm1_bias,
    query_weight,
    key_weight,
    value_weight,
    out_weight,
    slopes,
    norm2_gain,
    norm2_bias,
    in_weight,
    in_bias,
    hidden_weight,
    hidden_bias,
    compress_weight,
    compress_bias,
    grad_out,
    grad_compressed,
):
    tokens, memory, compressed = tokens[0], memory[0], compressed[0]
    grad_out, grad_compressed = grad_out[0], grad_compressed[0]
    rows, width = tokens.shape
    heads = slopes.shape[0]
    dp = lax.axis_size("dp")
    levels = dp.bit_length() - 1
    top = levels - 1
    d = lax.axis_index("dp")
    t = lax.axis_index("tm")
    segment = 2 * rows

    def swap(block):
        return lax.ppermute(block, "tm", [(0, 1), (1, 0)])

    def across(block, mask):
        return lax.ppermute(block, "dp", [(i, i ^ mask) for i in range(dp)])

    def after(array, *earlier):
        return lax.optimization_barrier((array,) + earlier)[0]

    def bit(level):
        return (d >> level) & 1

    class Shrink:
        def __init__(self, keep, send, order, columns=False):
            shape = keep.shape if keep.ndim == 4 else keep.shape[:1] + (1,) + keep.shape[1:]
            self.pending = keep.reshape(shape), send.reshape(shape), 1
            self.order = [0] + order
            self.left = [level for level in range(1, top if columns else levels)]
            self.step = 0
            self.array = None

        def cut(self):
            if self.pending is not None:
                return self.pending[1]
            if self.step == len(self.order):
                return self.array
            level = self.order[self.step]
            if level in self.left:
                low = 1 << self.left.index(level)
                blocks, rest = self.array.shape[0], self.array.shape[1:]
                split = self.array.reshape((blocks // (2 * low), 2, low) + rest)
                keep, send = [
                    lax.dynamic_index_in_dim(split, at, 1, keepdims=False).reshape(
                        (blocks // 2,) + rest
                    )
                    for at in (bit(level), 1 - bit(level))
                ]
                self.left.remove(level)
                self.pending = keep, send, 1 << level
            else:
                size = self.array.shape[3] // 2
                keep, send = [
                    lax.dynamic_slice_in_dim(self.array, at * size, size, 3) for at in (t, 1 - t)
                ]
                self.pending = keep, send, 0
            return send

        def move(self):
            send = self.cut()
            return across(send, self.pending[2]) if self.pending[2] else swap(send)

        def take(self, got):
            keep, _, mask = self.pending
            if mask == 0:
                same = bit(top) == t
                self.pending = jnp.where(same, keep, got), jnp.where(same, got, keep), 1 << top
                return self.pending[1]
            self.step += 1
            total = keep.astype(F32) + got.astype(F32)
            last = self.step == len(self.order)
            self.array = total if last else total.astype(BF16)
            self.pending = None
            return self.array

        def add(self):
            if self.step == len(self.order):
                return self.array
            self.cut()
            if self.pending[2] == 0:
                self.take(self.move())
            return self.take(self.move())

        def wait(self, *earlier):
            if self.pending is not None:
                self.pending = (after(self.pending[0], *earlier),) + self.pending[1:]

        def finish(self):
            while self.step < len(self.order):
                self.add()
            return self.array[0]

    def meet(groups, *others):
        groups = [group for group in groups if group.step < len(group.order)]
        got = lax.optimization_barrier(tuple(group.move() for group in groups) + others)
        for group, block in zip(groups, got):
            group.take(block)
        for group in groups:
            group.cut()
        return got[len(groups) :]

    sideways = list(range(1, levels))
    upward = list(range(2, levels)) + [1] if levels > 1 else []
    between = upward[:1] + upward[-1:] + upward[1:-1] if levels > 2 else upward

    sharing = min(levels, 4)
    share = 1 << sharing
    ups = [z << 2 for z in range(1 << max(sharing - 2, 0))]
    offsets = [x + z for x in ((0, 2) if sharing > 1 else (0,)) for z in ups]
    low_bits = d & (share - 1)
    targets = [low_bits ^ off for off in offsets] + [low_bits ^ off ^ 1 for off in offsets]
    where = jnp.stack([t, bit(0)] + targets).astype(jnp.int32)

    def gather_up(piece):
        return jnp.concatenate([piece] + [across(piece, z) for z in ups[1:]], 0)

    def gather_side(block):
        return jnp.concatenate((block, across(block, 2)), 0) if sharing > 1 else block

    (joined,) = pieces(
        jnp.stack((low_bits, 1 - t)).astype(jnp.int32),
        share,
        query_weight,
        key_weight,
        value_weight,
        out_weight,
        in_weight,
    )
    joined = swap(joined)
    first_size = 3 * query_weight.shape[1] // 2
    first, second = joined[:, :first_size], joined[:, first_size:]
    slots = grad_compressed.shape[0]
    dc = jnp.pad(grad_compressed, ((0, -slots % 16), (0, 0)))
    x_other = swap(jnp.concatenate((compressed, memory, tokens), 0))
    first_up = gather_up(first)
    first = gather_side(first_up)
    first_got = across(first, 1)
    second_up = gather_up(after(second, first_got))
    second = gather_side(second_up)

    *filled, qkv = project_own(
        where,
        compressed,
        memory,
        tokens,
        norm1_gain,
        norm1_bias,
        query_weight,
        key_weight,
        value_weight,
        first,
        first_got,
    )
    inputs_low, queries, keys, values = project_other(
        where, x_other, norm1_gain, norm1_bias, qkv, filled
    )
    dc_other = swap(after(dc, queries))

    index = jnp.arange(segment, dtype=jnp.int32)
    slot = jnp.where(index < rows, index + t * rows, index - rows + (1 - t) * rows)
    place = jnp.concatenate((-segment - 3 * (segment - slot), slot - segment, slot)).astype(F32)
    closed = jnp.where(slot >= mask_start[0], 0.0, NEG)
    closed = jnp.concatenate((closed, jnp.zeros((2 * segment,), F32)))
    place = jnp.stack((place, closed))
    own_heads = heads // 2
    slopes_own = lax.dynamic_slice_in_dim(slopes, t * own_heads, own_heads, 0)
    mix_other, lse_other = attend(
        where, 1, slopes_own, after(queries, second_up), keys, values, place
    )
    far_own = swap(mix_other)
    dy_other = swap(after(grad_out, mix_other))
    squeeze_stay, squeeze_away, keep, send, dc_sum = squeeze_rows(
        where, dp, slots, after(memory, mix_other), x_other, dc, dc_other, compress_weight
    )
    squeeze = Shrink(keep, send, sideways)
    squeeze_got = swap(squeeze_away)
    mix_own, lse_own = attend(
        where, 0, slopes_own, after(queries, squeeze_away), keys, values, place
    )
    far_other = swap(mix_own)
    second_got = across(after(second, mix_own), 1)
    dys = grad_out, dy_other
    mix = mix_own, mix_other
    chunk = max(in_weight.shape[1] // 8, 2 * in_weight.shape[1] // dp)

    def feed_rows(turn, mixed, far, tok, dy, parts, onto=None):
        return feed(
            where,
            dp,
            turn,
            mixed,
            far,
            tok,
            out_weight,
            norm2_gain,
            norm2_bias,
            dy,
            in_weight,
            in_bias,
            hidden_weight,
            (second, second_got),
            chunk,
            parts,
            onto,
        )

    squeeze.add()
    residual, *half_filled, g_own, bias_sum, dy_sum, sent = feed_rows(
        0, after(mix_own, squeeze.cut()), far_own, tokens, grad_out, (1,)
    )
    got_other = swap(sent)
    residual_o, *filled, g_other, bias_sum_o, _, sent = feed_rows(
        1,
        after(mix_other, sent, squeeze_got),
        far_other,
        x_other,
        dy_other,
        (1,),
        {1 + i: array for i, array in enumerate(half_filled)},
    )
    got = swap(sent), got_other
    normed, act, grad_keep, grad_send, dy_keep, dy_send = filled
    squeeze.wait(sent, got_other)
    squeeze.add()
    blocks = dp // 2

    def cut_rows(product, count):
        return product.astype(BF16).reshape(count, product.shape[0] // count, product.shape[1])

    hidden_send = dot(after(dy_send, squeeze.cut(), got_other), act).astype(BF16)
    entry_send = dot_tn(after(grad_send, hidden_send), normed).astype(BF16)
    hidden_keep = dot(after(dy_keep, entry_send), act).astype(BF16)
    entry_keep = dot_tn(after(grad_keep, hidden_keep), normed).astype(BF16)
    hidden = Shrink(cut_rows(hidden_keep, blocks), cut_rows(hidden_send, blocks), sideways)
    entry = Shrink(
        cut_rows(entry_keep, blocks // 2), cut_rows(entry_send, blocks // 2), between, True
    )
    got = after(got[0], entry_keep), got[1]
    grad_residual, grad_mixture, early, keep, send = middle(
        where,
        dp,
        (after(g_own, entry_keep), g_other),
        got,
        (residual, residual_o),
        norm2_gain,
        dys,
        out_weight,
        mix,
        (bias_sum, bias_sum_o, dy_sum, dc_sum),
    )
    mix_out = Shrink(keep, send, upward)
    squeeze.add()
    hidden.add()
    entry.add()
    height = key_weight.shape[1] // dp
    dq, dk, dv, all_keep, all_send, slope_parts = attend_back(
        where,
        height,
        slopes_own,
        queries,
        keys,
        values,
        after(grad_mixture, hidden.cut(), entry.cut(), squeeze.cut()),
        place,
        (lse_own, lse_other),
    )
    mix_out.wait(dq)

    def cut_heads(product):
        return product.reshape(blocks // 2, -1, height, width)

    all_send = dot(all_send, inputs_low).astype(BF16)
    all_keep = dot(after(all_keep, all_send), inputs_low).astype(BF16)
    hidden.add()
    entry.add()
    left = Shrink(cut_heads(all_keep), cut_heads(all_send), sideways, True)
    mix_out.add()
    left.add()
    mix_out.cut()
    mix_out.wait(left.cut())
    mix_out.add()
    squeeze.cut()
    squeeze.wait(dq)
    squeeze.add()
    g1_own, g1_sent, token_sums = tokens_back(
        where,
        tokens,
        x_other,
        after(dq, left.cut(), hidden.cut(), entry.cut(), mix_out.cut(), squeeze.array),
        dk,
        dv,
        qkv,
    )
    g1_got = swap(g1_sent)
    mix_out.wait(g1_sent)
    mix_out.add()
    for group in (hidden, entry):
        group.wait(g1_sent)
        group.add()
    (smalls,) = slots_back(
        where,
        compressed,
        memory,
        x_other,
        after(dk, mix_out.cut(), hidden.cut(), entry.cut()),
        dv,
        qkv,
        token_sums,
        slope_parts,
        early,
    )

    def joint(array, mask):
        return lax.ppermute(array, ("dp", "tm"), [(i, i ^ mask) for i in range(2 * dp)])

    smalls, g1_got = meet((left, hidden, entry, mix_out), smalls, g1_got)
    groups = (left, hidden, entry, mix_out, squeeze)
    masks = [1 << at for at in range(levels + 1)]
    out_part = None
    while masks:
        sends = [group.cut() for group in groups]
        smalls = after(smalls, *sends)
        if len(masks) > 1 and len(masks) % 2:
            smalls = smalls + joint(smalls, masks.pop(0))
        others = smalls, joint(smalls, masks.pop(0))
        if out_part is None:
            out_part = dot(after(act, *sends), hidden_weight)
            smalls, got, out_sent = meet(groups, *others, out_part[rows:].astype(BF16))
            out_got = swap(out_sent)
        else:
            smalls, got = meet(groups, *others)
        smalls = smalls + got
    output = (residual + (out_part[:rows] + out_got.astype(F32)) + hidden_bias).astype(BF16)
    new_compressed = (
        after(squeeze_stay, sends[0])[:slots] + squeeze_got[:slots].astype(F32) + compress_bias
    ).astype(BF16)
    g1 = g1_own + g1_got.astype(F32)
    unit1, rstd1 = rows_stats(tokens.astype(F32))
    grad_tokens = (grad_residual + norm_back(g1, norm1_gain, unit1, rstd1)).astype(BF16)

    grad_query_w, grad_key_w, grad_value_w = [part.T for part in left.finish()]
    grad_in_w = turned(entry.finish()[0])
    grad_hidden_w, grad_out_w, grad_compress_w = [
        group.finish()[0].T for group in (hidden, mix_out, squeeze)
    ]
    gain2, bias2, hidden_b, compress_b, gain1, bias1, slope = [
        smalls[i] for i in (0, 1, 6, 7, 8, 9, 10)
    ]
    in_b = smalls[2:6].reshape(-1)
    return (
        output[None],
        new_compressed[None],
        grad_tokens[None],
        gain1,
        bias1,
        grad_query_w,
        grad_key_w,
        grad_value_w,
        grad_out_w,
        slope[:heads],
        gain2,
        bias2,
        grad_in_w,
        in_b,
        grad_hidden_w,
        hidden_b,
        grad_compress_w,
        compress_b,
    )


def solution(mesh):
    split, whole, kept = P("dp", "tm", None), P(), P("tm", None)
    in_specs = (
        (split,) * 3
        + (P("dp"), whole, whole)
        + (kept,) * 4
        + (whole,) * 3
        + (kept, whole, kept, whole, kept, whole)
        + (split,) * 2
    )
    shared = P("tm", "dp")
    out_specs = (
        (split,) * 3
        + (whole,) * 2
        + (shared,) * 4
        + (whole,) * 3
        + (shared, whole, shared, whole, shared, whole)
    )
    return jax.shard_map(local, mesh=mesh, in_specs=in_specs, out_specs=out_specs, check_vma=False)
```

```python
import functools

import jax
import jax.numpy as jnp
from jax import lax
from jax.experimental import pallas as pl
from jax.experimental.pallas import tpu as pltpu
from jax.sharding import PartitionSpec as P

EPS = 1e-05
NEG = -1e30
LOG2E = 1.4426950408889634
F32 = jnp.float32
BF16 = jnp.bfloat16
TINY = pl.CostEstimate(flops=1000, bytes_accessed=1000, transcendentals=0)
LARGE = pl.CostEstimate(flops=20 * 10**9, bytes_accessed=10**6, transcendentals=0)
PARAMS = pltpu.CompilerParams(vmem_limit_bytes=32 * 2**20)
WIDE = pltpu.CompilerParams(vmem_limit_bytes=56 * 2**20)


def dot(a, b, dims=((1,), (0,))):
    return lax.dot_general(a, b, (dims, ((), ())), preferred_element_type=F32)


def dot_nt(a, b):
    return dot(a, b, ((1,), (1,)))


def dot_tn(a, b):
    return dot(a, b, ((0,), (0,)))


def rows_stats(x):
    mean = jnp.mean(x, -1, keepdims=True)
    centered = x - mean
    rstd = lax.rsqrt(jnp.mean(centered * centered, -1, keepdims=True) + EPS)
    return centered * rstd, rstd


def norm_back(grad, gain, normed, rstd):
    dn = grad * gain
    return rstd * (
        dn
        - jnp.mean(dn, -1, keepdims=True)
        - normed * jnp.mean(dn * normed, -1, keepdims=True)
    )


def spec(shape, at=None):
    zeros = (0,) * len(shape)
    return pl.BlockSpec(shape, at if at is not None else (lambda *_: zeros))


def call(
    kernel, name, where, grid, ins, outs, scratch=(), cost=TINY, onto=None, params=PARAMS
):
    onto = onto or {}
    count = len(ins)
    ins = list(ins) + [(array, pl.BlockSpec(memory_space=pl.ANY)) for array in onto.values()]

    def body(place, *refs):
        kernel(place, *refs[:count], *refs[len(ins) :])

    return pl.pallas_call(
        body,
        grid_spec=pltpu.PrefetchScalarGridSpec(
            num_scalar_prefetch=1,
            grid=grid,
            in_specs=[at for _, at in ins],
            out_specs=[at for _, _, at in outs],
            scratch_shapes=list(scratch),
        ),
        out_shape=[jax.ShapeDtypeStruct(shape, dtype) for shape, dtype, _ in outs],
        input_output_aliases={1 + count + i: out for i, out in enumerate(onto)},
        compiler_params=params,
        cost_estimate=cost,
        name=name,
    )(where, *[array for array, _ in ins])


def whole(array):
    return array, spec(array.shape)


def ordered(first, own, other, axis):
    return jnp.where(
        first, jnp.concatenate((own, other), axis), jnp.concatenate((other, own), axis)
    )


def place_pieces(where, parts, target, base=0, half=None):
    size = (half or target.shape[0]) // (where.shape[0] - 2)
    at = 0
    for part in parts:
        for block in range(part.shape[0] // size):
            row = pl.multiple_of(base + where[2 + at] * size, size)
            target[pl.ds(row, size), :] = part[block * size : (block + 1) * size, :]
            at += 1


def pieces_kernel(where, wq, wk, wv, wo, wi, joined):
    size = wq.shape[1]
    first, second = joined.at[:, : 3 * size], joined.at[:, 3 * size :]
    first[:, :size] = wq[...]
    first[:, size : 2 * size] = wk[...]
    first[:, 2 * size :] = wv[...]
    second[:, : wo.shape[1]] = wo[...]
    second[:, wo.shape[1] :] = wi[...]


def pieces(where, share, wq, wk, wv, wo, wi):
    rows = wq.shape[0] // share
    cols = wq.shape[1] // 2
    wide = wi.shape[1] // 2
    half = spec((rows, cols), lambda i, w: (w[0], w[1]))
    return call(
        pieces_kernel,
        "pieces",
        where,
        (1,),
        [
            (wq, half),
            (wk, half),
            (wv, half),
            (wo, spec((rows, wo.shape[1]), lambda i, w: (w[0], 0))),
            (wi, spec((rows, wide), lambda i, w: (w[0], w[1]))),
        ],
        [
            (
                (rows, 3 * cols + wo.shape[1] + wide),
                BF16,
                spec((rows, 3 * cols + wo.shape[1] + wide)),
            )
        ],
        params=WIDE,
    )


def project_rows(x, gain, shift, weights, low, q, k, v):
    cols = k.shape[1]
    unit, _ = rows_stats(x)
    n = (unit * gain[...] + shift[...]).astype(BF16)
    low[...] = n
    k[...] = dot(n, weights[:, cols : 2 * cols]).astype(BF16)
    v[...] = dot(n, weights[:, 2 * cols :]).astype(BF16)

    @pl.when(pl.program_id(0) == 2)
    def _():
        q[...] = dot(n, weights[:, :cols]).astype(BF16)


def project_own_kernel(
    where, comp, mem, tok, gain, shift, wq, wk, wv, mine, got, low, q, k, v, weights, x
):
    step = pl.program_id(0)
    half, cols = wq.shape
    for at, source in enumerate((comp, mem, tok)):

        @pl.when(step == at)
        def _(source=source):
            x[...] = source[...].astype(F32)

    @pl.when(step == 0)
    def _():
        own = pl.ds(pl.multiple_of(where[0] * half, half), half)
        for index, weight in enumerate((wq, wk, wv)):
            weights[own, index * cols : (index + 1) * cols] = weight[...]
        place_pieces(where, (mine, got), weights, (1 - where[0]) * half, half)

    project_rows(x[...], gain, shift, weights, low, q, k, v)


def project_other_kernel(where, other, gain, shift, weights, low, q, k, v):
    project_rows(other[...].astype(F32), gain, shift, weights, low, q, k, v)


def project_outs(rows, width, cols, turn):
    def by_step(size):
        return (6 * rows, size), BF16, spec((rows, size), lambda i, w: (2 * i + turn, 0))

    query = (2 * rows, cols), BF16, spec((rows, cols), lambda i, w: (turn, 0))
    return [by_step(width), query, by_step(cols), by_step(cols)]


def project_own(where, comp, mem, tok, gain, shift, wq, wk, wv, mine, got):
    rows, width = tok.shape
    cols = wq.shape[1] // 2
    half = spec((wq.shape[0], cols), lambda i, w: (0, w[0]))
    return call(
        project_own_kernel,
        "project_own",
        where,
        (3,),
        [whole(a) for a in (comp, mem, tok, gain[None], shift[None])]
        + [(wq, half), (wk, half), (wv, half), whole(mine), whole(got)],
        project_outs(rows, width, cols, 0)
        + [((width, 3 * cols), BF16, spec((width, 3 * cols)))],
        [pltpu.VMEM((rows, width), F32)],
        cost=LARGE,
    )


def project_other(where, other, gain, shift, weights, filled):
    rows, width = other.shape[0] // 3, other.shape[1]
    return call(
        project_other_kernel,
        "project_other",
        where,
        (3,),
        [(other, spec((rows, width), lambda i, w: (i, 0)))]
        + [whole(a) for a in (gain[None], shift[None], weights)],
        project_outs(rows, width, weights.shape[1] // 3, 1),
        cost=LARGE,
        onto=dict(enumerate(filled)),
    )


def split_pairs(where, total, height, keep, send):
    pairs = total.reshape(total.shape[0] // (2 * height), 2, height, total.shape[1])
    even = where[1] == 0
    keep[...] = jnp.where(even, pairs[:, 0], pairs[:, 1]).astype(BF16)
    send[...] = jnp.where(even, pairs[:, 1], pairs[:, 0]).astype(BF16)


def by_parity(where, total, height):
    pairs = total.reshape(total.shape[0] // (2 * height), 2, height, total.shape[1])
    even = where[1] == 0
    shape = (total.shape[0] // 2, total.shape[1])
    keep = jnp.where(even, pairs[:, 0], pairs[:, 1]).reshape(shape)
    return keep, jnp.where(even, pairs[:, 1], pairs[:, 0]).reshape(shape)


def squeeze_kernel(slots, where, mem, other, dc, dc_o, weight, stay, away, keep, send, dc_sum):
    t = where[0]
    dc_sum[...] = jnp.sum(dc[...].astype(F32), 0, keepdims=True)
    rows, width = mem.shape
    mem_o = other.at[rows : 2 * rows, :]
    padded = dc.shape[0]
    half = width // 2
    lead = 3 * 2 * slots - 2 * rows
    first = t == 0
    shape = (padded, rows)
    slot = lax.broadcasted_iota(jnp.int32, shape, 0)
    row = lax.broadcasted_iota(jnp.int32, shape, 1)
    mem_half = jnp.where(first, mem[:, :half], mem[:, half:])
    mem_o_half = jnp.where(first, mem_o[:, :half], mem_o[:, half:])

    def picked(slot_half, row_half, offset):
        place = 3 * (slot + slot_half * slots) + offset - lead
        hit = (place == row + row_half * rows) & (slot < slots)
        return jnp.where(hit, 1.0, 0.0).astype(BF16)

    def windows(slot_half):
        edge = dot(picked(slot_half, t, 2 * t), mem[...]) + dot(
            picked(slot_half, 1 - t, 2 * t), mem_o[...]
        )
        middle = dot(picked(slot_half, t, 1), mem_half) + dot(
            picked(slot_half, 1 - t, 1), mem_o_half
        )
        return ordered(first, edge, middle, 1).astype(BF16)

    both = jnp.concatenate((windows(t), windows(1 - t)), 0)
    slots_out = dot(both, weight[...])
    stay[...] = slots_out[:padded, :]
    away[...] = slots_out[padded:, :].astype(BF16)
    turned_dc = jnp.concatenate((dc[...], dc_o[...]), 0).T
    columns = both.shape[1]
    height = keep.shape[1]
    for at in range(0, columns, half):
        part = slice(at, at + half)
        total = dot(turned_dc, both[:, part])
        split_pairs(where, total, height, keep.at[:, :, part], send.at[:, :, part])


def squeeze_rows(where, dp, slots, mem, other, dc, dc_o, weight):
    padded, width = dc.shape
    half = ((dp // 2, width // dp, weight.shape[0]), BF16)
    ins = [whole(a) for a in (mem, other, dc, dc_o, weight)]
    return call(
        functools.partial(squeeze_kernel, slots),
        "squeeze",
        where,
        (1,),
        ins,
        [
            ((padded, width), F32, spec((padded, width))),
            ((padded, width), BF16, spec((padded, width))),
            half + (spec(half[0]),),
            half + (spec(half[0]),),
            ((1, width), F32, spec((1, width))),
        ],
    )


def masked_scores(place, slope, q, keys, scale, first, tail):
    bias = place[0:1, :] * slope + place[1:2, :]
    chunk = q.shape[0]
    query_place = (lax.broadcasted_iota(jnp.int32, (chunk, 1), 0) + first).astype(F32)
    scores = dot_nt(q, keys) * (scale * LOG2E) + bias
    recent = jnp.where(place[0:1, tail:] <= query_place, scores[:, tail:], NEG)
    return jnp.concatenate((scores[:, :tail], recent), 1), query_place


def attend_kernel(turn, scale, where, slopes, q, k, v, place, mix, lse):
    slope = slopes[pl.program_id(0)] * LOG2E
    rows = q.shape[0]
    first = jnp.abs(turn - where[0]) * rows
    scores, _ = masked_scores(place, slope, q[...], k[...], scale, first, k.shape[0] - 2 * rows)
    highest = jnp.max(scores, -1, keepdims=True)
    weights = jnp.exp2(scores - highest)
    total = jnp.sum(weights, -1, keepdims=True)
    mix[...] = (dot(weights.astype(BF16), v[...]) * (1.0 / total)).astype(BF16)
    lse[0] = highest + jnp.log2(total)


def attend(where, turn, slopes, q, k, v, place):
    rows, width = q.shape[0] // 2, q.shape[1]
    heads = slopes.shape[0]
    hw = width // heads
    keys = k.shape[0]
    by_head = spec((keys, hw), lambda h, w: (0, h))
    return call(
        functools.partial(attend_kernel, turn, hw**-0.5),
        "attend",
        where,
        (heads,),
        [
            (slopes, pl.BlockSpec(memory_space=pltpu.SMEM)),
            (q, spec((rows, hw), lambda h, w: (turn, h))),
            (k, by_head),
            (v, by_head),
            whole(place),
        ],
        [
            ((rows, width), BF16, spec((rows, hw), lambda h, w: (0, h))),
            ((heads, rows, 1), F32, spec((1, rows, 1), lambda h, w: (h, 0, 0))),
        ],
        cost=LARGE,
    )


def attend_back_kernel(
    chunk,
    scale,
    height,
    where,
    slopes,
    q,
    k,
    v,
    dm,
    place,
    lse_own,
    lse_other,
    dq,
    dk,
    dv,
    all_keep,
    all_send,
    slope_out,
    dk_sum,
    dv_sum,
):
    slope = slopes[pl.program_id(0)] * LOG2E
    keys = k.shape[0]
    rows = q.shape[0]
    half = rows // 2
    columns = jnp.zeros((1, keys), F32)
    by_row = jnp.zeros((1, 1), F32)
    dq_parts = []
    for step in range(rows // chunk):
        at = slice(step * chunk, (step + 1) * chunk)
        time_half = where[0] if step * chunk < half else 1 - where[0]
        scores, query_place = masked_scores(
            place,
            slope,
            q[at, :],
            k[...],
            scale,
            time_half * half + step * chunk % half,
            keys - rows,
        )
        weights = jnp.exp2(scores - (lse_own if step == 0 else lse_other)[0])
        low = weights.astype(BF16)
        grads = dot_nt(dm[at, :], v[...])
        shift = jnp.sum(weights * grads, -1, keepdims=True)
        ds = (weights * (grads - shift)).astype(BF16)
        dq_part = dot(ds, k[...]) * scale
        dq[at, :] = dq_part.astype(BF16)
        dq_parts.append(dq_part.T)
        dk_part = dot_tn(q[at, :], ds)
        dv_part = dot_tn(dm[at, :], low)
        if step == 0:
            dk_sum[...] = dk_part
            dv_sum[...] = dv_part
        else:
            dk_sum[...] += dk_part
            dv_sum[...] += dv_part
        wide = ds.astype(F32)
        columns += jnp.sum(wide, 0, keepdims=True)
        by_row += jnp.sum(jnp.sum(wide, -1, keepdims=True) * query_place, 0, keepdims=True)
    dk_all, dv_all = dk_sum[...] * scale, dv_sum[...]
    dq_all = jnp.concatenate([jnp.zeros((dk_all.shape[0], keys - rows), F32)] + dq_parts, 1)
    halves = [by_parity(where, part, height) for part in (dq_all, dk_all, dv_all)]
    for target, parts in zip((all_keep, all_send), zip(*halves)):
        blocks = [part.reshape(part.shape[0] // height, height, keys) for part in parts]
        target[...] = jnp.stack(blocks, 1).reshape(target.shape).astype(BF16)
    dk[...] = dk_all.T.astype(BF16)
    dv[...] = dv_all.T.astype(BF16)
    total = jnp.sum(columns * place[0:1, :], -1, keepdims=True) - by_row
    slope_out[...] = jnp.broadcast_to(total.reshape(1, 1, 1), slope_out.shape)


def attend_back(where, height, slopes, q, k, v, dm, place, lses):
    rows, width = q.shape
    heads = slopes.shape[0]
    hw = width // heads
    keys = k.shape[0]
    by_rows = spec((rows, hw), lambda h, w: (0, h))
    by_keys = spec((keys, hw), lambda h, w: (0, h))
    return call(
        functools.partial(attend_back_kernel, rows // 2, hw**-0.5, height),
        "attend_back",
        where,
        (heads,),
        [
            (slopes, pl.BlockSpec(memory_space=pltpu.SMEM)),
            (q, by_rows),
            (k, by_keys),
            (v, by_keys),
            (dm, by_rows),
            whole(place),
            (lses[0], spec((1, rows // 2, 1), lambda h, w: (h, 0, 0))),
            (lses[1], spec((1, rows // 2, 1), lambda h, w: (h, 0, 0))),
        ],
        [
            ((rows, width), BF16, by_rows),
            ((keys, width), BF16, by_keys),
            ((keys, width), BF16, by_keys),
            ((3 * width // 2, keys), BF16, spec((3 * hw // 2, keys), lambda h, w: (h, 0))),
            ((3 * width // 2, keys), BF16, spec((3 * hw // 2, keys), lambda h, w: (h, 0))),
            ((heads, 8, 128), F32, spec((1, 8, 128), lambda h, w: (h, 0, 0))),
        ],
        [pltpu.VMEM((hw, keys), F32), pltpu.VMEM((hw, keys), F32)],
        cost=LARGE,
    )


def gelu_pair(v):
    c = 0.7978845608028654
    inner = c * (v + 0.044715 * v * v * v)
    th = jnp.tanh(inner)
    slope = 0.5 * (1.0 + th) + 0.5 * v * (1.0 - th * th) * c * (1.0 + 3 * 0.044715 * v * v)
    return 0.5 * v * (1.0 + th), slope


def feed_kernel(height, block, where, *refs):
    (
        mix,
        far,
        tok,
        wo,
        wo_mine,
        wo_got,
        gain,
        shift,
        dy,
        wi,
        wi_mine,
        wi_got,
        bias,
        wh,
        residual,
        normed,
        act,
        grad_keep,
        grad_send,
        dy_keep,
        dy_send,
        g2,
        bias_sum,
        dy_sum,
        *sent,
        wo_far,
        weight,
    ) = refs
    step = pl.program_id(0)
    half = wi.shape[0]

    @pl.when(step == 0)
    def _():
        place_pieces(where, (wo_mine, wo_got), wo_far)
        wide_dy = dy[...].astype(F32)
        dy_sum[...] = jnp.sum(wide_dy, 0, keepdims=True)
        dy_stay, dy_away = by_parity(where, wide_dy.T, height)
        dy_keep[...] = dy_stay.astype(BF16)
        dy_send[...] = dy_away.astype(BF16)
        total = tok[...].astype(F32) + (dot(mix[...], wo[...]) + dot(far[...], wo_far[...]))
        residual[...] = total
        unit, _ = rows_stats(total)
        normed[...] = (unit * gain[...] + shift[...]).astype(BF16)

    weight[pl.ds(pl.multiple_of(where[0] * half, half), half), :] = wi[...]
    place_pieces(where, (wi_mine, wi_got), weight, (1 - where[0]) * half, half)
    pre = dot(normed[...], weight[...]) + bias[...]
    value, slope = gelu_pair(pre)
    low = value.astype(BF16)
    act[...] = low
    grad = (dot_nt(dy[...], wh[...]) * slope).astype(BF16)
    blocks = [grad[:, at : at + block] for at in range(0, grad.shape[1], block)]
    evens, odds = jnp.concatenate(blocks[::2], 1), jnp.concatenate(blocks[1::2], 1)
    even = where[1] == 0
    grad_keep[...] = jnp.where(even, evens, odds)
    grad_send[...] = jnp.where(even, odds, evens)
    bias_sum[...] = jnp.sum(grad.astype(F32), 0, keepdims=True)
    g2_part = dot_nt(grad, weight[...])

    @pl.when(step == 0)
    def _():
        g2[...] = g2_part

    @pl.when(step > 0)
    def _():
        g2[...] += g2_part

    @pl.when(step == pl.num_programs(0) - 1)
    def _():
        first_row = 0
        for piece in sent:
            piece[...] = g2[first_row : first_row + piece.shape[0], :].astype(BF16)
            first_row += piece.shape[0]


def feed(
    where, dp, turn, mix, far, tok, wo, gain, shift, dy, wi, bias, wh, second, chunk, parts, onto
):
    rows, width = dy.shape
    hidden = wh.shape[0]
    steps = hidden // chunk
    mine, got = second
    by_cols = spec((rows, chunk), lambda j, w: (turn, j))
    by_half = spec((rows, chunk // 2), lambda j, w: (turn, j))
    half = (2 * rows, hidden // 2), BF16, by_half
    turned = (width // 2, 2 * rows), BF16, spec((width // 2, rows), lambda j, w: (0, turn))
    wo_part = spec((mine.shape[0], width), lambda j, w: (0, 0))
    wi_part = spec((mine.shape[0], chunk), lambda j, w: (0, width // chunk + j))

    def once(dtype):
        return (rows, width), dtype, spec((rows, width))

    return call(
        functools.partial(feed_kernel, width // dp, hidden // (dp // 2)),
        "feed",
        where,
        (steps,),
        [
            whole(mix),
            whole(far),
            (tok, spec((rows, width), lambda j, w: (2 * turn, 0))),
            whole(wo),
            (mine, wo_part),
            (got, wo_part),
            whole(gain[None]),
            whole(shift[None]),
            whole(dy),
            (wi, spec((wi.shape[0], chunk), lambda j, w: (0, w[0] * steps + j))),
            (mine, wi_part),
            (got, wi_part),
            (bias[None], spec((1, chunk), lambda j, w: (0, w[0] * steps + j))),
            (wh, spec((chunk, width), lambda j, w: (j, 0))),
        ],
        [
            once(F32),
            ((2 * rows, width), BF16, spec((rows, width), lambda j, w: (turn, 0))),
            ((2 * rows, hidden), BF16, by_cols),
            half,
            half,
            turned,
            turned,
            once(F32),
            ((1, hidden), F32, spec((1, chunk), lambda j, w: (0, j))),
            ((1, width), F32, spec((1, width))),
        ]
        + [((rows // part, width), BF16, spec((rows // part, width))) for part in parts],
        [
            pltpu.VMEM(wo.shape, BF16),
            pltpu.VMEM((width, chunk), BF16),
        ],
        cost=LARGE,
        onto=onto,
    )


def middle_kernel(
    where,
    g_own,
    g_other,
    got_own,
    got_other,
    residual_own,
    residual_other,
    gain,
    dy,
    dy_o,
    wo,
    mix_own,
    mix_other,
    bias_sum,
    bias_sum_o,
    dy_sum,
    dc_sum,
    grad_res,
    dm,
    sums,
    keep,
    send,
):
    rows = dy.shape[0]
    lows = []
    halves = ((g_own, got_own, dy, residual_own), (g_other, got_other, dy_o, residual_other))
    for at, (g, got, d, residual) in enumerate(halves):
        here = slice(at * rows, (at + 1) * rows)
        grad = g[...] + got[...].astype(F32)
        unit, rstd = rows_stats(residual[...])
        total = d[...].astype(F32) + norm_back(grad, gain[...], unit, rstd)
        low = total.astype(BF16)
        lows.append(low)
        dm[here, :] = dot_nt(low, wo[...]).astype(BF16)
        if at == 0:
            grad_res[...] = total
            small = [jnp.sum(grad * unit, 0, keepdims=True), jnp.sum(grad, 0, keepdims=True)]
    width = dy.shape[1]
    first = where[0] == 0
    parts = [slice(at, at + width) for at in range(0, bias_sum.shape[1], width)]
    downs = [bias_sum[:, part] + bias_sum_o[:, part] for part in parts]
    small += [jnp.where(first, down, 0.0) for down in downs]
    small += [jnp.where(first, 0.0, down) for down in downs]
    small += [dy_sum[...], dc_sum[...]]
    sums[...] = jnp.concatenate(small, 0)
    split_pairs(
        where, dot_tn(lows[0], mix_own[...]) + dot_tn(lows[1], mix_other[...]), keep.shape[1], keep, send
    )


def middle(where, dp, g, got, residuals, gain, dys, wo, mix, small):
    rows, width = dys[0].shape
    heads = wo.shape[0]
    half = ((dp // 2, width // dp, heads), BF16, spec((dp // 2, width // dp, heads)))
    return call(
        middle_kernel,
        "middle",
        where,
        (1,),
        [whole(a) for a in (*g, *got, *residuals, gain[None], *dys, wo, *mix, *small)],
        [
            ((rows, width), F32, spec((rows, width))),
            ((2 * rows, heads), BF16, spec((2 * rows, heads))),
            ((8, width), F32, spec((8, width))),
            half,
            half,
        ],
        cost=LARGE,
    )


def norm_sums(step, grad, x, sums):
    unit, _ = rows_stats(x)
    rows = jnp.sum(grad * unit, 0, keepdims=True), jnp.sum(grad, 0, keepdims=True)

    @pl.when(step == 0)
    def _():
        sums[0:1, :], sums[1:2, :] = rows

    @pl.when(step > 0)
    def _():
        sums[0:1, :] += rows[0]
        sums[1:2, :] += rows[1]


def tokens_kernel(where, tok, other, dq, dk, dv, weights, g_own, sent, sums):
    step = pl.program_id(0)
    cols = dq.shape[1]
    grad = (
        dot_nt(dq[...], weights[:, :cols])
        + dot_nt(dk[...], weights[:, cols : 2 * cols])
        + dot_nt(dv[...], weights[:, 2 * cols :])
    )
    x = jnp.where(step == 0, tok[...].astype(F32), other[...].astype(F32))
    norm_sums(step, grad, x, sums)

    @pl.when(step == 0)
    def _():
        g_own[...] = grad

    @pl.when(step == 1)
    def _():
        sent[...] = grad.astype(BF16)


def tokens_back(where, tok, other, dq, dk, dv, weights):
    rows, width = tok.shape
    cols = dk.shape[1]
    late = spec((rows, cols), lambda i, w: (4 + i, 0))
    return call(
        tokens_kernel,
        "tokens_back",
        where,
        (2,),
        [
            whole(tok),
            (other, spec((rows, width), lambda i, w: (2, 0))),
            (dq, spec((rows, cols), lambda i, w: (i, 0))),
            (dk, late),
            (dv, late),
            whole(weights),
        ],
        [
            ((rows, width), F32, spec((rows, width))),
            ((rows, width), BF16, spec((rows, width))),
            ((2, width), F32, spec((2, width))),
        ],
    )


def slots_kernel(
    where, comp, mem, other, dk, dv, weights, start, slope_parts, early, sums, total
):
    step = pl.program_id(0)
    cols = dk.shape[1]
    grad = dot_nt(dk[...], weights[:, cols : 2 * cols]) + dot_nt(dv[...], weights[:, 2 * cols :])
    own = jnp.where(step == 0, comp[...].astype(F32), mem[...].astype(F32))
    x = jnp.where(step % 2 == 0, own, other[...].astype(F32))
    norm_sums(step, grad, x, total)

    @pl.when(step == pl.num_programs(0) - 1)
    def _():
        width = comp.shape[1]
        lane = lax.broadcasted_iota(jnp.int32, (1, width), 1)
        own_heads = slope_parts.shape[0]
        slope = jnp.zeros((1, width), F32)
        for head in range(own_heads):
            here = lane == where[0] * own_heads + head
            slope += jnp.where(here, slope_parts[head, 0:1, 0:1], 0.0)
        sums[:8, :] = early[...]
        rest = (total[...] + start[...], slope, jnp.zeros((5, width), F32))
        sums[8:, :] = jnp.concatenate(rest, 0)


def slots_back(where, comp, mem, other, dk, dv, weights, start, slope_parts, early):
    rows, width = comp.shape
    cols = dk.shape[1]
    by_step = spec((rows, cols), lambda i, w: (i, 0))
    return call(
        slots_kernel,
        "slots_back",
        where,
        (4,),
        [
            whole(comp),
            whole(mem),
            (other, spec((rows, width), lambda i, w: (i // 2, 0))),
            (dk, by_step),
            (dv, by_step),
            whole(weights),
            whole(start),
            whole(slope_parts),
            whole(early),
        ],
        [((16, width), F32, spec((16, width)))],
        [pltpu.VMEM((2, width), F32)],
        cost=LARGE,
    )


def turn_kernel(source, target):
    target[...] = source[...].T


def turned(array):
    return pl.pallas_call(
        turn_kernel,
        out_shape=jax.ShapeDtypeStruct(array.shape[::-1], F32),
        compiler_params=PARAMS,
        cost_estimate=TINY,
        name="turn",
    )(array)


def local(
    tokens,
    memory,
    compressed,
    mask_start,
    norm1_gain,
    norm1_bias,
    query_weight,
    key_weight,
    value_weight,
    out_weight,
    slopes,
    norm2_gain,
    norm2_bias,
    in_weight,
    in_bias,
    hidden_weight,
    hidden_bias,
    compress_weight,
    compress_bias,
    grad_out,
    grad_compressed,
):
    tokens, memory, compressed = tokens[0], memory[0], compressed[0]
    grad_out, grad_compressed = grad_out[0], grad_compressed[0]
    rows, width = tokens.shape
    heads = slopes.shape[0]
    dp = lax.axis_size("dp")
    levels = dp.bit_length() - 1
    top = levels - 1
    d = lax.axis_index("dp")
    t = lax.axis_index("tm")
    segment = 2 * rows

    def swap(block):
        return lax.ppermute(block, "tm", [(0, 1), (1, 0)])

    def across(block, mask):
        return lax.ppermute(block, "dp", [(i, i ^ mask) for i in range(dp)])

    def after(array, *earlier):
        return lax.optimization_barrier((array,) + earlier)[0]

    def bit(level):
        return (d >> level) & 1

    class Shrink:
        def __init__(self, keep, send, order, columns=False):
            shape = keep.shape if keep.ndim == 4 else keep.shape[:1] + (1,) + keep.shape[1:]
            self.pending = keep.reshape(shape), send.reshape(shape), 1
            self.order = [0] + order
            self.left = [level for level in range(1, top if columns else levels)]
            self.step = 0
            self.array = None

        def cut(self):
            if self.pending is not None:
                return self.pending[1]
            if self.step == len(self.order):
                return self.array
            level = self.order[self.step]
            if level in self.left:
                low = 1 << self.left.index(level)
                blocks, rest = self.array.shape[0], self.array.shape[1:]
                split = self.array.reshape((blocks // (2 * low), 2, low) + rest)
                keep, send = [
                    lax.dynamic_index_in_dim(split, at, 1, keepdims=False).reshape(
                        (blocks // 2,) + rest
                    )
                    for at in (bit(level), 1 - bit(level))
                ]
                self.left.remove(level)
                self.pending = keep, send, 1 << level
            else:
                size = self.array.shape[3] // 2
                keep, send = [
                    lax.dynamic_slice_in_dim(self.array, at * size, size, 3) for at in (t, 1 - t)
                ]
                self.pending = keep, send, 0
            return send

        def move(self):
            send = self.cut()
            return across(send, self.pending[2]) if self.pending[2] else swap(send)

        def take(self, got):
            keep, _, mask = self.pending
            if mask == 0:
                same = bit(top) == t
                self.pending = jnp.where(same, keep, got), jnp.where(same, got, keep), 1 << top
                return self.pending[1]
            self.step += 1
            total = keep.astype(F32) + got.astype(F32)
            last = self.step == len(self.order)
            self.array = total if last else total.astype(BF16)
            self.pending = None
            return self.array

        def add(self):
            if self.step == len(self.order):
                return self.array
            self.cut()
            if self.pending[2] == 0:
                self.take(self.move())
            return self.take(self.move())

        def wait(self, *earlier):
            if self.pending is not None:
                self.pending = (after(self.pending[0], *earlier),) + self.pending[1:]

        def finish(self):
            while self.step < len(self.order):
                self.add()
            return self.array[0]

    def meet(groups, *others):
        groups = [group for group in groups if group.step < len(group.order)]
        got = lax.optimization_barrier(tuple(group.move() for group in groups) + others)
        for group, block in zip(groups, got):
            group.take(block)
        for group in groups:
            group.cut()
        return got[len(groups) :]

    sideways = list(range(1, levels))
    upward = list(range(2, levels)) + [1] if levels > 1 else []
    between = upward[:1] + upward[-1:] + upward[1:-1] if levels > 2 else upward

    sharing = min(levels, 4)
    share = 1 << sharing
    ups = [z << 2 for z in range(1 << max(sharing - 2, 0))]
    offsets = [x + z for x in ((0, 2) if sharing > 1 else (0,)) for z in ups]
    low_bits = d & (share - 1)
    targets = [low_bits ^ off for off in offsets] + [low_bits ^ off ^ 1 for off in offsets]
    where = jnp.stack([t, bit(0)] + targets).astype(jnp.int32)

    def gather_up(piece):
        return jnp.concatenate([piece] + [across(piece, z) for z in ups[1:]], 0)

    def gather_side(block):
        return jnp.concatenate((block, across(block, 2)), 0) if sharing > 1 else block

    (joined,) = pieces(
        jnp.stack((low_bits, 1 - t)).astype(jnp.int32),
        share,
        query_weight,
        key_weight,
        value_weight,
        out_weight,
        in_weight,
    )
    joined = swap(joined)
    first_size = 3 * query_weight.shape[1] // 2
    first, second = joined[:, :first_size], joined[:, first_size:]
    slots = grad_compressed.shape[0]
    dc = jnp.pad(grad_compressed, ((0, -slots % 16), (0, 0)))
    x_other = swap(jnp.concatenate((compressed, memory, tokens), 0))
    first = gather_side(gather_up(first))
    first_got = across(first, 1)
    second_up = gather_up(after(second, first_got))
    second = gather_side(second_up)
    second_got = across(second, 1)

    *filled, qkv = project_own(
        where,
        compressed,
        memory,
        tokens,
        norm1_gain,
        norm1_bias,
        query_weight,
        key_weight,
        value_weight,
        first,
        first_got,
    )
    inputs_low, queries, keys, values = project_other(
        where, x_other, norm1_gain, norm1_bias, qkv, filled
    )
    dc_other = swap(after(dc, queries))

    index = jnp.arange(segment, dtype=jnp.int32)
    slot = jnp.where(index < rows, index + t * rows, index - rows + (1 - t) * rows)
    place = jnp.concatenate((-segment - 3 * (segment - slot), slot - segment, slot)).astype(F32)
    closed = jnp.where(slot >= mask_start[0], 0.0, NEG)
    closed = jnp.concatenate((closed, jnp.zeros((2 * segment,), F32)))
    place = jnp.stack((place, closed))
    own_heads = heads // 2
    slopes_own = lax.dynamic_slice_in_dim(slopes, t * own_heads, own_heads, 0)
    mix_other, lse_other = attend(
        where, 1, slopes_own, after(queries, second_up), keys, values, place
    )
    far_own = swap(mix_other)
    dy_other = swap(after(grad_out, mix_other))
    squeeze_stay, squeeze_away, keep, send, dc_sum = squeeze_rows(
        where, dp, slots, after(memory, mix_other), x_other, dc, dc_other, compress_weight
    )
    squeeze = Shrink(keep, send, sideways)
    squeeze_got = swap(squeeze_away)
    mix_own, lse_own = attend(
        where, 0, slopes_own, after(queries, squeeze_away), keys, values, place
    )
    far_other = swap(mix_own)
    dys = grad_out, dy_other
    mix = mix_own, mix_other
    chunk = max(in_weight.shape[1] // 8, 2 * in_weight.shape[1] // dp)

    def feed_rows(turn, mixed, far, tok, dy, parts, onto=None):
        return feed(
            where,
            dp,
            turn,
            mixed,
            far,
            tok,
            out_weight,
            norm2_gain,
            norm2_bias,
            dy,
            in_weight,
            in_bias,
            hidden_weight,
            (second, second_got),
            chunk,
            parts,
            onto,
        )

    squeeze.add()
    residual, *half_filled, g_own, bias_sum, dy_sum, sent = feed_rows(
        0, after(mix_own, squeeze.cut()), far_own, tokens, grad_out, (1,)
    )
    got_other = swap(sent)
    residual_o, *filled, g_other, bias_sum_o, _, sent = feed_rows(
        1,
        after(mix_other, sent, squeeze_got),
        far_other,
        x_other,
        dy_other,
        (1,),
        {1 + i: array for i, array in enumerate(half_filled)},
    )
    got = swap(sent), got_other
    normed, act, grad_keep, grad_send, dy_keep, dy_send = filled
    squeeze.wait(sent, got_other)
    squeeze.add()
    blocks = dp // 2

    def cut_rows(product, count):
        return product.astype(BF16).reshape(count, product.shape[0] // count, product.shape[1])

    hidden_send = dot(after(dy_send, squeeze.cut(), got_other), act).astype(BF16)
    entry_send = dot_tn(after(grad_send, hidden_send), normed).astype(BF16)
    hidden_keep = dot(after(dy_keep, entry_send), act).astype(BF16)
    entry_keep = dot_tn(after(grad_keep, hidden_keep), normed).astype(BF16)
    hidden = Shrink(cut_rows(hidden_keep, blocks), cut_rows(hidden_send, blocks), sideways)
    entry = Shrink(
        cut_rows(entry_keep, blocks // 2), cut_rows(entry_send, blocks // 2), between, True
    )
    got = after(got[0], entry_keep), got[1]
    grad_residual, grad_mixture, early, keep, send = middle(
        where,
        dp,
        (after(g_own, entry_keep), g_other),
        got,
        (residual, residual_o),
        norm2_gain,
        dys,
        out_weight,
        mix,
        (bias_sum, bias_sum_o, dy_sum, dc_sum),
    )
    mix_out = Shrink(keep, send, sideways)
    squeeze.add()
    hidden.add()
    entry.add()
    height = key_weight.shape[1] // dp
    dq, dk, dv, all_keep, all_send, slope_parts = attend_back(
        where,
        height,
        slopes_own,
        queries,
        keys,
        values,
        after(grad_mixture, hidden.cut(), entry.cut(), squeeze.cut()),
        place,
        (lse_own, lse_other),
    )
    mix_out.wait(dq)

    def cut_heads(product):
        return product.reshape(blocks // 2, -1, height, width)

    all_send = dot(all_send, inputs_low).astype(BF16)
    all_keep = dot(after(all_keep, all_send), inputs_low).astype(BF16)
    hidden.add()
    entry.add()
    left = Shrink(cut_heads(all_keep), cut_heads(all_send), sideways, True)
    mix_out.add()
    left.add()
    mix_out.cut()
    mix_out.wait(left.cut())
    mix_out.add()
    squeeze.cut()
    squeeze.wait(dq)
    squeeze.add()
    g1_own, g1_sent, token_sums = tokens_back(
        where,
        tokens,
        x_other,
        after(dq, left.cut(), hidden.cut(), entry.cut(), mix_out.cut(), squeeze.array),
        dk,
        dv,
        qkv,
    )
    g1_got = swap(g1_sent)
    mix_out.wait(g1_sent)
    mix_out.add()
    for group in (hidden, entry):
        group.wait(g1_sent)
        group.add()
    (smalls,) = slots_back(
        where,
        compressed,
        memory,
        x_other,
        after(dk, mix_out.cut(), hidden.cut(), entry.cut()),
        dv,
        qkv,
        token_sums,
        slope_parts,
        early,
    )

    def joint(array, mask):
        return lax.ppermute(array, ("dp", "tm"), [(i, i ^ mask) for i in range(2 * dp)])

    smalls, g1_got = meet((left, hidden, entry, mix_out), smalls, g1_got)
    groups = (left, hidden, entry, mix_out, squeeze)
    masks = [1 << at for at in range(levels + 1)]
    out_part = None
    while masks:
        sends = [group.cut() for group in groups]
        smalls = after(smalls, *sends)
        if len(masks) > 1 and len(masks) % 2:
            smalls = smalls + joint(smalls, masks.pop(0))
        others = smalls, joint(smalls, masks.pop(0))
        if out_part is None:
            out_part = dot(after(act, *sends), hidden_weight)
            smalls, got, out_sent = meet(groups, *others, out_part[rows:].astype(BF16))
            out_got = swap(out_sent)
        else:
            smalls, got = meet(groups, *others)
        smalls = smalls + got
    output = (residual + (out_part[:rows] + out_got.astype(F32)) + hidden_bias).astype(BF16)
    new_compressed = (
        after(squeeze_stay, sends[0])[:slots] + squeeze_got[:slots].astype(F32) + compress_bias
    ).astype(BF16)
    g1 = g1_own + g1_got.astype(F32)
    unit1, rstd1 = rows_stats(tokens.astype(F32))
    grad_tokens = (grad_residual + norm_back(g1, norm1_gain, unit1, rstd1)).astype(BF16)

    grad_query_w, grad_key_w, grad_value_w = [part.T for part in left.finish()]
    grad_in_w = turned(entry.finish()[0])
    grad_hidden_w, grad_out_w, grad_compress_w = [
        group.finish()[0].T for group in (hidden, mix_out, squeeze)
    ]
    gain2, bias2, hidden_b, compress_b, gain1, bias1, slope = [
        smalls[i] for i in (0, 1, 6, 7, 8, 9, 10)
    ]
    in_b = smalls[2:6].reshape(-1)
    return (
        output[None],
        new_compressed[None],
        grad_tokens[None],
        gain1,
        bias1,
        grad_query_w,
        grad_key_w,
        grad_value_w,
        grad_out_w,
        slope[:heads],
        gain2,
        bias2,
        grad_in_w,
        in_b,
        grad_hidden_w,
        hidden_b,
        grad_compress_w,
        compress_b,
    )


def solution(mesh):
    split, whole, kept = P("dp", "tm", None), P(), P("tm", None)
    in_specs = (
        (split,) * 3
        + (P("dp"), whole, whole)
        + (kept,) * 4
        + (whole,) * 3
        + (kept, whole, kept, whole, kept, whole)
        + (split,) * 2
    )
    shared = P("tm", "dp")
    out_specs = (
        (split,) * 3
        + (whole,) * 2
        + (shared,) * 4
        + (whole,) * 3
        + (shared, whole, shared, whole, shared, whole)
    )
    return jax.shard_map(local, mesh=mesh, in_specs=in_specs, out_specs=out_specs, check_vma=False)
```
